32 devices in a mesh: head: 4 (over x, core), blk: 8 (over z, y).
Axes of the slice: x: 2, y: 2, z: 4, core: 2. Of those that a mesh axis runs over, the one named last changes fastest.
Arguments:
- tokens: bfloat16 [8192, 2048], P(('blk', 'head')), may hold values from -6 to 6
- doc_lengths: int32 [4], replicated, may hold values from 1 to 4096, 8192 in all
- norm1_gain: bfloat16 [2048], P(('head', 'blk')), may hold values from 0.25 to 1.75
- w_query: bfloat16 [2048, 1536], P(('head', 'blk')), may hold values from -0.125 to 0.125
- w_key: bfloat16 [2048, 384], P(('head', 'blk')), may hold values from -0.125 to 0.125
- w_value: bfloat16 [2048, 384], P(('head', 'blk')), may hold values from -0.125 to 0.125
- query_gain: bfloat16 [64], replicated, may hold values from 0.25 to 1.75
- key_gain: bfloat16 [64], replicated, may hold values from 0.25 to 1.75
- w_out: bfloat16 [1536, 2048], P(('head', 'blk')), may hold values from -1.25 to 1.25
- norm2_gain: bfloat16 [2048], P(('head', 'blk')), may hold values from 0.25 to 1.75
- w_gate: bfloat16 [2048, 5120], P(('head', 'blk')), may hold values from -0.125 to 0.125
- w_up: bfloat16 [2048, 5120], P(('head', 'blk')), may hold values from -0.125 to 0.125
- w_down: bfloat16 [5120, 2048], P(('head', 'blk')), may hold values from -0.078125 to 0.078125
- cotangent: bfloat16 [8192, 2048], P(('blk', 'head')), may hold values from -6 to 6
Outputs:
- out_act: bfloat16 [8192, 2048], P(('blk', 'head'))
- d_tokens: float32 [8192, 2048], P(('blk', 'head'))
- d_norm1_gain: float32 [2048], P(('head', 'blk'))
- d_w_query: float32 [2048, 1536], P(('head', 'blk'))
- d_w_key: float32 [2048, 384], P(('head', 'blk'))
- d_w_value: float32 [2048, 384], P(('head', 'blk'))
- d_query_gain: float32 [64], replicated
- d_key_gain: float32 [64], replicated
- d_w_out: float32 [1536, 2048], P(('head', 'blk'))
- d_norm2_gain: float32 [2048], P(('head', 'blk'))
- d_w_gate: float32 [2048, 5120], P(('head', 'blk'))
- d_w_up: float32 [2048, 5120], P(('head', 'blk'))
- d_w_down: float32 [5120, 2048], P(('head', 'blk'))
The draws below stay inside these ranges and needn't reach their ends.
Inputs may be any that keep to these rules, and one draw needn't show every extreme that they name: `doc_lengths`: the documents lie end to end in order from token 0; their lengths sum to 8192 and one is exactly 4096 long.
All inputs are finite; a program needn't handle non-finite values.
Results may differ from the reference program's by a relative error of at most 0.018.
Values may be sent and summed in bfloat16 or wider, within the bound.
A program may use at most 320 MiB of HBM per device.

```python
import math
import jax
import jax.numpy as jnp
import numpy as np
from jax import lax

D = 2048
FF = 5120
QHEADS = 24
KVHEADS = 6
HEAD = 64
MAXDOC = 4096
TOKENS = 8192
DOCS = 4


def with_spikes(drawn, stream_key, source, target, blocks, factor):
    owner, partner = [(jnp.arange(drawn.shape[dim]) // (drawn.shape[dim] // blocks)).reshape([-1 if axis == dim else 1 for axis in range(drawn.ndim)]) for dim in (source, target)]
    chosen = jax.random.permutation(stream_key, blocks)[partner]
    strong = (owner == chosen) | (owner == (partner + blocks // 2) % blocks)
    return jnp.where(strong, factor * drawn, drawn)


def levels(rng, shape, cuts, least, largest):
    loudness, own = 1.0, jax.random.fold_in(rng, 6)
    for dim, blocks in cuts:
        heights = jnp.exp(jax.random.uniform(jax.random.fold_in(own, dim), (blocks,), jnp.float32, least / len(cuts), largest / len(cuts)))
        loudness = loudness * jnp.repeat(heights, shape[dim] // blocks).reshape([-1 if axis == dim else 1 for axis in range(len(shape))])
    return loudness


def profile(count, total, most, lean):
    loads = [(1 << 20) // math.isqrt(standing ** lean) + 1 for standing in range(2, count + 1)]
    rest, given = total - most - (count - 1), [1] * (count - 1)
    while rest > 0:
        candidates = [i for i in range(count - 1) if given[i] < most]
        whole, left = sum([loads[i] for i in candidates]), rest
        for i in candidates:
            extra = min(most - given[i], max(1, left * loads[i] // whole), rest)
            given[i] = given[i] + extra
            rest = rest - extra
    return np.array([most] + given)


def uneven(stream_key, amount, total, bound, skew):
    if amount == 2:
        one = jax.random.randint(stream_key, (), max(1, total - bound), min(bound, total - 1) + 1)
        return jnp.stack([one, total - one])
    lengths = jnp.asarray(profile(amount, total, bound, skew), jnp.int32)
    twos = (amount - 1) // 2
    giver, taker = lengths[1:1 + 2 * twos:2], lengths[2:2 + 2 * twos:2]
    slack = jnp.minimum(giver - 1, bound - taker)
    shifted = jax.random.randint(jax.random.fold_in(stream_key, 1), (twos,), 0, 1 << 20) % (slack + 1)
    lengths = lengths.at[1:1 + 2 * twos:2].set(giver - shifted).at[2:2 + 2 * twos:2].set(taker + shifted)
    return lengths[jax.random.permutation(jax.random.fold_in(stream_key, 2), amount)]


def noise(key, extent, width, limit, split=(), held_as=jnp.bfloat16):
    values = width * jax.random.normal(key, extent, jnp.float32)
    if split:
        values = values * levels(key, extent, split, -0.22, 0.18)
    return jnp.clip(values, -limit, limit).astype(held_as)


def gaussian_with(own_key, extent, width, most, shards, heavy, kind=jnp.bfloat16):
    array = width * jax.random.normal(own_key, extent, jnp.float32)
    if shards:
        array = array * levels(own_key, extent, shards, -0.22, 0.18)
    return jnp.clip(with_spikes(array, jax.random.fold_in(own_key, 3), *heavy), -most, most).astype(kind)


def setup_inputs(seed: int = 0) -> dict:
    keys = jax.random.split(jax.random.key(seed), 15)
    return {
        "tokens": noise(keys[0], (TOKENS, D), 1.0, 6.0, ((0, 32),)),
        "doc_lengths": uneven(keys[1], DOCS, TOKENS, MAXDOC, 1).astype(jnp.int32),
        "norm1_gain": jnp.clip(1.0 + 0.15 * jax.random.normal(keys[2], (D,), jnp.float32), 0.25, 1.75).astype(jnp.bfloat16),
        "w_query": noise(keys[3], (D, QHEADS * HEAD), D ** -0.5, 0.125, ((0, 32),)),
        "w_key": noise(keys[4], (D, KVHEADS * HEAD), D ** -0.5, 0.125, ((0, 32),)),
        "w_value": noise(keys[5], (D, KVHEADS * HEAD), D ** -0.5, 0.125, ((0, 32),)),
        "query_gain": jnp.clip(1.0 + 0.15 * jax.random.normal(keys[6], (HEAD,), jnp.float32), 0.25, 1.75).astype(jnp.bfloat16),
        "key_gain": jnp.clip(1.0 + 0.15 * jax.random.normal(keys[7], (HEAD,), jnp.float32), 0.25, 1.75).astype(jnp.bfloat16),
        "w_out": noise(keys[8], (QHEADS * HEAD, D), (QHEADS * HEAD // 64) ** -0.5, 1.25, ((0, 32),)),
        "norm2_gain": jnp.clip(1.0 + 0.15 * jax.random.normal(keys[9], (D,), jnp.float32), 0.25, 1.75).astype(jnp.bfloat16),
        "w_gate": noise(keys[10], (D, FF), D ** -0.5, 0.125, ((0, 32),)),
        "w_up": noise(keys[11], (D, FF), D ** -0.5, 0.125, ((0, 32),)),
        "w_down": noise(keys[12], (FF, D), FF ** -0.5, 0.078125, ((0, 32),)),
        "cotangent": gaussian_with(keys[13], (TOKENS, D), 1.0, 6.0, ((0, 32),), (0, 1, 32, 2.75)),
    }


@jax.custom_vjp
def low(v):
    return lax.optimization_barrier(v.astype(jnp.bfloat16)).astype(jnp.float32)

@jax.custom_vjp
def low_back(v):
    return v

def low_keep(v):
    return (low(v), None)

def low_pass(kept, grad):
    return (grad,)

def back_keep(v):
    return (v, None)

def back_low(kept, grad):
    return (low(grad),)
low.defvjp(low_keep, low_pass)
low_back.defvjp(back_keep, back_low)
EPS = 1e-06
SCALE = 0.125
NEG = -1e+30
HIGHEST = lax.Precision.HIGHEST

def norm_rows(tensor, gain_vec):
    return tensor * lax.rsqrt(lax.optimization_barrier(jnp.mean(tensor * tensor, axis=-1, keepdims=True)) + EPS) * gain_vec

def rotate(tensor, cosine, sine_table):
    half_width = tensor.shape[-1] // 2
    first_half = tensor[..., :half_width]
    second = tensor[..., half_width:]
    return jnp.concatenate([first_half * cosine - second * sine_table, second * cosine + first_half * sine_table], axis=-1)

def matmul(left_side, right_side):
    return jnp.dot(left_side, right_side, precision=HIGHEST, preferred_element_type=jnp.float32)

def attend_block(queries, key_rows, values, query_doc, query_pos, key_doc, key_pos):
    head_ratio = QHEADS // KVHEADS
    keys_all = jnp.repeat(key_rows, head_ratio, axis=1)
    values_all = jnp.repeat(values, head_ratio, axis=1)
    scores = low_back(jnp.einsum('qhd,khd->hqk', queries, keys_all, precision=HIGHEST) * SCALE)
    allowed = (query_doc[:, None] == key_doc[None, :]) & (key_pos[None, :] <= query_pos[:, None])
    scores = jnp.where(allowed[None], scores, NEG)
    row_top = lax.optimization_barrier(jnp.max(scores, axis=-1, keepdims=True))
    weights = jnp.exp(scores - row_top)
    attn_probs = weights / lax.optimization_barrier(jnp.sum(weights, axis=-1, keepdims=True))
    return jnp.einsum('hqk,khd->qhd', low(attn_probs), values_all, precision=HIGHEST)

def reference(tokens, doc_lengths, norm1_gain, w_query, w_key, w_value, query_gain, key_gain, w_out, norm2_gain, w_gate, w_up, w_down, cotangent):
    token_count = TOKENS
    key_reach = MAXDOC - 1
    block_rows = 512
    window = block_rows + key_reach
    starts = jnp.cumsum(doc_lengths) - doc_lengths
    position = jnp.arange(token_count, dtype=jnp.int32)
    inside = starts[None, :] <= position[:, None]
    doc_of = lax.optimization_barrier(jnp.sum(inside.astype(jnp.int32), axis=1)) - 1
    offset = position - lax.optimization_barrier(jnp.max(jnp.where(inside, starts[None, :], 0), axis=1))
    rope_freq = jnp.exp(-math.log(10000.0) * jnp.arange(HEAD // 2, dtype=jnp.float32) / (HEAD // 2))
    rope_angle = offset.astype(jnp.float32)[:, None] * rope_freq[None, :]
    cosine = jnp.cos(rope_angle)[:, None, :]
    sine_table = jnp.sin(rope_angle)[:, None, :]
    pad_doc = jnp.concatenate([jnp.full((key_reach,), -1, jnp.int32), doc_of.astype(jnp.int32)])
    pad_pos = jnp.arange(token_count + key_reach, dtype=jnp.int32) - key_reach
    block_ids = jnp.arange(token_count // block_rows, dtype=jnp.int32)
    block_fn = jax.checkpoint(attend_block)

    def attention(queries, key_rows, values):
        key_pad = jnp.pad(key_rows, ((key_reach, 0), (0, 0), (0, 0)))
        value_pad = jnp.pad(values, ((key_reach, 0), (0, 0), (0, 0)))

        def one_block(block_index):
            first_row = (block_index * block_rows).astype(jnp.int32)
            return block_fn(lax.dynamic_slice_in_dim(queries, first_row, block_rows, 0), lax.dynamic_slice_in_dim(key_pad, first_row, window, 0), lax.dynamic_slice_in_dim(value_pad, first_row, window, 0), lax.dynamic_slice_in_dim(doc_of, first_row, block_rows, 0), lax.dynamic_slice_in_dim(position, first_row, block_rows, 0), lax.dynamic_slice_in_dim(pad_doc, first_row, window, 0), lax.dynamic_slice_in_dim(pad_pos, first_row, window, 0))
        return lax.map(one_block, block_ids).reshape(token_count, QHEADS * HEAD)

    def layer(inputs, gain_one, query_w, key_w, value_w, query_g, key_g, out_w, gain_two, gate_w, up_w, down_w):
        normed_one = low(norm_rows(inputs, gain_one))
        query_raw = low_back(matmul(normed_one, query_w))
        key_raw = low_back(matmul(normed_one, key_w))
        value_raw = low_back(matmul(normed_one, value_w))
        query_rot = rotate(norm_rows(query_raw.reshape(token_count, QHEADS, HEAD), query_g), cosine, sine_table)
        key_rot = rotate(norm_rows(key_raw.reshape(token_count, KVHEADS, HEAD), key_g), cosine, sine_table)
        mixed = attention(low(query_rot), low(key_rot), low(value_raw.reshape(token_count, KVHEADS, HEAD)))
        mixed = low_back(low(mixed))
        resid = inputs + low_back(matmul(mixed, out_w))
        normed_two = low(norm_rows(resid, gain_two))
        gate_val = low_back(matmul(normed_two, gate_w))
        up_val = low_back(matmul(normed_two, up_w))
        hidden = low(jax.nn.silu(gate_val) * up_val)
        return resid + matmul(hidden, down_w)
    floats = [item_in.astype(jnp.float32) for item_in in (tokens, norm1_gain, w_query, w_key, w_value, query_gain, key_gain, w_out, norm2_gain, w_gate, w_up, w_down)]
    result, pull_back = jax.vjp(layer, *floats)
    grads = pull_back(cotangent.astype(jnp.float32))
    return (result.astype(jnp.bfloat16), grads[0], grads[1], grads[2], grads[3], grads[4], grads[5], grads[6], grads[7], grads[8], grads[9], grads[10], grads[11])
```

```python
import functools
import math

import jax
import jax.numpy as jnp
from jax import lax
from jax.experimental import pallas as pl
from jax.experimental.pallas import tpu as pltpu
from jax.sharding import PartitionSpec as P

QHEADS = 24
KVHEADS = 6
HEAD = 64
MAXDOC = 4096

EPS = 1e-06
SCALE = 0.125
LOG2E = 1.4426950408889634
NEG = -1e30
TILE = 256
BACK = 4
BF = jnp.bfloat16
F32 = jnp.float32


def matmul(left_side, right_side):
    return jnp.dot(left_side, right_side, preferred_element_type=F32)


def matmul_tn(left_side, right_side):
    return lax.dot_general(
        left_side, right_side, (((0,), (0,)), ((), ())), preferred_element_type=F32
    )


def matmul_nt(left_side, right_side):
    return lax.dot_general(
        left_side, right_side, (((1,), (1,)), ((), ())), preferred_element_type=F32
    )


def swap(block, axis, bit):
    count = lax.axis_size(axis)
    return lax.ppermute(block, axis, [(i, i ^ bit) for i in range(count)])


def ring(block, step):
    count = lax.axis_size("blk")
    return lax.ppermute(block, "blk", [(i, (i + step) % count) for i in range(count)])


def put(full, part, index, axis=0):
    return lax.dynamic_update_index_in_dim(full, part, index, axis)


def take(full, index, axis=0):
    return lax.dynamic_index_in_dim(full, index, axis, keepdims=False)


def gather_head(part):
    me = lax.axis_index("head")
    far = swap(part, "head", 2)
    near = swap(part, "head", 1)
    diagonal = swap(far, "head", 1)
    full = jnp.zeros((4,) + part.shape, part.dtype)
    full = put(full, part, me)
    full = put(full, near, me ^ 1)
    full = put(full, far, me ^ 2)
    return put(full, diagonal, me ^ 3)


def scatter_head(terms):
    me = lax.axis_index("head")
    got_far = swap(take(terms, me ^ 3), "head", 1)
    far = (take(terms, me ^ 2).astype(F32) + got_far.astype(F32)).astype(terms.dtype)
    got_near = swap(take(terms, me ^ 1), "head", 1)
    arrived = swap(far, "head", 2)
    return take(terms, me).astype(F32) + got_near.astype(F32) + arrived.astype(F32)


def gather_blk(part, axis=0):
    count = lax.axis_size("blk")
    line = count // 2
    place, side = lax.axis_index("blk") // 2, lax.axis_index("blk") % 2
    shape = part.shape[:axis] + (count,) + part.shape[axis:]
    full = jnp.zeros(shape, part.dtype)
    held = part
    for step in range(line):
        if step:
            held = ring(held, 2)
        other = swap(held, "blk", 1)
        source = (place - step) % line
        full = put(full, held, 2 * source + side, axis)
        full = put(full, other, 2 * source + 1 - side, axis)
    return full


def scatter_blk(chunk):
    count = lax.axis_size("blk")
    line = count // 2
    place, side = lax.axis_index("blk") // 2, lax.axis_index("blk") % 2
    total = None
    for step in range(1, line + 1):
        target = (place - step) % line
        mine = chunk(2 * target + side)
        got = swap(chunk(2 * target + 1 - side), "blk", 1)
        term = mine.astype(F32) + got.astype(F32)
        if total is not None:
            term = term + total.astype(F32)
        if step < line:
            total = ring(term.astype(BF), 2)
        else:
            total = term
    return total


def nt(left_side, right_side):
    return lax.dot_general(
        left_side, right_side, (((1,), (1,)), ((), ())), preferred_element_type=F32
    )


def nn(left_side, right_side):
    return lax.dot_general(
        left_side, right_side, (((1,), (0,)), ((), ())), preferred_element_type=F32
    )


def head_groups(meta_ref):
    odd = meta_ref[0]
    return ((4, 2 * odd, odd), (2, 4 * (1 - odd), 1 - odd))


def attend_kernel(meta_ref, query_ref, key_ref, value_ref, start_ref, out_ref, acc_ref):
    rows = query_ref.shape[1]
    base = key_ref.shape[1] - rows
    lane = lax.broadcasted_iota(jnp.int32, (TILE, 2 * HEAD), 1)
    for count, first, slot in head_groups(meta_ref):
        for tile in range(rows // TILE):
            q_at = tile * TILE
            low, high = meta_ref[1 + 2 * tile], meta_ref[2 + 2 * tile]
            queries = query_ref[pl.ds(first, count), q_at : q_at + TILE, :].reshape(
                count * TILE, 2 * HEAD
            )
            acc = acc_ref.at[pl.ds(0, count * TILE)]
            acc[...] = jnp.zeros((count * TILE, 2 * HEAD), F32)
            start_col = start_ref[q_at : q_at + TILE, :]
            q_pos = base + q_at + lax.broadcasted_iota(jnp.int32, (TILE, 1), 0)

            def step(at, carry, masked):
                k_at = pl.multiple_of(at * TILE, TILE)
                scores = nt(queries, key_ref[slot, pl.ds(k_at, TILE), :])
                if masked:
                    k_pos = k_at + lax.broadcasted_iota(jnp.int32, (1, TILE), 1)
                    allowed = (start_col <= k_pos) & (k_pos <= q_pos)
                    scores = jnp.where(
                        allowed[None], scores.reshape(count, TILE, TILE), NEG
                    ).reshape(count * TILE, TILE)
                weights = jnp.exp2(scores).astype(BF)
                acc[...] += nn(weights, value_ref[slot, pl.ds(k_at, TILE), :])
                return carry

            begin = low // TILE
            clear = jnp.minimum((high + TILE - 1) // TILE, (base + q_at) // TILE)
            last = (base + q_at) // TILE
            lax.fori_loop(begin, clear, functools.partial(step, masked=True), 0)
            lax.fori_loop(clear, last, functools.partial(step, masked=False), 0)
            step(last, 0, True)
            for j in range(count):
                part = acc_ref[j * TILE : (j + 1) * TILE, :]
                total = part[:, HEAD : HEAD + 1]
                out_ref[first + j, q_at : q_at + TILE, :] = jnp.where(
                    lane < HEAD, part / total, jnp.log2(total)
                )


def attend(meta, queries, keys, values, starts):
    heads, rows, _ = queries.shape
    return pl.pallas_call(
        attend_kernel,
        out_shape=jax.ShapeDtypeStruct((heads, rows, 2 * HEAD), F32),
        in_specs=[pl.BlockSpec(memory_space=pltpu.SMEM)]
        + [pl.BlockSpec(memory_space=pltpu.VMEM)] * 4,
        out_specs=pl.BlockSpec(memory_space=pltpu.VMEM),
        scratch_shapes=[pltpu.VMEM((4 * TILE, 2 * HEAD), F32)],
        compiler_params=pltpu.CompilerParams(vmem_limit_bytes=48 << 20),
        cost_estimate=pl.CostEstimate(
            flops=30_000_000_000, bytes_accessed=20_000_000, transcendentals=20_000_000
        ),
        name="attend",
    )(meta, queries, keys, values, starts)


def attend_back_kernel(
    meta_ref,
    key_ref,
    value_ref,
    key_t_ref,
    query_t_ref,
    grad_t_ref,
    query_ref,
    grad_ref,
    start_ref,
    dq_ref,
    dkv_ref,
):
    rows = query_ref.shape[1]
    base = key_ref.shape[1] - rows
    dkv_ref[...] = jnp.zeros_like(dkv_ref)
    dq_ref[...] = jnp.zeros_like(dq_ref)
    for count, first, slot in head_groups(meta_ref):
        for tile in range(rows // TILE):
            q_at = tile * TILE
            q_cols = slice(q_at, q_at + TILE)
            low, high = meta_ref[1 + 2 * tile], meta_ref[2 + 2 * tile]
            start_row = start_ref[:, q_cols]
            q_pos = base + q_at + lax.broadcasted_iota(jnp.int32, (1, TILE), 1)

            def step(at, carry, masked):
                k_at = pl.multiple_of(at * TILE, TILE)
                k_rows = pl.ds(k_at, TILE)
                keys = key_ref[slot, k_rows, :]
                values = value_ref[slot, k_rows, :]
                key_t = key_t_ref[slot, :, k_rows]
                if masked:
                    k_pos = k_at + lax.broadcasted_iota(jnp.int32, (TILE, 1), 0)
                    allowed = (start_row <= k_pos) & (k_pos <= q_pos)
                total = dkv_ref[slot, k_rows, :]
                for j in range(count):
                    scores = nn(keys, query_t_ref[first + j, :, q_cols])
                    if masked:
                        scores = jnp.where(allowed, scores, NEG)
                    probs = jnp.exp2(scores)
                    diff = nn(values, grad_t_ref[first + j, :, q_cols])
                    grad_score = (probs * diff).astype(BF)
                    total = (
                        total
                        + nn(probs.astype(BF), grad_ref[first + j, q_cols, :])
                        + nn(grad_score, query_ref[first + j, q_cols, :])
                    )
                    dq_ref[first + j, :, q_cols] += nn(key_t, grad_score)
                dkv_ref[slot, k_rows, :] = total
                return carry

            begin = low // TILE
            clear = jnp.minimum((high + TILE - 1) // TILE, (base + q_at) // TILE)
            last = (base + q_at) // TILE
            lax.fori_loop(begin, clear, functools.partial(step, masked=True), 0)
            lax.fori_loop(clear, last, functools.partial(step, masked=False), 0)
            step(last, 0, True)


def attend_back(meta, keys, values, keys_t, queries_t, grads_t, queries, grads, starts):
    heads, rows, _ = queries.shape
    return pl.pallas_call(
        attend_back_kernel,
        out_shape=(
            jax.ShapeDtypeStruct((heads, HEAD, rows), F32),
            jax.ShapeDtypeStruct((2, keys.shape[1], 2 * HEAD), F32),
        ),
        in_specs=[pl.BlockSpec(memory_space=pltpu.SMEM)]
        + [pl.BlockSpec(memory_space=pltpu.VMEM)] * 8,
        out_specs=(pl.BlockSpec(memory_space=pltpu.VMEM),) * 2,
        compiler_params=pltpu.CompilerParams(vmem_limit_bytes=56 << 20),
        cost_estimate=pl.CostEstimate(
            flops=70_000_000_000, bytes_accessed=40_000_000, transcendentals=20_000_000
        ),
        name="attend_back",
    )(meta, keys, values, keys_t, queries_t, grads_t, queries, grads, starts)


def norm_rows(tensor, gain_vec):
    return tensor * lax.rsqrt(jnp.mean(tensor * tensor, axis=-1, keepdims=True) + EPS) * gain_vec


def rotate(tensor, cosine, sine_table):
    half_width = tensor.shape[-1] // 2
    first_half = tensor[..., :half_width]
    second = tensor[..., half_width:]
    return jnp.concatenate(
        [first_half * cosine - second * sine_table, second * cosine + first_half * sine_table],
        axis=-1,
    )


def split_low(value, parts):
    out = []
    for _ in range(parts):
        term = lax.reduce_precision(value, 8, 7)
        out.append(term.astype(BF))
        value = value - term
    return out


def shards(
    tokens,
    doc_lengths,
    norm1_gain,
    w_query,
    w_key,
    w_value,
    query_gain,
    key_gain,
    w_out,
    norm2_gain,
    w_gate,
    w_up,
    w_down,
    cotangent,
):
    tok_rows, width = tokens.shape
    blocks = lax.axis_size("blk")
    groups = lax.axis_size("head")
    group_id = lax.axis_index("head")
    blk_place = lax.axis_index("blk")
    block_len = groups * tok_rows
    per_group = QHEADS // groups
    head_ratio = QHEADS // KVHEADS
    w_rows = w_query.shape[0]
    hidden_cols = w_gate.shape[1] // groups
    q_cols = per_group * HEAD
    firsts = [g * per_group // head_ratio for g in range(groups)]
    odd = group_id % 2

    columns = []
    for g in range(groups):
        kv = slice(firsts[g] * HEAD, (firsts[g] + 2) * HEAD)
        columns += [
            w_query[:, g * q_cols : (g + 1) * q_cols],
            w_key[:, kv],
            w_value[:, kv],
            norm1_gain[:, None],
            norm2_gain[:, None],
            jnp.zeros((w_rows, 126), BF),
        ]
    qkv_cols = q_cols + 4 * HEAD
    qkv_wide = qkv_cols + 2 * HEAD
    w_in = jnp.concatenate(columns, axis=1).reshape(w_rows, groups, qkv_wide)
    w_in = lax.all_to_all(w_in, "head", split_axis=1, concat_axis=1, tiled=True)
    w_in = gather_blk(jnp.swapaxes(w_in, 0, 1), 1).reshape(width, qkv_wide)
    w_qkv = w_in[:, :qkv_cols]
    gains = w_in[:, qkv_cols : qkv_cols + 2].astype(F32).T
    gain_one, gain_two = gains[0], gains[1]

    block_tokens = gather_head(tokens).reshape(block_len, width)

    def spread(weight):
        split = weight.reshape(w_rows, groups, hidden_cols)
        split = lax.all_to_all(split, "head", split_axis=1, concat_axis=1, tiled=True)
        return gather_blk(jnp.swapaxes(split, 0, 1), 1).reshape(width, hidden_cols)

    starts = jnp.cumsum(doc_lengths) - doc_lengths
    offsets = jnp.arange(block_len, dtype=jnp.int32)
    token_pos = blk_place * block_len + offsets
    inside = starts[None, :] <= token_pos[:, None]
    token_start = jnp.max(jnp.where(inside, starts[None, :], 0), axis=1)
    in_doc = token_pos - token_start
    rope_freq = jnp.exp(-math.log(10000.0) * jnp.arange(HEAD // 2, dtype=F32) / (HEAD // 2))
    rope_angle = in_doc.astype(F32)[:, None] * rope_freq[None, :]
    cosine = jnp.cos(rope_angle)[:, None, :]
    sine_table = jnp.sin(rope_angle)[:, None, :]
    window_start = token_start - (blk_place - BACK) * block_len
    tiles = block_len // TILE
    edges = jnp.stack(
        [window_start[:: TILE], window_start[TILE - 1 :: TILE]], axis=1
    ).reshape(2 * tiles)
    meta = jnp.concatenate([odd[None].astype(jnp.int32), edges.astype(jnp.int32)])

    query_g = query_gain.astype(F32)
    key_g = key_gain.astype(F32)
    block_inputs = block_tokens.astype(F32)
    normed_one = norm_rows(block_inputs, gain_one).astype(BF)
    raw = matmul(normed_one, w_qkv)

    def prepare(query_raw, key_raw, query_gain_in, key_gain_in):
        return (
            rotate(norm_rows(query_raw, query_gain_in), cosine, sine_table),
            rotate(norm_rows(key_raw, key_gain_in), cosine, sine_table),
        )

    query_raw = raw[:, :q_cols].reshape(block_len, per_group, HEAD)
    key_raw = raw[:, q_cols : q_cols + 2 * HEAD].reshape(block_len, 2, HEAD)
    value_own = raw[:, q_cols + 2 * HEAD :].reshape(block_len, 2, HEAD).astype(BF)
    (query_rot, key_rot), prep_pull = jax.vjp(prepare, query_raw, key_raw, query_g, key_g)
    queries = jnp.swapaxes(query_rot.astype(BF), 0, 1)
    kv_own = jnp.swapaxes(
        jnp.concatenate([key_rot.astype(BF), value_own], axis=-1), 0, 1
    )

    even = blk_place % 2 == 0
    kv_two = ring(kv_own, 2)
    kv_one = swap(jnp.where(even, kv_own, kv_two), "blk", 1)
    kv_four = ring(kv_two, 2)
    kv_three = swap(jnp.where(even, kv_two, kv_four), "blk", 1)
    window = jnp.concatenate([kv_four, kv_three, kv_two, kv_one, kv_own], axis=1)
    key_win, value_win = window[..., :HEAD], window[..., HEAD:]
    ones = jnp.ones(key_win.shape, BF)
    keys_wide = jnp.concatenate([key_win, key_win, ones, ones], axis=-1)
    values_wide = jnp.concatenate([value_win, ones], axis=-1)

    scaled = split_low(queries.astype(F32) * (SCALE * LOG2E), 2)
    attended = attend(
        meta,
        jnp.concatenate(scaled, axis=-1),
        keys_wide[..., : 2 * HEAD],
        values_wide,
        window_start[:, None],
    )
    attn_keep = attended[..., :HEAD]
    log_total = attended[..., HEAD]
    attn_out = jnp.swapaxes(attn_keep.astype(BF), 0, 1).reshape(groups, tok_rows, q_cols)
    mixed = lax.all_to_all(attn_out, "head", split_axis=0, concat_axis=0, tiled=True)
    mixed = jnp.swapaxes(mixed, 0, 1).reshape(tok_rows, QHEADS * HEAD)

    w_o = gather_head(gather_blk(w_out, 0)).reshape(QHEADS * HEAD, width)
    inputs = tokens.astype(F32)
    resid = inputs + matmul(mixed, w_o)
    normed_two_own = norm_rows(resid, gain_two).astype(BF)

    w_g, w_u = spread(w_gate), spread(w_up)
    w_d = gather_blk(w_down, 0).reshape(hidden_cols, width)
    top = gather_head(cotangent).reshape(block_len, width)
    normed_two = gather_head(normed_two_own).reshape(block_len, width)
    gate_val = matmul(normed_two, w_g)
    up_val = matmul(normed_two, w_u)
    gate_sig = jax.nn.sigmoid(gate_val)
    gate_silu = gate_val * gate_sig
    hidden = (gate_silu * up_val).astype(BF)
    out_part = matmul(hidden, w_d).astype(BF).reshape(groups, tok_rows, width)
    out_act = (resid + scatter_head(out_part)).astype(BF)
    grad_hidden = matmul_nt(top, w_d)
    grad_gate = (grad_hidden * up_val * gate_sig * (1 + gate_val * (1 - gate_sig))).astype(BF)
    grad_up = (grad_hidden * gate_silu).astype(BF)
    grad_part = (matmul_nt(grad_gate, w_g) + matmul_nt(grad_up, w_u)).astype(BF)
    grad_normed = scatter_head(grad_part.reshape(groups, tok_rows, width))
    norm_two_out, norm_two_pull = jax.vjp(norm_rows, resid, gain_two)
    grad_resid_part, grad_gain_two = norm_two_pull(grad_normed)
    grad_resid = cotangent.astype(F32) + grad_resid_part
    grad_attn = grad_resid.astype(BF)

    def by_rows(grad):
        parts = grad.astype(BF).reshape(groups, blocks, w_rows, grad.shape[1])
        return scatter_blk(lambda b: take(parts, b, 1))

    def to_owner(grad):
        back = lax.all_to_all(
            grad.astype(BF), "head", split_axis=0, concat_axis=0, tiled=True
        )
        return jnp.swapaxes(back, 0, 1).astype(F32)

    down_parts = matmul_tn(hidden, top).astype(BF).reshape(blocks, w_down.shape[0], width)
    d_w_down = scatter_blk(lambda b: take(down_parts, b))
    d_w_gate = to_owner(by_rows(matmul_tn(normed_two, grad_gate))).reshape(w_gate.shape)
    d_w_up = to_owner(by_rows(matmul_tn(normed_two, grad_up))).reshape(w_up.shape)

    out_parts = matmul_tn(mixed, grad_attn).astype(BF).reshape(groups, -1, width)
    out_slab = scatter_head(out_parts).astype(BF).reshape(blocks, w_out.shape[0], width)
    d_w_out = scatter_blk(lambda b: take(out_slab, b))
    grad_mixed = matmul_nt(grad_attn, w_o).astype(BF).reshape(tok_rows, groups, q_cols)
    grad_mix = lax.all_to_all(
        jnp.swapaxes(grad_mixed, 0, 1), "head", split_axis=0, concat_axis=0, tiled=True
    )
    grad_mix = jnp.swapaxes(grad_mix.reshape(block_len, per_group, HEAD), 0, 1)
    row_dots = jnp.sum(grad_mix.astype(F32) * attn_keep, axis=-1, keepdims=True)
    low_logs = split_low(-log_total[..., None], 3)
    low_dots = split_low(-row_dots, 2)
    blank = jnp.zeros(queries.shape, BF)
    query_t = jnp.concatenate(
        scaled + low_logs + [blank, blank[..., : HEAD - 3]], axis=-1
    )
    grad_t = jnp.concatenate([grad_mix] + low_dots + [blank[..., : HEAD - 2]], axis=-1)
    dq_t, dkv = attend_back(
        meta,
        keys_wide,
        values_wide,
        jnp.swapaxes(key_win, 1, 2),
        jnp.swapaxes(query_t, 1, 2),
        jnp.swapaxes(grad_t, 1, 2),
        jnp.concatenate([queries, blank], axis=-1),
        jnp.concatenate([blank, grad_mix], axis=-1),
        window_start[None, :],
    )
    grad_queries = jnp.transpose(dq_t, (2, 0, 1)) * SCALE

    four, three, two, one, own = [
        dkv[:, i * block_len : (i + 1) * block_len] for i in range(BACK + 1)
    ]
    got_one = swap(one.astype(BF), "blk", 1).astype(F32)
    got_three = swap(three.astype(BF), "blk", 1).astype(F32)
    four = four + jnp.where(even, 0.0, got_three)
    two = two + jnp.where(even, got_three, got_one)
    own = own + jnp.where(even, got_one, 0.0)
    two = two + ring(four.astype(BF), -2).astype(F32)
    own = own + ring(two.astype(BF), -2).astype(F32)
    kv_grad = jnp.swapaxes(own, 0, 1)
    grad_keys = kv_grad[..., :HEAD] * SCALE
    grad_values = kv_grad[..., HEAD:]

    grad_query_raw, grad_key_raw, grad_query_g, grad_key_g = prep_pull((grad_queries, grad_keys))
    raw_grads = jnp.concatenate(
        [
            grad_query_raw.reshape(block_len, q_cols),
            grad_key_raw.reshape(block_len, 2 * HEAD),
            grad_values.reshape(block_len, 2 * HEAD),
        ],
        axis=1,
    ).astype(BF)
    grad_w_in = matmul_tn(normed_one, raw_grads)
    normed_part = matmul_nt(raw_grads, w_qkv).astype(BF)
    grad_normed_one = scatter_head(normed_part.reshape(groups, tok_rows, width))
    norm_one_out, norm_one_pull = jax.vjp(norm_rows, inputs, gain_one)
    grad_input_part, grad_gain_one = norm_one_pull(grad_normed_one)
    d_tokens = grad_resid + grad_input_part
    grad_w_in = jnp.concatenate(
        [
            grad_w_in,
            grad_gain_one[:, None],
            grad_gain_two[:, None],
            jnp.zeros((width, 126), F32),
        ],
        axis=1,
    )
    owned = to_owner(by_rows(grad_w_in))
    d_w_query = owned[:, :, :q_cols].reshape(w_rows, QHEADS * HEAD)
    key_heads, value_heads = [], []
    for head_id in range(KVHEADS):
        keys_of, values_of = [], []
        for g in range(groups):
            for slot in range(2):
                if firsts[g] + slot == head_id:
                    at = q_cols + slot * HEAD
                    keys_of.append(owned[:, g, at : at + HEAD])
                    at += 2 * HEAD
                    values_of.append(owned[:, g, at : at + HEAD])
        key_heads.append(functools.reduce(jnp.add, keys_of))
        value_heads.append(functools.reduce(jnp.add, values_of))
    d_w_key = jnp.concatenate(key_heads, axis=1)
    d_w_value = jnp.concatenate(value_heads, axis=1)
    d_norm1_gain = jnp.sum(owned[:, :, qkv_cols], axis=1)
    d_norm2_gain = jnp.sum(owned[:, :, qkv_cols + 1], axis=1)
    gain_sums = lax.psum((grad_query_g, grad_key_g), ("head", "blk"))
    return (
        out_act,
        d_tokens,
        d_norm1_gain,
        d_w_query,
        d_w_key,
        d_w_value,
        gain_sums[0],
        gain_sums[1],
        d_w_out,
        d_norm2_gain,
        d_w_gate,
        d_w_up,
        d_w_down,
    )


def solution(mesh):
    by_token = P(("blk", "head"), None)
    by_row = P(("head", "blk"), None)
    by_entry = P(("head", "blk"))
    in_specs = (
        by_token,
        P(),
        by_entry,
        by_row,
        by_row,
        by_row,
        P(),
        P(),
        by_row,
        by_entry,
        by_row,
        by_row,
        by_row,
        by_token,
    )
    out_specs = (
        by_token,
        by_token,
        by_entry,
        by_row,
        by_row,
        by_row,
        P(),
        P(),
        by_row,
        by_entry,
        by_row,
        by_row,
        by_row,
    )
    return jax.shard_map(shards, mesh=mesh, in_specs=in_specs, out_specs=out_specs, check_vma=False)
```

```python
import functools
import math

import jax
import jax.numpy as jnp
from jax import lax
from jax.experimental import pallas as pl
from jax.experimental.pallas import tpu as pltpu
from jax.sharding import PartitionSpec as P

QHEADS = 24
KVHEADS = 6
HEAD = 64
MAXDOC = 4096

EPS = 1e-06
SCALE = 0.125
LOG2E = 1.4426950408889634
NEG = -1e30
TILE = 256
BACK = 4
BF = jnp.bfloat16
F32 = jnp.float32


def matmul(left_side, right_side):
    return jnp.dot(left_side, right_side, preferred_element_type=F32)


def matmul_tn(left_side, right_side):
    return lax.dot_general(
        left_side, right_side, (((0,), (0,)), ((), ())), preferred_element_type=F32
    )


def matmul_nt(left_side, right_side):
    return lax.dot_general(
        left_side, right_side, (((1,), (1,)), ((), ())), preferred_element_type=F32
    )


def swap(block, axis, bit):
    count = lax.axis_size(axis)
    return lax.ppermute(block, axis, [(i, i ^ bit) for i in range(count)])


def ring(block, step):
    count = lax.axis_size("blk")
    return lax.ppermute(block, "blk", [(i, (i + step) % count) for i in range(count)])


def put(full, part, index, axis=0):
    return lax.dynamic_update_index_in_dim(full, part, index, axis)


def take(full, index, axis=0):
    return lax.dynamic_index_in_dim(full, index, axis, keepdims=False)


def gather_head(part):
    me = lax.axis_index("head")
    far = swap(part, "head", 2)
    near = swap(part, "head", 1)
    diagonal = swap(far, "head", 1)
    full = jnp.zeros((4,) + part.shape, part.dtype)
    full = put(full, part, me)
    full = put(full, near, me ^ 1)
    full = put(full, far, me ^ 2)
    return put(full, diagonal, me ^ 3)


def scatter_head(terms):
    me = lax.axis_index("head")
    got_far = swap(take(terms, me ^ 3), "head", 1)
    far = (take(terms, me ^ 2).astype(F32) + got_far.astype(F32)).astype(terms.dtype)
    got_near = swap(take(terms, me ^ 1), "head", 1)
    arrived = swap(far, "head", 2)
    return take(terms, me).astype(F32) + got_near.astype(F32) + arrived.astype(F32)


def place_of():
    at = lax.axis_index("blk")
    return at // 2, at % 2, lax.axis_size("blk") // 2


class LineGather:
    def __init__(self, part, axis=0):
        self.place, _, self.line = place_of()
        self.axis = axis
        shape = part.shape[:axis] + (self.line,) + part.shape[axis:]
        self.full = put(jnp.zeros(shape, part.dtype), part, self.place, axis)
        self.held = part
        self.step = 0

    def send(self):
        self.step += 1
        self.held = ring(self.held, 2)
        return self.held

    def keep(self):
        source = (self.place - self.step) % self.line
        self.full = put(self.full, self.held, source, self.axis)

    def ahead(self, steps):
        for _ in range(steps):
            self.send()
            self.keep()


class LineScatter:
    def __init__(self, chunk):
        self.place, _, self.line = place_of()
        self.chunk = chunk
        self.step = 1
        self.total = chunk((self.place - 1) % self.line)

    def send(self):
        self.total = ring(self.total.astype(BF), 2)
        return self.total

    def add(self):
        self.step += 1
        mine = self.chunk((self.place - self.step) % self.line)
        self.total = self.total.astype(F32) + mine.astype(F32)

    def ahead(self, steps):
        for _ in range(steps):
            self.send()
            self.add()


def gather_blk(part, axis=0):
    place, side, line = place_of()
    shape = part.shape[:axis] + (line, 2) + part.shape[axis:]
    full = jnp.zeros(shape, part.dtype)
    held = part

    def store(full, block, source, side):
        block = block.reshape(block.shape[:axis] + (1, 1) + block.shape[axis:])
        at = [0] * full.ndim
        at[axis], at[axis + 1] = source, side
        return lax.dynamic_update_slice(full, block, at)

    for step in range(line):
        if step:
            held = ring(held, 2)
        other = swap(held, "blk", 1)
        source = (place - step) % line
        full = store(full, held, source, side)
        full = store(full, other, source, 1 - side)
    return full


def scatter_blk(chunk):
    place, side, line = place_of()
    total = None
    for step in range(1, line + 1):
        target = (place - step) % line
        mine = chunk(2 * target + side)
        got = swap(chunk(2 * target + 1 - side), "blk", 1)
        term = mine.astype(F32) + got.astype(F32)
        if total is not None:
            term = term + total.astype(F32)
        if step < line:
            total = ring(term.astype(BF), 2)
        else:
            total = term
    return total


def gather_pair(part):
    me = lax.axis_index("head")
    side = lax.axis_index("blk") % 2
    half = part.shape[0] // 2
    near = swap(part, "head", 1)
    far = swap(part, "head", 2)
    across = swap(part, "blk", 1)
    corner = jnp.concatenate(
        [swap(far[:half], "blk", 1), swap(across[half:], "head", 2)], axis=0
    )
    full = jnp.zeros((2, 4) + part.shape, part.dtype)

    def store(full, block, side, head):
        return lax.dynamic_update_slice(
            full, block[None, None], [side, head] + [0] * part.ndim
        )

    full = store(full, part, side, me)
    full = store(full, near, side, me ^ 1)
    for block, to_side, to_head in (
        (far, side, me ^ 2),
        (across, 1 - side, me),
        (corner, 1 - side, me ^ 2),
    ):
        full = store(full, block, to_side, to_head)
        full = store(full, swap(block, "head", 1), to_side, to_head ^ 1)
    return full


def scatter_pair(terms):
    me = lax.axis_index("head")
    side = lax.axis_index("blk") % 2
    half = terms.shape[2] // 2

    def pick(to_side, to_head):
        rest = [0] * (terms.ndim - 2)
        return lax.dynamic_slice(
            terms, [to_side, to_head] + rest, (1, 1) + terms.shape[2:]
        ).reshape(terms.shape[2:])

    def both(to_side, to_head):
        got = swap(pick(to_side, to_head ^ 1), "head", 1)
        return pick(to_side, to_head).astype(F32) + got.astype(F32)

    corner = both(1 - side, me ^ 2).astype(BF)
    top = swap(corner[:half], "blk", 1)
    bottom = swap(corner[half:], "head", 2)
    far = both(side, me ^ 2)
    across = both(1 - side, me)
    far = jnp.concatenate([far[:half] + top.astype(F32), far[half:]], axis=0)
    across = jnp.concatenate([across[:half], across[half:] + bottom.astype(F32)], axis=0)
    got_far = swap(far.astype(BF), "head", 2)
    got_across = swap(across.astype(BF), "blk", 1)
    return both(side, me) + got_far.astype(F32) + got_across.astype(F32)


def sum_all(values):
    for bit in (1, 2):
        values = values + swap(values, "head", bit)
    bit = 1
    while bit < lax.axis_size("blk"):
        values = values + swap(values, "blk", bit)
        bit *= 2
    return values


def sync(*trees):
    return lax.optimization_barrier(trees)


def nt(left_side, right_side):
    return lax.dot_general(
        left_side, right_side, (((1,), (1,)), ((), ())), preferred_element_type=F32
    )


def nn(left_side, right_side):
    return lax.dot_general(
        left_side, right_side, (((1,), (0,)), ((), ())), preferred_element_type=F32
    )


def head_groups(meta_ref):
    odd = meta_ref[0]
    return ((4, 2 * odd, odd), (2, 4 * (1 - odd), 1 - odd))


def attend_kernel(meta_ref, query_ref, key_ref, value_ref, start_ref, out_ref, acc_ref):
    rows = query_ref.shape[1]
    base = key_ref.shape[1] - rows
    lane = lax.broadcasted_iota(jnp.int32, (TILE, 2 * HEAD), 1)
    for count, first, slot in head_groups(meta_ref):
        for tile in range(rows // TILE):
            q_at = tile * TILE
            low, high = meta_ref[1 + 2 * tile], meta_ref[2 + 2 * tile]
            queries = query_ref[pl.ds(first, count), q_at : q_at + TILE, :].reshape(
                count * TILE, 2 * HEAD
            )
            acc = acc_ref.at[pl.ds(0, count * TILE)]
            acc[...] = jnp.zeros((count * TILE, 2 * HEAD), F32)
            start_col = start_ref[q_at : q_at + TILE, :]
            q_pos = base + q_at + lax.broadcasted_iota(jnp.int32, (TILE, 1), 0)

            def step(at, carry, masked):
                k_at = pl.multiple_of(at * TILE, TILE)
                scores = nt(queries, key_ref[slot, pl.ds(k_at, TILE), :])
                if masked:
                    k_pos = k_at + lax.broadcasted_iota(jnp.int32, (1, TILE), 1)
                    allowed = (start_col <= k_pos) & (k_pos <= q_pos)
                    scores = jnp.where(
                        allowed[None], scores.reshape(count, TILE, TILE), NEG
                    ).reshape(count * TILE, TILE)
                weights = jnp.exp2(scores).astype(BF)
                acc[...] += nn(weights, value_ref[slot, pl.ds(k_at, TILE), :])
                return carry

            begin = low // TILE
            clear = jnp.minimum((high + TILE - 1) // TILE, (base + q_at) // TILE)
            last = (base + q_at) // TILE
            lax.fori_loop(begin, clear, functools.partial(step, masked=True), 0)
            lax.fori_loop(clear, last, functools.partial(step, masked=False), 0)
            step(last, 0, True)
            for j in range(count):
                part = acc_ref[j * TILE : (j + 1) * TILE, :]
                total = part[:, HEAD : HEAD + 1]
                out_ref[first + j, q_at : q_at + TILE, :] = jnp.where(
                    lane < HEAD, part / total, jnp.log2(total)
                )


def attend(meta, queries, keys, values, starts):
    heads, rows, _ = queries.shape
    return pl.pallas_call(
        attend_kernel,
        out_shape=jax.ShapeDtypeStruct((heads, rows, 2 * HEAD), F32),
        in_specs=[pl.BlockSpec(memory_space=pltpu.SMEM)]
        + [pl.BlockSpec(memory_space=pltpu.VMEM)] * 4,
        out_specs=pl.BlockSpec(memory_space=pltpu.VMEM),
        scratch_shapes=[pltpu.VMEM((4 * TILE, 2 * HEAD), F32)],
        compiler_params=pltpu.CompilerParams(vmem_limit_bytes=48 << 20),
        cost_estimate=pl.CostEstimate(
            flops=30_000_000_000, bytes_accessed=20_000_000, transcendentals=20_000_000
        ),
        name="attend",
    )(meta, queries, keys, values, starts)


def attend_back_kernel(
    meta_ref,
    key_ref,
    value_ref,
    key_t_ref,
    query_t_ref,
    grad_t_ref,
    query_ref,
    grad_ref,
    start_ref,
    dq_ref,
    dkv_ref,
):
    rows = query_ref.shape[1]
    base = key_ref.shape[1] - rows
    dkv_ref[...] = jnp.zeros_like(dkv_ref)
    dq_ref[...] = jnp.zeros_like(dq_ref)
    for count, first, slot in head_groups(meta_ref):
        for tile in range(rows // TILE):
            q_at = tile * TILE
            q_cols = slice(q_at, q_at + TILE)
            low, high = meta_ref[1 + 2 * tile], meta_ref[2 + 2 * tile]
            start_row = start_ref[:, q_cols]
            q_pos = base + q_at + lax.broadcasted_iota(jnp.int32, (1, TILE), 1)

            def step(at, carry, masked):
                k_at = pl.multiple_of(at * TILE, TILE)
                k_rows = pl.ds(k_at, TILE)
                keys = key_ref[slot, k_rows, :]
                values = value_ref[slot, k_rows, :]
                key_t = key_t_ref[slot, :, k_rows]
                if masked:
                    k_pos = k_at + lax.broadcasted_iota(jnp.int32, (TILE, 1), 0)
                    allowed = (start_row <= k_pos) & (k_pos <= q_pos)
                total = dkv_ref[slot, k_rows, :]
                for j in range(count):
                    scores = nn(keys, query_t_ref[first + j, :, q_cols])
                    if masked:
                        scores = jnp.where(allowed, scores, NEG)
                    probs = jnp.exp2(scores)
                    diff = nn(values, grad_t_ref[first + j, :, q_cols])
                    grad_score = (probs * diff).astype(BF)
                    total = (
                        total
                        + nn(probs.astype(BF), grad_ref[first + j, q_cols, :])
                        + nn(grad_score, query_ref[first + j, q_cols, :])
                    )
                    dq_ref[first + j, :, q_cols] += nn(key_t, grad_score)
                dkv_ref[slot, k_rows, :] = total
                return carry

            begin = low // TILE
            clear = jnp.minimum((high + TILE - 1) // TILE, (base + q_at) // TILE)
            last = (base + q_at) // TILE
            lax.fori_loop(begin, clear, functools.partial(step, masked=True), 0)
            lax.fori_loop(clear, last, functools.partial(step, masked=False), 0)
            step(last, 0, True)


def attend_back(meta, keys, values, keys_t, queries_t, grads_t, queries, grads, starts):
    heads, rows, _ = queries.shape
    return pl.pallas_call(
        attend_back_kernel,
        out_shape=(
            jax.ShapeDtypeStruct((heads, HEAD, rows), F32),
            jax.ShapeDtypeStruct((2, keys.shape[1], 2 * HEAD), F32),
        ),
        in_specs=[pl.BlockSpec(memory_space=pltpu.SMEM)]
        + [pl.BlockSpec(memory_space=pltpu.VMEM)] * 8,
        out_specs=(pl.BlockSpec(memory_space=pltpu.VMEM),) * 2,
        compiler_params=pltpu.CompilerParams(vmem_limit_bytes=56 << 20),
        cost_estimate=pl.CostEstimate(
            flops=70_000_000_000, bytes_accessed=40_000_000, transcendentals=20_000_000
        ),
        name="attend_back",
    )(meta, keys, values, keys_t, queries_t, grads_t, queries, grads, starts)


def norm_rows(tensor, gain_vec):
    return tensor * lax.rsqrt(jnp.mean(tensor * tensor, axis=-1, keepdims=True) + EPS) * gain_vec


def rotate(tensor, cosine, sine_table):
    half_width = tensor.shape[-1] // 2
    first_half = tensor[..., :half_width]
    second = tensor[..., half_width:]
    return jnp.concatenate(
        [first_half * cosine - second * sine_table, second * cosine + first_half * sine_table],
        axis=-1,
    )


def split_low(value, parts):
    out = []
    for _ in range(parts):
        term = lax.reduce_precision(value, 8, 7)
        out.append(term.astype(BF))
        value = value - term
    return out


def shards(
    tokens,
    doc_lengths,
    norm1_gain,
    w_query,
    w_key,
    w_value,
    query_gain,
    key_gain,
    w_out,
    norm2_gain,
    w_gate,
    w_up,
    w_down,
    cotangent,
):
    tok_rows, width = tokens.shape
    blocks = lax.axis_size("blk")
    groups = lax.axis_size("head")
    group_id = lax.axis_index("head")
    blk_place = lax.axis_index("blk")
    block_len = groups * tok_rows
    per_group = QHEADS // groups
    head_ratio = QHEADS // KVHEADS
    w_rows = w_query.shape[0]
    line = blocks // 2
    side = blk_place % 2
    ff_rows = w_down.shape[0]
    ff_cols = line * ff_rows
    q_cols = per_group * HEAD
    firsts = [g * per_group // head_ratio for g in range(groups)]
    odd = group_id % 2

    columns = []
    for g in range(groups):
        kv = slice(firsts[g] * HEAD, (firsts[g] + 2) * HEAD)
        columns += [
            w_query[:, g * q_cols : (g + 1) * q_cols],
            w_key[:, kv],
            w_value[:, kv],
            norm1_gain[:, None],
            norm2_gain[:, None],
            jnp.zeros((w_rows, 126), BF),
        ]
    qkv_cols = q_cols + 4 * HEAD
    qkv_wide = qkv_cols + 2 * HEAD
    w_in = jnp.concatenate(columns, axis=1).reshape(w_rows, groups, qkv_wide)
    w_in = lax.all_to_all(w_in, "head", split_axis=1, concat_axis=1, tiled=True)
    down = LineGather(w_down)
    down.ahead(line - 4)
    down_moved = down.send()
    w_in = gather_blk(jnp.swapaxes(w_in, 0, 1), 1).reshape(width, qkv_wide)
    block_tokens = gather_head(tokens).reshape(block_len, width)

    def by_unit(weight):
        return weight.reshape(w_rows, groups, line, 2, ff_rows)

    both = jnp.stack([by_unit(w_gate), by_unit(w_up)], axis=3)
    both = jnp.transpose(both, (4, 1, 0, 3, 2, 5)).reshape(2, groups, w_rows, 2 * ff_cols)
    w_in, block_tokens, both, down_moved = sync(w_in, block_tokens, both, down_moved)
    down.held = down_moved
    down.keep()

    other = swap(take(both, 1 - side), "blk", 1)
    both = put(jnp.zeros(both.shape, BF), take(both, side), side)
    both = put(both, other, 1 - side)
    both = lax.all_to_all(
        jnp.swapaxes(both, 0, 1), "head", split_axis=0, concat_axis=0, tiled=True
    )
    gate_up = LineGather(both, 1)
    gate_up.ahead(line - 4)
    down_moved = down.send()
    gate_up_moved = gate_up.send()

    w_qkv = w_in[:, :qkv_cols]
    gains = w_in[:, qkv_cols : qkv_cols + 2].astype(F32).T
    gain_one, gain_two = gains[0], gains[1]

    starts = jnp.cumsum(doc_lengths) - doc_lengths
    offsets = jnp.arange(block_len, dtype=jnp.int32)
    token_pos = blk_place * block_len + offsets
    inside = starts[None, :] <= token_pos[:, None]
    token_start = jnp.max(jnp.where(inside, starts[None, :], 0), axis=1)
    in_doc = token_pos - token_start
    rope_freq = jnp.exp(-math.log(10000.0) * jnp.arange(HEAD // 2, dtype=F32) / (HEAD // 2))
    rope_angle = in_doc.astype(F32)[:, None] * rope_freq[None, :]
    cosine = jnp.cos(rope_angle)[:, None, :]
    sine_table = jnp.sin(rope_angle)[:, None, :]
    window_start = token_start - (blk_place - BACK) * block_len
    tiles = block_len // TILE
    edges = jnp.stack(
        [window_start[::TILE], window_start[TILE - 1 :: TILE]], axis=1
    ).reshape(2 * tiles)
    meta = jnp.concatenate([odd[None].astype(jnp.int32), edges.astype(jnp.int32)])

    query_g = query_gain.astype(F32)
    key_g = key_gain.astype(F32)
    block_inputs = block_tokens.astype(F32)
    normed_one = norm_rows(block_inputs, gain_one).astype(BF)
    raw = matmul(normed_one, w_qkv)

    def prepare(query_raw, key_raw, query_gain_in, key_gain_in):
        return (
            rotate(norm_rows(query_raw, query_gain_in), cosine, sine_table),
            rotate(norm_rows(key_raw, key_gain_in), cosine, sine_table),
        )

    query_raw = raw[:, :q_cols].reshape(block_len, per_group, HEAD)
    key_raw = raw[:, q_cols : q_cols + 2 * HEAD].reshape(block_len, 2, HEAD)
    value_own = raw[:, q_cols + 2 * HEAD :].reshape(block_len, 2, HEAD).astype(BF)
    (query_rot, key_rot), prep_pull = jax.vjp(prepare, query_raw, key_raw, query_g, key_g)
    queries = jnp.swapaxes(query_rot.astype(BF), 0, 1)
    kv_own = jnp.swapaxes(
        jnp.concatenate([key_rot.astype(BF), value_own], axis=-1), 0, 1
    )
    kv_own, down_moved, gate_up_moved = sync(kv_own, down_moved, gate_up_moved)
    down.held, gate_up.held = down_moved, gate_up_moved
    down.keep()
    gate_up.keep()

    down_moved = down.send()
    even = side == 0
    kv_two = ring(kv_own, 2)
    kv_one = swap(jnp.where(even, kv_own, kv_two), "blk", 1)
    kv_four = ring(kv_two, 2)
    kv_three = swap(jnp.where(even, kv_two, kv_four), "blk", 1)
    window = jnp.concatenate([kv_four, kv_three, kv_two, kv_one, kv_own], axis=1)
    key_win, value_win = window[..., :HEAD], window[..., HEAD:]
    ones = jnp.ones(key_win.shape, BF)
    keys_wide = jnp.concatenate([key_win, key_win, ones, ones], axis=-1)
    values_wide = jnp.concatenate([value_win, ones], axis=-1)

    scaled = split_low(queries.astype(F32) * (SCALE * LOG2E), 2)
    keys_wide, values_wide, down_moved, w_out, cotangent = sync(
        keys_wide, values_wide, down_moved, w_out, cotangent
    )
    down.held = down_moved
    down.keep()
    gate_up_moved = gate_up.send()
    top = gather_pair(cotangent).reshape(2 * block_len, width)
    w_o = gather_blk(w_out, 0).reshape(blocks * w_out.shape[0], width)
    attended = attend(
        meta,
        jnp.concatenate(scaled, axis=-1),
        keys_wide[..., : 2 * HEAD],
        values_wide,
        window_start[:, None],
    )
    attended, gate_up_moved, top, w_o = sync(attended, gate_up_moved, top, w_o)
    gate_up.held = gate_up_moved
    gate_up.keep()
    gate_up_moved = gate_up.send()
    w_o = gather_head(w_o).reshape(QHEADS * HEAD, width)
    attn_keep = attended[..., :HEAD]
    log_total = attended[..., HEAD]
    attn_out = jnp.swapaxes(attn_keep.astype(BF), 0, 1).reshape(groups, tok_rows, q_cols)
    mixed = lax.all_to_all(attn_out, "head", split_axis=0, concat_axis=0, tiled=True)
    mixed = jnp.swapaxes(mixed, 0, 1).reshape(tok_rows, QHEADS * HEAD)
    inputs = tokens.astype(F32)
    resid = inputs + matmul(mixed, w_o)
    normed_two_own = norm_rows(resid, gain_two).astype(BF)

    normed_two = gather_pair(normed_two_own).reshape(2 * block_len, width)
    gate_up.held = gate_up_moved
    gate_up.keep()
    w_gu = gate_up.full
    w_gu = w_gu.reshape(width, 2 * ff_cols)
    w_d = down.full.reshape(ff_cols, width)
    gate_up_val = matmul(normed_two, w_gu)
    gate_val, up_val = gate_up_val[:, :ff_cols], gate_up_val[:, ff_cols:]
    gate_sig = jax.nn.sigmoid(gate_val)
    gate_silu = gate_val * gate_sig
    hidden = (gate_silu * up_val).astype(BF)
    out_part = matmul(hidden, w_d).astype(BF).reshape(2, groups, tok_rows, width)
    grad_hidden = matmul_nt(top, w_d)
    grad_gate = (grad_hidden * up_val * gate_sig * (1 + gate_val * (1 - gate_sig))).astype(BF)
    grad_up = (grad_hidden * gate_silu).astype(BF)
    grad_gu = jnp.concatenate([grad_gate, grad_up], axis=1)
    grad_part = matmul_nt(grad_gu, w_gu).astype(BF)
    grad_part, hidden, grad_gu, out_part = sync(grad_part, hidden, grad_gu, out_part)

    down_parts = matmul_tn(hidden, top).astype(BF).reshape(line, ff_rows, width)
    gu_parts = matmul_tn(normed_two, grad_gu).astype(BF)
    gu_parts = gu_parts.reshape(groups, line, 2, w_rows, 2 * ff_cols)
    grad_normed = scatter_pair(grad_part.reshape(2, groups, tok_rows, width))
    norm_two_out, norm_two_pull = jax.vjp(norm_rows, resid, gain_two)
    grad_resid_part, grad_gain_two = norm_two_pull(grad_normed)
    grad_resid = cotangent.astype(F32) + grad_resid_part
    grad_attn = grad_resid.astype(BF)
    grad_attn, down_parts, gu_parts, out_part = sync(grad_attn, down_parts, gu_parts, out_part)

    down_sum = LineScatter(lambda p: take(down_parts, p))
    gu_sum = LineScatter(lambda p: take(gu_parts, p, 1))
    down_sum.ahead(line - 4)
    gu_sum.ahead(line - 4)
    down_moved, gu_moved = down_sum.send(), gu_sum.send()
    grad_mixed = matmul_nt(grad_attn, w_o).astype(BF).reshape(tok_rows, groups, q_cols)
    grad_mix = lax.all_to_all(
        jnp.swapaxes(grad_mixed, 0, 1), "head", split_axis=0, concat_axis=0, tiled=True
    )
    out_parts = matmul_tn(mixed, grad_attn).astype(BF).reshape(groups, -1, width)
    grad_mix = jnp.swapaxes(grad_mix.reshape(block_len, per_group, HEAD), 0, 1)
    row_dots = jnp.sum(grad_mix.astype(F32) * attn_keep, axis=-1, keepdims=True)
    low_logs = split_low(-log_total[..., None], 3)
    low_dots = split_low(-row_dots, 2)
    blank = jnp.zeros(queries.shape, BF)
    query_t = jnp.concatenate(
        scaled + low_logs + [blank, blank[..., : HEAD - 3]], axis=-1
    )
    grad_t = jnp.concatenate([grad_mix] + low_dots + [blank[..., : HEAD - 2]], axis=-1)
    query_t, grad_t = jnp.swapaxes(query_t, 1, 2), jnp.swapaxes(grad_t, 1, 2)
    query_t, grad_t, down_moved, gu_moved, out_part, out_parts = sync(
        query_t, grad_t, down_moved, gu_moved, out_part, out_parts
    )
    down_sum.total, gu_sum.total = down_moved, gu_moved
    down_sum.add()
    gu_sum.add()
    down_moved, gu_moved = down_sum.send(), gu_sum.send()
    out_act = (resid + scatter_pair(out_part)).astype(BF)
    out_slab = scatter_head(out_parts).astype(BF).reshape(blocks, w_out.shape[0], width)
    dq_t, dkv = attend_back(
        meta,
        keys_wide,
        values_wide,
        jnp.swapaxes(key_win, 1, 2),
        query_t,
        grad_t,
        jnp.concatenate([queries, blank], axis=-1),
        jnp.concatenate([blank, grad_mix], axis=-1),
        window_start[None, :],
    )
    dq_t, dkv, down_moved, gu_moved, out_act, out_slab = sync(
        dq_t, dkv, down_moved, gu_moved, out_act, out_slab
    )
    down_sum.total, gu_sum.total = down_moved, gu_moved
    down_sum.add()
    gu_sum.add()
    grad_queries = jnp.transpose(dq_t, (2, 0, 1)) * SCALE

    four, three, two, one, own = [
        dkv[:, i * block_len : (i + 1) * block_len] for i in range(BACK + 1)
    ]
    got_three = swap(three.astype(BF), "blk", 1).astype(F32)
    got_one = swap(one.astype(BF), "blk", 1).astype(F32)
    four = four + jnp.where(even, 0.0, got_three)
    two = two + jnp.where(even, got_three, got_one)
    own = own + jnp.where(even, got_one, 0.0)
    two = two + ring(four.astype(BF), -2).astype(F32)
    own = own + ring(two.astype(BF), -2).astype(F32)
    down_moved, gu_moved = down_sum.send(), gu_sum.send()
    own, down_moved, gu_moved = sync(own, down_moved, gu_moved)
    down_sum.total, gu_sum.total = down_moved, gu_moved
    down_sum.add()
    gu_sum.add()
    d_w_down = down_sum.total
    kv_grad = jnp.swapaxes(own, 0, 1)
    grad_keys = kv_grad[..., :HEAD] * SCALE
    grad_values = kv_grad[..., HEAD:]

    def to_owner(grad):
        back = lax.all_to_all(
            grad.astype(BF), "head", split_axis=0, concat_axis=0, tiled=True
        )
        return jnp.swapaxes(back, 0, 1).astype(F32)

    gu_own = gu_sum.total.astype(BF)
    mine = take(gu_own, side, 1)
    got = swap(take(gu_own, 1 - side, 1), "blk", 1)
    gu_own = put(jnp.zeros((groups, w_rows, 2, 2 * ff_cols), BF), mine, side, 2)
    gu_own = put(gu_own, got, 1 - side, 2)
    gu_own = to_owner(gu_own)
    gu_own = gu_own.reshape(w_rows, groups, 2, 2, line, ff_rows)
    gu_own = jnp.transpose(gu_own, (3, 0, 1, 4, 2, 5)).reshape((2,) + w_gate.shape)
    d_w_gate, d_w_up = gu_own[0], gu_own[1]

    d_w_out = scatter_blk(lambda b: take(out_slab, b))

    grad_query_raw, grad_key_raw, grad_query_g, grad_key_g = prep_pull((grad_queries, grad_keys))
    gain_sums = sum_all(jnp.stack([grad_query_g, grad_key_g]))
    raw_grads = jnp.concatenate(
        [
            grad_query_raw.reshape(block_len, q_cols),
            grad_key_raw.reshape(block_len, 2 * HEAD),
            grad_values.reshape(block_len, 2 * HEAD),
        ],
        axis=1,
    ).astype(BF)
    grad_w_in = matmul_tn(normed_one, raw_grads)
    normed_part = matmul_nt(raw_grads, w_qkv).astype(BF)
    grad_normed_one = scatter_head(normed_part.reshape(groups, tok_rows, width))
    norm_one_out, norm_one_pull = jax.vjp(norm_rows, inputs, gain_one)
    grad_input_part, grad_gain_one = norm_one_pull(grad_normed_one)
    d_tokens = grad_resid + grad_input_part
    grad_w_in = jnp.concatenate(
        [
            grad_w_in,
            grad_gain_one[:, None],
            grad_gain_two[:, None],
            jnp.zeros((width, 126), F32),
        ],
        axis=1,
    )
    in_parts = grad_w_in.astype(BF).reshape(groups, blocks, w_rows, qkv_wide)
    owned = to_owner(scatter_blk(lambda b: take(in_parts, b, 1)))
    d_w_query = owned[:, :, :q_cols].reshape(w_rows, QHEADS * HEAD)
    key_heads, value_heads = [], []
    for head_id in range(KVHEADS):
        keys_of, values_of = [], []
        for g in range(groups):
            for slot in range(2):
                if firsts[g] + slot == head_id:
                    at = q_cols + slot * HEAD
                    keys_of.append(owned[:, g, at : at + HEAD])
                    at += 2 * HEAD
                    values_of.append(owned[:, g, at : at + HEAD])
        key_heads.append(functools.reduce(jnp.add, keys_of))
        value_heads.append(functools.reduce(jnp.add, values_of))
    d_w_key = jnp.concatenate(key_heads, axis=1)
    d_w_value = jnp.concatenate(value_heads, axis=1)
    d_norm1_gain = jnp.sum(owned[:, :, qkv_cols], axis=1)
    d_norm2_gain = jnp.sum(owned[:, :, qkv_cols + 1], axis=1)
    return (
        out_act,
        d_tokens,
        d_norm1_gain,
        d_w_query,
        d_w_key,
        d_w_value,
        gain_sums[0],
        gain_sums[1],
        d_w_out,
        d_norm2_gain,
        d_w_gate,
        d_w_up,
        d_w_down,
    )


def solution(mesh):
    by_token = P(("blk", "head"), None)
    by_row = P(("head", "blk"), None)
    by_entry = P(("head", "blk"))
    in_specs = (
        by_token,
        P(),
        by_entry,
        by_row,
        by_row,
        by_row,
        P(),
        P(),
        by_row,
        by_entry,
        by_row,
        by_row,
        by_row,
        by_token,
    )
    out_specs = (
        by_token,
        by_token,
        by_entry,
        by_row,
        by_row,
        by_row,
        P(),
        P(),
        by_row,
        by_entry,
        by_row,
        by_row,
        by_row,
    )
    return jax.shard_map(shards, mesh=mesh, in_specs=in_specs, out_specs=out_specs, check_vma=False)
```

```python
import functools
import math

import jax
import jax.numpy as jnp
from jax import lax
from jax.experimental import pallas as pl
from jax.experimental.pallas import tpu as pltpu
from jax.sharding import PartitionSpec as P

QHEADS = 24
KVHEADS = 6
HEAD = 64
MAXDOC = 4096

EPS = 1e-06
SCALE = 0.125
LOG2E = 1.4426950408889634
NEG = -1e30
TILE = 256
BACK = 4
BF = jnp.bfloat16
F32 = jnp.float32


def matmul(left_side, right_side):
    return jnp.dot(left_side, right_side, preferred_element_type=F32)


def matmul_tn(left_side, right_side):
    return lax.dot_general(
        left_side, right_side, (((0,), (0,)), ((), ())), preferred_element_type=F32
    )


def matmul_nt(left_side, right_side):
    return lax.dot_general(
        left_side, right_side, (((1,), (1,)), ((), ())), preferred_element_type=F32
    )


def swap(block, axis, bit):
    count = lax.axis_size(axis)
    return lax.ppermute(block, axis, [(i, i ^ bit) for i in range(count)])


def ring(block, step):
    count = lax.axis_size("blk")
    return lax.ppermute(block, "blk", [(i, (i + step) % count) for i in range(count)])


def put(full, part, index, axis=0):
    return lax.dynamic_update_index_in_dim(full, part, index, axis)


def take(full, index, axis=0):
    return lax.dynamic_index_in_dim(full, index, axis, keepdims=False)


def gather_head(part):
    me = lax.axis_index("head")
    far = swap(part, "head", 2)
    near = swap(part, "head", 1)
    diagonal = swap(far, "head", 1)
    full = jnp.zeros((4,) + part.shape, part.dtype)
    full = put(full, part, me)
    full = put(full, near, me ^ 1)
    full = put(full, far, me ^ 2)
    return put(full, diagonal, me ^ 3)


def scatter_head(terms):
    me = lax.axis_index("head")
    got_far = swap(take(terms, me ^ 3), "head", 1)
    far = (take(terms, me ^ 2).astype(F32) + got_far.astype(F32)).astype(terms.dtype)
    got_near = swap(take(terms, me ^ 1), "head", 1)
    arrived = swap(far, "head", 2)
    return take(terms, me).astype(F32) + got_near.astype(F32) + arrived.astype(F32)


def place_of():
    at = lax.axis_index("blk")
    return at // 2, at % 2, lax.axis_size("blk") // 2


class LineGather:
    def __init__(self, part, axis=0):
        self.place, _, self.line = place_of()
        self.axis = axis
        shape = part.shape[:axis] + (self.line,) + part.shape[axis:]
        self.full = put(jnp.zeros(shape, part.dtype), part, self.place, axis)
        self.held = part
        self.step = 0

    def send(self):
        self.step += 1
        self.held = ring(self.held, 2)
        return self.held

    def keep(self):
        source = (self.place - self.step) % self.line
        self.full = put(self.full, self.held, source, self.axis)

    def ahead(self, steps):
        for _ in range(steps):
            self.send()
            self.keep()


class LineScatter:
    def __init__(self, chunk):
        self.place, _, self.line = place_of()
        self.chunk = chunk
        self.step = 1
        self.total = chunk((self.place - 1) % self.line)

    def send(self):
        self.total = ring(self.total.astype(BF), 2)
        return self.total

    def add(self):
        self.step += 1
        mine = self.chunk((self.place - self.step) % self.line)
        self.total = self.total.astype(F32) + mine.astype(F32)

    def ahead(self, steps):
        for _ in range(steps):
            self.send()
            self.add()


def gather_blk(part, axis=0):
    place, side, line = place_of()
    shape = part.shape[:axis] + (line, 2) + part.shape[axis:]
    full = jnp.zeros(shape, part.dtype)
    held = part

    def store(full, block, source, side):
        block = block.reshape(block.shape[:axis] + (1, 1) + block.shape[axis:])
        at = [0] * full.ndim
        at[axis], at[axis + 1] = source, side
        return lax.dynamic_update_slice(full, block, at)

    for step in range(line):
        if step:
            held = ring(held, 2)
        other = swap(held, "blk", 1)
        source = (place - step) % line
        full = store(full, held, source, side)
        full = store(full, other, source, 1 - side)
    return full


def scatter_blk(chunk):
    place, side, line = place_of()
    total = None
    for step in range(1, line + 1):
        target = (place - step) % line
        mine = chunk(2 * target + side)
        got = swap(chunk(2 * target + 1 - side), "blk", 1)
        term = mine.astype(F32) + got.astype(F32)
        if total is not None:
            term = term + total.astype(F32)
        if step < line:
            total = ring(term.astype(BF), 2)
        else:
            total = term
    return total


def gather_pair(part):
    me = lax.axis_index("head")
    side = lax.axis_index("blk") % 2
    half = part.shape[0] // 2
    near = swap(part, "head", 1)
    far = swap(part, "head", 2)
    across = swap(part, "blk", 1)
    corner = jnp.concatenate(
        [swap(far[:half], "blk", 1), swap(across[half:], "head", 2)], axis=0
    )
    full = jnp.zeros((2, 4) + part.shape, part.dtype)

    def store(full, block, side, head):
        return lax.dynamic_update_slice(
            full, block[None, None], [side, head] + [0] * part.ndim
        )

    full = store(full, part, side, me)
    full = store(full, near, side, me ^ 1)
    for block, to_side, to_head in (
        (far, side, me ^ 2),
        (across, 1 - side, me),
        (corner, 1 - side, me ^ 2),
    ):
        full = store(full, block, to_side, to_head)
        full = store(full, swap(block, "head", 1), to_side, to_head ^ 1)
    return full


def scatter_pair(terms):
    me = lax.axis_index("head")
    side = lax.axis_index("blk") % 2
    half = terms.shape[2] // 2

    def pick(to_side, to_head):
        rest = [0] * (terms.ndim - 2)
        return lax.dynamic_slice(
            terms, [to_side, to_head] + rest, (1, 1) + terms.shape[2:]
        ).reshape(terms.shape[2:])

    def both(to_side, to_head):
        got = swap(pick(to_side, to_head ^ 1), "head", 1)
        return pick(to_side, to_head).astype(F32) + got.astype(F32)

    corner = both(1 - side, me ^ 2).astype(BF)
    top = swap(corner[:half], "blk", 1)
    bottom = swap(corner[half:], "head", 2)
    far = both(side, me ^ 2)
    across = both(1 - side, me)
    far = jnp.concatenate([far[:half] + top.astype(F32), far[half:]], axis=0)
    across = jnp.concatenate([across[:half], across[half:] + bottom.astype(F32)], axis=0)
    got_far = swap(far.astype(BF), "head", 2)
    got_across = swap(across.astype(BF), "blk", 1)
    return both(side, me) + got_far.astype(F32) + got_across.astype(F32)


def sum_all(values):
    for bit in (1, 2):
        values = values + swap(values, "head", bit)
    bit = 1
    while bit < lax.axis_size("blk"):
        values = values + swap(values, "blk", bit)
        bit *= 2
    return values


def sync(*trees):
    return lax.optimization_barrier(trees)


def nt(left_side, right_side):
    return lax.dot_general(
        left_side, right_side, (((1,), (1,)), ((), ())), preferred_element_type=F32
    )


def nn(left_side, right_side):
    return lax.dot_general(
        left_side, right_side, (((1,), (0,)), ((), ())), preferred_element_type=F32
    )


def head_groups(meta_ref):
    odd = meta_ref[0]
    return ((4, 2 * odd, odd), (2, 4 * (1 - odd), 1 - odd))


def attend_kernel(meta_ref, query_ref, key_ref, value_ref, start_ref, out_ref, acc_ref):
    rows = query_ref.shape[1]
    base = key_ref.shape[1] - rows
    lane = lax.broadcasted_iota(jnp.int32, (TILE, 2 * HEAD), 1)
    for count, first, slot in head_groups(meta_ref):
        for tile in range(rows // TILE):
            q_at = tile * TILE
            low, high = meta_ref[1 + 2 * tile], meta_ref[2 + 2 * tile]
            queries = query_ref[pl.ds(first, count), q_at : q_at + TILE, :].reshape(
                count * TILE, 2 * HEAD
            )
            acc = acc_ref.at[pl.ds(0, count * TILE)]
            acc[...] = jnp.zeros((count * TILE, 2 * HEAD), F32)
            start_col = start_ref[q_at : q_at + TILE, :]
            q_pos = base + q_at + lax.broadcasted_iota(jnp.int32, (TILE, 1), 0)

            def step(at, carry, masked):
                k_at = pl.multiple_of(at * TILE, TILE)
                scores = nt(queries, key_ref[slot, pl.ds(k_at, TILE), :])
                if masked:
                    k_pos = k_at + lax.broadcasted_iota(jnp.int32, (1, TILE), 1)
                    allowed = (start_col <= k_pos) & (k_pos <= q_pos)
                    scores = jnp.where(
                        allowed[None], scores.reshape(count, TILE, TILE), NEG
                    ).reshape(count * TILE, TILE)
                weights = jnp.exp2(scores).astype(BF)
                acc[...] += nn(weights, value_ref[slot, pl.ds(k_at, TILE), :])
                return carry

            begin = low // TILE
            clear = jnp.minimum((high + TILE - 1) // TILE, (base + q_at) // TILE)
            last = (base + q_at) // TILE
            lax.fori_loop(begin, clear, functools.partial(step, masked=True), 0)
            lax.fori_loop(clear, last, functools.partial(step, masked=False), 0)
            step(last, 0, True)
            for j in range(count):
                part = acc_ref[j * TILE : (j + 1) * TILE, :]
                total = part[:, HEAD : HEAD + 1]
                out_ref[first + j, q_at : q_at + TILE, :] = jnp.where(
                    lane < HEAD, part / total, jnp.log2(total)
                )


def attend(meta, queries, keys, values, starts):
    heads, rows, _ = queries.shape
    return pl.pallas_call(
        attend_kernel,
        out_shape=jax.ShapeDtypeStruct((heads, rows, 2 * HEAD), F32),
        in_specs=[pl.BlockSpec(memory_space=pltpu.SMEM)]
        + [pl.BlockSpec(memory_space=pltpu.VMEM)] * 4,
        out_specs=pl.BlockSpec(memory_space=pltpu.VMEM),
        scratch_shapes=[pltpu.VMEM((4 * TILE, 2 * HEAD), F32)],
        compiler_params=pltpu.CompilerParams(vmem_limit_bytes=48 << 20),
        cost_estimate=pl.CostEstimate(
            flops=30_000_000_000, bytes_accessed=20_000_000, transcendentals=20_000_000
        ),
        name="attend",
    )(meta, queries, keys, values, starts)


def attend_back_kernel(
    meta_ref,
    key_ref,
    value_ref,
    key_t_ref,
    query_t_ref,
    grad_t_ref,
    query_ref,
    grad_ref,
    start_ref,
    dq_ref,
    dkv_ref,
):
    rows = query_ref.shape[1]
    base = key_ref.shape[1] - rows
    dkv_ref[...] = jnp.zeros_like(dkv_ref)
    dq_ref[...] = jnp.zeros_like(dq_ref)
    for count, first, slot in head_groups(meta_ref):
        for tile in range(rows // TILE):
            q_at = tile * TILE
            q_cols = slice(q_at, q_at + TILE)
            low, high = meta_ref[1 + 2 * tile], meta_ref[2 + 2 * tile]
            start_row = start_ref[:, q_cols]
            q_pos = base + q_at + lax.broadcasted_iota(jnp.int32, (1, TILE), 1)

            def step(at, carry, masked):
                k_at = pl.multiple_of(at * TILE, TILE)
                k_rows = pl.ds(k_at, TILE)
                keys = key_ref[slot, k_rows, :]
                values = value_ref[slot, k_rows, :]
                key_t = key_t_ref[slot, :, k_rows]
                if masked:
                    k_pos = k_at + lax.broadcasted_iota(jnp.int32, (TILE, 1), 0)
                    allowed = (start_row <= k_pos) & (k_pos <= q_pos)
                total = dkv_ref[slot, k_rows, :]
                for j in range(count):
                    scores = nn(keys, query_t_ref[first + j, :, q_cols])
                    if masked:
                        scores = jnp.where(allowed, scores, NEG)
                    probs = jnp.exp2(scores)
                    diff = nn(values, grad_t_ref[first + j, :, q_cols])
                    grad_score = (probs * diff).astype(BF)
                    total = (
                        total
                        + nn(probs.astype(BF), grad_ref[first + j, q_cols, :])
                        + nn(grad_score, query_ref[first + j, q_cols, :])
                    )
                    dq_ref[first + j, :, q_cols] += nn(key_t, grad_score)
                dkv_ref[slot, k_rows, :] = total
                return carry

            begin = low // TILE
            clear = jnp.minimum((high + TILE - 1) // TILE, (base + q_at) // TILE)
            last = (base + q_at) // TILE
            lax.fori_loop(begin, clear, functools.partial(step, masked=True), 0)
            lax.fori_loop(clear, last, functools.partial(step, masked=False), 0)
            step(last, 0, True)


def attend_back(meta, keys, values, keys_t, queries_t, grads_t, queries, grads, starts):
    heads, rows, _ = queries.shape
    return pl.pallas_call(
        attend_back_kernel,
        out_shape=(
            jax.ShapeDtypeStruct((heads, HEAD, rows), F32),
            jax.ShapeDtypeStruct((2, keys.shape[1], 2 * HEAD), F32),
        ),
        in_specs=[pl.BlockSpec(memory_space=pltpu.SMEM)]
        + [pl.BlockSpec(memory_space=pltpu.VMEM)] * 8,
        out_specs=(pl.BlockSpec(memory_space=pltpu.VMEM),) * 2,
        compiler_params=pltpu.CompilerParams(vmem_limit_bytes=56 << 20),
        cost_estimate=pl.CostEstimate(
            flops=70_000_000_000, bytes_accessed=40_000_000, transcendentals=20_000_000
        ),
        name="attend_back",
    )(meta, keys, values, keys_t, queries_t, grads_t, queries, grads, starts)


MESH = pl.DeviceIdType.MESH
HEADS_OUT, SLAB, NEAR, FAR, ACROSS, FAR_ON, ACROSS_ON = 0, 3, 7, 8, 9, 10, 11
CORNER_TOP, CORNER_LOW, CORNER_ON, TO_MATE = 12, 13, 14, 15
BACK_TOP, BACK_LOW, BACK_FAR, BACK_ACROSS, HEADS_BACK, SUM_ON = 19, 20, 21, 22, 23, 26
TRANSFERS = 30
SPANS = ((0, 256), (256, 256), (512, 128))


def transposed(block):
    return jnp.swapaxes(block, 0, 1)


def middle_kernel(
    slabs,
    line,
    attn_ref,
    tokens_ref,
    w_out_ref,
    gain_ref,
    w_down_ref,
    top_ref,
    *refs,
):
    slab_refs = refs[:slabs]
    (
        resid_out,
        grad_out,
        grad_low_out,
        mixed_out,
        heads_out,
        part_out,
        gu_out,
        gu_next,
        down_out,
        gain_out,
        mixed,
        acts,
        tops,
        w_gu,
        w_dn,
        hidden,
        grad_gu,
        pairs,
        got,
        stage,
        in_far,
        in_across,
        in_top,
        in_low,
        resid,
        turned,
        gu_stage,
        sends,
        recvs,
        locals_,
    ) = refs[slabs:]
    me, at = lax.axis_index("head"), lax.axis_index("blk")
    count = lax.axis_size("blk")
    side, place = at % 2, at // 2
    odd = me % 2
    mate, beside, corner = me + 1 - 2 * odd, (me + 2) % 4, (me + 3 - 2 * odd) % 4
    other = at + 1 - 2 * side
    after, before = (at + 2) % count, (at + count - 2) % count
    rows, width = tokens_ref.shape
    half = rows // 2
    cols = mixed.shape[1] // 4
    units = w_dn.shape[0]
    slab_rows = slab_refs[0].shape[1]

    barrier = pltpu.get_barrier_semaphore()
    peers = ((mate, at), (beside, at), (corner, at), (me, other), (me, after), (me, before))
    for peer in peers:
        pl.semaphore_signal(barrier, inc=1, device_id=peer, device_id_type=MESH)
    pl.semaphore_wait(barrier, len(peers))

    def remote(index, source, target, device):
        return pltpu.make_async_remote_copy(
            src_ref=source,
            dst_ref=target,
            send_sem=sends.at[index],
            recv_sem=recvs.at[index],
            device_id=device,
            device_id_type=MESH,
        )

    def local(index, source, target):
        return pltpu.make_async_copy(source, target, locals_.at[index])

    def mixed_cols(head):
        return mixed.at[:, pl.ds(pl.multiple_of(head * cols, 128), cols)]

    heads = [
        remote(HEADS_OUT + i, attn_ref.at[to], mixed_cols(me), (to, at))
        for i, to in enumerate((mate, beside, corner))
    ]
    for copy in heads:
        copy.start()
    own_heads = local(0, attn_ref.at[me], mixed_cols(me))
    own_heads.start()
    load_out = [
        local(1 + i, w_out_ref.at[pl.ds(i * rows, rows)], pairs.at[i]) for i in range(6)
    ]
    for copy in load_out:
        copy.start()

    def slab_at(head, source):
        start = pl.multiple_of((head * line + source) * slab_rows, 16)
        return w_gu.at[pl.ds(start, slab_rows)]

    last = (place + line - (slabs - 1)) % line
    slab_on = [
        remote(SLAB + h, slab_refs[-1].at[h], slab_at(h, last), (me, after)) for h in range(4)
    ]
    for copy in slab_on:
        copy.start()
    load_slabs = [
        local(7 + 4 * i + h, ref.at[h], slab_at(h, (place + line - i) % line))
        for i, ref in enumerate(slab_refs)
        for h in range(4)
    ]
    for copy in load_slabs:
        copy.start()
    base_sem = 7 + 4 * slabs
    load_down = local(base_sem, w_down_ref, w_dn)
    load_down.start()
    load_top = local(base_sem + 1, top_ref, tops)
    load_top.start()

    for copy in heads:
        copy.wait_recv()
    own_heads.wait()
    for copy in load_out:
        copy.wait()
    keep_mixed = local(base_sem + 2, mixed, mixed_out)
    keep_mixed.start()

    def resid_cols(step, carry):
        span = pl.ds(pl.multiple_of(step * 256, 256), 256)
        weight = pairs[0:6, :, span].reshape(6 * rows, 256)
        resid[:, span] = tokens_ref[:, span].astype(F32) + nn(mixed[...], weight)
        return carry

    lax.fori_loop(0, width // 256, resid_cols, 0)
    slot = side * 4 + me

    def norm_tile(step, carry):
        tile = pl.ds(pl.multiple_of(step * 32, 32), 32)
        block = resid[tile, :]
        scale = lax.rsqrt(jnp.mean(block * block, axis=1, keepdims=True) + EPS)
        acts[slot, tile, :] = (block * scale * gain_ref[...]).astype(BF)
        return carry

    lax.fori_loop(0, rows // 32, norm_tile, 0)
    keep_resid = local(base_sem + 3, resid, resid_out)
    keep_resid.start()

    far_slot, across_slot = side * 4 + beside, (1 - side) * 4 + me
    corner_slot = (1 - side) * 4 + beside
    near = remote(NEAR, acts.at[slot], acts.at[slot], (mate, at))
    far = remote(FAR, acts.at[slot], acts.at[slot], (beside, at))
    across = remote(ACROSS, acts.at[slot], acts.at[slot], (me, other))
    far_on = remote(FAR_ON, acts.at[far_slot], acts.at[far_slot], (mate, at))
    across_on = remote(ACROSS_ON, acts.at[across_slot], acts.at[across_slot], (mate, at))
    corner_on = remote(CORNER_ON, acts.at[corner_slot], acts.at[corner_slot], (mate, at))
    far_top = acts.at[far_slot, pl.ds(0, half)]
    across_low = acts.at[across_slot, pl.ds(half, half)]
    corner_top = remote(CORNER_TOP, far_top, far_top, (me, other))
    corner_low = remote(CORNER_LOW, across_low, across_low, (beside, at))
    near.start()
    far.start()
    across.start()
    for copy in load_slabs:
        copy.wait()
    for copy in slab_on:
        copy.wait_recv()
    load_down.wait()
    load_top.wait()

    def chunk(c, carry):
        its_side = (side + c // 2) % 2
        its_head = (me + 2 * (c % 2)) % 4
        pair = its_side * 4 + its_head - its_head % 2

        @pl.when(c == 0)
        def _():
            near.wait_recv()

        @pl.when(c == 1)
        def _():
            far.wait_recv()
            far_on.start()
            corner_top.start()
            across.wait_recv()
            across_on.start()
            corner_low.start()
            far_on.wait_recv()

        @pl.when(c == 2)
        def _():
            corner_top.wait_recv()
            corner_low.wait_recv()
            corner_on.start()
            across_on.wait_recv()

        @pl.when(c == 3)
        def _():
            corner_on.wait_recv()

        for first, size in SPANS:
            block = acts[pl.ds(pair, 2)].reshape(2 * rows, width)
            gate = nn(block, w_gu[:, first : first + size])
            up = nn(block, w_gu[:, units + first : units + first + size])
            grad = nt(
                tops[pl.ds(pair, 2)].reshape(2 * rows, width), w_dn[first : first + size, :]
            )
            sig = jax.nn.sigmoid(gate)
            silu = gate * sig
            shape = (2, rows, size)
            hidden[pl.ds(pair, 2), :, first : first + size] = (
                (silu * up).astype(BF).reshape(shape)
            )
            grad_gu[pl.ds(pair, 2), :, first : first + size] = (
                (grad * up * sig * (1 + gate * (1 - sig))).astype(BF).reshape(shape)
            )
            grad_gu[pl.ds(pair, 2), :, units + first : units + first + size] = (
                (grad * silu).astype(BF).reshape(shape)
            )

        def grad_cols(step, carry):
            span = pl.ds(pl.multiple_of(step * 256, 256), 256)
            block = grad_gu[pl.ds(pair, 2)].reshape(2 * rows, 2 * units)
            part = nt(block, w_gu[span, :])
            pairs[pl.ds(2 * c, 2), :, span] = part.astype(BF).reshape(2, rows, 256)
            return carry

        lax.fori_loop(0, width // 256, grad_cols, 0)
        remote(TO_MATE + c, pairs.at[2 * c + 1 - odd], got.at[c], (mate, at)).start()

        @pl.when(c > 0)
        def _():
            local(base_sem + 4, stage, part_out.at[pl.ds(0, 2)]).wait()

        def out_cols(step, carry):
            span = pl.ds(pl.multiple_of(step * 256, 256), 256)
            block = hidden[pl.ds(pair, 2)].reshape(2 * rows, units)
            part = nn(block, w_dn[:, span])
            stage[:, :, span] = part.astype(BF).reshape(2, rows, 256)
            return carry

        lax.fori_loop(0, width // 256, out_cols, 0)
        local(base_sem + 4, stage, part_out.at[pl.ds(pair, 2)]).start()
        return carry

    lax.fori_loop(0, 4, chunk, 0)

    def to_mate(c):
        return remote(TO_MATE + c, pairs.at[2 * c + 1 - odd], got.at[c], (mate, at))

    def add_rows(c, first, extra):
        def tile(step, carry):
            span = pl.ds(pl.multiple_of(first + step * 32, 32), 32)
            total = pairs[2 * c + odd, span, :].astype(F32) + got[c, span, :].astype(F32)
            for ref in extra:
                total = total + ref[pl.ds(pl.multiple_of(step * 32, 32), 32), :].astype(F32)
            pairs[2 * c + odd, span, :] = total.astype(BF)
            return carry

        lax.fori_loop(0, half // 32, tile, 0)

    back_top = remote(
        BACK_TOP, pairs.at[6 + odd, pl.ds(0, half)], in_top, (me, other)
    )
    back_low = remote(
        BACK_LOW, pairs.at[6 + odd, pl.ds(half, half)], in_low, (beside, at)
    )
    back_far = remote(BACK_FAR, pairs.at[2 + odd], in_far, (beside, at))
    back_across = remote(BACK_ACROSS, pairs.at[4 + odd], in_across, (me, other))
    to_mate(3).wait_recv()
    add_rows(3, 0, ())
    back_top.start()
    add_rows(3, half, ())
    back_low.start()
    to_mate(1).wait_recv()
    to_mate(2).wait_recv()
    add_rows(1, half, ())
    add_rows(2, 0, ())

    local(base_sem + 4, stage, part_out.at[pl.ds(0, 2)]).wait()

    def gu_rows(step, carry):
        span = pl.ds(pl.multiple_of(step * 256, 256), 256)
        turned[...] = transposed(acts[:, :, span].reshape(8 * rows, 256))
        buffer = step % 2

        @pl.when(step > 1)
        def _():
            local(base_sem + 5 + buffer, gu_stage.at[buffer], gu_out.at[pl.ds(0, 256)]).wait()

        for n in range(2 * units // 256):
            part = nn(
                turned[...],
                grad_gu[:, :, n * 256 : (n + 1) * 256].reshape(8 * rows, 256),
            )
            gu_stage[buffer, :, n * 256 : (n + 1) * 256] = part.astype(BF)
        local(base_sem + 5 + buffer, gu_stage.at[buffer], gu_out.at[span]).start()
        return carry

    lax.fori_loop(0, 5, gu_rows, 0)
    back_top.wait_recv()
    add_rows(1, 0, (in_top,))
    back_far.start()
    back_low.wait_recv()
    add_rows(2, half, (in_low,))
    back_across.start()
    lax.fori_loop(5, width // 256, gu_rows, 0)
    for buffer in range(2):
        local(base_sem + 5 + buffer, gu_stage.at[buffer], gu_out.at[pl.ds(0, 256)]).wait()

    target = (place + line - 1) % line
    sum_on = [
        remote(
            SUM_ON + h,
            gu_out.at[pl.ds(pl.multiple_of((h * line + target) * slab_rows, 16), slab_rows)],
            gu_next.at[h],
            (me, after),
        )
        for h in range(4)
    ]
    for copy in sum_on:
        copy.start()

    for copy in (near, far, across, far_on, across_on, corner_on, corner_top, corner_low):
        copy.wait_send()
    load_again = [
        local(1 + i, w_out_ref.at[pl.ds(i * rows, rows)], acts.at[i]) for i in range(6)
    ]
    for copy in load_again:
        copy.start()

    for i, (first, size) in enumerate(SPANS):
        turned[0:size, :] = transposed(
            hidden[:, :, first : first + size].reshape(8 * rows, size)
        )
        buffer = i % 2
        if i > 1:
            local(base_sem + 7, stage.at[0], down_out.at[pl.ds(0, rows)]).wait()

        def down_cols(step, carry):
            span = pl.ds(pl.multiple_of(step * 256, 256), 256)
            part = nn(turned[0:size, :], tops[:, :, span].reshape(8 * rows, 256))
            stage[buffer, 0:size, span] = part.astype(BF)
            return carry

        lax.fori_loop(0, width // 256, down_cols, 0)
        local(
            base_sem + 7 + buffer,
            stage.at[buffer, pl.ds(0, size)],
            down_out.at[pl.ds(first, size)],
        ).start()

    to_mate(0).wait_recv()
    back_far.wait_recv()
    back_across.wait_recv()
    keep_resid.wait()
    gain_out[...] = jnp.zeros_like(gain_out)
    low = got.at[0]

    def norm_back(step, carry):
        tile = pl.ds(pl.multiple_of(step * 32, 32), 32)
        grad = (
            pairs[odd, tile, :].astype(F32)
            + got[0, tile, :].astype(F32)
            + in_far[tile, :].astype(F32)
            + in_across[tile, :].astype(F32)
        )
        block = resid[tile, :]
        scale = lax.rsqrt(jnp.mean(block * block, axis=1, keepdims=True) + EPS)
        gain_out[...] += jnp.sum(grad * block * scale, axis=0, keepdims=True)
        inner = grad * gain_ref[...]
        mean = jnp.mean(inner * block, axis=1, keepdims=True)
        total = (
            tops[slot, tile, :].astype(F32)
            + scale * inner
            - block * (scale * scale * scale * mean)
        )
        resid[tile, :] = total
        low[tile, :] = total.astype(BF)
        return carry

    lax.fori_loop(0, rows // 32, norm_back, 0)
    keep_grad = local(base_sem + 3, resid, grad_out)
    keep_grad.start()
    keep_low = local(base_sem + 4, low, grad_low_out)
    keep_low.start()
    keep_mixed.wait()
    for copy in load_again:
        copy.wait()

    def heads_cols(step, carry):
        span = pl.ds(pl.multiple_of(step * 256, 256), 256)
        mixed[:, span] = nt(low[...], acts[step]).astype(BF)
        return carry

    lax.fori_loop(0, 6, heads_cols, 0)
    heads_on = [
        remote(HEADS_BACK + i, mixed_cols(to), heads_out.at[me], (to, at))
        for i, to in enumerate((mate, beside, corner))
    ]
    for copy in heads_on:
        copy.start()
    own_back = local(0, mixed_cols(me), heads_out.at[me])
    own_back.start()

    own_back.wait()
    keep_grad.wait()
    keep_low.wait()
    local(base_sem + 7, stage.at[0, pl.ds(0, SPANS[2][1])], down_out.at[pl.ds(0, SPANS[2][1])]).wait()
    local(base_sem + 8, stage.at[1], down_out.at[pl.ds(0, rows)]).wait()
    for copy in heads_on + sum_on:
        copy.wait()
    for copy in heads + slab_on:
        copy.wait_send()
    for c in range(4):
        to_mate(c).wait_send()
    for copy in (back_top, back_low, back_far, back_across):
        copy.wait_send()


def middle(attn_out, tokens, w_o, gain, slabs, w_d, top):
    rows, width = tokens.shape
    units = w_d.shape[0]
    cols = attn_out.shape[2]
    line = lax.axis_size("blk") // 2
    slab_shape = slabs[0].shape
    anywhere = pl.BlockSpec(memory_space=pl.ANY)
    vmem = pl.BlockSpec(memory_space=pltpu.VMEM)
    shape = jax.ShapeDtypeStruct
    eight = (8, rows, width)
    return pl.pallas_call(
        functools.partial(middle_kernel, len(slabs), line),
        out_shape=(
            shape((rows, width), F32),
            shape((rows, width), F32),
            shape((rows, width), BF),
            shape((rows, 4 * cols), BF),
            shape(attn_out.shape, BF),
            shape(eight, BF),
            shape((width, 2 * units), BF),
            shape(slab_shape, BF),
            shape((units, width), BF),
            shape((1, width), F32),
        ),
        in_specs=[anywhere, vmem, anywhere, vmem, anywhere, anywhere]
        + [anywhere] * len(slabs),
        out_specs=(anywhere,) * 9 + (vmem,),
        scratch_shapes=[
            pltpu.VMEM((rows, 4 * cols), BF),
            pltpu.VMEM(eight, BF),
            pltpu.VMEM(eight, BF),
            pltpu.VMEM((width, 2 * units), BF),
            pltpu.VMEM((units, width), BF),
            pltpu.VMEM((8, rows, units), BF),
            pltpu.VMEM((8, rows, 2 * units), BF),
            pltpu.VMEM(eight, BF),
            pltpu.VMEM((4, rows, width), BF),
            pltpu.VMEM((2, rows, width), BF),
            pltpu.VMEM((rows, width), BF),
            pltpu.VMEM((rows, width), BF),
            pltpu.VMEM((rows // 2, width), BF),
            pltpu.VMEM((rows // 2, width), BF),
            pltpu.VMEM((rows, width), F32),
            pltpu.VMEM((256, 8 * rows), BF),
            pltpu.VMEM((2, 256, 2 * units), BF),
            pltpu.SemaphoreType.DMA((TRANSFERS,)),
            pltpu.SemaphoreType.DMA((TRANSFERS,)),
            pltpu.SemaphoreType.DMA((16 + 4 * len(slabs),)),
        ],
        compiler_params=pltpu.CompilerParams(
            collective_id=1, has_side_effects=True, vmem_limit_bytes=60 << 20
        ),
        cost_estimate=pl.CostEstimate(
            flops=60_000_000_000, bytes_accessed=100_000_000, transcendentals=2_000_000
        ),
        name="middle",
    )(attn_out, tokens, w_o, gain, w_d, top, *slabs)


def norm_rows(tensor, gain_vec):
    return tensor * lax.rsqrt(jnp.mean(tensor * tensor, axis=-1, keepdims=True) + EPS) * gain_vec


def rotate(tensor, cosine, sine_table):
    half_width = tensor.shape[-1] // 2
    first_half = tensor[..., :half_width]
    second = tensor[..., half_width:]
    return jnp.concatenate(
        [first_half * cosine - second * sine_table, second * cosine + first_half * sine_table],
        axis=-1,
    )


def split_low(value, parts):
    out = []
    for _ in range(parts):
        term = lax.reduce_precision(value, 8, 7)
        out.append(term.astype(BF))
        value = value - term
    return out


def shards(
    tokens,
    doc_lengths,
    norm1_gain,
    w_query,
    w_key,
    w_value,
    query_gain,
    key_gain,
    w_out,
    norm2_gain,
    w_gate,
    w_up,
    w_down,
    cotangent,
):
    tok_rows, width = tokens.shape
    blocks = lax.axis_size("blk")
    groups = lax.axis_size("head")
    group_id = lax.axis_index("head")
    blk_place = lax.axis_index("blk")
    block_len = groups * tok_rows
    per_group = QHEADS // groups
    head_ratio = QHEADS // KVHEADS
    w_rows = w_query.shape[0]
    line = blocks // 2
    side = blk_place % 2
    ff_rows = w_down.shape[0]
    ff_cols = line * ff_rows
    q_cols = per_group * HEAD
    firsts = [g * per_group // head_ratio for g in range(groups)]
    odd = group_id % 2

    columns = []
    for g in range(groups):
        kv = slice(firsts[g] * HEAD, (firsts[g] + 2) * HEAD)
        columns += [
            w_query[:, g * q_cols : (g + 1) * q_cols],
            w_key[:, kv],
            w_value[:, kv],
            norm1_gain[:, None],
            norm2_gain[:, None],
            jnp.zeros((w_rows, 126), BF),
        ]
    qkv_cols = q_cols + 4 * HEAD
    qkv_wide = qkv_cols + 2 * HEAD
    w_in = jnp.concatenate(columns, axis=1).reshape(w_rows, groups, qkv_wide)
    w_in = lax.all_to_all(w_in, "head", split_axis=1, concat_axis=1, tiled=True)
    down = LineGather(w_down)
    down.ahead(line - 4)
    down_moved = down.send()
    w_in = gather_blk(jnp.swapaxes(w_in, 0, 1), 1).reshape(width, qkv_wide)
    block_tokens = gather_head(tokens).reshape(block_len, width)

    def by_unit(weight):
        return weight.reshape(w_rows, groups, line, 2, ff_rows)

    both = jnp.stack([by_unit(w_gate), by_unit(w_up)], axis=3)
    both = jnp.transpose(both, (4, 1, 0, 3, 2, 5)).reshape(2, groups, w_rows, 2 * ff_cols)
    w_in, block_tokens, both, down_moved = sync(w_in, block_tokens, both, down_moved)
    down.held = down_moved
    down.keep()

    other = swap(take(both, 1 - side), "blk", 1)
    both = put(jnp.zeros(both.shape, BF), take(both, side), side)
    both = put(both, other, 1 - side)
    both = lax.all_to_all(
        jnp.swapaxes(both, 0, 1), "head", split_axis=0, concat_axis=0, tiled=True
    )
    slabs = [both.reshape(groups, 2 * w_rows, 2 * ff_cols)]
    for _ in range(line - 3):
        slabs.append(ring(slabs[-1], 2))
    down_moved = down.send()
    top = gather_pair(cotangent)

    w_qkv = w_in[:, :qkv_cols]
    gains = w_in[:, qkv_cols : qkv_cols + 2].astype(F32).T
    gain_one, gain_two = gains[0], gains[1]

    starts = jnp.cumsum(doc_lengths) - doc_lengths
    offsets = jnp.arange(block_len, dtype=jnp.int32)
    token_pos = blk_place * block_len + offsets
    inside = starts[None, :] <= token_pos[:, None]
    token_start = jnp.max(jnp.where(inside, starts[None, :], 0), axis=1)
    in_doc = token_pos - token_start
    rope_freq = jnp.exp(-math.log(10000.0) * jnp.arange(HEAD // 2, dtype=F32) / (HEAD // 2))
    rope_angle = in_doc.astype(F32)[:, None] * rope_freq[None, :]
    cosine = jnp.cos(rope_angle)[:, None, :]
    sine_table = jnp.sin(rope_angle)[:, None, :]
    window_start = token_start - (blk_place - BACK) * block_len
    tiles = block_len // TILE
    edges = jnp.stack(
        [window_start[::TILE], window_start[TILE - 1 :: TILE]], axis=1
    ).reshape(2 * tiles)
    meta = jnp.concatenate([odd[None].astype(jnp.int32), edges.astype(jnp.int32)])

    query_g = query_gain.astype(F32)
    key_g = key_gain.astype(F32)
    block_inputs = block_tokens.astype(F32)
    normed_one = norm_rows(block_inputs, gain_one).astype(BF)
    raw = matmul(normed_one, w_qkv)

    def prepare(query_raw, key_raw, query_gain_in, key_gain_in):
        return (
            rotate(norm_rows(query_raw, query_gain_in), cosine, sine_table),
            rotate(norm_rows(key_raw, key_gain_in), cosine, sine_table),
        )

    query_raw = raw[:, :q_cols].reshape(block_len, per_group, HEAD)
    key_raw = raw[:, q_cols : q_cols + 2 * HEAD].reshape(block_len, 2, HEAD)
    value_own = raw[:, q_cols + 2 * HEAD :].reshape(block_len, 2, HEAD).astype(BF)
    (query_rot, key_rot), prep_pull = jax.vjp(prepare, query_raw, key_raw, query_g, key_g)
    queries = jnp.swapaxes(query_rot.astype(BF), 0, 1)
    kv_own = jnp.swapaxes(
        jnp.concatenate([key_rot.astype(BF), value_own], axis=-1), 0, 1
    )
    kv_own, down_moved, slabs = sync(kv_own, down_moved, slabs)
    down.held = down_moved
    down.keep()

    down_moved = down.send()
    even = side == 0
    kv_two = ring(kv_own, 2)
    kv_one = swap(jnp.where(even, kv_own, kv_two), "blk", 1)
    kv_four = ring(kv_two, 2)
    kv_three = swap(jnp.where(even, kv_two, kv_four), "blk", 1)
    window = jnp.concatenate([kv_four, kv_three, kv_two, kv_one, kv_own], axis=1)
    key_win, value_win = window[..., :HEAD], window[..., HEAD:]
    ones = jnp.ones(key_win.shape, BF)
    keys_wide = jnp.concatenate([key_win, key_win, ones, ones], axis=-1)
    values_wide = jnp.concatenate([value_win, ones], axis=-1)

    scaled = split_low(queries.astype(F32) * (SCALE * LOG2E), 2)
    keys_wide, values_wide, down_moved, w_out, top, slabs = sync(
        keys_wide, values_wide, down_moved, w_out, top, slabs
    )
    down.held = down_moved
    down.keep()
    slabs.append(ring(slabs[-1], 2))
    w_o = gather_blk(w_out, 0).reshape(blocks * w_out.shape[0], width)
    w_o = gather_head(w_o).reshape(QHEADS * HEAD, width)
    attended = attend(
        meta,
        jnp.concatenate(scaled, axis=-1),
        keys_wide[..., : 2 * HEAD],
        values_wide,
        window_start[:, None],
    )
    attended, slabs, w_o = sync(attended, slabs, w_o)
    attn_keep = attended[..., :HEAD]
    log_total = attended[..., HEAD]
    attn_out = jnp.swapaxes(attn_keep.astype(BF), 0, 1).reshape(groups, tok_rows, q_cols)

    (
        resid,
        grad_resid,
        grad_attn,
        mixed,
        grad_mix,
        out_part,
        gu_parts,
        gu_moved,
        down_parts,
        grad_gain_two,
    ) = middle(
        attn_out,
        tokens,
        w_o,
        gain_two[None, :],
        slabs,
        down.full.reshape(ff_cols, width),
        top.reshape(2 * groups, tok_rows, width),
    )
    grad_gain_two = grad_gain_two[0]
    inputs = tokens.astype(F32)
    down_parts = down_parts.reshape(line, ff_rows, width)
    gu_parts = gu_parts.reshape(groups, line, 2 * w_rows, 2 * ff_cols)
    down_sum = LineScatter(lambda p: take(down_parts, p))
    gu_sum = LineScatter(lambda p: take(gu_parts, p, 1))
    gu_sum.total = gu_moved
    gu_sum.add()
    out_part = out_part.reshape(2, groups, tok_rows, width)
    out_parts = matmul_tn(mixed, grad_attn).astype(BF).reshape(groups, -1, width)
    grad_mix = jnp.swapaxes(grad_mix.reshape(block_len, per_group, HEAD), 0, 1)
    row_dots = jnp.sum(grad_mix.astype(F32) * attn_keep, axis=-1, keepdims=True)
    low_logs = split_low(-log_total[..., None], 3)
    low_dots = split_low(-row_dots, 2)
    blank = jnp.zeros(queries.shape, BF)
    query_t = jnp.concatenate(
        scaled + low_logs + [blank, blank[..., : HEAD - 3]], axis=-1
    )
    grad_t = jnp.concatenate([grad_mix] + low_dots + [blank[..., : HEAD - 2]], axis=-1)
    query_t, grad_t = jnp.swapaxes(query_t, 1, 2), jnp.swapaxes(grad_t, 1, 2)
    down_sum.ahead(line - 4)
    gu_sum.ahead(line - 4)
    down_moved, gu_moved = down_sum.send(), gu_sum.send()
    out_act = (resid + scatter_pair(out_part)).astype(BF)
    out_slab = scatter_head(out_parts).astype(BF).reshape(blocks, w_out.shape[0], width)
    dq_t, dkv = attend_back(
        meta,
        keys_wide,
        values_wide,
        jnp.swapaxes(key_win, 1, 2),
        query_t,
        grad_t,
        jnp.concatenate([queries, blank], axis=-1),
        jnp.concatenate([blank, grad_mix], axis=-1),
        window_start[None, :],
    )
    dq_t, dkv, down_moved, gu_moved, out_act, out_slab = sync(
        dq_t, dkv, down_moved, gu_moved, out_act, out_slab
    )
    down_sum.total, gu_sum.total = down_moved, gu_moved
    down_sum.add()
    gu_sum.add()
    grad_queries = jnp.transpose(dq_t, (2, 0, 1)) * SCALE

    four, three, two, one, own = [
        dkv[:, i * block_len : (i + 1) * block_len] for i in range(BACK + 1)
    ]
    got_three = swap(three.astype(BF), "blk", 1).astype(F32)
    got_one = swap(one.astype(BF), "blk", 1).astype(F32)
    four = four + jnp.where(even, 0.0, got_three)
    two = two + jnp.where(even, got_three, got_one)
    own = own + jnp.where(even, got_one, 0.0)
    two = two + ring(four.astype(BF), -2).astype(F32)
    own = own + ring(two.astype(BF), -2).astype(F32)
    down_moved, gu_moved = down_sum.send(), gu_sum.send()
    own, down_moved, gu_moved = sync(own, down_moved, gu_moved)
    down_sum.total, gu_sum.total = down_moved, gu_moved
    down_sum.add()
    gu_sum.add()
    down_sum.send()
    down_sum.add()
    d_w_down = down_sum.total
    kv_grad = jnp.swapaxes(own, 0, 1)
    grad_keys = kv_grad[..., :HEAD] * SCALE
    grad_values = kv_grad[..., HEAD:]

    def to_owner(grad):
        back = lax.all_to_all(
            grad.astype(BF), "head", split_axis=0, concat_axis=0, tiled=True
        )
        return jnp.swapaxes(back, 0, 1).astype(F32)

    gu_own = gu_sum.total.astype(BF).reshape(groups, 2, w_rows, 2 * ff_cols)
    mine = take(gu_own, side, 1)
    got = swap(take(gu_own, 1 - side, 1), "blk", 1)
    gu_own = put(jnp.zeros((groups, w_rows, 2, 2 * ff_cols), BF), mine, side, 2)
    gu_own = put(gu_own, got, 1 - side, 2)
    gu_own = to_owner(gu_own)
    gu_own = gu_own.reshape(w_rows, groups, 2, 2, line, ff_rows)
    gu_own = jnp.transpose(gu_own, (3, 0, 1, 4, 2, 5)).reshape((2,) + w_gate.shape)
    d_w_gate, d_w_up = gu_own[0], gu_own[1]

    d_w_out = scatter_blk(lambda b: take(out_slab, b))

    grad_query_raw, grad_key_raw, grad_query_g, grad_key_g = prep_pull((grad_queries, grad_keys))
    gain_sums = sum_all(jnp.stack([grad_query_g, grad_key_g]))
    raw_grads = jnp.concatenate(
        [
            grad_query_raw.reshape(block_len, q_cols),
            grad_key_raw.reshape(block_len, 2 * HEAD),
            grad_values.reshape(block_len, 2 * HEAD),
        ],
        axis=1,
    ).astype(BF)
    grad_w_in = matmul_tn(normed_one, raw_grads)
    normed_part = matmul_nt(raw_grads, w_qkv).astype(BF)
    grad_normed_one = scatter_head(normed_part.reshape(groups, tok_rows, width))
    norm_one_out, norm_one_pull = jax.vjp(norm_rows, inputs, gain_one)
    grad_input_part, grad_gain_one = norm_one_pull(grad_normed_one)
    d_tokens = grad_resid + grad_input_part
    grad_w_in = jnp.concatenate(
        [
            grad_w_in,
            grad_gain_one[:, None],
            grad_gain_two[:, None],
            jnp.zeros((width, 126), F32),
        ],
        axis=1,
    )
    in_parts = grad_w_in.astype(BF).reshape(groups, blocks, w_rows, qkv_wide)
    owned = to_owner(scatter_blk(lambda b: take(in_parts, b, 1)))
    d_w_query = owned[:, :, :q_cols].reshape(w_rows, QHEADS * HEAD)
    key_heads, value_heads = [], []
    for head_id in range(KVHEADS):
        keys_of, values_of = [], []
        for g in range(groups):
            for slot in range(2):
                if firsts[g] + slot == head_id:
                    at = q_cols + slot * HEAD
                    keys_of.append(owned[:, g, at : at + HEAD])
                    at += 2 * HEAD
                    values_of.append(owned[:, g, at : at + HEAD])
        key_heads.append(functools.reduce(jnp.add, keys_of))
        value_heads.append(functools.reduce(jnp.add, values_of))
    d_w_key = jnp.concatenate(key_heads, axis=1)
    d_w_value = jnp.concatenate(value_heads, axis=1)
    d_norm1_gain = jnp.sum(owned[:, :, qkv_cols], axis=1)
    d_norm2_gain = jnp.sum(owned[:, :, qkv_cols + 1], axis=1)
    return (
        out_act,
        d_tokens,
        d_norm1_gain,
        d_w_query,
        d_w_key,
        d_w_value,
        gain_sums[0],
        gain_sums[1],
        d_w_out,
        d_norm2_gain,
        d_w_gate,
        d_w_up,
        d_w_down,
    )


def solution(mesh):
    by_token = P(("blk", "head"), None)
    by_row = P(("head", "blk"), None)
    by_entry = P(("head", "blk"))
    in_specs = (
        by_token,
        P(),
        by_entry,
        by_row,
        by_row,
        by_row,
        P(),
        P(),
        by_row,
        by_entry,
        by_row,
        by_row,
        by_row,
        by_token,
    )
    out_specs = (
        by_token,
        by_token,
        by_entry,
        by_row,
        by_row,
        by_row,
        P(),
        P(),
        by_row,
        by_entry,
        by_row,
        by_row,
        by_row,
    )
    return jax.shard_map(shards, mesh=mesh, in_specs=in_specs, out_specs=out_specs, check_vma=False)
```

```python
import functools
import math

import jax
import jax.numpy as jnp
from jax import lax
from jax.experimental import pallas as pl
from jax.experimental.pallas import tpu as pltpu
from jax.sharding import PartitionSpec as P

QHEADS = 24
KVHEADS = 6
HEAD = 64
MAXDOC = 4096

EPS = 1e-06
SCALE = 0.125
LOG2E = 1.4426950408889634
NEG = -1e30
TILE = 256
BACK = 4
BF = jnp.bfloat16
F32 = jnp.float32


def matmul(left_side, right_side):
    return jnp.dot(left_side, right_side, preferred_element_type=F32)


def matmul_tn(left_side, right_side):
    return lax.dot_general(
        left_side, right_side, (((0,), (0,)), ((), ())), preferred_element_type=F32
    )


def matmul_nt(left_side, right_side):
    return lax.dot_general(
        left_side, right_side, (((1,), (1,)), ((), ())), preferred_element_type=F32
    )


def swap(block, axis, bit):
    count = lax.axis_size(axis)
    return lax.ppermute(block, axis, [(i, i ^ bit) for i in range(count)])


def ring(block, step):
    count = lax.axis_size("blk")
    return lax.ppermute(block, "blk", [(i, (i + step) % count) for i in range(count)])


def put(full, part, index, axis=0):
    return lax.dynamic_update_index_in_dim(full, part, index, axis)


def take(full, index, axis=0):
    return lax.dynamic_index_in_dim(full, index, axis, keepdims=False)


def gather_head(part):
    me = lax.axis_index("head")
    far = swap(part, "head", 2)
    near = swap(part, "head", 1)
    diagonal = swap(far, "head", 1)
    full = jnp.zeros((4,) + part.shape, part.dtype)
    full = put(full, part, me)
    full = put(full, near, me ^ 1)
    full = put(full, far, me ^ 2)
    return put(full, diagonal, me ^ 3)


def scatter_head(terms):
    me = lax.axis_index("head")
    got_far = swap(take(terms, me ^ 3), "head", 1)
    far = (take(terms, me ^ 2).astype(F32) + got_far.astype(F32)).astype(terms.dtype)
    got_near = swap(take(terms, me ^ 1), "head", 1)
    arrived = swap(far, "head", 2)
    return take(terms, me).astype(F32) + got_near.astype(F32) + arrived.astype(F32)


def place_of():
    at = lax.axis_index("blk")
    return at // 2, at % 2, lax.axis_size("blk") // 2


class LineScatter:
    def __init__(self, chunk):
        self.place, _, self.line = place_of()
        self.chunk = chunk
        self.step = 1
        self.total = chunk((self.place - 1) % self.line)

    def send(self):
        self.total = ring(self.total.astype(BF), 2)
        return self.total

    def add(self):
        self.step += 1
        mine = self.chunk((self.place - self.step) % self.line)
        self.total = self.total.astype(F32) + mine.astype(F32)

    def ahead(self, steps):
        for _ in range(steps):
            self.send()
            self.add()


def gather_blk(part, axis=0):
    place, side, line = place_of()
    shape = part.shape[:axis] + (line, 2) + part.shape[axis:]
    full = jnp.zeros(shape, part.dtype)
    held = part

    def store(full, block, source, side):
        block = block.reshape(block.shape[:axis] + (1, 1) + block.shape[axis:])
        at = [0] * full.ndim
        at[axis], at[axis + 1] = source, side
        return lax.dynamic_update_slice(full, block, at)

    for step in range(line):
        if step:
            held = ring(held, 2)
        other = swap(held, "blk", 1)
        source = (place - step) % line
        full = store(full, held, source, side)
        full = store(full, other, source, 1 - side)
    return full


def scatter_blk(chunk):
    place, side, line = place_of()
    total = None
    for step in range(1, line + 1):
        target = (place - step) % line
        mine = chunk(2 * target + side)
        got = swap(chunk(2 * target + 1 - side), "blk", 1)
        term = mine.astype(F32) + got.astype(F32)
        if total is not None:
            term = term + total.astype(F32)
        if step < line:
            total = ring(term.astype(BF), 2)
        else:
            total = term
    return total


def scatter_pair(terms):
    me = lax.axis_index("head")
    side = lax.axis_index("blk") % 2
    half = terms.shape[2] // 2

    def pick(to_side, to_head):
        rest = [0] * (terms.ndim - 2)
        return lax.dynamic_slice(
            terms, [to_side, to_head] + rest, (1, 1) + terms.shape[2:]
        ).reshape(terms.shape[2:])

    def both(to_side, to_head):
        got = swap(pick(to_side, to_head ^ 1), "head", 1)
        return pick(to_side, to_head).astype(F32) + got.astype(F32)

    corner = both(1 - side, me ^ 2).astype(BF)
    top = swap(corner[:half], "blk", 1)
    bottom = swap(corner[half:], "head", 2)
    far = both(side, me ^ 2)
    across = both(1 - side, me)
    far = jnp.concatenate([far[:half] + top.astype(F32), far[half:]], axis=0)
    across = jnp.concatenate([across[:half], across[half:] + bottom.astype(F32)], axis=0)
    got_far = swap(far.astype(BF), "head", 2)
    got_across = swap(across.astype(BF), "blk", 1)
    return both(side, me) + got_far.astype(F32) + got_across.astype(F32)


def sum_all(values):
    for bit in (1, 2):
        values = values + swap(values, "head", bit)
    bit = 1
    while bit < lax.axis_size("blk"):
        values = values + swap(values, "blk", bit)
        bit *= 2
    return values


def sync(*trees):
    return lax.optimization_barrier(trees)


def nt(left_side, right_side):
    return lax.dot_general(
        left_side, right_side, (((1,), (1,)), ((), ())), preferred_element_type=F32
    )


def nn(left_side, right_side):
    return lax.dot_general(
        left_side, right_side, (((1,), (0,)), ((), ())), preferred_element_type=F32
    )


def lanes(shape):
    return lax.broadcasted_iota(jnp.int32, shape, len(shape) - 1)


def transposed(block):
    return jnp.swapaxes(block, 0, 1)


def head_groups(meta_ref):
    odd = meta_ref[0]
    return ((4, 2 * odd, odd), (2, 4 * (1 - odd), 1 - odd))


def split_window(kv_ref, keys, values, step):
    per_block = kv_ref.shape[2] // TILE
    block, part = step // per_block, step % per_block
    source = pl.ds(pl.multiple_of(part * TILE, TILE), TILE)
    target = pl.ds(pl.multiple_of(step * TILE, TILE), TILE)
    low = lanes((TILE, 128)) < HEAD
    for slot in range(2):
        both = kv_ref[block, slot, source, :].astype(F32)
        moved = pltpu.roll(both, HEAD, 1)
        keys[slot, target, 0:128] = jnp.where(low, both, moved).astype(BF)
        values[slot, target, :] = jnp.where(low, moved, 1.0).astype(BF)
    return target


def attend_kernel(
    meta_ref, query_ref, kv_ref, start_ref, out_ref, low_ref, acc_ref, keys, values
):
    heads, rows, _ = query_ref.shape
    base = keys.shape[1] - rows
    lane = lanes((TILE, 128))

    def fill(step, carry):
        split_window(kv_ref, keys, values, step)
        return carry

    lax.fori_loop(0, keys.shape[1] // TILE, fill, 0)
    for count, first, slot in head_groups(meta_ref):
        for tile in range(rows // TILE):
            q_at = tile * TILE
            low, high = meta_ref[1 + 2 * tile], meta_ref[2 + 2 * tile]
            queries = query_ref[pl.ds(first, count), q_at : q_at + TILE, :].reshape(
                count * TILE, 2 * HEAD
            )
            acc = acc_ref.at[pl.ds(0, count * TILE)]
            acc[...] = jnp.zeros((count * TILE, 2 * HEAD), F32)
            start_col = start_ref[q_at : q_at + TILE, :]
            q_pos = base + q_at + lax.broadcasted_iota(jnp.int32, (TILE, 1), 0)

            def step(at, carry, masked):
                k_at = pl.multiple_of(at * TILE, TILE)
                scores = nt(queries, keys[slot, pl.ds(k_at, TILE), :])
                if masked:
                    k_pos = k_at + lax.broadcasted_iota(jnp.int32, (1, TILE), 1)
                    allowed = (start_col <= k_pos) & (k_pos <= q_pos)
                    scores = jnp.where(
                        allowed[None], scores.reshape(count, TILE, TILE), NEG
                    ).reshape(count * TILE, TILE)
                weights = jnp.exp2(scores).astype(BF)
                acc[...] += nn(weights, values[slot, pl.ds(k_at, TILE), :])
                return carry

            begin = low // TILE
            last = (base + q_at) // TILE
            clear = jnp.minimum((high + TILE - 1) // TILE, last)
            lax.fori_loop(begin, clear, functools.partial(step, masked=True), 0)
            lax.fori_loop(clear, last, functools.partial(step, masked=False), 0)
            step(last, 0, True)
            for j in range(count):
                part = acc_ref[j * TILE : (j + 1) * TILE, :]
                total = part[:, HEAD : HEAD + 1]
                out_ref[first + j, q_at : q_at + TILE, :] = jnp.where(
                    lane < HEAD, part / total, jnp.log2(total)
                )

    def lay(step, carry):
        tile = pl.ds(pl.multiple_of(step * TILE, TILE), TILE)
        for t in range(heads // 2):
            pair = jnp.where(
                lane < HEAD, out_ref[2 * t, tile, :], pltpu.roll(out_ref[2 * t + 1, tile, :], HEAD, 1)
            )
            low_ref[tile, t * 128 : (t + 1) * 128] = pair.astype(BF)
        return carry

    lax.fori_loop(0, rows // TILE, lay, 0)


def attend(meta, queries, kv, starts):
    heads, rows, _ = queries.shape
    window = kv.shape[0] * rows
    vmem = pl.BlockSpec(memory_space=pltpu.VMEM)
    return pl.pallas_call(
        attend_kernel,
        out_shape=(
            jax.ShapeDtypeStruct((heads, rows, 2 * HEAD), F32),
            jax.ShapeDtypeStruct((rows, heads * HEAD), BF),
        ),
        in_specs=[pl.BlockSpec(memory_space=pltpu.SMEM)] + [vmem] * 3,
        out_specs=(vmem, vmem),
        scratch_shapes=[
            pltpu.VMEM((4 * TILE, 2 * HEAD), F32),
            pltpu.VMEM((2, window, 2 * HEAD), BF),
            pltpu.VMEM((2, window, 2 * HEAD), BF),
        ],
        compiler_params=pltpu.CompilerParams(vmem_limit_bytes=48 << 20),
        cost_estimate=pl.CostEstimate(
            flops=60_000_000_000, bytes_accessed=20_000_000, transcendentals=20_000_000
        ),
        name="attend",
    )(meta, queries, kv, starts)


def attend_back_kernel(
    meta_ref,
    wide_ref,
    query_ref,
    kv_ref,
    out_ref,
    grad_ref,
    start_ref,
    dq_ref,
    dkv_low_ref,
    dkv_own_ref,
    keys,
    values,
    keys_t,
    query_t,
    grad_t,
    grads,
    dq,
    dkv,
):
    heads, rows, _ = query_ref.shape
    window = keys.shape[1]
    base = window - rows
    lane = lanes((TILE, 128))
    low_lane = lane < HEAD

    def fill(step, carry):
        target = split_window(kv_ref, keys, values, step)
        for slot in range(2):
            keys[slot, target, 128:256] = jnp.ones((TILE, 128), BF)
            keys_t[slot, :, target] = transposed(keys[slot, target, 0:128])[0:HEAD, :]
            dkv[slot, target, :] = jnp.zeros((TILE, 128), F32)
        return carry

    lax.fori_loop(0, window // TILE, fill, 0)

    def low_terms(value, first):
        out = jnp.zeros_like(value)
        for i in range(3):
            term = value.astype(BF).astype(F32)
            out = jnp.where(lane == first + i, term, out)
            value = value - term
        return out

    def turn(step, carry):
        tile = pl.ds(pl.multiple_of(step * TILE, TILE), TILE)
        for j in range(heads):
            query_t[j, 0:128, tile] = transposed(wide_ref[j, tile, :])
            kept = out_ref[j, tile, :]
            query_t[j, 128:256, tile] = transposed(low_terms(-kept, HEAD).astype(BF))
            grad = grad_ref[tile, (j // 2) * 128 : (j // 2) * 128 + 128].astype(F32)
            moved = pltpu.roll(grad, HEAD, 1)
            if j % 2:
                grad, moved = moved, grad
            dots = jnp.sum(jnp.where(low_lane, grad * kept, 0.0), axis=1, keepdims=True)
            dots = jnp.broadcast_to(-dots, (TILE, 128))
            block = jnp.where(low_lane, grad, low_terms(dots, HEAD))
            grad_t[j, :, tile] = transposed(block.astype(BF))
            grads[j, tile, :] = jnp.where(low_lane, 0.0, moved).astype(BF)
            dq[j, :, tile] = jnp.zeros((HEAD, TILE), F32)
        return carry

    lax.fori_loop(0, rows // TILE, turn, 0)
    for count, first, slot in head_groups(meta_ref):
        for tile in range(rows // TILE):
            q_at = tile * TILE
            q_cols = slice(q_at, q_at + TILE)
            low, high = meta_ref[1 + 2 * tile], meta_ref[2 + 2 * tile]
            start_row = start_ref[:, q_cols]
            q_pos = base + q_at + lax.broadcasted_iota(jnp.int32, (1, TILE), 1)

            def step(at, carry, masked):
                k_at = pl.multiple_of(at * TILE, TILE)
                k_rows = pl.ds(k_at, TILE)
                key_block = keys[slot, k_rows, :]
                value_block = values[slot, k_rows, :]
                key_t = keys_t[slot, :, k_rows]
                if masked:
                    k_pos = k_at + lax.broadcasted_iota(jnp.int32, (TILE, 1), 0)
                    allowed = (start_row <= k_pos) & (k_pos <= q_pos)
                total = dkv[slot, k_rows, :]
                for j in range(count):
                    scores = nn(key_block, query_t[first + j, :, q_cols])
                    if masked:
                        scores = jnp.where(allowed, scores, NEG)
                    probs = jnp.exp2(scores)
                    diff = nn(value_block, grad_t[first + j, :, q_cols])
                    grad_score = (probs * diff).astype(BF)
                    total = (
                        total
                        + nn(probs.astype(BF), grads[first + j, q_cols, :])
                        + nn(grad_score, query_ref[first + j, q_cols, :])
                    )
                    dq[first + j, :, q_cols] += nn(key_t, grad_score)
                dkv[slot, k_rows, :] = total
                return carry

            begin = low // TILE
            last = (base + q_at) // TILE
            clear = jnp.minimum((high + TILE - 1) // TILE, last)
            lax.fori_loop(begin, clear, functools.partial(step, masked=True), 0)
            lax.fori_loop(clear, last, functools.partial(step, masked=False), 0)
            step(last, 0, True)

    def finish(step, carry):
        tile = pl.ds(pl.multiple_of(step * TILE, TILE), TILE)
        for t in range(heads // 2):
            pair = jnp.concatenate([dq[2 * t, :, tile], dq[2 * t + 1, :, tile]], axis=0)
            dq_ref[tile, t * 128 : (t + 1) * 128] = transposed(pair) * SCALE
        per_block = rows // TILE
        for slot in range(2):
            for block in range(BACK + 1):
                source = pl.ds(pl.multiple_of(block * rows + step * TILE, TILE), TILE)
                part = dkv[slot, source, :]
                part = jnp.where(low_lane, part * SCALE, part)
                if block < BACK:
                    dkv_low_ref[block, slot, tile, :] = part.astype(BF)
                else:
                    dkv_own_ref[slot, tile, :] = part
        return carry

    lax.fori_loop(0, rows // TILE, finish, 0)


def attend_back(meta, wide, queries, kv, kept, grads, starts):
    heads, rows, _ = queries.shape
    window = kv.shape[0] * rows
    vmem = pl.BlockSpec(memory_space=pltpu.VMEM)
    shape = jax.ShapeDtypeStruct
    return pl.pallas_call(
        attend_back_kernel,
        out_shape=(
            shape((rows, heads * HEAD), F32),
            shape((BACK, 2, rows, 128), BF),
            shape((2, rows, 128), F32),
        ),
        in_specs=[pl.BlockSpec(memory_space=pltpu.SMEM)] + [vmem] * 6,
        out_specs=(vmem,) * 3,
        scratch_shapes=[
            pltpu.VMEM((2, window, 256), BF),
            pltpu.VMEM((2, window, 128), BF),
            pltpu.VMEM((2, HEAD, window), BF),
            pltpu.VMEM((heads, 256, rows), BF),
            pltpu.VMEM((heads, 128, rows), BF),
            pltpu.VMEM((heads, rows, 128), BF),
            pltpu.VMEM((heads, HEAD, rows), F32),
            pltpu.VMEM((2, window, 128), F32),
        ],
        compiler_params=pltpu.CompilerParams(vmem_limit_bytes=56 << 20),
        cost_estimate=pl.CostEstimate(
            flops=120_000_000_000, bytes_accessed=40_000_000, transcendentals=20_000_000
        ),
        name="attend_back",
    )(meta, wide, queries, kv, kept, grads, starts)


MESH = pl.DeviceIdType.MESH
HEADS_OUT, SLAB, NEAR, FAR, ACROSS, FAR_ON, ACROSS_ON = 0, 3, 7, 8, 9, 10, 11
CORNER_TOP, CORNER_LOW, CORNER_ON, TO_MATE = 12, 13, 14, 15
BACK_TOP, BACK_LOW, BACK_FAR, BACK_ACROSS, HEADS_BACK, SUM_ON = 19, 20, 21, 22, 23, 26
TRANSFERS = 30
SPANS = ((0, 256), (256, 256), (512, 128))


def middle_kernel(
    slabs,
    line,
    attn_ref,
    tokens_ref,
    w_out_ref,
    gain_ref,
    w_down_ref,
    top_ref,
    *refs,
):
    slab_refs = refs[:slabs]
    (
        resid_out,
        grad_out,
        grad_low_out,
        mixed_out,
        heads_out,
        part_out,
        gu_out,
        gu_next,
        down_out,
        gain_out,
        mixed,
        acts,
        tops,
        w_gu,
        w_dn,
        hidden,
        grad_gu,
        pairs,
        got,
        stage,
        in_far,
        in_across,
        in_top,
        in_low,
        resid,
        turned,
        gu_stage,
        sends,
        recvs,
        locals_,
    ) = refs[slabs:]
    me, at = lax.axis_index("head"), lax.axis_index("blk")
    count = lax.axis_size("blk")
    side, place = at % 2, at // 2
    odd = me % 2
    mate, beside, corner = me + 1 - 2 * odd, (me + 2) % 4, (me + 3 - 2 * odd) % 4
    other = at + 1 - 2 * side
    after, before = (at + 2) % count, (at + count - 2) % count
    rows, width = tokens_ref.shape
    half = rows // 2
    cols = mixed.shape[1] // 4
    units = w_dn.shape[0]
    slab_rows = slab_refs[0].shape[1]

    barrier = pltpu.get_barrier_semaphore()
    peers = ((mate, at), (beside, at), (corner, at), (me, other), (me, after), (me, before))
    for peer in peers:
        pl.semaphore_signal(barrier, inc=1, device_id=peer, device_id_type=MESH)
    pl.semaphore_wait(barrier, len(peers))

    def remote(index, source, target, device):
        return pltpu.make_async_remote_copy(
            src_ref=source,
            dst_ref=target,
            send_sem=sends.at[index],
            recv_sem=recvs.at[index],
            device_id=device,
            device_id_type=MESH,
        )

    def local(index, source, target):
        return pltpu.make_async_copy(source, target, locals_.at[index])

    def mixed_cols(head):
        return mixed.at[:, pl.ds(pl.multiple_of(head * cols, 128), cols)]

    heads = [
        remote(HEADS_OUT + i, attn_ref.at[to], mixed_cols(me), (to, at))
        for i, to in enumerate((mate, beside, corner))
    ]
    for copy in heads:
        copy.start()
    own_heads = local(0, attn_ref.at[me], mixed_cols(me))
    own_heads.start()
    load_out = [
        local(1 + i, w_out_ref.at[pl.ds(i * rows, rows)], pairs.at[i]) for i in range(6)
    ]
    for copy in load_out:
        copy.start()

    def slab_at(head, source):
        start = pl.multiple_of((head * line + source) * slab_rows, 16)
        return w_gu.at[pl.ds(start, slab_rows)]

    last = (place + line - (slabs - 1)) % line
    slab_on = [
        remote(SLAB + h, slab_refs[-1].at[h], slab_at(h, last), (me, after)) for h in range(4)
    ]
    for copy in slab_on:
        copy.start()
    load_slabs = [
        local(7 + 4 * i + h, ref.at[h], slab_at(h, (place + line - i) % line))
        for i, ref in enumerate(slab_refs)
        for h in range(4)
    ]
    for copy in load_slabs:
        copy.start()
    base_sem = 7 + 4 * slabs
    load_down = local(base_sem, w_down_ref, w_dn)
    load_down.start()
    load_top = local(base_sem + 1, top_ref, tops)
    load_top.start()

    for copy in heads:
        copy.wait_recv()
    own_heads.wait()
    for copy in load_out:
        copy.wait()
    keep_mixed = local(base_sem + 2, mixed, mixed_out)
    keep_mixed.start()

    def resid_cols(step, carry):
        span = pl.ds(pl.multiple_of(step * 256, 256), 256)
        weight = pairs[0:6, :, span].reshape(6 * rows, 256)
        resid[:, span] = tokens_ref[:, span].astype(F32) + nn(mixed[...], weight)
        return carry

    lax.fori_loop(0, width // 256, resid_cols, 0)
    slot = side * 4 + me

    def norm_tile(step, carry):
        tile = pl.ds(pl.multiple_of(step * 32, 32), 32)
        block = resid[tile, :]
        scale = lax.rsqrt(jnp.mean(block * block, axis=1, keepdims=True) + EPS)
        acts[slot, tile, :] = (block * scale * gain_ref[...]).astype(BF)
        return carry

    lax.fori_loop(0, rows // 32, norm_tile, 0)
    keep_resid = local(base_sem + 3, resid, resid_out)
    keep_resid.start()

    far_slot, across_slot = side * 4 + beside, (1 - side) * 4 + me
    corner_slot = (1 - side) * 4 + beside
    near = remote(NEAR, acts.at[slot], acts.at[slot], (mate, at))
    far = remote(FAR, acts.at[slot], acts.at[slot], (beside, at))
    across = remote(ACROSS, acts.at[slot], acts.at[slot], (me, other))
    far_on = remote(FAR_ON, acts.at[far_slot], acts.at[far_slot], (mate, at))
    across_on = remote(ACROSS_ON, acts.at[across_slot], acts.at[across_slot], (mate, at))
    corner_on = remote(CORNER_ON, acts.at[corner_slot], acts.at[corner_slot], (mate, at))
    far_top = acts.at[far_slot, pl.ds(0, half)]
    across_low = acts.at[across_slot, pl.ds(half, half)]
    corner_top = remote(CORNER_TOP, far_top, far_top, (me, other))
    corner_low = remote(CORNER_LOW, across_low, across_low, (beside, at))
    near.start()
    far.start()
    across.start()
    for copy in load_slabs:
        copy.wait()
    for copy in slab_on:
        copy.wait_recv()
    load_down.wait()
    load_top.wait()

    def chunk(c, carry):
        its_side = (side + c // 2) % 2
        its_head = (me + 2 * (c % 2)) % 4
        pair = its_side * 4 + its_head - its_head % 2

        @pl.when(c == 0)
        def _():
            near.wait_recv()

        @pl.when(c == 1)
        def _():
            far.wait_recv()
            far_on.start()
            corner_top.start()
            across.wait_recv()
            across_on.start()
            corner_low.start()
            far_on.wait_recv()

        @pl.when(c == 2)
        def _():
            corner_top.wait_recv()
            corner_low.wait_recv()
            corner_on.start()
            across_on.wait_recv()

        @pl.when(c == 3)
        def _():
            corner_on.wait_recv()

        for first, size in SPANS:
            block = acts[pl.ds(pair, 2)].reshape(2 * rows, width)
            gate = nn(block, w_gu[:, first : first + size])
            up = nn(block, w_gu[:, units + first : units + first + size])
            grad = nt(
                tops[pl.ds(pair, 2)].reshape(2 * rows, width), w_dn[first : first + size, :]
            )
            sig = jax.nn.sigmoid(gate)
            silu = gate * sig
            shape = (2, rows, size)
            hidden[pl.ds(pair, 2), :, first : first + size] = (
                (silu * up).astype(BF).reshape(shape)
            )
            grad_gu[pl.ds(pair, 2), :, first : first + size] = (
                (grad * up * sig * (1 + gate * (1 - sig))).astype(BF).reshape(shape)
            )
            grad_gu[pl.ds(pair, 2), :, units + first : units + first + size] = (
                (grad * silu).astype(BF).reshape(shape)
            )

        def grad_cols(step, carry):
            span = pl.ds(pl.multiple_of(step * 256, 256), 256)
            block = grad_gu[pl.ds(pair, 2)].reshape(2 * rows, 2 * units)
            part = nt(block, w_gu[span, :])
            pairs[pl.ds(2 * c, 2), :, span] = part.astype(BF).reshape(2, rows, 256)
            return carry

        lax.fori_loop(0, width // 256, grad_cols, 0)
        remote(TO_MATE + c, pairs.at[2 * c + 1 - odd], got.at[c], (mate, at)).start()

        @pl.when(c > 0)
        def _():
            local(base_sem + 4, stage, part_out.at[pl.ds(0, 2)]).wait()

        def out_cols(step, carry):
            span = pl.ds(pl.multiple_of(step * 256, 256), 256)
            block = hidden[pl.ds(pair, 2)].reshape(2 * rows, units)
            part = nn(block, w_dn[:, span])
            stage[:, :, span] = part.astype(BF).reshape(2, rows, 256)
            return carry

        lax.fori_loop(0, width // 256, out_cols, 0)
        local(base_sem + 4, stage, part_out.at[pl.ds(pair, 2)]).start()
        return carry

    lax.fori_loop(0, 4, chunk, 0)

    def to_mate(c):
        return remote(TO_MATE + c, pairs.at[2 * c + 1 - odd], got.at[c], (mate, at))

    def add_rows(c, first, extra):
        def tile(step, carry):
            span = pl.ds(pl.multiple_of(first + step * 32, 32), 32)
            total = pairs[2 * c + odd, span, :].astype(F32) + got[c, span, :].astype(F32)
            for ref in extra:
                total = total + ref[pl.ds(pl.multiple_of(step * 32, 32), 32), :].astype(F32)
            pairs[2 * c + odd, span, :] = total.astype(BF)
            return carry

        lax.fori_loop(0, half // 32, tile, 0)

    back_top = remote(
        BACK_TOP, pairs.at[6 + odd, pl.ds(0, half)], in_top, (me, other)
    )
    back_low = remote(
        BACK_LOW, pairs.at[6 + odd, pl.ds(half, half)], in_low, (beside, at)
    )
    back_far = remote(BACK_FAR, pairs.at[2 + odd], in_far, (beside, at))
    back_across = remote(BACK_ACROSS, pairs.at[4 + odd], in_across, (me, other))
    to_mate(3).wait_recv()
    add_rows(3, 0, ())
    back_top.start()
    add_rows(3, half, ())
    back_low.start()
    to_mate(1).wait_recv()
    to_mate(2).wait_recv()
    add_rows(1, half, ())
    add_rows(2, 0, ())

    local(base_sem + 4, stage, part_out.at[pl.ds(0, 2)]).wait()

    def gu_rows(step, carry):
        span = pl.ds(pl.multiple_of(step * 256, 256), 256)
        turned[...] = transposed(acts[:, :, span].reshape(8 * rows, 256))
        buffer = step % 2

        @pl.when(step > 1)
        def _():
            local(base_sem + 5 + buffer, gu_stage.at[buffer], gu_out.at[pl.ds(0, 256)]).wait()

        for n in range(2 * units // 256):
            part = nn(
                turned[...],
                grad_gu[:, :, n * 256 : (n + 1) * 256].reshape(8 * rows, 256),
            )
            gu_stage[buffer, :, n * 256 : (n + 1) * 256] = part.astype(BF)
        local(base_sem + 5 + buffer, gu_stage.at[buffer], gu_out.at[span]).start()
        return carry

    lax.fori_loop(0, 5, gu_rows, 0)
    back_top.wait_recv()
    add_rows(1, 0, (in_top,))
    back_far.start()
    back_low.wait_recv()
    add_rows(2, half, (in_low,))
    back_across.start()
    lax.fori_loop(5, width // 256, gu_rows, 0)
    for buffer in range(2):
        local(base_sem + 5 + buffer, gu_stage.at[buffer], gu_out.at[pl.ds(0, 256)]).wait()

    target = (place + line - 1) % line
    sum_on = [
        remote(
            SUM_ON + h,
            gu_out.at[pl.ds(pl.multiple_of((h * line + target) * slab_rows, 16), slab_rows)],
            gu_next.at[h],
            (me, after),
        )
        for h in range(4)
    ]
    for copy in sum_on:
        copy.start()

    for copy in (near, far, across, far_on, across_on, corner_on, corner_top, corner_low):
        copy.wait_send()
    load_again = [
        local(1 + i, w_out_ref.at[pl.ds(i * rows, rows)], acts.at[i]) for i in range(6)
    ]
    for copy in load_again:
        copy.start()

    for i, (first, size) in enumerate(SPANS):
        turned[0:size, :] = transposed(
            hidden[:, :, first : first + size].reshape(8 * rows, size)
        )
        buffer = i % 2
        if i > 1:
            local(base_sem + 7, stage.at[0], down_out.at[pl.ds(0, rows)]).wait()

        def down_cols(step, carry):
            span = pl.ds(pl.multiple_of(step * 256, 256), 256)
            part = nn(turned[0:size, :], tops[:, :, span].reshape(8 * rows, 256))
            stage[buffer, 0:size, span] = part.astype(BF)
            return carry

        lax.fori_loop(0, width // 256, down_cols, 0)
        local(
            base_sem + 7 + buffer,
            stage.at[buffer, pl.ds(0, size)],
            down_out.at[pl.ds(first, size)],
        ).start()

    to_mate(0).wait_recv()
    back_far.wait_recv()
    back_across.wait_recv()
    keep_resid.wait()
    gain_out[...] = jnp.zeros_like(gain_out)
    low = got.at[0]

    def norm_back(step, carry):
        tile = pl.ds(pl.multiple_of(step * 32, 32), 32)
        grad = (
            pairs[odd, tile, :].astype(F32)
            + got[0, tile, :].astype(F32)
            + in_far[tile, :].astype(F32)
            + in_across[tile, :].astype(F32)
        )
        block = resid[tile, :]
        scale = lax.rsqrt(jnp.mean(block * block, axis=1, keepdims=True) + EPS)
        gain_out[...] += jnp.sum(grad * block * scale, axis=0, keepdims=True)
        inner = grad * gain_ref[...]
        mean = jnp.mean(inner * block, axis=1, keepdims=True)
        total = (
            tops[slot, tile, :].astype(F32)
            + scale * inner
            - block * (scale * scale * scale * mean)
        )
        resid[tile, :] = total
        low[tile, :] = total.astype(BF)
        return carry

    lax.fori_loop(0, rows // 32, norm_back, 0)
    keep_grad = local(base_sem + 3, resid, grad_out)
    keep_grad.start()
    keep_low = local(base_sem + 4, low, grad_low_out)
    keep_low.start()
    keep_mixed.wait()
    for copy in load_again:
        copy.wait()

    def heads_cols(step, carry):
        span = pl.ds(pl.multiple_of(step * 256, 256), 256)
        mixed[:, span] = nt(low[...], acts[step]).astype(BF)
        return carry

    lax.fori_loop(0, 6, heads_cols, 0)
    heads_on = [
        remote(HEADS_BACK + i, mixed_cols(to), heads_out.at[me], (to, at))
        for i, to in enumerate((mate, beside, corner))
    ]
    for copy in heads_on:
        copy.start()
    own_back = local(0, mixed_cols(me), heads_out.at[me])
    own_back.start()

    own_back.wait()
    keep_grad.wait()
    keep_low.wait()
    local(base_sem + 7, stage.at[0, pl.ds(0, SPANS[2][1])], down_out.at[pl.ds(0, SPANS[2][1])]).wait()
    local(base_sem + 8, stage.at[1], down_out.at[pl.ds(0, rows)]).wait()
    for copy in heads_on + sum_on:
        copy.wait()
    for copy in heads + slab_on:
        copy.wait_send()
    for c in range(4):
        to_mate(c).wait_send()
    for copy in (back_top, back_low, back_far, back_across):
        copy.wait_send()


def middle(attn_out, tokens, w_o, gain, slabs, w_d, top):
    rows, width = tokens.shape
    units = w_d.shape[0]
    cols = attn_out.shape[2]
    line = lax.axis_size("blk") // 2
    slab_shape = slabs[0].shape
    anywhere = pl.BlockSpec(memory_space=pl.ANY)
    vmem = pl.BlockSpec(memory_space=pltpu.VMEM)
    shape = jax.ShapeDtypeStruct
    eight = (8, rows, width)
    return pl.pallas_call(
        functools.partial(middle_kernel, len(slabs), line),
        out_shape=(
            shape((rows, width), F32),
            shape((rows, width), F32),
            shape((rows, width), BF),
            shape((rows, 4 * cols), BF),
            shape(attn_out.shape, BF),
            shape(eight, BF),
            shape((width, 2 * units), BF),
            shape(slab_shape, BF),
            shape((units, width), BF),
            shape((1, width), F32),
        ),
        in_specs=[anywhere, vmem, anywhere, vmem, anywhere, anywhere]
        + [anywhere] * len(slabs),
        out_specs=(anywhere,) * 9 + (vmem,),
        scratch_shapes=[
            pltpu.VMEM((rows, 4 * cols), BF),
            pltpu.VMEM(eight, BF),
            pltpu.VMEM(eight, BF),
            pltpu.VMEM((width, 2 * units), BF),
            pltpu.VMEM((units, width), BF),
            pltpu.VMEM((8, rows, units), BF),
            pltpu.VMEM((8, rows, 2 * units), BF),
            pltpu.VMEM(eight, BF),
            pltpu.VMEM((4, rows, width), BF),
            pltpu.VMEM((2, rows, width), BF),
            pltpu.VMEM((rows, width), BF),
            pltpu.VMEM((rows, width), BF),
            pltpu.VMEM((rows // 2, width), BF),
            pltpu.VMEM((rows // 2, width), BF),
            pltpu.VMEM((rows, width), F32),
            pltpu.VMEM((256, 8 * rows), BF),
            pltpu.VMEM((2, 256, 2 * units), BF),
            pltpu.SemaphoreType.DMA((TRANSFERS,)),
            pltpu.SemaphoreType.DMA((TRANSFERS,)),
            pltpu.SemaphoreType.DMA((16 + 4 * len(slabs),)),
        ],
        compiler_params=pltpu.CompilerParams(
            collective_id=1, has_side_effects=True, vmem_limit_bytes=60 << 20
        ),
        cost_estimate=pl.CostEstimate(
            flops=60_000_000_000, bytes_accessed=100_000_000, transcendentals=2_000_000
        ),
        name="middle",
    )(attn_out, tokens, w_o, gain, w_d, top, *slabs)


TOK_NEAR, TOK_FAR, TOK_ON, IN_QUERY, IN_REST = 0, 1, 2, 3, 6
TOP_NEAR, TOP_FAR, TOP_ACROSS, TOP_FAR_ON, TOP_ACROSS_ON = 9, 10, 11, 12, 13
TOP_CORNER_HIGH, TOP_CORNER_LOW, TOP_CORNER_ON = 14, 15, 16
UNITS_MOVE, SLAB_ON, DOWN_MOVE, DOWN_ONE, DOWN_TWO = 17, 31, 32, 33, 34
KV_ONE, KV_TWO, KV_PAIR_ONE, KV_PAIR_TWO, FIRST_TRANSFERS = 35, 36, 37, 38, 39
COLS_Q = QHEADS // 4 * HEAD
COLS_IN = COLS_Q + 4 * HEAD


def head_scale(block):
    low = lanes(block.shape) < HEAD
    square = block * block
    first = jnp.sum(jnp.where(low, square, 0.0), axis=1, keepdims=True)
    second = jnp.sum(jnp.where(low, 0.0, square), axis=1, keepdims=True)
    return jnp.where(
        low, lax.rsqrt(first / HEAD + EPS), lax.rsqrt(second / HEAD + EPS)
    )


def swap_halves(block):
    low = lanes(block.shape) % HEAD < HEAD // 2
    return jnp.where(low, pltpu.roll(block, 96, 1), pltpu.roll(block, 32, 1))


def first_kernel(
    line,
    tokens_ref,
    query_ref,
    rest_ref,
    gate_ref,
    up_ref,
    down_ref,
    top_ref,
    cos_ref,
    sin_ref,
    query_gain_ref,
    key_gain_ref,
    wide_out,
    query_out,
    kv_out,
    raw_out,
    normed_out,
    w_in_out,
    tops_out,
    slab_out,
    slab_next,
    down_out,
    down_one,
    down_two,
    gain_out,
    toks,
    normed,
    w_in,
    raw,
    wide,
    query,
    kv_own,
    sends,
    recvs,
    ring_sends,
    ring_recvs,
    swap_sends,
    swap_recvs,
    locals_,
):
    me, at = lax.axis_index("head"), lax.axis_index("blk")
    count = lax.axis_size("blk")
    side, place = at % 2, at // 2
    odd = me % 2
    mate, beside, corner = me + 1 - 2 * odd, (me + 2) % 4, (me + 3 - 2 * odd) % 4
    other = at + 1 - 2 * side
    after, before = (at + 2) % count, (at + count - 2) % count
    rows, width = tokens_ref.shape
    half = rows // 2
    w_rows = query_ref.shape[0]
    units = slab_out.shape[2] // 2
    piece_to = 2 * (at % line) + at // line
    piece_from = (at % 2) * line + at // 2
    stays = piece_to == at

    barrier = pltpu.get_barrier_semaphore()
    peers = [(mate, at), (beside, at), (corner, at), (me, after), (me, before)]
    peers += [(head, other) for head in (me, mate, beside, corner)]
    for peer in peers:
        pl.semaphore_signal(barrier, inc=1, device_id=peer, device_id_type=MESH)

    @pl.when(jnp.logical_not(stays))
    def _():
        for peer in ((me, piece_to), (me, piece_from)):
            pl.semaphore_signal(barrier, inc=1, device_id=peer, device_id_type=MESH)

    pl.semaphore_wait(barrier, jnp.where(stays, len(peers), len(peers) + 2))

    def remote(index, source, target, device, send=sends, recv=recvs):
        return pltpu.make_async_remote_copy(
            src_ref=source,
            dst_ref=target,
            send_sem=send.at[index],
            recv_sem=recv.at[index],
            device_id=device,
            device_id_type=MESH,
        )

    def local(index, source, target):
        return pltpu.make_async_copy(source, target, locals_.at[index])

    def cols_of(ref, start, size):
        return ref.at[:, pl.ds(pl.multiple_of(start, 128), size)]

    own_q = w_in.at[me, at, :, pl.ds(0, COLS_Q)]
    own_rest = w_in.at[me, at, :, pl.ds(COLS_Q, COLS_Q)]
    split = []
    for i, to in enumerate((mate, beside, corner)):
        split.append(
            remote(IN_QUERY + i, cols_of(query_ref, to * COLS_Q, COLS_Q), own_q, (to, at))
        )
        split.append(remote(IN_REST + i, rest_ref.at[to], own_rest, (to, at)))
    for copy in split:
        copy.start()
    own = [
        local(0, cols_of(query_ref, me * COLS_Q, COLS_Q), own_q),
        local(1, rest_ref.at[me], own_rest),
        local(2, tokens_ref, toks.at[me]),
        local(3, top_ref, tops_out.at[side * 4 + me]),
    ]
    for copy in own:
        copy.start()
    tok_near = remote(TOK_NEAR, tokens_ref, toks.at[me], (mate, at))
    tok_far = remote(TOK_FAR, tokens_ref, toks.at[me], (beside, at))
    tok_on = remote(TOK_ON, toks.at[beside], toks.at[beside], (mate, at))
    tok_far.start()
    tok_near.start()
    down_move = remote(DOWN_MOVE, down_ref, down_out, (me, piece_to))
    down_stay = local(4, down_ref, down_out)

    @pl.when(jnp.logical_not(stays))
    def _():
        down_move.start()

    @pl.when(stays)
    def _():
        down_stay.start()

    def units_at(ref, to_side, to_head):
        return cols_of(ref, (to_head * 2 + to_side) * units, units)

    slab_rows = pl.ds(pl.multiple_of(side * w_rows, 16), w_rows)
    targets = [(side, mate), (side, beside), (side, corner)]
    targets += [(1 - side, head) for head in (me, mate, beside, corner)]
    spread = []
    for i, (to_side, to_head) in enumerate(targets):
        device = (to_head, at if i < 3 else other)
        for j, ref in enumerate((gate_ref, up_ref)):
            spread.append(
                remote(
                    UNITS_MOVE + 2 * i + j,
                    units_at(ref, to_side, to_head),
                    slab_out.at[me, slab_rows, pl.ds(j * units, units)],
                    device,
                )
            )
    for copy in spread:
        copy.start()
    own_units = [
        local(
            5 + j,
            units_at(ref, side, me),
            slab_out.at[me, slab_rows, pl.ds(j * units, units)],
        )
        for j, ref in enumerate((gate_ref, up_ref))
    ]
    for copy in own_units:
        copy.start()

    def ring_copy(step):
        block = w_in.at[:, (at + count - 2 * (step - 1)) % count]
        return remote(step, block, block, (me, after), ring_sends, ring_recvs)

    def swap_copy(step):
        block = w_in.at[:, (at + count - 2 * step) % count]
        return remote(step, block, block, (me, other), swap_sends, swap_recvs)

    for copy in split:
        copy.wait_recv()
    own[0].wait()
    own[1].wait()
    ring_copy(1).start()
    swap_copy(0).start()
    tok_far.wait_recv()
    tok_on.start()
    top_slot = side * 4 + me
    far_slot, across_slot = side * 4 + beside, (1 - side) * 4 + me
    corner_slot = (1 - side) * 4 + beside
    top_near = remote(TOP_NEAR, top_ref, tops_out.at[top_slot], (mate, at))
    top_far = remote(TOP_FAR, top_ref, tops_out.at[top_slot], (beside, at))
    top_across = remote(TOP_ACROSS, top_ref, tops_out.at[top_slot], (me, other))
    top_far_on = remote(
        TOP_FAR_ON, tops_out.at[far_slot], tops_out.at[far_slot], (mate, at)
    )
    top_across_on = remote(
        TOP_ACROSS_ON, tops_out.at[across_slot], tops_out.at[across_slot], (mate, at)
    )
    top_corner_on = remote(
        TOP_CORNER_ON, tops_out.at[corner_slot], tops_out.at[corner_slot], (mate, at)
    )
    high = tops_out.at[far_slot, pl.ds(0, half)]
    low = tops_out.at[across_slot, pl.ds(half, half)]
    top_corner_high = remote(TOP_CORNER_HIGH, high, high, (me, other))
    top_corner_low = remote(TOP_CORNER_LOW, low, low, (beside, at))
    top_near.start()
    top_far.start()
    for step in range(1, line):
        ring_copy(step).wait_recv()
        if step < line - 1:
            ring_copy(step + 1).start()
        swap_copy(step).start()

    @pl.when(jnp.logical_not(stays))
    def _():
        down_move.wait_recv()

    @pl.when(stays)
    def _():
        down_stay.wait()

    down_on = remote(DOWN_ONE, down_out, down_one, (me, after))
    down_on.start()
    for copy in spread:
        copy.wait_recv()
    for copy in own_units:
        copy.wait()
    slab_on = remote(SLAB_ON, slab_out, slab_next, (me, after))
    slab_on.start()
    tok_near.wait_recv()
    tok_on.wait_recv()
    own[2].wait()
    own[3].wait()
    for step in range(line):
        swap_copy(step).wait_recv()
    top_across.start()
    keep_in = [
        local(7 + h, w_in.at[h], w_in_out.at[h]) for h in range(4)
    ]
    for copy in keep_in:
        copy.start()

    gains = w_in[:, :, :, COLS_IN : COLS_IN + 128].reshape(width, 128).astype(F32)
    gain_out[...] = transposed(gains)[0:8, :]

    def norm_tile(step, carry):
        head, tile = step // (rows // 32), pl.ds(pl.multiple_of(step % (rows // 32) * 32, 32), 32)
        block = toks[head, tile, :].astype(F32)
        scale = lax.rsqrt(jnp.mean(block * block, axis=1, keepdims=True) + EPS)
        normed[pl.ds(pl.multiple_of(step * 32, 32), 32), :] = (
            block * scale * gain_out[0:1, :]
        ).astype(BF)
        return carry

    lax.fori_loop(0, 4 * rows // 32, norm_tile, 0)
    keep_normed = local(11, normed, normed_out)
    keep_normed.start()

    def project(step, carry):
        tile = pl.ds(pl.multiple_of(step * 256, 256), 256)
        for first, size in SPANS:
            weight = w_in[:, :, :, first : first + size].reshape(width, size)
            raw[tile, first : first + size] = nn(normed[tile, :], weight)
        return carry

    lax.fori_loop(0, 4 * rows // 256, project, 0)
    keep_raw = local(12, raw.at[:, pl.ds(0, COLS_Q + 128)], raw_out)
    keep_raw.start()

    def rotated(block, gain, tile):
        block = block * head_scale(block) * gain
        return block * cos_ref[tile, :] + swap_halves(block) * sin_ref[tile, :]

    def prepare(step, carry):
        tile = pl.ds(pl.multiple_of(step * 64, 64), 64)
        first_half = lanes((64, 128)) < HEAD
        for t in range(QHEADS // 4 // 2):
            block = rotated(raw[tile, t * 128 : (t + 1) * 128], query_gain_ref[...], tile)
            block = block.astype(BF).astype(F32)
            moved = pltpu.roll(block, HEAD, 1)
            query[2 * t, tile, :] = jnp.where(first_half, block, 0.0).astype(BF)
            query[2 * t + 1, tile, :] = jnp.where(first_half, moved, 0.0).astype(BF)
            scaled = block * (SCALE * LOG2E)
            upper = scaled.astype(BF).astype(F32)
            lower = scaled - upper
            wide[2 * t, tile, :] = jnp.where(
                first_half, upper, pltpu.roll(lower, HEAD, 1)
            ).astype(BF)
            wide[2 * t + 1, tile, :] = jnp.where(
                first_half, pltpu.roll(upper, HEAD, 1), lower
            ).astype(BF)
        keys = rotated(raw[tile, COLS_Q : COLS_Q + 128], key_gain_ref[...], tile)
        values = raw[tile, COLS_Q + 128 : COLS_Q + 256]
        kv_own[0, tile, :] = jnp.where(
            first_half, keys, pltpu.roll(values, HEAD, 1)
        ).astype(BF)
        kv_own[1, tile, :] = jnp.where(
            first_half, pltpu.roll(keys, HEAD, 1), values
        ).astype(BF)
        return carry

    lax.fori_loop(0, 4 * rows // 64, prepare, 0)

    kv_one = remote(KV_ONE, kv_own, kv_out.at[2], (me, after))
    kv_two = remote(KV_TWO, kv_out.at[2], kv_out.at[0], (me, after))
    pair_one_even = remote(KV_PAIR_ONE, kv_own, kv_out.at[3], (me, other))
    pair_one_odd = remote(KV_PAIR_ONE, kv_out.at[2], kv_out.at[3], (me, other))
    pair_two_even = remote(KV_PAIR_TWO, kv_out.at[2], kv_out.at[1], (me, other))
    pair_two_odd = remote(KV_PAIR_TWO, kv_out.at[0], kv_out.at[1], (me, other))
    kv_one.start()

    @pl.when(side == 0)
    def _():
        pair_one_even.start()

    keep = [
        local(13, kv_own, kv_out.at[4]),
        local(14, wide, wide_out),
        local(15, query, query_out),
    ]
    for copy in keep:
        copy.start()
    top_far.wait_recv()
    top_far_on.start()
    top_corner_high.start()
    kv_one.wait_recv()
    kv_two.start()

    @pl.when(side == 0)
    def _():
        pair_two_even.start()

    @pl.when(side == 1)
    def _():
        pair_one_odd.start()

    down_on.wait_recv()
    top_across.wait_recv()
    top_across_on.start()
    top_corner_low.start()
    kv_two.wait_recv()

    @pl.when(side == 1)
    def _():
        pair_two_odd.start()

    down_last = remote(DOWN_TWO, down_one, down_two, (me, after))
    down_last.start()
    top_corner_high.wait_recv()
    top_corner_low.wait_recv()
    top_corner_on.start()

    pair_one_even.wait_recv()
    pair_two_even.wait_recv()
    down_last.wait_recv()
    slab_on.wait_recv()
    for copy in (top_near, top_far_on, top_across_on, top_corner_on):
        copy.wait_recv()
    for copy in keep + keep_in + [keep_normed, keep_raw]:
        copy.wait()
    for copy in split + spread:
        copy.wait_send()
    for copy in (tok_near, tok_far, tok_on, top_near, top_far, top_across, top_far_on):
        copy.wait_send()
    for copy in (top_across_on, top_corner_high, top_corner_low, top_corner_on):
        copy.wait_send()
    for copy in (slab_on, down_on, down_last, kv_one, kv_two):
        copy.wait_send()
    pair_one_even.wait_send()
    pair_two_even.wait_send()

    @pl.when(jnp.logical_not(stays))
    def _():
        down_move.wait_send()

    for step in range(line):
        swap_copy(step).wait_send()
        if step:
            ring_copy(step).wait_send()


def first(
    tokens, w_query, rest, w_gate, w_up, w_down, cotangent, cosine, sine, query_gain, key_gain
):
    rows, width = tokens.shape
    count = lax.axis_size("blk")
    w_rows, ff = w_gate.shape
    units = ff // 8
    block = 4 * rows
    anywhere = pl.BlockSpec(memory_space=pl.ANY)
    vmem = pl.BlockSpec(memory_space=pltpu.VMEM)
    shape = jax.ShapeDtypeStruct
    heads = QHEADS // 4
    slab = shape((4, 2 * w_rows, 2 * units), BF)
    dma = pltpu.SemaphoreType.DMA
    return pl.pallas_call(
        functools.partial(first_kernel, count // 2),
        out_shape=(
            shape((heads, block, 128), BF),
            shape((heads, block, 128), BF),
            shape((BACK + 1, 2, block, 128), BF),
            shape((block, COLS_Q + 128), F32),
            shape((block, width), BF),
            shape((4, count, w_rows, 2 * COLS_Q), BF),
            shape((8, rows, width), BF),
            slab,
            slab,
            shape(w_down.shape, BF),
            shape(w_down.shape, BF),
            shape(w_down.shape, BF),
            shape((8, width), F32),
        ),
        in_specs=[anywhere] * 7 + [vmem] * 4,
        out_specs=(anywhere,) * 12 + (vmem,),
        scratch_shapes=[
            pltpu.VMEM((4, rows, width), BF),
            pltpu.VMEM((block, width), BF),
            pltpu.VMEM((4, count, w_rows, 2 * COLS_Q), BF),
            pltpu.VMEM((block, COLS_IN), F32),
            pltpu.VMEM((heads, block, 128), BF),
            pltpu.VMEM((heads, block, 128), BF),
            pltpu.VMEM((2, block, 128), BF),
            dma((FIRST_TRANSFERS,)),
            dma((FIRST_TRANSFERS,)),
            dma((count // 2,)),
            dma((count // 2,)),
            dma((count // 2,)),
            dma((count // 2,)),
            dma((16,)),
        ],
        compiler_params=pltpu.CompilerParams(
            collective_id=2, has_side_effects=True, vmem_limit_bytes=48 << 20
        ),
        cost_estimate=pl.CostEstimate(
            flops=60_000_000_000, bytes_accessed=60_000_000, transcendentals=1_000_000
        ),
        name="first",
    )(
        tokens, w_query, rest, w_gate, w_up, w_down, cotangent, cosine, sine, query_gain, key_gain
    )


def norm_rows(tensor, gain_vec):
    return tensor * lax.rsqrt(jnp.mean(tensor * tensor, axis=-1, keepdims=True) + EPS) * gain_vec


def rotate(tensor, cosine, sine_table):
    half_width = tensor.shape[-1] // 2
    first_half = tensor[..., :half_width]
    second = tensor[..., half_width:]
    return jnp.concatenate(
        [first_half * cosine - second * sine_table, second * cosine + first_half * sine_table],
        axis=-1,
    )


def shards(
    tokens,
    doc_lengths,
    norm1_gain,
    w_query,
    w_key,
    w_value,
    query_gain,
    key_gain,
    w_out,
    norm2_gain,
    w_gate,
    w_up,
    w_down,
    cotangent,
):
    tok_rows, width = tokens.shape
    blocks = lax.axis_size("blk")
    groups = lax.axis_size("head")
    group_id = lax.axis_index("head")
    blk_place = lax.axis_index("blk")
    block_len = groups * tok_rows
    per_group = QHEADS // groups
    head_ratio = QHEADS // KVHEADS
    w_rows = w_query.shape[0]
    line = blocks // 2
    side = blk_place % 2
    ff_rows = w_down.shape[0]
    ff_cols = line * ff_rows
    q_cols = per_group * HEAD
    firsts = [g * per_group // head_ratio for g in range(groups)]
    odd = group_id % 2

    starts = jnp.cumsum(doc_lengths) - doc_lengths
    offsets = jnp.arange(block_len, dtype=jnp.int32)
    token_pos = blk_place * block_len + offsets
    inside = starts[None, :] <= token_pos[:, None]
    token_start = jnp.max(jnp.where(inside, starts[None, :], 0), axis=1)
    in_doc = token_pos - token_start
    rope_freq = jnp.exp(-math.log(10000.0) * jnp.arange(HEAD // 2, dtype=F32) / (HEAD // 2))
    rope_angle = in_doc.astype(F32)[:, None] * rope_freq[None, :]
    cosine, sine = jnp.cos(rope_angle), jnp.sin(rope_angle)
    cosine = jnp.concatenate([cosine] * 4, axis=1)
    sine = jnp.concatenate([-sine, sine] * 2, axis=1)
    window_start = token_start - (blk_place - BACK) * block_len
    tiles = block_len // TILE
    edges = jnp.stack(
        [window_start[::TILE], window_start[TILE - 1 :: TILE]], axis=1
    ).reshape(2 * tiles)
    meta = jnp.concatenate([odd[None].astype(jnp.int32), edges.astype(jnp.int32)])

    rest = []
    for g in range(groups):
        kv = slice(firsts[g] * HEAD, (firsts[g] + 2) * HEAD)
        rest += [
            w_key[:, kv],
            w_value[:, kv],
            norm1_gain[:, None],
            norm2_gain[:, None],
            jnp.zeros((w_rows, 126), BF),
        ]
    rest = jnp.concatenate(rest, axis=1).reshape(w_rows, groups, COLS_Q)
    rest = jnp.swapaxes(rest, 0, 1)
    query_g = query_gain.astype(F32)
    key_g = key_gain.astype(F32)
    (
        wide,
        queries,
        kv_window,
        raw,
        normed_one,
        w_in,
        top,
        slab,
        slab_next,
        down_own,
        down_one,
        down_two,
        gains,
    ) = first(
        tokens,
        w_query,
        rest,
        w_gate,
        w_up,
        w_down,
        cotangent,
        cosine,
        sine,
        jnp.concatenate([query_g, query_g])[None, :],
        jnp.concatenate([key_g, key_g])[None, :],
    )
    w_in = w_in.reshape(width, 2 * q_cols)
    gain_one, gain_two = gains[0], gains[1]
    slabs, downs = [slab, slab_next], [down_own, down_one, down_two]
    for _ in range(line - 4):
        slabs.append(ring(slabs[-1], 2))
        downs.append(ring(downs[-1], 2))
    slabs, downs, w_out, queries = sync(slabs, downs, w_out, queries)
    slabs.append(ring(slabs[-1], 2))
    downs.append(ring(downs[-1], 2))
    w_o = gather_blk(w_out, 0).reshape(blocks * w_out.shape[0], width)
    w_o = gather_head(w_o).reshape(QHEADS * HEAD, width)
    kept, attn_out = attend(meta, wide, kv_window, window_start[:, None])
    kept, attn_out, slabs, downs, w_o = sync(kept, attn_out, slabs, downs, w_o)
    place = blk_place // 2
    w_d = jnp.zeros((line, ff_rows, width), BF)
    for step, block in enumerate(downs):
        w_d = put(w_d, block, (place - step) % line)
    attn_out = attn_out.reshape(groups, tok_rows, q_cols)

    (
        resid,
        grad_resid,
        grad_attn,
        mixed,
        grad_mix,
        out_part,
        gu_parts,
        gu_moved,
        down_parts,
        grad_gain_two,
    ) = middle(
        attn_out,
        tokens,
        w_o,
        gain_two[None, :],
        slabs,
        w_d.reshape(ff_cols, width),
        top,
    )
    grad_gain_two = grad_gain_two[0]
    inputs = tokens.astype(F32)
    down_parts = down_parts.reshape(line, ff_rows, width)
    gu_parts = gu_parts.reshape(groups, line, 2 * w_rows, 2 * ff_cols)
    down_sum = LineScatter(lambda p: take(down_parts, p))
    gu_sum = LineScatter(lambda p: take(gu_parts, p, 1))
    gu_sum.total = gu_moved
    gu_sum.add()
    out_part = out_part.reshape(2, groups, tok_rows, width)
    out_parts = matmul_tn(mixed, grad_attn).astype(BF).reshape(groups, -1, width)
    down_sum.ahead(line - 4)
    gu_sum.ahead(line - 4)
    down_moved, gu_moved = down_sum.send(), gu_sum.send()
    out_act = (resid + scatter_pair(out_part)).astype(BF)
    out_slab = scatter_head(out_parts).astype(BF).reshape(blocks, w_out.shape[0], width)
    dq, dkv, own = attend_back(
        meta,
        wide,
        queries,
        kv_window,
        kept,
        grad_mix.reshape(block_len, q_cols),
        window_start[None, :],
    )
    dq, dkv, own, down_moved, gu_moved, out_act, out_slab = sync(
        dq, dkv, own, down_moved, gu_moved, out_act, out_slab
    )
    down_sum.total, gu_sum.total = down_moved, gu_moved
    down_sum.add()
    gu_sum.add()
    grad_queries = dq.reshape(block_len, per_group, HEAD)

    even = side == 0
    four, three, two, one = [dkv[i] for i in range(BACK)]
    got_three = swap(three, "blk", 1).astype(F32)
    got_one = swap(one, "blk", 1).astype(F32)
    four = four.astype(F32) + jnp.where(even, 0.0, got_three)
    two = two.astype(F32) + jnp.where(even, got_three, got_one)
    own = own + jnp.where(even, got_one, 0.0)
    two = two + ring(four.astype(BF), -2).astype(F32)
    own = own + ring(two.astype(BF), -2).astype(F32)
    down_moved, gu_moved = down_sum.send(), gu_sum.send()
    own, down_moved, gu_moved = sync(own, down_moved, gu_moved)
    down_sum.total, gu_sum.total = down_moved, gu_moved
    down_sum.add()
    gu_sum.add()
    down_sum.send()
    down_sum.add()
    d_w_down = lax.ppermute(
        down_sum.total.astype(BF),
        "blk",
        [(i, i % 2 * line + i // 2) for i in range(blocks)],
    ).astype(F32)
    kv_grad = jnp.swapaxes(own, 0, 1)
    grad_keys = kv_grad[..., :HEAD]
    grad_values = kv_grad[..., HEAD:]

    def to_owner(grad):
        back = lax.all_to_all(
            grad.astype(BF), "head", split_axis=0, concat_axis=0, tiled=True
        )
        return jnp.swapaxes(back, 0, 1).astype(F32)

    gu_own = gu_sum.total.astype(BF).reshape(groups, 2, w_rows, 2 * ff_cols)
    mine = take(gu_own, side, 1)
    got = swap(take(gu_own, 1 - side, 1), "blk", 1)
    gu_own = put(jnp.zeros((groups, w_rows, 2, 2 * ff_cols), BF), mine, side, 2)
    gu_own = put(gu_own, got, 1 - side, 2)
    gu_own = to_owner(gu_own)
    gu_own = gu_own.reshape(w_rows, groups, 2, 2, ff_cols)
    d_w_gate = gu_own[:, :, :, 0].reshape(w_gate.shape)
    d_w_up = gu_own[:, :, :, 1].reshape(w_up.shape)

    d_w_out = scatter_blk(lambda b: take(out_slab, b))

    def prepare(query_raw, key_raw, query_gain_in, key_gain_in):
        cos_half, sin_half = (
            cosine[:, None, : HEAD // 2],
            sine[:, None, HEAD // 2 : HEAD],
        )
        return (
            rotate(norm_rows(query_raw, query_gain_in), cos_half, sin_half),
            rotate(norm_rows(key_raw, key_gain_in), cos_half, sin_half),
        )

    query_raw = raw[:, :q_cols].reshape(block_len, per_group, HEAD)
    key_raw = raw[:, q_cols:].reshape(block_len, 2, HEAD)
    rot_out, prep_pull = jax.vjp(prepare, query_raw, key_raw, query_g, key_g)
    grad_query_raw, grad_key_raw, grad_query_g, grad_key_g = prep_pull((grad_queries, grad_keys))
    gain_sums = sum_all(jnp.stack([grad_query_g, grad_key_g]))
    raw_grads = jnp.concatenate(
        [
            grad_query_raw.reshape(block_len, q_cols),
            grad_key_raw.reshape(block_len, 2 * HEAD),
            grad_values.reshape(block_len, 2 * HEAD),
        ],
        axis=1,
    ).astype(BF)
    grad_w_in = matmul_tn(normed_one, raw_grads)
    normed_part = matmul_nt(raw_grads, w_in[:, : q_cols + 4 * HEAD]).astype(BF)
    grad_normed_one = scatter_head(normed_part.reshape(groups, tok_rows, width))
    norm_one_out, norm_one_pull = jax.vjp(norm_rows, inputs, gain_one)
    grad_input_part, grad_gain_one = norm_one_pull(grad_normed_one)
    d_tokens = grad_resid + grad_input_part
    grad_w_in = jnp.concatenate(
        [
            grad_w_in,
            grad_gain_one[:, None],
            grad_gain_two[:, None],
            jnp.zeros((width, 126), F32),
        ],
        axis=1,
    )
    in_parts = grad_w_in.astype(BF).reshape(groups, blocks, w_rows, 2 * q_cols)
    owned = to_owner(scatter_blk(lambda b: take(in_parts, b, 1)))
    d_w_query = owned[:, :, :q_cols].reshape(w_rows, QHEADS * HEAD)
    key_heads, value_heads = [], []
    for head_id in range(KVHEADS):
        keys_of, values_of = [], []
        for g in range(groups):
            for slot in range(2):
                if firsts[g] + slot == head_id:
                    at = q_cols + slot * HEAD
                    keys_of.append(owned[:, g, at : at + HEAD])
                    at += 2 * HEAD
                    values_of.append(owned[:, g, at : at + HEAD])
        key_heads.append(functools.reduce(jnp.add, keys_of))
        value_heads.append(functools.reduce(jnp.add, values_of))
    d_w_key = jnp.concatenate(key_heads, axis=1)
    d_w_value = jnp.concatenate(value_heads, axis=1)
    d_norm1_gain = jnp.sum(owned[:, :, q_cols + 4 * HEAD], axis=1)
    d_norm2_gain = jnp.sum(owned[:, :, q_cols + 4 * HEAD + 1], axis=1)
    return (
        out_act,
        d_tokens,
        d_norm1_gain,
        d_w_query,
        d_w_key,
        d_w_value,
        gain_sums[0],
        gain_sums[1],
        d_w_out,
        d_norm2_gain,
        d_w_gate,
        d_w_up,
        d_w_down,
    )


def solution(mesh):
    by_token = P(("blk", "head"), None)
    by_row = P(("head", "blk"), None)
    by_entry = P(("head", "blk"))
    in_specs = (
        by_token,
        P(),
        by_entry,
        by_row,
        by_row,
        by_row,
        P(),
        P(),
        by_row,
        by_entry,
        by_row,
        by_row,
        by_row,
        by_token,
    )
    out_specs = (
        by_token,
        by_token,
        by_entry,
        by_row,
        by_row,
        by_row,
        P(),
        P(),
        by_row,
        by_entry,
        by_row,
        by_row,
        by_row,
    )
    return jax.shard_map(shards, mesh=mesh, in_specs=in_specs, out_specs=out_specs, check_vma=False)
```

```python
import functools
import math

import jax
import jax.numpy as jnp
from jax import lax
from jax.experimental import pallas as pl
from jax.experimental.pallas import tpu as pltpu
from jax.sharding import PartitionSpec as P

QHEADS = 24
KVHEADS = 6
HEAD = 64
MAXDOC = 4096

EPS = 1e-06
SCALE = 0.125
LOG2E = 1.4426950408889634
NEG = -1e30
TILE = 256
BACK = 4
BF = jnp.bfloat16
F32 = jnp.float32


def matmul(left_side, right_side):
    return jnp.dot(left_side, right_side, preferred_element_type=F32)


def matmul_tn(left_side, right_side):
    return lax.dot_general(
        left_side, right_side, (((0,), (0,)), ((), ())), preferred_element_type=F32
    )


def matmul_nt(left_side, right_side):
    return lax.dot_general(
        left_side, right_side, (((1,), (1,)), ((), ())), preferred_element_type=F32
    )


def swap(block, axis, bit):
    count = lax.axis_size(axis)
    return lax.ppermute(block, axis, [(i, i ^ bit) for i in range(count)])


def ring(block, step):
    count = lax.axis_size("blk")
    return lax.ppermute(block, "blk", [(i, (i + step) % count) for i in range(count)])


def put(full, part, index, axis=0):
    return lax.dynamic_update_index_in_dim(full, part, index, axis)


def take(full, index, axis=0):
    return lax.dynamic_index_in_dim(full, index, axis, keepdims=False)


def gather_head(part):
    me = lax.axis_index("head")
    far = swap(part, "head", 2)
    near = swap(part, "head", 1)
    diagonal = swap(far, "head", 1)
    full = jnp.zeros((4,) + part.shape, part.dtype)
    full = put(full, part, me)
    full = put(full, near, me ^ 1)
    full = put(full, far, me ^ 2)
    return put(full, diagonal, me ^ 3)


def scatter_head(terms):
    me = lax.axis_index("head")
    got_far = swap(take(terms, me ^ 3), "head", 1)
    far = (take(terms, me ^ 2).astype(F32) + got_far.astype(F32)).astype(terms.dtype)
    got_near = swap(take(terms, me ^ 1), "head", 1)
    arrived = swap(far, "head", 2)
    return take(terms, me).astype(F32) + got_near.astype(F32) + arrived.astype(F32)


def place_of():
    at = lax.axis_index("blk")
    return at // 2, at % 2, lax.axis_size("blk") // 2


class LineScatter:
    def __init__(self, chunk):
        self.place, _, self.line = place_of()
        self.chunk = chunk
        self.step = 1
        self.total = chunk((self.place - 1) % self.line)

    def send(self):
        self.total = ring(self.total.astype(BF), 2)
        return self.total

    def add(self):
        self.step += 1
        mine = self.chunk((self.place - self.step) % self.line)
        self.total = self.total.astype(F32) + mine.astype(F32)

    def ahead(self, steps):
        for _ in range(steps):
            self.send()
            self.add()


def gather_blk(part, axis=0):
    place, side, line = place_of()
    shape = part.shape[:axis] + (line, 2) + part.shape[axis:]
    full = jnp.zeros(shape, part.dtype)
    held = part

    def store(full, block, source, side):
        block = block.reshape(block.shape[:axis] + (1, 1) + block.shape[axis:])
        at = [0] * full.ndim
        at[axis], at[axis + 1] = source, side
        return lax.dynamic_update_slice(full, block, at)

    for step in range(line):
        if step:
            held = ring(held, 2)
        other = swap(held, "blk", 1)
        source = (place - step) % line
        full = store(full, held, source, side)
        full = store(full, other, source, 1 - side)
    return full


def scatter_pair(terms):
    me = lax.axis_index("head")
    side = lax.axis_index("blk") % 2
    half = terms.shape[2] // 2

    def pick(to_side, to_head):
        rest = [0] * (terms.ndim - 2)
        return lax.dynamic_slice(
            terms, [to_side, to_head] + rest, (1, 1) + terms.shape[2:]
        ).reshape(terms.shape[2:])

    def both(to_side, to_head):
        got = swap(pick(to_side, to_head ^ 1), "head", 1)
        return pick(to_side, to_head).astype(F32) + got.astype(F32)

    corner = both(1 - side, me ^ 2).astype(BF)
    top = swap(corner[:half], "blk", 1)
    bottom = swap(corner[half:], "head", 2)
    far = both(side, me ^ 2)
    across = both(1 - side, me)
    far = jnp.concatenate([far[:half] + top.astype(F32), far[half:]], axis=0)
    across = jnp.concatenate([across[:half], across[half:] + bottom.astype(F32)], axis=0)
    got_far = swap(far.astype(BF), "head", 2)
    got_across = swap(across.astype(BF), "blk", 1)
    return both(side, me) + got_far.astype(F32) + got_across.astype(F32)


def sync(*trees):
    return lax.optimization_barrier(trees)


def nt(left_side, right_side):
    return lax.dot_general(
        left_side, right_side, (((1,), (1,)), ((), ())), preferred_element_type=F32
    )


def nn(left_side, right_side):
    return lax.dot_general(
        left_side, right_side, (((1,), (0,)), ((), ())), preferred_element_type=F32
    )


def lanes(shape):
    return lax.broadcasted_iota(jnp.int32, shape, len(shape) - 1)


def transposed(block):
    return jnp.swapaxes(block, 0, 1)


def head_groups(meta_ref):
    odd = meta_ref[0]
    return ((4, 2 * odd, odd), (2, 4 * (1 - odd), 1 - odd))


def split_window(kv_ref, keys, values, step, slot):
    per_block = kv_ref.shape[2] // TILE
    block, part = step // per_block, step % per_block
    source = pl.ds(pl.multiple_of(part * TILE, TILE), TILE)
    target = pl.ds(pl.multiple_of(step * TILE, TILE), TILE)
    low = lanes((TILE, 128)) < HEAD
    both = kv_ref[block, slot, source, :].astype(F32)
    moved = pltpu.roll(both, HEAD, 1)
    keys[target, 0:128] = jnp.where(low, both, moved).astype(BF)
    values[target, :] = jnp.where(low, moved, 1.0).astype(BF)
    return target


def attend_kernel(
    meta_ref, query_ref, kv_ref, start_ref, out_ref, low_ref, acc_ref, keys, values
):
    heads, rows, _ = query_ref.shape
    base = keys.shape[1] - rows
    lane = lanes((TILE, 128))

    def fill(step, carry):
        for slot in range(2):
            split_window(kv_ref, keys.at[slot], values.at[slot], step, slot)
        return carry

    lax.fori_loop(0, keys.shape[1] // TILE, fill, 0)
    for count, first, slot in head_groups(meta_ref):
        for tile in range(rows // TILE):
            q_at = tile * TILE
            low, high = meta_ref[1 + 2 * tile], meta_ref[2 + 2 * tile]
            queries = query_ref[pl.ds(first, count), q_at : q_at + TILE, :].reshape(
                count * TILE, 2 * HEAD
            )
            acc = acc_ref.at[pl.ds(0, count * TILE)]
            acc[...] = jnp.zeros((count * TILE, 2 * HEAD), F32)
            start_col = start_ref[q_at : q_at + TILE, :]
            q_pos = base + q_at + lax.broadcasted_iota(jnp.int32, (TILE, 1), 0)

            def step(at, carry, masked):
                k_at = pl.multiple_of(at * TILE, TILE)
                scores = nt(queries, keys[slot, pl.ds(k_at, TILE), :])
                if masked:
                    k_pos = k_at + lax.broadcasted_iota(jnp.int32, (1, TILE), 1)
                    allowed = (start_col <= k_pos) & (k_pos <= q_pos)
                    scores = jnp.where(
                        allowed[None], scores.reshape(count, TILE, TILE), NEG
                    ).reshape(count * TILE, TILE)
                weights = jnp.exp2(scores).astype(BF)
                acc[...] += nn(weights, values[slot, pl.ds(k_at, TILE), :])
                return carry

            begin = low // TILE
            last = (base + q_at) // TILE
            clear = jnp.minimum((high + TILE - 1) // TILE, last)
            lax.fori_loop(begin, clear, functools.partial(step, masked=True), 0)
            lax.fori_loop(clear, last, functools.partial(step, masked=False), 0)
            step(last, 0, True)
            for j in range(count):
                part = acc_ref[j * TILE : (j + 1) * TILE, :]
                total = part[:, HEAD : HEAD + 1]
                out_ref[first + j, q_at : q_at + TILE, :] = jnp.where(
                    lane < HEAD, part / total, jnp.log2(total)
                )

    def lay(step, carry):
        tile = pl.ds(pl.multiple_of(step * TILE, TILE), TILE)
        for t in range(heads // 2):
            pair = jnp.where(
                lane < HEAD, out_ref[2 * t, tile, :], pltpu.roll(out_ref[2 * t + 1, tile, :], HEAD, 1)
            )
            low_ref[tile, t * 128 : (t + 1) * 128] = pair.astype(BF)
        return carry

    lax.fori_loop(0, rows // TILE, lay, 0)


def attend(meta, queries, kv, starts):
    heads, rows, _ = queries.shape
    window = kv.shape[0] * rows
    vmem = pl.BlockSpec(memory_space=pltpu.VMEM)
    return pl.pallas_call(
        attend_kernel,
        out_shape=(
            jax.ShapeDtypeStruct((heads, rows, 2 * HEAD), F32),
            jax.ShapeDtypeStruct((rows, heads * HEAD), BF),
        ),
        in_specs=[pl.BlockSpec(memory_space=pltpu.SMEM)] + [vmem] * 3,
        out_specs=(vmem, vmem),
        scratch_shapes=[
            pltpu.VMEM((4 * TILE, 2 * HEAD), F32),
            pltpu.VMEM((2, window, 2 * HEAD), BF),
            pltpu.VMEM((2, window, 2 * HEAD), BF),
        ],
        compiler_params=pltpu.CompilerParams(vmem_limit_bytes=48 << 20),
        cost_estimate=pl.CostEstimate(
            flops=60_000_000_000, bytes_accessed=20_000_000, transcendentals=20_000_000
        ),
        name="attend",
    )(meta, queries, kv, starts)


def attend_back_kernel(
    which,
    meta_ref,
    wide_ref,
    query_ref,
    kv_ref,
    out_ref,
    grad_ref,
    start_ref,
    dq_ref,
    low_ref,
    own_ref,
    keys,
    values,
    keys_t,
    query_t,
    grad_t,
    grads,
    dq,
    dkv,
):
    rows = query_ref.shape[1]
    window = keys.shape[0]
    base = window - rows
    lane = lanes((TILE, 128))
    low_lane = lane < HEAD
    count, first, slot = head_groups(meta_ref)[which]

    def fill(step, carry):
        target = split_window(kv_ref, keys, values, step, slot)
        keys[target, 128:256] = jnp.ones((TILE, 128), BF)
        keys_t[:, target] = transposed(keys[target, 0:128])[0:HEAD, :]
        dkv[target, :] = jnp.zeros((TILE, 128), F32)
        return carry

    lax.fori_loop(0, window // TILE, fill, 0)

    def low_terms(value, first):
        out = jnp.zeros_like(value)
        for i in range(3):
            term = value.astype(BF).astype(F32)
            out = jnp.where(lane == first + i, term, out)
            value = value - term
        return out

    def turn(step, carry):
        tile = pl.ds(pl.multiple_of(step * TILE, TILE), TILE)
        for j in range(count):
            query_t[j, 0:128, tile] = transposed(wide_ref[first + j, tile, :])
            kept = out_ref[first + j, tile, :]
            query_t[j, 128:256, tile] = transposed(low_terms(-kept, HEAD).astype(BF))
            pair = pl.ds(pl.multiple_of((first // 2 + j // 2) * 128, 128), 128)
            grad = grad_ref[tile, pair].astype(F32)
            moved = pltpu.roll(grad, HEAD, 1)
            if j % 2:
                grad, moved = moved, grad
            dots = jnp.sum(jnp.where(low_lane, grad * kept, 0.0), axis=1, keepdims=True)
            dots = jnp.broadcast_to(-dots, (TILE, 128))
            block = jnp.where(low_lane, grad, low_terms(dots, HEAD))
            grad_t[j, :, tile] = transposed(block.astype(BF))
            grads[j, tile, :] = jnp.where(low_lane, 0.0, moved).astype(BF)
            dq[j, :, tile] = jnp.zeros((HEAD, TILE), F32)
        return carry

    lax.fori_loop(0, rows // TILE, turn, 0)
    for tile in range(rows // TILE):
        q_at = tile * TILE
        q_cols = slice(q_at, q_at + TILE)
        low, high = meta_ref[1 + 2 * tile], meta_ref[2 + 2 * tile]
        start_row = start_ref[:, q_cols]
        q_pos = base + q_at + lax.broadcasted_iota(jnp.int32, (1, TILE), 1)

        def step(at, carry, masked):
            k_at = pl.multiple_of(at * TILE, TILE)
            k_rows = pl.ds(k_at, TILE)
            key_block = keys[k_rows, :]
            value_block = values[k_rows, :]
            key_t = keys_t[:, k_rows]
            if masked:
                k_pos = k_at + lax.broadcasted_iota(jnp.int32, (TILE, 1), 0)
                allowed = (start_row <= k_pos) & (k_pos <= q_pos)
            total = dkv[k_rows, :]
            for j in range(count):
                scores = nn(key_block, query_t[j, :, q_cols])
                if masked:
                    scores = jnp.where(allowed, scores, NEG)
                probs = jnp.exp2(scores)
                diff = nn(value_block, grad_t[j, :, q_cols])
                grad_score = (probs * diff).astype(BF)
                total = (
                    total
                    + nn(probs.astype(BF), grads[j, q_cols, :])
                    + nn(grad_score, query_ref[first + j, q_cols, :])
                )
                dq[j, :, q_cols] += nn(key_t, grad_score)
            dkv[k_rows, :] = total
            return carry

        begin = low // TILE
        last = (base + q_at) // TILE
        clear = jnp.minimum((high + TILE - 1) // TILE, last)
        lax.fori_loop(begin, clear, functools.partial(step, masked=True), 0)
        lax.fori_loop(clear, last, functools.partial(step, masked=False), 0)
        step(last, 0, True)

    def finish(step, carry):
        tile = pl.ds(pl.multiple_of(step * TILE, TILE), TILE)
        for t in range(count // 2):
            pair = jnp.concatenate([dq[2 * t, :, tile], dq[2 * t + 1, :, tile]], axis=0)
            dq_ref[tile, t * 128 : (t + 1) * 128] = transposed(pair) * SCALE
        for block in range(BACK + 1):
            source = pl.ds(pl.multiple_of(block * rows + step * TILE, TILE), TILE)
            part = dkv[source, :]
            part = jnp.where(low_lane, part * SCALE, part)
            if block < BACK:
                low_ref[block, tile, :] = part.astype(BF)
            else:
                own_ref[tile, :] = part
        return carry

    lax.fori_loop(0, rows // TILE, finish, 0)


def attend_back(which, meta, wide, queries, kv, kept, grads, starts):
    _, rows, _ = queries.shape
    window = kv.shape[0] * rows
    count = (4, 2)[which]
    vmem = pl.BlockSpec(memory_space=pltpu.VMEM)
    shape = jax.ShapeDtypeStruct
    return pl.pallas_call(
        functools.partial(attend_back_kernel, which),
        out_shape=(
            shape((rows, count * HEAD), F32),
            shape((BACK, rows, 128), BF),
            shape((rows, 128), F32),
        ),
        in_specs=[pl.BlockSpec(memory_space=pltpu.SMEM)] + [vmem] * 6,
        out_specs=(vmem,) * 3,
        scratch_shapes=[
            pltpu.VMEM((window, 256), BF),
            pltpu.VMEM((window, 128), BF),
            pltpu.VMEM((HEAD, window), BF),
            pltpu.VMEM((count, 256, rows), BF),
            pltpu.VMEM((count, 128, rows), BF),
            pltpu.VMEM((count, rows, 128), BF),
            pltpu.VMEM((count, HEAD, rows), F32),
            pltpu.VMEM((window, 128), F32),
        ],
        compiler_params=pltpu.CompilerParams(vmem_limit_bytes=48 << 20),
        cost_estimate=pl.CostEstimate(
            flops=count * 20_000_000_000, bytes_accessed=40_000_000, transcendentals=20_000_000
        ),
        name=("attend_back_four", "attend_back_two")[which],
    )(meta, wide, queries, kv, kept, grads, starts)


MESH = pl.DeviceIdType.MESH
HEADS_OUT, SLAB, NEAR, FAR, ACROSS, FAR_ON, ACROSS_ON = 0, 3, 7, 8, 9, 10, 11
CORNER_TOP, CORNER_LOW, CORNER_ON, TO_MATE = 12, 13, 14, 15
BACK_TOP, BACK_LOW, BACK_FAR, BACK_ACROSS, HEADS_BACK, SUM_ON = 19, 20, 21, 22, 23, 26
TRANSFERS = 30
SPANS = ((0, 256), (256, 256), (512, 128))


def middle_kernel(
    slabs,
    line,
    attn_ref,
    tokens_ref,
    w_out_ref,
    gain_ref,
    w_down_ref,
    top_ref,
    *refs,
):
    slab_refs = refs[:slabs]
    (
        resid_out,
        grad_out,
        grad_low_out,
        mixed_out,
        heads_out,
        part_out,
        gu_out,
        gu_next,
        down_out,
        gain_out,
        mixed,
        acts,
        tops,
        w_gu,
        w_dn,
        hidden,
        grad_gu,
        pairs,
        got,
        stage,
        in_far,
        in_across,
        in_top,
        in_low,
        resid,
        turned,
        gu_stage,
        sends,
        recvs,
        locals_,
    ) = refs[slabs:]
    me, at = lax.axis_index("head"), lax.axis_index("blk")
    count = lax.axis_size("blk")
    side, place = at % 2, at // 2
    odd = me % 2
    mate, beside, corner = me + 1 - 2 * odd, (me + 2) % 4, (me + 3 - 2 * odd) % 4
    other = at + 1 - 2 * side
    after, before = (at + 2) % count, (at + count - 2) % count
    rows, width = tokens_ref.shape
    half = rows // 2
    cols = mixed.shape[1] // 4
    units = w_dn.shape[0]
    slab_rows = slab_refs[0].shape[1]

    barrier = pltpu.get_barrier_semaphore()
    peers = ((mate, at), (beside, at), (corner, at), (me, other), (me, after), (me, before))
    for peer in peers:
        pl.semaphore_signal(barrier, inc=1, device_id=peer, device_id_type=MESH)
    pl.semaphore_wait(barrier, len(peers))

    def remote(index, source, target, device):
        return pltpu.make_async_remote_copy(
            src_ref=source,
            dst_ref=target,
            send_sem=sends.at[index],
            recv_sem=recvs.at[index],
            device_id=device,
            device_id_type=MESH,
        )

    def local(index, source, target):
        return pltpu.make_async_copy(source, target, locals_.at[index])

    def mixed_cols(head):
        return mixed.at[:, pl.ds(pl.multiple_of(head * cols, 128), cols)]

    heads = [
        remote(HEADS_OUT + i, attn_ref.at[to], mixed_cols(me), (to, at))
        for i, to in enumerate((mate, beside, corner))
    ]
    for copy in heads:
        copy.start()
    own_heads = local(0, attn_ref.at[me], mixed_cols(me))
    own_heads.start()
    load_out = [
        local(1 + i, w_out_ref.at[pl.ds(i * rows, rows)], pairs.at[i]) for i in range(6)
    ]
    for copy in load_out:
        copy.start()

    def slab_at(head, source):
        start = pl.multiple_of((head * line + source) * slab_rows, 16)
        return w_gu.at[pl.ds(start, slab_rows)]

    last = (place + line - (slabs - 1)) % line
    slab_on = [
        remote(SLAB + h, slab_refs[-1].at[h], slab_at(h, last), (me, after)) for h in range(4)
    ]
    for copy in slab_on:
        copy.start()
    load_slabs = [
        local(7 + 4 * i + h, ref.at[h], slab_at(h, (place + line - i) % line))
        for i, ref in enumerate(slab_refs)
        for h in range(4)
    ]
    for copy in load_slabs:
        copy.start()
    base_sem = 7 + 4 * slabs
    load_down = local(base_sem, w_down_ref, w_dn)
    load_down.start()
    load_top = local(base_sem + 1, top_ref, tops)
    load_top.start()

    for copy in heads:
        copy.wait_recv()
    own_heads.wait()
    for copy in load_out:
        copy.wait()
    keep_mixed = local(base_sem + 2, mixed, mixed_out)
    keep_mixed.start()

    def resid_cols(step, carry):
        span = pl.ds(pl.multiple_of(step * 256, 256), 256)
        weight = pairs[0:6, :, span].reshape(6 * rows, 256)
        resid[:, span] = tokens_ref[:, span].astype(F32) + nn(mixed[...], weight)
        return carry

    lax.fori_loop(0, width // 256, resid_cols, 0)
    slot = side * 4 + me

    def norm_tile(step, carry):
        tile = pl.ds(pl.multiple_of(step * 32, 32), 32)
        block = resid[tile, :]
        scale = lax.rsqrt(jnp.mean(block * block, axis=1, keepdims=True) + EPS)
        acts[slot, tile, :] = (block * scale * gain_ref[...]).astype(BF)
        return carry

    lax.fori_loop(0, rows // 32, norm_tile, 0)
    keep_resid = local(base_sem + 3, resid, resid_out)
    keep_resid.start()

    far_slot, across_slot = side * 4 + beside, (1 - side) * 4 + me
    corner_slot = (1 - side) * 4 + beside
    near = remote(NEAR, acts.at[slot], acts.at[slot], (mate, at))
    far = remote(FAR, acts.at[slot], acts.at[slot], (beside, at))
    across = remote(ACROSS, acts.at[slot], acts.at[slot], (me, other))
    far_on = remote(FAR_ON, acts.at[far_slot], acts.at[far_slot], (mate, at))
    across_on = remote(ACROSS_ON, acts.at[across_slot], acts.at[across_slot], (mate, at))
    corner_on = remote(CORNER_ON, acts.at[corner_slot], acts.at[corner_slot], (mate, at))
    far_top = acts.at[far_slot, pl.ds(0, half)]
    across_low = acts.at[across_slot, pl.ds(half, half)]
    corner_top = remote(CORNER_TOP, far_top, far_top, (me, other))
    corner_low = remote(CORNER_LOW, across_low, across_low, (beside, at))
    near.start()
    far.start()
    across.start()
    for copy in load_slabs:
        copy.wait()
    for copy in slab_on:
        copy.wait_recv()
    load_down.wait()
    load_top.wait()

    def chunk(c, carry):
        its_side = (side + c // 2) % 2
        its_head = (me + 2 * (c % 2)) % 4
        pair = its_side * 4 + its_head - its_head % 2

        @pl.when(c == 0)
        def _():
            near.wait_recv()

        @pl.when(c == 1)
        def _():
            far.wait_recv()
            far_on.start()
            corner_top.start()
            across.wait_recv()
            across_on.start()
            corner_low.start()
            far_on.wait_recv()

        @pl.when(c == 2)
        def _():
            corner_top.wait_recv()
            corner_low.wait_recv()
            corner_on.start()
            across_on.wait_recv()

        @pl.when(c == 3)
        def _():
            corner_on.wait_recv()

        for first, size in SPANS:
            block = acts[pl.ds(pair, 2)].reshape(2 * rows, width)
            gate = nn(block, w_gu[:, first : first + size])
            up = nn(block, w_gu[:, units + first : units + first + size])
            grad = nt(
                tops[pl.ds(pair, 2)].reshape(2 * rows, width), w_dn[first : first + size, :]
            )
            sig = jax.nn.sigmoid(gate)
            silu = gate * sig
            shape = (2, rows, size)
            hidden[pl.ds(pair, 2), :, first : first + size] = (
                (silu * up).astype(BF).reshape(shape)
            )
            grad_gu[pl.ds(pair, 2), :, first : first + size] = (
                (grad * up * sig * (1 + gate * (1 - sig))).astype(BF).reshape(shape)
            )
            grad_gu[pl.ds(pair, 2), :, units + first : units + first + size] = (
                (grad * silu).astype(BF).reshape(shape)
            )

        def grad_cols(step, carry):
            span = pl.ds(pl.multiple_of(step * 256, 256), 256)
            block = grad_gu[pl.ds(pair, 2)].reshape(2 * rows, 2 * units)
            part = nt(block, w_gu[span, :])
            pairs[pl.ds(2 * c, 2), :, span] = part.astype(BF).reshape(2, rows, 256)
            return carry

        lax.fori_loop(0, width // 256, grad_cols, 0)
        remote(TO_MATE + c, pairs.at[2 * c + 1 - odd], got.at[c], (mate, at)).start()

        @pl.when(c > 0)
        def _():
            local(base_sem + 4, stage, part_out.at[pl.ds(0, 2)]).wait()

        def out_cols(step, carry):
            span = pl.ds(pl.multiple_of(step * 256, 256), 256)
            block = hidden[pl.ds(pair, 2)].reshape(2 * rows, units)
            part = nn(block, w_dn[:, span])
            stage[:, :, span] = part.astype(BF).reshape(2, rows, 256)
            return carry

        lax.fori_loop(0, width // 256, out_cols, 0)
        local(base_sem + 4, stage, part_out.at[pl.ds(pair, 2)]).start()
        return carry

    lax.fori_loop(0, 4, chunk, 0)

    def to_mate(c):
        return remote(TO_MATE + c, pairs.at[2 * c + 1 - odd], got.at[c], (mate, at))

    def add_rows(c, first, extra):
        def tile(step, carry):
            span = pl.ds(pl.multiple_of(first + step * 32, 32), 32)
            total = pairs[2 * c + odd, span, :].astype(F32) + got[c, span, :].astype(F32)
            for ref in extra:
                total = total + ref[pl.ds(pl.multiple_of(step * 32, 32), 32), :].astype(F32)
            pairs[2 * c + odd, span, :] = total.astype(BF)
            return carry

        lax.fori_loop(0, half // 32, tile, 0)

    back_top = remote(
        BACK_TOP, pairs.at[6 + odd, pl.ds(0, half)], in_top, (me, other)
    )
    back_low = remote(
        BACK_LOW, pairs.at[6 + odd, pl.ds(half, half)], in_low, (beside, at)
    )
    back_far = remote(BACK_FAR, pairs.at[2 + odd], in_far, (beside, at))
    back_across = remote(BACK_ACROSS, pairs.at[4 + odd], in_across, (me, other))
    to_mate(3).wait_recv()
    add_rows(3, 0, ())
    back_top.start()
    add_rows(3, half, ())
    back_low.start()
    to_mate(1).wait_recv()
    to_mate(2).wait_recv()
    add_rows(1, half, ())
    add_rows(2, 0, ())

    local(base_sem + 4, stage, part_out.at[pl.ds(0, 2)]).wait()

    def gu_rows(step, carry):
        span = pl.ds(pl.multiple_of(step * 256, 256), 256)
        turned[...] = transposed(acts[:, :, span].reshape(8 * rows, 256))
        buffer = step % 2

        @pl.when(step > 1)
        def _():
            local(base_sem + 5 + buffer, gu_stage.at[buffer], gu_out.at[pl.ds(0, 256)]).wait()

        for n in range(2 * units // 256):
            part = nn(
                turned[...],
                grad_gu[:, :, n * 256 : (n + 1) * 256].reshape(8 * rows, 256),
            )
            gu_stage[buffer, :, n * 256 : (n + 1) * 256] = part.astype(BF)
        local(base_sem + 5 + buffer, gu_stage.at[buffer], gu_out.at[span]).start()
        return carry

    lax.fori_loop(0, 5, gu_rows, 0)
    back_top.wait_recv()
    add_rows(1, 0, (in_top,))
    back_far.start()
    back_low.wait_recv()
    add_rows(2, half, (in_low,))
    back_across.start()
    lax.fori_loop(5, width // 256, gu_rows, 0)
    for buffer in range(2):
        local(base_sem + 5 + buffer, gu_stage.at[buffer], gu_out.at[pl.ds(0, 256)]).wait()

    target = (place + line - 1) % line
    sum_on = [
        remote(
            SUM_ON + h,
            gu_out.at[pl.ds(pl.multiple_of((h * line + target) * slab_rows, 16), slab_rows)],
            gu_next.at[h],
            (me, after),
        )
        for h in range(4)
    ]
    for copy in sum_on:
        copy.start()

    for copy in (near, far, across, far_on, across_on, corner_on, corner_top, corner_low):
        copy.wait_send()
    load_again = [
        local(1 + i, w_out_ref.at[pl.ds(i * rows, rows)], acts.at[i]) for i in range(6)
    ]
    for copy in load_again:
        copy.start()

    for i, (first, size) in enumerate(SPANS):
        turned[0:size, :] = transposed(
            hidden[:, :, first : first + size].reshape(8 * rows, size)
        )
        buffer = i % 2
        if i > 1:
            local(base_sem + 7, stage.at[0], down_out.at[pl.ds(0, rows)]).wait()

        def down_cols(step, carry):
            span = pl.ds(pl.multiple_of(step * 256, 256), 256)
            part = nn(turned[0:size, :], tops[:, :, span].reshape(8 * rows, 256))
            stage[buffer, 0:size, span] = part.astype(BF)
            return carry

        lax.fori_loop(0, width // 256, down_cols, 0)
        local(
            base_sem + 7 + buffer,
            stage.at[buffer, pl.ds(0, size)],
            down_out.at[pl.ds(first, size)],
        ).start()

    to_mate(0).wait_recv()
    back_far.wait_recv()
    back_across.wait_recv()
    keep_resid.wait()
    gain_out[...] = jnp.zeros_like(gain_out)
    low = got.at[0]

    def norm_back(step, carry):
        tile = pl.ds(pl.multiple_of(step * 32, 32), 32)
        grad = (
            pairs[odd, tile, :].astype(F32)
            + got[0, tile, :].astype(F32)
            + in_far[tile, :].astype(F32)
            + in_across[tile, :].astype(F32)
        )
        block = resid[tile, :]
        scale = lax.rsqrt(jnp.mean(block * block, axis=1, keepdims=True) + EPS)
        gain_out[...] += jnp.sum(grad * block * scale, axis=0, keepdims=True)
        inner = grad * gain_ref[...]
        mean = jnp.mean(inner * block, axis=1, keepdims=True)
        total = (
            tops[slot, tile, :].astype(F32)
            + scale * inner
            - block * (scale * scale * scale * mean)
        )
        resid[tile, :] = total
        low[tile, :] = total.astype(BF)
        return carry

    lax.fori_loop(0, rows // 32, norm_back, 0)
    keep_grad = local(base_sem + 3, resid, grad_out)
    keep_grad.start()
    keep_low = local(base_sem + 4, low, grad_low_out)
    keep_low.start()
    keep_mixed.wait()
    for copy in load_again:
        copy.wait()

    def heads_cols(step, carry):
        span = pl.ds(pl.multiple_of(step * 256, 256), 256)
        mixed[:, span] = nt(low[...], acts[step]).astype(BF)
        return carry

    lax.fori_loop(0, 6, heads_cols, 0)
    heads_on = [
        remote(HEADS_BACK + i, mixed_cols(to), heads_out.at[me], (to, at))
        for i, to in enumerate((mate, beside, corner))
    ]
    for copy in heads_on:
        copy.start()
    own_back = local(0, mixed_cols(me), heads_out.at[me])
    own_back.start()

    own_back.wait()
    keep_grad.wait()
    keep_low.wait()
    local(base_sem + 7, stage.at[0, pl.ds(0, SPANS[2][1])], down_out.at[pl.ds(0, SPANS[2][1])]).wait()
    local(base_sem + 8, stage.at[1], down_out.at[pl.ds(0, rows)]).wait()
    for copy in heads_on + sum_on:
        copy.wait()
    for copy in heads + slab_on:
        copy.wait_send()
    for c in range(4):
        to_mate(c).wait_send()
    for copy in (back_top, back_low, back_far, back_across):
        copy.wait_send()


def middle(attn_out, tokens, w_o, gain, slabs, w_d, top):
    rows, width = tokens.shape
    units = w_d.shape[0]
    cols = attn_out.shape[2]
    line = lax.axis_size("blk") // 2
    slab_shape = slabs[0].shape
    anywhere = pl.BlockSpec(memory_space=pl.ANY)
    vmem = pl.BlockSpec(memory_space=pltpu.VMEM)
    shape = jax.ShapeDtypeStruct
    eight = (8, rows, width)
    return pl.pallas_call(
        functools.partial(middle_kernel, len(slabs), line),
        out_shape=(
            shape((rows, width), F32),
            shape((rows, width), F32),
            shape((rows, width), BF),
            shape((rows, 4 * cols), BF),
            shape(attn_out.shape, BF),
            shape(eight, BF),
            shape((width, 2 * units), BF),
            shape(slab_shape, BF),
            shape((units, width), BF),
            shape((1, width), F32),
        ),
        in_specs=[anywhere, vmem, anywhere, vmem, anywhere, anywhere]
        + [anywhere] * len(slabs),
        out_specs=(anywhere,) * 9 + (vmem,),
        scratch_shapes=[
            pltpu.VMEM((rows, 4 * cols), BF),
            pltpu.VMEM(eight, BF),
            pltpu.VMEM(eight, BF),
            pltpu.VMEM((width, 2 * units), BF),
            pltpu.VMEM((units, width), BF),
            pltpu.VMEM((8, rows, units), BF),
            pltpu.VMEM((8, rows, 2 * units), BF),
            pltpu.VMEM(eight, BF),
            pltpu.VMEM((4, rows, width), BF),
            pltpu.VMEM((2, rows, width), BF),
            pltpu.VMEM((rows, width), BF),
            pltpu.VMEM((rows, width), BF),
            pltpu.VMEM((rows // 2, width), BF),
            pltpu.VMEM((rows // 2, width), BF),
            pltpu.VMEM((rows, width), F32),
            pltpu.VMEM((256, 8 * rows), BF),
            pltpu.VMEM((2, 256, 2 * units), BF),
            pltpu.SemaphoreType.DMA((TRANSFERS,)),
            pltpu.SemaphoreType.DMA((TRANSFERS,)),
            pltpu.SemaphoreType.DMA((16 + 4 * len(slabs),)),
        ],
        compiler_params=pltpu.CompilerParams(
            collective_id=1, has_side_effects=True, vmem_limit_bytes=60 << 20
        ),
        cost_estimate=pl.CostEstimate(
            flops=60_000_000_000, bytes_accessed=100_000_000, transcendentals=2_000_000
        ),
        name="middle",
    )(attn_out, tokens, w_o, gain, w_d, top, *slabs)


TOK_NEAR, TOK_FAR, TOK_ON, IN_QUERY, IN_REST = 0, 1, 2, 3, 6
TOP_NEAR, TOP_FAR, TOP_ACROSS, TOP_FAR_ON, TOP_ACROSS_ON = 9, 10, 11, 12, 13
TOP_CORNER_HIGH, TOP_CORNER_LOW, TOP_CORNER_ON = 14, 15, 16
UNITS_MOVE, SLAB_ON, DOWN_MOVE, DOWN_ONE, DOWN_TWO = 17, 31, 32, 33, 34
KV_ONE, KV_TWO, KV_PAIR_ONE, KV_PAIR_TWO, FIRST_TRANSFERS = 35, 36, 37, 38, 39
COLS_Q = QHEADS // 4 * HEAD
COLS_IN = COLS_Q + 4 * HEAD


def head_scale(block):
    low = lanes(block.shape) < HEAD
    square = block * block
    first = jnp.sum(jnp.where(low, square, 0.0), axis=1, keepdims=True)
    second = jnp.sum(jnp.where(low, 0.0, square), axis=1, keepdims=True)
    return jnp.where(
        low, lax.rsqrt(first / HEAD + EPS), lax.rsqrt(second / HEAD + EPS)
    )


def swap_halves(block):
    low = lanes(block.shape) % HEAD < HEAD // 2
    return jnp.where(low, pltpu.roll(block, 96, 1), pltpu.roll(block, 32, 1))


def first_kernel(
    line,
    tokens_ref,
    query_ref,
    rest_ref,
    gate_ref,
    up_ref,
    down_ref,
    top_ref,
    cos_ref,
    sin_ref,
    query_gain_ref,
    key_gain_ref,
    wide_out,
    query_out,
    kv_out,
    raw_out,
    normed_out,
    w_in_out,
    tops_out,
    slab_out,
    slab_next,
    down_out,
    down_one,
    down_two,
    toks_out,
    gain_out,
    toks,
    normed,
    w_in,
    raw,
    wide,
    query,
    kv_own,
    sends,
    recvs,
    ring_sends,
    ring_recvs,
    swap_sends,
    swap_recvs,
    locals_,
):
    me, at = lax.axis_index("head"), lax.axis_index("blk")
    count = lax.axis_size("blk")
    side, place = at % 2, at // 2
    odd = me % 2
    mate, beside, corner = me + 1 - 2 * odd, (me + 2) % 4, (me + 3 - 2 * odd) % 4
    other = at + 1 - 2 * side
    after, before = (at + 2) % count, (at + count - 2) % count
    rows, width = tokens_ref.shape
    half = rows // 2
    w_rows = query_ref.shape[0]
    units = slab_out.shape[2] // 2
    piece_to = 2 * (at % line) + at // line
    piece_from = (at % 2) * line + at // 2
    stays = piece_to == at

    barrier = pltpu.get_barrier_semaphore()
    peers = [(mate, at), (beside, at), (corner, at), (me, after), (me, before)]
    peers += [(head, other) for head in (me, mate, beside, corner)]
    for peer in peers:
        pl.semaphore_signal(barrier, inc=1, device_id=peer, device_id_type=MESH)

    @pl.when(jnp.logical_not(stays))
    def _():
        for peer in ((me, piece_to), (me, piece_from)):
            pl.semaphore_signal(barrier, inc=1, device_id=peer, device_id_type=MESH)

    pl.semaphore_wait(barrier, jnp.where(stays, len(peers), len(peers) + 2))

    def remote(index, source, target, device, send=sends, recv=recvs):
        return pltpu.make_async_remote_copy(
            src_ref=source,
            dst_ref=target,
            send_sem=send.at[index],
            recv_sem=recv.at[index],
            device_id=device,
            device_id_type=MESH,
        )

    def local(index, source, target):
        return pltpu.make_async_copy(source, target, locals_.at[index])

    def cols_of(ref, start, size):
        return ref.at[:, pl.ds(pl.multiple_of(start, 128), size)]

    own_q = w_in.at[me, at, :, pl.ds(0, COLS_Q)]
    own_rest = w_in.at[me, at, :, pl.ds(COLS_Q, COLS_Q)]
    split = []
    for i, to in enumerate((mate, beside, corner)):
        split.append(
            remote(IN_QUERY + i, cols_of(query_ref, to * COLS_Q, COLS_Q), own_q, (to, at))
        )
        split.append(remote(IN_REST + i, rest_ref.at[to], own_rest, (to, at)))
    for copy in split:
        copy.start()
    own = [
        local(0, cols_of(query_ref, me * COLS_Q, COLS_Q), own_q),
        local(1, rest_ref.at[me], own_rest),
        local(2, tokens_ref, toks.at[me]),
        local(3, top_ref, tops_out.at[side * 4 + me]),
    ]
    for copy in own:
        copy.start()
    tok_near = remote(TOK_NEAR, tokens_ref, toks.at[me], (mate, at))
    tok_far = remote(TOK_FAR, tokens_ref, toks.at[me], (beside, at))
    tok_on = remote(TOK_ON, toks.at[beside], toks.at[beside], (mate, at))
    tok_far.start()
    tok_near.start()
    down_move = remote(DOWN_MOVE, down_ref, down_out, (me, piece_to))
    down_stay = local(4, down_ref, down_out)

    @pl.when(jnp.logical_not(stays))
    def _():
        down_move.start()

    @pl.when(stays)
    def _():
        down_stay.start()

    def units_at(ref, to_side, to_head):
        return cols_of(ref, (to_head * 2 + to_side) * units, units)

    slab_rows = pl.ds(pl.multiple_of(side * w_rows, 16), w_rows)
    targets = [(side, mate), (side, beside), (side, corner)]
    targets += [(1 - side, head) for head in (me, mate, beside, corner)]
    spread = []
    for i, (to_side, to_head) in enumerate(targets):
        device = (to_head, at if i < 3 else other)
        for j, ref in enumerate((gate_ref, up_ref)):
            spread.append(
                remote(
                    UNITS_MOVE + 2 * i + j,
                    units_at(ref, to_side, to_head),
                    slab_out.at[me, slab_rows, pl.ds(j * units, units)],
                    device,
                )
            )
    for copy in spread:
        copy.start()
    own_units = [
        local(
            5 + j,
            units_at(ref, side, me),
            slab_out.at[me, slab_rows, pl.ds(j * units, units)],
        )
        for j, ref in enumerate((gate_ref, up_ref))
    ]
    for copy in own_units:
        copy.start()

    def ring_copy(step):
        block = w_in.at[:, (at + count - 2 * (step - 1)) % count]
        return remote(step, block, block, (me, after), ring_sends, ring_recvs)

    def swap_copy(step):
        block = w_in.at[:, (at + count - 2 * step) % count]
        return remote(step, block, block, (me, other), swap_sends, swap_recvs)

    for copy in split:
        copy.wait_recv()
    own[0].wait()
    own[1].wait()
    ring_copy(1).start()
    swap_copy(0).start()
    tok_far.wait_recv()
    tok_on.start()
    top_slot = side * 4 + me
    far_slot, across_slot = side * 4 + beside, (1 - side) * 4 + me
    corner_slot = (1 - side) * 4 + beside
    top_near = remote(TOP_NEAR, top_ref, tops_out.at[top_slot], (mate, at))
    top_far = remote(TOP_FAR, top_ref, tops_out.at[top_slot], (beside, at))
    top_across = remote(TOP_ACROSS, top_ref, tops_out.at[top_slot], (me, other))
    top_far_on = remote(
        TOP_FAR_ON, tops_out.at[far_slot], tops_out.at[far_slot], (mate, at)
    )
    top_across_on = remote(
        TOP_ACROSS_ON, tops_out.at[across_slot], tops_out.at[across_slot], (mate, at)
    )
    top_corner_on = remote(
        TOP_CORNER_ON, tops_out.at[corner_slot], tops_out.at[corner_slot], (mate, at)
    )
    high = tops_out.at[far_slot, pl.ds(0, half)]
    low = tops_out.at[across_slot, pl.ds(half, half)]
    top_corner_high = remote(TOP_CORNER_HIGH, high, high, (me, other))
    top_corner_low = remote(TOP_CORNER_LOW, low, low, (beside, at))
    top_near.start()
    top_far.start()
    for step in range(1, line):
        ring_copy(step).wait_recv()
        if step < line - 1:
            ring_copy(step + 1).start()
        swap_copy(step).start()

    @pl.when(jnp.logical_not(stays))
    def _():
        down_move.wait_recv()

    @pl.when(stays)
    def _():
        down_stay.wait()

    down_on = remote(DOWN_ONE, down_out, down_one, (me, after))
    down_on.start()
    for copy in spread:
        copy.wait_recv()
    for copy in own_units:
        copy.wait()
    slab_on = remote(SLAB_ON, slab_out, slab_next, (me, after))
    slab_on.start()
    tok_near.wait_recv()
    tok_on.wait_recv()
    own[2].wait()
    own[3].wait()
    for step in range(line):
        swap_copy(step).wait_recv()
    top_across.start()
    keep_in = [
        local(7 + h, w_in.at[h], w_in_out.at[h]) for h in range(4)
    ]
    for copy in keep_in:
        copy.start()

    gains = w_in[:, :, :, COLS_IN : COLS_IN + 128].reshape(width, 128).astype(F32)
    gain_out[...] = transposed(gains)[0:8, :]

    def norm_tile(step, carry):
        head, tile = step // (rows // 32), pl.ds(pl.multiple_of(step % (rows // 32) * 32, 32), 32)
        block = toks[head, tile, :].astype(F32)
        scale = lax.rsqrt(jnp.mean(block * block, axis=1, keepdims=True) + EPS)
        normed[pl.ds(pl.multiple_of(step * 32, 32), 32), :] = (
            block * scale * gain_out[0:1, :]
        ).astype(BF)
        return carry

    lax.fori_loop(0, 4 * rows // 32, norm_tile, 0)
    keep_normed = local(11, normed, normed_out)
    keep_normed.start()
    keep_toks = local(16, toks, toks_out)
    keep_toks.start()

    def project(step, carry):
        tile = pl.ds(pl.multiple_of(step * 256, 256), 256)
        for first, size in SPANS:
            weight = w_in[:, :, :, first : first + size].reshape(width, size)
            raw[tile, first : first + size] = nn(normed[tile, :], weight)
        return carry

    lax.fori_loop(0, 4 * rows // 256, project, 0)
    keep_raw = local(12, raw.at[:, pl.ds(0, COLS_Q + 128)], raw_out)
    keep_raw.start()

    def rotated(block, gain, tile):
        block = block * head_scale(block) * gain
        return block * cos_ref[tile, :] + swap_halves(block) * sin_ref[tile, :]

    def prepare(step, carry):
        tile = pl.ds(pl.multiple_of(step * 64, 64), 64)
        first_half = lanes((64, 128)) < HEAD
        for t in range(QHEADS // 4 // 2):
            block = rotated(raw[tile, t * 128 : (t + 1) * 128], query_gain_ref[...], tile)
            block = block.astype(BF).astype(F32)
            moved = pltpu.roll(block, HEAD, 1)
            query[2 * t, tile, :] = jnp.where(first_half, block, 0.0).astype(BF)
            query[2 * t + 1, tile, :] = jnp.where(first_half, moved, 0.0).astype(BF)
            scaled = block * (SCALE * LOG2E)
            upper = scaled.astype(BF).astype(F32)
            lower = scaled - upper
            wide[2 * t, tile, :] = jnp.where(
                first_half, upper, pltpu.roll(lower, HEAD, 1)
            ).astype(BF)
            wide[2 * t + 1, tile, :] = jnp.where(
                first_half, pltpu.roll(upper, HEAD, 1), lower
            ).astype(BF)
        keys = rotated(raw[tile, COLS_Q : COLS_Q + 128], key_gain_ref[...], tile)
        values = raw[tile, COLS_Q + 128 : COLS_Q + 256]
        kv_own[0, tile, :] = jnp.where(
            first_half, keys, pltpu.roll(values, HEAD, 1)
        ).astype(BF)
        kv_own[1, tile, :] = jnp.where(
            first_half, pltpu.roll(keys, HEAD, 1), values
        ).astype(BF)
        return carry

    lax.fori_loop(0, 4 * rows // 64, prepare, 0)

    kv_one = remote(KV_ONE, kv_own, kv_out.at[2], (me, after))
    kv_two = remote(KV_TWO, kv_out.at[2], kv_out.at[0], (me, after))
    pair_one_even = remote(KV_PAIR_ONE, kv_own, kv_out.at[3], (me, other))
    pair_one_odd = remote(KV_PAIR_ONE, kv_out.at[2], kv_out.at[3], (me, other))
    pair_two_even = remote(KV_PAIR_TWO, kv_out.at[2], kv_out.at[1], (me, other))
    pair_two_odd = remote(KV_PAIR_TWO, kv_out.at[0], kv_out.at[1], (me, other))
    kv_one.start()

    @pl.when(side == 0)
    def _():
        pair_one_even.start()

    keep = [
        local(13, kv_own, kv_out.at[4]),
        local(14, wide, wide_out),
        local(15, query, query_out),
    ]
    for copy in keep:
        copy.start()
    top_far.wait_recv()
    top_far_on.start()
    top_corner_high.start()
    kv_one.wait_recv()
    kv_two.start()

    @pl.when(side == 0)
    def _():
        pair_two_even.start()

    @pl.when(side == 1)
    def _():
        pair_one_odd.start()

    down_on.wait_recv()
    top_across.wait_recv()
    top_across_on.start()
    top_corner_low.start()
    kv_two.wait_recv()

    @pl.when(side == 1)
    def _():
        pair_two_odd.start()

    down_last = remote(DOWN_TWO, down_one, down_two, (me, after))
    down_last.start()
    top_corner_high.wait_recv()
    top_corner_low.wait_recv()
    top_corner_on.start()

    pair_one_even.wait_recv()
    pair_two_even.wait_recv()
    down_last.wait_recv()
    slab_on.wait_recv()
    for copy in (top_near, top_far_on, top_across_on, top_corner_on):
        copy.wait_recv()
    for copy in keep + keep_in + [keep_normed, keep_raw, keep_toks]:
        copy.wait()
    for copy in split + spread:
        copy.wait_send()
    for copy in (tok_near, tok_far, tok_on, top_near, top_far, top_across, top_far_on):
        copy.wait_send()
    for copy in (top_across_on, top_corner_high, top_corner_low, top_corner_on):
        copy.wait_send()
    for copy in (slab_on, down_on, down_last, kv_one, kv_two):
        copy.wait_send()
    pair_one_even.wait_send()
    pair_two_even.wait_send()

    @pl.when(jnp.logical_not(stays))
    def _():
        down_move.wait_send()

    for step in range(line):
        swap_copy(step).wait_send()
        if step:
            ring_copy(step).wait_send()


def first(
    tokens, w_query, rest, w_gate, w_up, w_down, cotangent, cosine, sine, query_gain, key_gain
):
    rows, width = tokens.shape
    count = lax.axis_size("blk")
    w_rows, ff = w_gate.shape
    units = ff // 8
    block = 4 * rows
    anywhere = pl.BlockSpec(memory_space=pl.ANY)
    vmem = pl.BlockSpec(memory_space=pltpu.VMEM)
    shape = jax.ShapeDtypeStruct
    heads = QHEADS // 4
    slab = shape((4, 2 * w_rows, 2 * units), BF)
    dma = pltpu.SemaphoreType.DMA
    return pl.pallas_call(
        functools.partial(first_kernel, count // 2),
        out_shape=(
            shape((heads, block, 128), BF),
            shape((heads, block, 128), BF),
            shape((BACK + 1, 2, block, 128), BF),
            shape((block, COLS_Q + 128), F32),
            shape((block, width), BF),
            shape((4, count, w_rows, 2 * COLS_Q), BF),
            shape((8, rows, width), BF),
            slab,
            slab,
            shape(w_down.shape, BF),
            shape(w_down.shape, BF),
            shape(w_down.shape, BF),
            shape((4, rows, width), BF),
            shape((8, width), F32),
        ),
        in_specs=[anywhere] * 7 + [vmem] * 4,
        out_specs=(anywhere,) * 13 + (vmem,),
        scratch_shapes=[
            pltpu.VMEM((4, rows, width), BF),
            pltpu.VMEM((block, width), BF),
            pltpu.VMEM((4, count, w_rows, 2 * COLS_Q), BF),
            pltpu.VMEM((block, COLS_IN), F32),
            pltpu.VMEM((heads, block, 128), BF),
            pltpu.VMEM((heads, block, 128), BF),
            pltpu.VMEM((2, block, 128), BF),
            dma((FIRST_TRANSFERS,)),
            dma((FIRST_TRANSFERS,)),
            dma((count // 2,)),
            dma((count // 2,)),
            dma((count // 2,)),
            dma((count // 2,)),
            dma((17,)),
        ],
        compiler_params=pltpu.CompilerParams(
            collective_id=2, has_side_effects=True, vmem_limit_bytes=48 << 20
        ),
        cost_estimate=pl.CostEstimate(
            flops=60_000_000_000, bytes_accessed=60_000_000, transcendentals=1_000_000
        ),
        name="first",
    )(
        tokens, w_query, rest, w_gate, w_up, w_down, cotangent, cosine, sine, query_gain, key_gain
    )


THREE, ONE, FOUR_ON, TWO_ON = 0, 2, 4, 6
UNITS_HOME, DOWN_ON, DOWN_HOME = 8, 15, 16
PART_MATE, PART_CORNER, PART_FAR, QUERY_HOME, REST_HOME = 17, 18, 19, 20, 23
LAST_TRANSFERS = 26


def head_means(block):
    low = lanes(block.shape) < HEAD
    first = jnp.sum(jnp.where(low, block, 0.0), axis=1, keepdims=True)
    second = jnp.sum(jnp.where(low, 0.0, block), axis=1, keepdims=True)
    return jnp.where(low, first, second) * (1.0 / HEAD)


class LineSum:
    def __init__(self, part, got, hold, arrive, sems, places, remote):
        self.part, self.got, self.hold, self.arrive = part, got, hold, arrive
        self.swap_sems, self.ring_sems = sems
        self.side, self.place, self.line, self.other, self.after = places
        self.remote = remote

    def target(self, step):
        return (self.place + self.line - step) % self.line

    def swap(self, step):
        to = self.target(step)
        return self.remote(
            step - 1,
            self.part(2 * to + 1 - self.side),
            self.got.at[to],
            self.other,
            *self.swap_sems,
        )

    def pass_on(self, step):
        return self.remote(
            step - 1, self.hold.at[step - 1], self.arrive.at[step - 1], self.after, *self.ring_sems
        )

    def start(self):
        for step in range(1, self.line + 1):
            self.swap(step).start()

    def step(self, step, out=None):
        to = self.target(step)
        self.swap(step).wait_recv()
        total = self.part(2 * to + self.side)[...].astype(F32) + self.got[to].astype(F32)
        if step > 1:
            self.pass_on(step - 1).wait_recv()
            total = total + self.arrive[step - 2].astype(F32)
        if step < self.line:
            self.hold[step - 1] = total.astype(BF)
            self.pass_on(step).start()
        else:
            out[...] = total.astype(out.dtype)

    def drain(self):
        for step in range(1, self.line + 1):
            self.swap(step).wait_send()
            if step < self.line:
                self.pass_on(step).wait_send()


def last_kernel(
    line,
    dq_four_ref,
    dq_two_ref,
    low_four_ref,
    low_two_ref,
    own_four_ref,
    own_two_ref,
    raw_ref,
    cos_ref,
    sin_ref,
    query_gain_ref,
    key_gain_ref,
    normed_ref,
    w_in_ref,
    toks_ref,
    gain_ref,
    gain_two_ref,
    units_ref,
    down_ref,
    down_parts_ref,
    slab_ref,
    dx_out,
    query_out,
    rest_out,
    units_out,
    down_out,
    w_out_out,
    gains_out,
    low,
    three,
    one,
    four_in,
    two_in,
    raw,
    normed,
    turned,
    w_in,
    toks,
    scales,
    grads,
    query_part,
    rest_part,
    query_got,
    rest_got,
    query_hold,
    rest_hold,
    query_arrive,
    rest_arrive,
    query_sum,
    rest_sum,
    slab,
    slab_got,
    slab_hold,
    slab_arrive,
    down_own,
    down_in,
    parts,
    part_got,
    part_far,
    gain_rows,
    head_gains,
    gains_in,
    sends,
    recvs,
    line_sems,
    gain_sends,
    gain_recvs,
    locals_,
):
    me, at = lax.axis_index("head"), lax.axis_index("blk")
    count = lax.axis_size("blk")
    side, place = at % 2, at // 2
    odd = me % 2
    mate, beside, corner = me + 1 - 2 * odd, (me + 2) % 4, (me + 3 - 2 * odd) % 4
    other = at + 1 - 2 * side
    after, before = (at + 2) % count, (at + count - 2) % count
    rows, width = dx_out.shape
    block = 4 * rows
    w_rows = w_in_ref.shape[2]
    piece_from = (at % 2) * line + at // 2
    piece_to = 2 * (at % line) + at // line
    stays = piece_to == at

    rounds = [(mate, at), (beside, at), (me, other)]
    bit = 1
    while bit < line:
        rounds.append((me, at + 2 * bit * (1 - 2 * ((place // bit) % 2))))
        bit *= 2
    barrier = pltpu.get_barrier_semaphore()
    peers = [(corner, at), (me, after), (me, before)]
    peers += [(head, other) for head in (mate, beside, corner)] + rounds
    for peer in peers:
        pl.semaphore_signal(barrier, inc=1, device_id=peer, device_id_type=MESH)

    @pl.when(jnp.logical_not(stays))
    def _():
        for peer in ((me, piece_to), (me, piece_from)):
            pl.semaphore_signal(barrier, inc=1, device_id=peer, device_id_type=MESH)

    pl.semaphore_wait(barrier, jnp.where(stays, len(peers), len(peers) + 2))

    def remote(index, source, target, device, send=sends, recv=recvs):
        return pltpu.make_async_remote_copy(
            src_ref=source,
            dst_ref=target,
            send_sem=send.at[index],
            recv_sem=recv.at[index],
            device_id=device,
            device_id_type=MESH,
        )

    def local(index, source, target):
        return pltpu.make_async_copy(source, target, locals_.at[index])

    low_refs, own_refs = (low_four_ref, low_two_ref), (own_four_ref, own_two_ref)
    three_on = [remote(THREE + g, low_refs[g].at[1], three.at[g], (me, other)) for g in (0, 1)]
    one_on = [remote(ONE + g, low_refs[g].at[3], one.at[g], (me, other)) for g in (0, 1)]
    for copy in three_on + one_on:
        copy.start()
    loads = [
        local(0, normed_ref, normed),
        local(1, raw_ref, raw),
        local(2, w_in_ref, w_in),
        local(3, toks_ref, toks),
        local(4, slab_ref, slab),
        local(5, down_parts_ref.at[place], down_own),
    ]
    for copy in loads:
        copy.start()
    low_loads = [
        local(6 + 2 * g + i, low_refs[g].at[2 * i], low.at[g, i]) for g in (0, 1) for i in (0, 1)
    ]
    for copy in low_loads:
        copy.start()
    down_on = remote(DOWN_ON, down_ref, down_in, (me, after))
    down_on.start()
    targets = [(side, mate), (side, beside), (side, corner)]
    targets += [(1 - side, head) for head in (me, mate, beside, corner)]
    homes = []
    for i, (to_side, to_head) in enumerate(targets):
        device = (to_head, at if i < 3 else other)
        source = units_ref.at[to_head, pl.ds(pl.multiple_of(to_side * w_rows, 16), w_rows)]
        homes.append(remote(UNITS_HOME + i, source, units_out.at[side * 4 + me], device))
    units_own = local(
        10,
        units_ref.at[me, pl.ds(pl.multiple_of(side * w_rows, 16), w_rows)],
        units_out.at[side * 4 + me],
    )

    places = (side, place, line, (me, other), (me, after))

    def line_sum(which, part, got, hold, arrive):
        sems = [(line_sems.at[which, i, 0], line_sems.at[which, i, 1]) for i in (0, 1)]
        return LineSum(part, got, hold, arrive, sems, places, remote)

    query_line = line_sum(
        0, lambda b: query_part.at[:, b], query_got, query_hold, query_arrive
    )
    rest_line = line_sum(1, lambda b: rest_part.at[:, b], rest_got, rest_hold, rest_arrive)
    slab_line = line_sum(2, lambda b: slab.at[b], slab_got, slab_hold, slab_arrive)

    head_gains[...] = jnp.zeros_like(head_gains)
    gain_rows[...] = jnp.zeros_like(gain_rows)
    loads[0].wait()
    loads[1].wait()

    def head_back(out, cols, tile, gain_tile, gain_row):
        value = raw[tile, cols]
        scale = head_scale(value)
        grad = out * cos_ref[tile, :] + swap_halves(out * sin_ref[tile, :])
        head_gains[0, gain_row : gain_row + 1, :] += jnp.sum(
            grad * value * scale, axis=0, keepdims=True
        )
        inner = grad * gain_tile
        mean = head_means(inner * value)
        return (scale * inner - value * (scale * scale * scale * mean)).astype(BF)

    def query_rows(step, carry):
        tile = pl.ds(pl.multiple_of(step * 64, 64), 64)
        for i in range(3):
            t = odd + i if i < 2 else 2 * (1 - odd)
            cols = pl.ds(pl.multiple_of(t * 128, 128), 128)
            if i < 2:
                out = dq_four_ref[tile, i * 128 : (i + 1) * 128]
            else:
                out = dq_two_ref[tile, :]
            grads[tile, cols] = head_back(out, cols, tile, query_gain_ref[...], 0)
        return carry

    lax.fori_loop(0, block // 64, query_rows, 0)
    per_tile = 256 // w_rows
    tiles_per_head = count // per_tile

    def query_weights(step, carry):
        span = pl.ds(pl.multiple_of(step * 256, 256), 256)
        turned[span, :] = transposed(normed[:, span])
        first = pl.ds(step % tiles_per_head * per_tile, per_tile)
        part = nn(turned[span, :], grads[:, 0:COLS_Q])
        query_part[step // tiles_per_head, first] = part.astype(BF).reshape(
            per_tile, w_rows, COLS_Q
        )
        return carry

    lax.fori_loop(0, width // 256, query_weights, 0)
    for copy in low_loads:
        copy.wait()

    for copy in three_on + one_on:
        copy.wait_recv()

    def add_pair(step, carry):
        tile = pl.ds(pl.multiple_of(step * 128, 128), 128)
        for g in (0, 1):
            got_three, got_one = three[g, tile, :].astype(F32), one[g, tile, :].astype(F32)
            to_four = jnp.where(side == 0, 0.0, got_three)
            to_two = jnp.where(side == 0, got_three, got_one)
            low[g, 0, tile, :] = (low[g, 0, tile, :].astype(F32) + to_four).astype(BF)
            low[g, 1, tile, :] = (low[g, 1, tile, :].astype(F32) + to_two).astype(BF)
        return carry

    lax.fori_loop(0, block // 128, add_pair, 0)
    four_on = [remote(FOUR_ON + g, low.at[g, 0], four_in.at[g], (me, before)) for g in (0, 1)]
    two_on = [remote(TWO_ON + g, low.at[g, 1], two_in.at[g], (me, before)) for g in (0, 1)]
    for copy in four_on:
        copy.start()
    query_line.start()
    for copy in homes:
        copy.start()
    units_own.start()
    loads[4].wait()
    slab_line.start()

    loads[3].wait()

    def token_scales(step, carry):
        tile = pl.ds(pl.multiple_of(step % (rows // 32) * 32, 32), 32)
        value = toks[step // (rows // 32), tile, :].astype(F32)
        scales[pl.ds(pl.multiple_of(step * 32, 32), 32), :] = lax.rsqrt(
            jnp.mean(value * value, axis=1, keepdims=True) + EPS
        )
        return carry

    lax.fori_loop(0, block // 32, token_scales, 0)
    query_line.step(1)
    for copy in four_on:
        copy.wait_recv()

    def add_four(step, carry):
        tile = pl.ds(pl.multiple_of(step * 128, 128), 128)
        for g in (0, 1):
            low[g, 1, tile, :] = (
                low[g, 1, tile, :].astype(F32) + four_in[g, tile, :].astype(F32)
            ).astype(BF)
        return carry

    lax.fori_loop(0, block // 128, add_four, 0)
    for copy in two_on:
        copy.start()
    loads[5].wait()
    down_on.wait_recv()

    def add_down(step, carry):
        span = pl.ds(pl.multiple_of(step * 256, 256), 256)
        down_own[:, span] = (
            down_own[:, span].astype(F32) + down_in[:, span].astype(F32)
        ).astype(BF)
        return carry

    lax.fori_loop(0, width // 256, add_down, 0)
    down_home = remote(DOWN_HOME, down_own, down_out, (me, piece_from))
    down_stay = local(11, down_own, down_out)

    @pl.when(jnp.logical_not(stays))
    def _():
        down_home.start()

    @pl.when(stays)
    def _():
        down_stay.start()

    slab_line.step(1)
    for step in range(2, line + 1):
        query_line.step(step, query_sum)
    query_home = [
        remote(QUERY_HOME + i, query_sum.at[to], query_out.at[me], (to, at))
        for i, to in enumerate((mate, beside, corner))
    ]
    query_own = local(12, query_sum.at[me], query_out.at[me])
    for copy in query_home:
        copy.start()
    query_own.start()
    for copy in two_on:
        copy.wait_recv()

    def key_rows(step, carry):
        tile = pl.ds(pl.multiple_of(step * 64, 64), 64)
        first_half = lanes((64, 128)) < HEAD
        both = []
        for g in (0, 1):
            from_pair = jnp.where(side == 0, one[g, tile, :].astype(F32), 0.0)
            both.append(own_refs[g][tile, :] + from_pair + two_in[g, tile, :].astype(F32))
        zero = jnp.where(odd == 0, both[0], both[1])
        unit = jnp.where(odd == 0, both[1], both[0])
        keys = jnp.where(first_half, zero, pltpu.roll(unit, HEAD, 1))
        values = jnp.where(first_half, pltpu.roll(zero, HEAD, 1), unit)
        cols = pl.ds(COLS_Q, 128)
        grads[tile, cols] = head_back(keys, cols, tile, key_gain_ref[...], 1)
        grads[tile, COLS_Q + 128 : COLS_Q + 256] = values.astype(BF)
        return carry

    lax.fori_loop(0, block // 64, key_rows, 0)

    loads[2].wait()

    def token_cols(step, carry):
        span = pl.ds(pl.multiple_of(step * 256, 256), 256)
        first = pl.ds(step % tiles_per_head * per_tile, per_tile)
        weight = w_in[step // tiles_per_head, first, :, 0:COLS_IN].reshape(256, COLS_IN)
        part = nt(grads[...], weight)
        parts[:, :, span] = part.astype(BF).reshape(4, rows, 256)
        value = toks[:, :, span].reshape(block, 256).astype(F32)
        gain_rows[0:1, span] = jnp.sum(part * value * scales[...], axis=0, keepdims=True)
        return carry

    lax.fori_loop(0, width // 256, token_cols, 0)
    to_mate = [
        remote(PART_CORNER, parts.at[corner], part_got.at[1], (mate, at)),
        remote(PART_MATE, parts.at[mate], part_got.at[0], (mate, at)),
    ]
    for copy in to_mate:
        copy.start()
    gain_rows[1:2, :] = gain_two_ref[...]

    def rest_weights(step, carry):
        span = pl.ds(pl.multiple_of(step * 256, 256), 256)
        first = pl.ds(step % tiles_per_head * per_tile, per_tile)
        head = step // tiles_per_head
        part = nn(turned[span, :], grads[:, COLS_Q : COLS_Q + 256])
        rest_part[head, first, :, 0:256] = part.astype(BF).reshape(per_tile, w_rows, 256)
        gain_cols = transposed(gain_rows[:, span])
        rest_part[head, first, :, 256:384] = gain_cols.astype(BF).reshape(per_tile, w_rows, 128)
        return carry

    lax.fori_loop(0, width // 256, rest_weights, 0)
    rest_line.start()
    to_mate[0].wait_recv()

    def add_part(step, carry):
        tile = pl.ds(pl.multiple_of(step * 32, 32), 32)
        parts[beside, tile, :] = (
            parts[beside, tile, :].astype(F32) + part_got[1, tile, :].astype(F32)
        ).astype(BF)
        return carry

    lax.fori_loop(0, rows // 32, add_part, 0)
    part_on = remote(PART_FAR, parts.at[beside], part_far, (beside, at))
    part_on.start()

    def gain_round(i):
        return remote(i, head_gains.at[i], gains_in.at[i], rounds[i], gain_sends, gain_recvs)

    rest_line.step(1)
    for i in range(len(rounds)):
        gain_round(i).start()
        gain_round(i).wait_recv()
        head_gains[i + 1] = head_gains[i] + gains_in[i]
        if i + 2 <= line:
            slab_line.step(i + 2, w_out_out)
            rest_line.step(i + 2, rest_sum)
    for step in range(len(rounds) + 2, line + 1):
        slab_line.step(step, w_out_out)
        rest_line.step(step, rest_sum)
    gains_out[...] = head_gains[len(rounds)]
    rest_home = [
        remote(REST_HOME + i, rest_sum.at[to], rest_out.at[me], (to, at))
        for i, to in enumerate((mate, beside, corner))
    ]
    rest_own = local(13, rest_sum.at[me], rest_out.at[me])
    for copy in rest_home:
        copy.start()
    rest_own.start()

    to_mate[1].wait_recv()
    part_on.wait_recv()

    def norm_back(step, carry):
        tile = pl.ds(pl.multiple_of(step * 32, 32), 32)
        grad = (
            parts[me, tile, :].astype(F32)
            + part_got[0, tile, :].astype(F32)
            + part_far[tile, :].astype(F32)
        )
        value = toks[me, tile, :].astype(F32)
        scale = lax.rsqrt(jnp.mean(value * value, axis=1, keepdims=True) + EPS)
        inner = grad * gain_ref[0:1, :]
        mean = jnp.mean(inner * value, axis=1, keepdims=True)
        dx_out[tile, :] = scale * inner - value * (scale * scale * scale * mean)
        return carry

    lax.fori_loop(0, rows // 32, norm_back, 0)

    for copy in homes + query_home + rest_home:
        copy.wait()
    for copy in (units_own, query_own, rest_own):
        copy.wait()
    for copy in three_on + one_on + four_on + two_on + to_mate + [down_on, part_on]:
        copy.wait_send()

    @pl.when(jnp.logical_not(stays))
    def _():
        down_home.wait()

    @pl.when(stays)
    def _():
        down_stay.wait()

    for total in (query_line, rest_line, slab_line):
        total.drain()
    for i in range(len(rounds)):
        gain_round(i).wait_send()


def last(
    dq, dkv_low, dkv_own, raw, cosine, sine, query_gain, key_gain, normed, w_in, toks, gains,
    gain_two, units, down, down_parts, slab,
):
    _, rows, width = toks.shape
    _, count, w_rows, _ = w_in.shape
    line = count // 2
    block = 4 * rows
    anywhere = pl.BlockSpec(memory_space=pl.ANY)
    vmem = pl.BlockSpec(memory_space=pltpu.VMEM)
    shape = jax.ShapeDtypeStruct
    dma = pltpu.SemaphoreType.DMA
    rounds = 3 + int(math.log2(line))
    part = (4, w_rows, COLS_Q)
    out_rows = slab.shape[1]
    return pl.pallas_call(
        functools.partial(last_kernel, line),
        out_shape=(
            shape((rows, width), F32),
            shape(part, BF),
            shape(part, BF),
            shape((8, w_rows, units.shape[2]), BF),
            shape(down.shape, BF),
            shape((out_rows, width), F32),
            shape((8, 128), F32),
        ),
        in_specs=[vmem] * 2 + [anywhere] * 2 + [vmem] * 2 + [anywhere] + [vmem] * 4
        + [anywhere] * 3 + [vmem] * 2 + [anywhere] * 4,
        out_specs=(vmem,) + (anywhere,) * 4 + (vmem,) * 2,
        scratch_shapes=[
            pltpu.VMEM((2, 2, block, 128), BF),
            pltpu.VMEM((2, block, 128), BF),
            pltpu.VMEM((2, block, 128), BF),
            pltpu.VMEM((2, block, 128), BF),
            pltpu.VMEM((2, block, 128), BF),
            pltpu.VMEM((block, COLS_Q + 128), F32),
            pltpu.VMEM((block, width), BF),
            pltpu.VMEM((width, block), BF),
            pltpu.VMEM(w_in.shape, BF),
            pltpu.VMEM(toks.shape, BF),
            pltpu.VMEM((block, 1), F32),
            pltpu.VMEM((block, COLS_IN), BF),
            pltpu.VMEM((4, count, w_rows, COLS_Q), BF),
            pltpu.VMEM((4, count, w_rows, COLS_Q), BF),
            pltpu.VMEM((line,) + part, BF),
            pltpu.VMEM((line,) + part, BF),
            pltpu.VMEM((line - 1,) + part, BF),
            pltpu.VMEM((line - 1,) + part, BF),
            pltpu.VMEM((line - 1,) + part, BF),
            pltpu.VMEM((line - 1,) + part, BF),
            pltpu.VMEM(part, BF),
            pltpu.VMEM(part, BF),
            pltpu.VMEM(slab.shape, BF),
            pltpu.VMEM((line,) + slab.shape[1:], BF),
            pltpu.VMEM((line - 1,) + slab.shape[1:], BF),
            pltpu.VMEM((line - 1,) + slab.shape[1:], BF),
            pltpu.VMEM(down.shape, BF),
            pltpu.VMEM(down.shape, BF),
            pltpu.VMEM((4, rows, width), BF),
            pltpu.VMEM((2, rows, width), BF),
            pltpu.VMEM((rows, width), BF),
            pltpu.VMEM((128, width), F32),
            pltpu.VMEM((rounds + 1, 8, 128), F32),
            pltpu.VMEM((rounds, 8, 128), F32),
            dma((LAST_TRANSFERS,)),
            dma((LAST_TRANSFERS,)),
            dma((3, 2, 2, line)),
            dma((rounds,)),
            dma((rounds,)),
            dma((14,)),
        ],
        compiler_params=pltpu.CompilerParams(
            collective_id=3, has_side_effects=True, vmem_limit_bytes=58 << 20
        ),
        cost_estimate=pl.CostEstimate(
            flops=60_000_000_000, bytes_accessed=60_000_000, transcendentals=1_000_000
        ),
        name="last",
    )(
        *dq, *dkv_low, *dkv_own, raw, cosine, sine, query_gain, key_gain, normed, w_in, toks, gains,
        gain_two, units, down, down_parts, slab,
    )


def shards(
    tokens,
    doc_lengths,
    norm1_gain,
    w_query,
    w_key,
    w_value,
    query_gain,
    key_gain,
    w_out,
    norm2_gain,
    w_gate,
    w_up,
    w_down,
    cotangent,
):
    tok_rows, width = tokens.shape
    blocks = lax.axis_size("blk")
    groups = lax.axis_size("head")
    group_id = lax.axis_index("head")
    blk_place = lax.axis_index("blk")
    block_len = groups * tok_rows
    per_group = QHEADS // groups
    head_ratio = QHEADS // KVHEADS
    w_rows = w_query.shape[0]
    line = blocks // 2
    side = blk_place % 2
    ff_rows = w_down.shape[0]
    ff_cols = line * ff_rows
    q_cols = per_group * HEAD
    firsts = [g * per_group // head_ratio for g in range(groups)]
    odd = group_id % 2

    starts = jnp.cumsum(doc_lengths) - doc_lengths
    offsets = jnp.arange(block_len, dtype=jnp.int32)
    token_pos = blk_place * block_len + offsets
    inside = starts[None, :] <= token_pos[:, None]
    token_start = jnp.max(jnp.where(inside, starts[None, :], 0), axis=1)
    in_doc = token_pos - token_start
    rope_freq = jnp.exp(-math.log(10000.0) * jnp.arange(HEAD // 2, dtype=F32) / (HEAD // 2))
    rope_angle = in_doc.astype(F32)[:, None] * rope_freq[None, :]
    cosine, sine = jnp.cos(rope_angle), jnp.sin(rope_angle)
    cosine = jnp.concatenate([cosine] * 4, axis=1)
    sine = jnp.concatenate([-sine, sine] * 2, axis=1)
    window_start = token_start - (blk_place - BACK) * block_len
    tiles = block_len // TILE
    edges = jnp.stack(
        [window_start[::TILE], window_start[TILE - 1 :: TILE]], axis=1
    ).reshape(2 * tiles)
    meta = jnp.concatenate([odd[None].astype(jnp.int32), edges.astype(jnp.int32)])

    rest = []
    for g in range(groups):
        kv = slice(firsts[g] * HEAD, (firsts[g] + 2) * HEAD)
        rest += [
            w_key[:, kv],
            w_value[:, kv],
            norm1_gain[:, None],
            norm2_gain[:, None],
            jnp.zeros((w_rows, 126), BF),
        ]
    rest = jnp.concatenate(rest, axis=1).reshape(w_rows, groups, COLS_Q)
    rest = jnp.swapaxes(rest, 0, 1)
    query_row = jnp.concatenate([query_gain, query_gain]).astype(F32)[None, :]
    key_row = jnp.concatenate([key_gain, key_gain]).astype(F32)[None, :]
    (
        wide,
        queries,
        kv_window,
        raw,
        normed_one,
        w_in,
        top,
        slab,
        slab_next,
        down_own,
        down_one,
        down_two,
        toks,
        gains,
    ) = first(
        tokens,
        w_query,
        rest,
        w_gate,
        w_up,
        w_down,
        cotangent,
        cosine,
        sine,
        query_row,
        key_row,
    )
    slabs, downs = [slab, slab_next], [down_own, down_one, down_two]
    for _ in range(line - 4):
        slabs.append(ring(slabs[-1], 2))
        downs.append(ring(downs[-1], 2))
    slabs, downs, w_out, queries = sync(slabs, downs, w_out, queries)
    slabs.append(ring(slabs[-1], 2))
    downs.append(ring(downs[-1], 2))
    w_o = gather_blk(w_out, 0).reshape(blocks * w_out.shape[0], width)
    w_o = gather_head(w_o).reshape(QHEADS * HEAD, width)
    kept, attn_out = attend(meta, wide, kv_window, window_start[:, None])
    kept, attn_out, slabs, downs, w_o = sync(kept, attn_out, slabs, downs, w_o)
    place = blk_place // 2
    w_d = jnp.zeros((line, ff_rows, width), BF)
    for step, block in enumerate(downs):
        w_d = put(w_d, block, (place - step) % line)
    attn_out = attn_out.reshape(groups, tok_rows, q_cols)

    (
        resid,
        grad_resid,
        grad_attn,
        mixed,
        grad_mix,
        out_part,
        gu_parts,
        gu_moved,
        down_parts,
        grad_gain_two,
    ) = middle(
        attn_out,
        tokens,
        w_o,
        gains[1:2],
        slabs,
        w_d.reshape(ff_cols, width),
        top,
    )
    down_parts = down_parts.reshape(line, ff_rows, width)
    gu_parts = gu_parts.reshape(groups, line, 2 * w_rows, 2 * ff_cols)
    down_sum = LineScatter(lambda p: take(down_parts, p))
    gu_sum = LineScatter(lambda p: take(gu_parts, p, 1))
    gu_sum.total = gu_moved
    gu_sum.add()
    out_part = out_part.reshape(2, groups, tok_rows, width)
    out_parts = matmul_tn(mixed, grad_attn).astype(BF).reshape(groups, -1, width)
    down_sum.ahead(line - 4)
    gu_sum.ahead(line - 4)
    down_moved, gu_moved = down_sum.send(), gu_sum.send()
    out_act = (resid + scatter_pair(out_part)).astype(BF)
    back = functools.partial(
        attend_back,
        meta=meta,
        wide=wide,
        queries=queries,
        kv=kv_window,
        kept=kept,
        grads=grad_mix.reshape(block_len, q_cols),
        starts=window_start[None, :],
    )
    four = back(0)
    four, down_moved, gu_moved, out_act, kv_window = sync(
        four, down_moved, gu_moved, out_act, kv_window
    )
    down_sum.total, gu_sum.total = down_moved, gu_moved
    down_sum.add()
    gu_sum.add()
    down_moved, gu_moved = down_sum.send(), gu_sum.send()
    out_slab = scatter_head(out_parts).astype(BF).reshape(blocks, w_out.shape[0], width)
    two = back(1, kv=kv_window)
    four, two, down_moved, gu_moved, out_slab = sync(
        four, two, down_moved, gu_moved, out_slab
    )
    down_sum.total, gu_sum.total = down_moved, gu_moved
    down_sum.add()
    gu_sum.add()
    token_part, query_owned, rest_owned, units_owned, down_owned, d_w_out, head_gains = last(
        (four[0], two[0]),
        (four[1], two[1]),
        (four[2], two[2]),
        raw,
        cosine,
        sine,
        query_row,
        key_row,
        normed_one,
        w_in,
        toks,
        gains,
        grad_gain_two,
        gu_sum.total.astype(BF),
        down_sum.total.astype(BF),
        down_parts,
        out_slab,
    )
    d_tokens = grad_resid + token_part
    d_w_down = down_owned.astype(F32)
    units = units_owned.reshape(2, groups, w_rows, 2, ff_cols).astype(F32)
    units = jnp.transpose(units, (3, 2, 1, 0, 4)).reshape((2,) + w_gate.shape)
    d_w_gate, d_w_up = units[0], units[1]
    gain_sums = head_gains[:2, :HEAD] + head_gains[:2, HEAD:]
    owned = jnp.concatenate([query_owned, rest_owned], axis=2).astype(F32)
    owned = jnp.swapaxes(owned, 0, 1)
    d_w_query = owned[:, :, :q_cols].reshape(w_rows, QHEADS * HEAD)
    key_heads, value_heads = [], []
    for head_id in range(KVHEADS):
        keys_of, values_of = [], []
        for g in range(groups):
            for slot in range(2):
                if firsts[g] + slot == head_id:
                    at = q_cols + slot * HEAD
                    keys_of.append(owned[:, g, at : at + HEAD])
                    at += 2 * HEAD
                    values_of.append(owned[:, g, at : at + HEAD])
        key_heads.append(functools.reduce(jnp.add, keys_of))
        value_heads.append(functools.reduce(jnp.add, values_of))
    d_w_key = jnp.concatenate(key_heads, axis=1)
    d_w_value = jnp.concatenate(value_heads, axis=1)
    d_norm1_gain = jnp.sum(owned[:, :, q_cols + 4 * HEAD], axis=1)
    d_norm2_gain = jnp.sum(owned[:, :, q_cols + 4 * HEAD + 1], axis=1)
    return (
        out_act,
        d_tokens,
        d_norm1_gain,
        d_w_query,
        d_w_key,
        d_w_value,
        gain_sums[0],
        gain_sums[1],
        d_w_out,
        d_norm2_gain,
        d_w_gate,
        d_w_up,
        d_w_down,
    )


def solution(mesh):
    by_token = P(("blk", "head"), None)
    by_row = P(("head", "blk"), None)
    by_entry = P(("head", "blk"))
    in_specs = (
        by_token,
        P(),
        by_entry,
        by_row,
        by_row,
        by_row,
        P(),
        P(),
        by_row,
        by_entry,
        by_row,
        by_row,
        by_row,
        by_token,
    )
    out_specs = (
        by_token,
        by_token,
        by_entry,
        by_row,
        by_row,
        by_row,
        P(),
        P(),
        by_row,
        by_entry,
        by_row,
        by_row,
        by_row,
    )
    return jax.shard_map(shards, mesh=mesh, in_specs=in_specs, out_specs=out_specs, check_vma=False)
```

```python
import functools
import math

import jax
import jax.numpy as jnp
from jax import lax
from jax.experimental import pallas as pl
from jax.experimental.pallas import tpu as pltpu
from jax.sharding import PartitionSpec as P

QHEADS = 24
KVHEADS = 6
HEAD = 64
MAXDOC = 4096

EPS = 1e-06
SCALE = 0.125
LOG2E = 1.4426950408889634
NEG = -1e30
TILE = 256
BACK = 4
BF = jnp.bfloat16
F32 = jnp.float32


def matmul(left_side, right_side):
    return jnp.dot(left_side, right_side, preferred_element_type=F32)


def matmul_tn(left_side, right_side):
    return lax.dot_general(
        left_side, right_side, (((0,), (0,)), ((), ())), preferred_element_type=F32
    )


def matmul_nt(left_side, right_side):
    return lax.dot_general(
        left_side, right_side, (((1,), (1,)), ((), ())), preferred_element_type=F32
    )


def swap(block, axis, bit):
    count = lax.axis_size(axis)
    return lax.ppermute(block, axis, [(i, i ^ bit) for i in range(count)])


def ring(block, step):
    count = lax.axis_size("blk")
    return lax.ppermute(block, "blk", [(i, (i + step) % count) for i in range(count)])


def put(full, part, index, axis=0):
    return lax.dynamic_update_index_in_dim(full, part, index, axis)


def take(full, index, axis=0):
    return lax.dynamic_index_in_dim(full, index, axis, keepdims=False)


def place_of():
    at = lax.axis_index("blk")
    return at // 2, at % 2, lax.axis_size("blk") // 2


class LineScatter:
    def __init__(self, chunk):
        self.place, _, self.line = place_of()
        self.chunk = chunk
        self.step = 1
        self.total = chunk((self.place - 1) % self.line)

    def send(self):
        self.total = ring(self.total.astype(BF), 2)
        return self.total

    def add(self):
        self.step += 1
        mine = self.chunk((self.place - self.step) % self.line)
        self.total = self.total.astype(F32) + mine.astype(F32)

    def ahead(self, steps):
        for _ in range(steps):
            self.send()
            self.add()


def gather_blk(part, axis=0):
    place, side, line = place_of()
    shape = part.shape[:axis] + (line, 2) + part.shape[axis:]
    full = jnp.zeros(shape, part.dtype)
    held = part

    def store(full, block, source, side):
        block = block.reshape(block.shape[:axis] + (1, 1) + block.shape[axis:])
        at = [0] * full.ndim
        at[axis], at[axis + 1] = source, side
        return lax.dynamic_update_slice(full, block, at)

    for step in range(line):
        if step:
            held = ring(held, 2)
        other = swap(held, "blk", 1)
        source = (place - step) % line
        full = store(full, held, source, side)
        full = store(full, other, source, 1 - side)
    return full


def sync(*trees):
    return lax.optimization_barrier(trees)


def nt(left_side, right_side):
    return lax.dot_general(
        left_side, right_side, (((1,), (1,)), ((), ())), preferred_element_type=F32
    )


def nn(left_side, right_side):
    return lax.dot_general(
        left_side, right_side, (((1,), (0,)), ((), ())), preferred_element_type=F32
    )


def lanes(shape):
    return lax.broadcasted_iota(jnp.int32, shape, len(shape) - 1)


def transposed(block):
    return jnp.swapaxes(block, 0, 1)


def head_groups(meta_ref):
    odd = meta_ref[0]
    return ((4, 2 * odd, odd), (2, 4 * (1 - odd), 1 - odd))


def split_window(kv_ref, keys, values, step, slot):
    per_block = kv_ref.shape[2] // TILE
    block, part = step // per_block, step % per_block
    source = pl.ds(pl.multiple_of(part * TILE, TILE), TILE)
    target = pl.ds(pl.multiple_of(step * TILE, TILE), TILE)
    low = lanes((TILE, 128)) < HEAD
    both = kv_ref[block, slot, source, :].astype(F32)
    moved = pltpu.roll(both, HEAD, 1)
    keys[target, 0:128] = jnp.where(low, both, moved).astype(BF)
    values[target, :] = jnp.where(low, moved, 1.0).astype(BF)
    return target


def attend_kernel(
    meta_ref, query_ref, kv_ref, start_ref, out_ref, low_ref, acc_ref, keys, values
):
    heads, rows, _ = query_ref.shape
    base = keys.shape[1] - rows
    lane = lanes((TILE, 128))

    def fill(step, carry):
        for slot in range(2):
            split_window(kv_ref, keys.at[slot], values.at[slot], step, slot)
        return carry

    lax.fori_loop(0, keys.shape[1] // TILE, fill, 0)
    for count, first, slot in head_groups(meta_ref):
        for tile in range(rows // TILE):
            q_at = tile * TILE
            low, high = meta_ref[1 + 2 * tile], meta_ref[2 + 2 * tile]
            queries = query_ref[pl.ds(first, count), q_at : q_at + TILE, :].reshape(
                count * TILE, 2 * HEAD
            )
            acc = acc_ref.at[pl.ds(0, count * TILE)]
            acc[...] = jnp.zeros((count * TILE, 2 * HEAD), F32)
            start_col = start_ref[q_at : q_at + TILE, :]
            q_pos = base + q_at + lax.broadcasted_iota(jnp.int32, (TILE, 1), 0)

            def step(at, carry, masked):
                k_at = pl.multiple_of(at * TILE, TILE)
                scores = nt(queries, keys[slot, pl.ds(k_at, TILE), :])
                if masked:
                    k_pos = k_at + lax.broadcasted_iota(jnp.int32, (1, TILE), 1)
                    allowed = (start_col <= k_pos) & (k_pos <= q_pos)
                    scores = jnp.where(
                        allowed[None], scores.reshape(count, TILE, TILE), NEG
                    ).reshape(count * TILE, TILE)
                weights = jnp.exp2(scores).astype(BF)
                acc[...] += nn(weights, values[slot, pl.ds(k_at, TILE), :])
                return carry

            begin = low // TILE
            last = (base + q_at) // TILE
            clear = jnp.minimum((high + TILE - 1) // TILE, last)
            lax.fori_loop(begin, clear, functools.partial(step, masked=True), 0)
            lax.fori_loop(clear, last, functools.partial(step, masked=False), 0)
            step(last, 0, True)
            for j in range(count):
                part = acc_ref[j * TILE : (j + 1) * TILE, :]
                total = part[:, HEAD : HEAD + 1]
                out_ref[first + j, q_at : q_at + TILE, :] = jnp.where(
                    lane < HEAD, part / total, jnp.log2(total)
                )

    def lay(step, carry):
        tile = pl.ds(pl.multiple_of(step * TILE, TILE), TILE)
        for t in range(heads // 2):
            pair = jnp.where(
                lane < HEAD, out_ref[2 * t, tile, :], pltpu.roll(out_ref[2 * t + 1, tile, :], HEAD, 1)
            )
            low_ref[tile, t * 128 : (t + 1) * 128] = pair.astype(BF)
        return carry

    lax.fori_loop(0, rows // TILE, lay, 0)


def attend(meta, queries, kv, starts):
    heads, rows, _ = queries.shape
    window = kv.shape[0] * rows
    vmem = pl.BlockSpec(memory_space=pltpu.VMEM)
    return pl.pallas_call(
        attend_kernel,
        out_shape=(
            jax.ShapeDtypeStruct((heads, rows, 2 * HEAD), F32),
            jax.ShapeDtypeStruct((rows, heads * HEAD), BF),
        ),
        in_specs=[pl.BlockSpec(memory_space=pltpu.SMEM)] + [vmem] * 3,
        out_specs=(vmem, vmem),
        scratch_shapes=[
            pltpu.VMEM((4 * TILE, 2 * HEAD), F32),
            pltpu.VMEM((2, window, 2 * HEAD), BF),
            pltpu.VMEM((2, window, 2 * HEAD), BF),
        ],
        compiler_params=pltpu.CompilerParams(vmem_limit_bytes=48 << 20),
        cost_estimate=pl.CostEstimate(
            flops=60_000_000_000, bytes_accessed=20_000_000, transcendentals=20_000_000
        ),
        name="attend",
    )(meta, queries, kv, starts)


def attend_back_kernel(
    which,
    meta_ref,
    wide_ref,
    query_ref,
    kv_ref,
    out_ref,
    grad_ref,
    start_ref,
    dq_ref,
    low_ref,
    own_ref,
    keys,
    values,
    keys_t,
    query_t,
    grad_t,
    grads,
    dq,
    dkv,
):
    rows = query_ref.shape[1]
    window = keys.shape[0]
    base = window - rows
    lane = lanes((TILE, 128))
    low_lane = lane < HEAD
    count, first, slot = head_groups(meta_ref)[which]

    def fill(step, carry):
        target = split_window(kv_ref, keys, values, step, slot)
        keys[target, 128:256] = jnp.ones((TILE, 128), BF)
        keys_t[:, target] = transposed(keys[target, 0:128])[0:HEAD, :]
        dkv[target, :] = jnp.zeros((TILE, 128), F32)
        return carry

    lax.fori_loop(0, window // TILE, fill, 0)

    def low_terms(value, first):
        out = jnp.zeros_like(value)
        for i in range(3):
            term = value.astype(BF).astype(F32)
            out = jnp.where(lane == first + i, term, out)
            value = value - term
        return out

    def turn(step, carry):
        tile = pl.ds(pl.multiple_of(step * TILE, TILE), TILE)
        for j in range(count):
            query_t[j, 0:128, tile] = transposed(wide_ref[first + j, tile, :])
            kept = out_ref[first + j, tile, :]
            query_t[j, 128:256, tile] = transposed(low_terms(-kept, HEAD).astype(BF))
            pair = pl.ds(pl.multiple_of((first // 2 + j // 2) * 128, 128), 128)
            grad = grad_ref[tile, pair].astype(F32)
            moved = pltpu.roll(grad, HEAD, 1)
            if j % 2:
                grad, moved = moved, grad
            dots = jnp.sum(jnp.where(low_lane, grad * kept, 0.0), axis=1, keepdims=True)
            dots = jnp.broadcast_to(-dots, (TILE, 128))
            block = jnp.where(low_lane, grad, low_terms(dots, HEAD))
            grad_t[j, :, tile] = transposed(block.astype(BF))
            grads[j, tile, :] = jnp.where(low_lane, 0.0, moved).astype(BF)
            dq[j, :, tile] = jnp.zeros((HEAD, TILE), F32)
        return carry

    lax.fori_loop(0, rows // TILE, turn, 0)
    for tile in range(rows // TILE):
        q_at = tile * TILE
        q_cols = slice(q_at, q_at + TILE)
        low, high = meta_ref[1 + 2 * tile], meta_ref[2 + 2 * tile]
        start_row = start_ref[:, q_cols]
        q_pos = base + q_at + lax.broadcasted_iota(jnp.int32, (1, TILE), 1)

        def step(at, carry, masked):
            k_at = pl.multiple_of(at * TILE, TILE)
            k_rows = pl.ds(k_at, TILE)
            key_block = keys[k_rows, :]
            value_block = values[k_rows, :]
            key_t = keys_t[:, k_rows]
            if masked:
                k_pos = k_at + lax.broadcasted_iota(jnp.int32, (TILE, 1), 0)
                allowed = (start_row <= k_pos) & (k_pos <= q_pos)
            total = dkv[k_rows, :]
            for j in range(count):
                scores = nn(key_block, query_t[j, :, q_cols])
                if masked:
                    scores = jnp.where(allowed, scores, NEG)
                probs = jnp.exp2(scores)
                diff = nn(value_block, grad_t[j, :, q_cols])
                grad_score = (probs * diff).astype(BF)
                total = (
                    total
                    + nn(probs.astype(BF), grads[j, q_cols, :])
                    + nn(grad_score, query_ref[first + j, q_cols, :])
                )
                dq[j, :, q_cols] += nn(key_t, grad_score)
            dkv[k_rows, :] = total
            return carry

        begin = low // TILE
        last = (base + q_at) // TILE
        clear = jnp.minimum((high + TILE - 1) // TILE, last)
        lax.fori_loop(begin, clear, functools.partial(step, masked=True), 0)
        lax.fori_loop(clear, last, functools.partial(step, masked=False), 0)
        step(last, 0, True)

    def finish(step, carry):
        tile = pl.ds(pl.multiple_of(step * TILE, TILE), TILE)
        for t in range(count // 2):
            pair = jnp.concatenate([dq[2 * t, :, tile], dq[2 * t + 1, :, tile]], axis=0)
            dq_ref[tile, t * 128 : (t + 1) * 128] = transposed(pair) * SCALE
        for block in range(BACK + 1):
            source = pl.ds(pl.multiple_of(block * rows + step * TILE, TILE), TILE)
            part = dkv[source, :]
            part = jnp.where(low_lane, part * SCALE, part)
            if block < BACK:
                low_ref[block, tile, :] = part.astype(BF)
            else:
                own_ref[tile, :] = part
        return carry

    lax.fori_loop(0, rows // TILE, finish, 0)


def attend_back(which, meta, wide, queries, kv, kept, grads, starts):
    _, rows, _ = queries.shape
    window = kv.shape[0] * rows
    count = (4, 2)[which]
    vmem = pl.BlockSpec(memory_space=pltpu.VMEM)
    shape = jax.ShapeDtypeStruct
    return pl.pallas_call(
        functools.partial(attend_back_kernel, which),
        out_shape=(
            shape((rows, count * HEAD), F32),
            shape((BACK, rows, 128), BF),
            shape((rows, 128), F32),
        ),
        in_specs=[pl.BlockSpec(memory_space=pltpu.SMEM)] + [vmem] * 6,
        out_specs=(vmem,) * 3,
        scratch_shapes=[
            pltpu.VMEM((window, 256), BF),
            pltpu.VMEM((window, 128), BF),
            pltpu.VMEM((HEAD, window), BF),
            pltpu.VMEM((count, 256, rows), BF),
            pltpu.VMEM((count, 128, rows), BF),
            pltpu.VMEM((count, rows, 128), BF),
            pltpu.VMEM((count, HEAD, rows), F32),
            pltpu.VMEM((window, 128), F32),
        ],
        compiler_params=pltpu.CompilerParams(vmem_limit_bytes=48 << 20),
        cost_estimate=pl.CostEstimate(
            flops=count * 20_000_000_000, bytes_accessed=40_000_000, transcendentals=20_000_000
        ),
        name=("attend_back_four", "attend_back_two")[which],
    )(meta, wide, queries, kv, kept, grads, starts)


MESH = pl.DeviceIdType.MESH
HEADS_OUT, SLAB, NEAR, FAR, ACROSS, FAR_ON, ACROSS_ON = 0, 3, 7, 8, 9, 10, 11
CORNER_TOP, CORNER_LOW, CORNER_ON, TO_MATE = 12, 13, 14, 15
BACK_TOP, BACK_LOW, BACK_FAR, BACK_ACROSS, HEADS_BACK, SUM_ON = 19, 20, 21, 22, 23, 26
WEIGHT_ON, TOP_ON, OUT_MATE, TRANSFERS = 30, 32, 37, 41
SPANS = ((0, 256), (256, 256), (512, 128))


def middle_kernel(
    slabs,
    downs,
    line,
    attn_ref,
    tokens_ref,
    w_own_ref,
    w_far_ref,
    gain_ref,
    top_ref,
    top_far_ref,
    top_across_ref,
    top_high_ref,
    top_low_ref,
    *refs,
):
    slab_refs, down_refs = refs[:slabs], refs[slabs : slabs + downs]
    (
        resid_out,
        grad_out,
        grad_low_out,
        mixed_out,
        heads_out,
        part_out,
        part_in,
        w_out_ref,
        gu_out,
        gu_next,
        down_out,
        gain_out,
        mixed,
        acts,
        tops,
        w_gu,
        w_dn,
        hidden,
        grad_gu,
        pairs,
        got,
        stage,
        in_far,
        in_across,
        in_top,
        in_low,
        resid,
        turned,
        gu_stage,
        sends,
        recvs,
        locals_,
    ) = refs[slabs + downs :]
    me, at = lax.axis_index("head"), lax.axis_index("blk")
    count = lax.axis_size("blk")
    side, place = at % 2, at // 2
    odd = me % 2
    mate, beside, corner = me + 1 - 2 * odd, (me + 2) % 4, (me + 3 - 2 * odd) % 4
    other = at + 1 - 2 * side
    after, before = (at + 2) % count, (at + count - 2) % count
    rows, width = tokens_ref.shape
    half = rows // 2
    cols = mixed.shape[1] // 4
    units = w_dn.shape[0]
    slab_rows = slab_refs[0].shape[1]

    barrier = pltpu.get_barrier_semaphore()
    peers = ((mate, at), (beside, at), (corner, at), (me, other), (me, after), (me, before))
    for peer in peers:
        pl.semaphore_signal(barrier, inc=1, device_id=peer, device_id_type=MESH)
    pl.semaphore_wait(barrier, len(peers))

    def remote(index, source, target, device):
        return pltpu.make_async_remote_copy(
            src_ref=source,
            dst_ref=target,
            send_sem=sends.at[index],
            recv_sem=recvs.at[index],
            device_id=device,
            device_id_type=MESH,
        )

    def local(index, source, target):
        return pltpu.make_async_copy(source, target, locals_.at[index])

    def mixed_cols(head):
        return mixed.at[:, pl.ds(pl.multiple_of(head * cols, 128), cols)]

    heads = [
        remote(HEADS_OUT + i, attn_ref.at[to], mixed_cols(me), (to, at))
        for i, to in enumerate((mate, beside, corner))
    ]
    for copy in heads:
        copy.start()
    own_heads = local(0, attn_ref.at[me], mixed_cols(me))
    own_heads.start()

    def w_rows_of(head):
        return pairs.at[pl.ds(pl.multiple_of(head * cols, 128), cols)]

    weight_on = [
        remote(WEIGHT_ON, w_own_ref, w_rows_of(me), (mate, at)),
        remote(WEIGHT_ON + 1, w_far_ref, w_rows_of(beside), (mate, at)),
    ]
    for copy in weight_on:
        copy.start()
    load_out = [
        local(1, w_own_ref, w_rows_of(me)),
        local(2, w_far_ref, w_rows_of(beside)),
    ]
    for copy in load_out:
        copy.start()

    def slab_at(head, source):
        start = pl.multiple_of((head * line + source) * slab_rows, 16)
        return w_gu.at[pl.ds(start, slab_rows)]

    last = (place + line - (slabs - 1)) % line
    slab_on = [
        remote(SLAB + h, slab_refs[-1].at[h], slab_at(h, last), (me, after)) for h in range(4)
    ]
    for copy in slab_on:
        copy.start()
    load_slabs = [
        local(7 + 4 * i + h, ref.at[h], slab_at(h, (place + line - i) % line))
        for i, ref in enumerate(slab_refs)
        for h in range(4)
    ]
    for copy in load_slabs:
        copy.start()
    base_sem = 14 + 4 * slabs + downs
    part_rows = units // downs
    load_down = []
    for i, ref in enumerate(down_refs):
        start = pl.multiple_of((place + line - i) % line * part_rows, 16) if i or downs > 1 else 0
        load_down.append(
            local(14 + 4 * slabs + i, ref, w_dn.at[pl.ds(start, part_rows)])
        )
    slot = side * 4 + me
    far_slot, across_slot = side * 4 + beside, (1 - side) * 4 + me
    corner_slot = (1 - side) * 4 + beside
    top_parts = (
        (top_ref, tops.at[slot]),
        (top_far_ref, tops.at[far_slot]),
        (top_across_ref, tops.at[across_slot]),
        (top_high_ref, tops.at[corner_slot, pl.ds(0, half)]),
        (top_low_ref, tops.at[corner_slot, pl.ds(half, half)]),
    )
    load_top = [
        local(7 + 4 * slabs + i, source, target) for i, (source, target) in enumerate(top_parts)
    ]
    for copy in load_down + load_top:
        copy.start()

    for copy in heads + weight_on:
        copy.wait_recv()
    own_heads.wait()
    for copy in load_out:
        copy.wait()
    top_on = [
        remote(TOP_ON + i, source, target, (mate, at))
        for i, (source, target) in enumerate(top_parts)
    ]
    for copy in top_on:
        copy.start()
    keep_weight = local(base_sem, pairs.at[pl.ds(0, 4 * cols)], w_out_ref)
    keep_weight.start()
    keep_mixed = local(base_sem + 2, mixed, mixed_out)
    keep_mixed.start()

    def resid_cols(step, carry):
        span = pl.ds(pl.multiple_of(step * 256, 256), 256)
        weight = pairs[0 : 4 * cols, span]
        resid[:, span] = tokens_ref[:, span].astype(F32) + nn(mixed[...], weight)
        return carry

    lax.fori_loop(0, width // 256, resid_cols, 0)

    def norm_tile(step, carry):
        tile = pl.ds(pl.multiple_of(step * 32, 32), 32)
        block = resid[tile, :]
        scale = lax.rsqrt(jnp.mean(block * block, axis=1, keepdims=True) + EPS)
        acts[slot, tile, :] = (block * scale * gain_ref[...]).astype(BF)
        return carry

    lax.fori_loop(0, rows // 32, norm_tile, 0)
    keep_resid = local(base_sem + 3, resid, resid_out)
    keep_resid.start()

    near = remote(NEAR, acts.at[slot], acts.at[slot], (mate, at))
    far = remote(FAR, acts.at[slot], acts.at[slot], (beside, at))
    across = remote(ACROSS, acts.at[slot], acts.at[slot], (me, other))
    far_on = remote(FAR_ON, acts.at[far_slot], acts.at[far_slot], (mate, at))
    across_on = remote(ACROSS_ON, acts.at[across_slot], acts.at[across_slot], (mate, at))
    corner_on = remote(CORNER_ON, acts.at[corner_slot], acts.at[corner_slot], (mate, at))
    far_top = acts.at[far_slot, pl.ds(0, half)]
    across_low = acts.at[across_slot, pl.ds(half, half)]
    corner_top = remote(CORNER_TOP, far_top, far_top, (me, other))
    corner_low = remote(CORNER_LOW, across_low, across_low, (beside, at))
    near.start()
    far.start()
    across.start()
    for copy in load_slabs:
        copy.wait()
    for copy in slab_on:
        copy.wait_recv()
    for copy in load_down + load_top + [keep_weight]:
        copy.wait()
    for copy in top_on:
        copy.wait_recv()

    def pair_rows(index, first=0, size=rows):
        return pl.ds(pl.multiple_of(index * rows + first, 16), size)

    def to_mate(c):
        return remote(
            TO_MATE + c, pairs.at[pair_rows(2 * c + 1 - odd)], got.at[c], (mate, at)
        )

    def keep_part(c):
        return local(base_sem + 4, stage.at[odd], part_out.at[c])

    def part_on(c):
        return remote(OUT_MATE + c, stage.at[1 - odd], part_in.at[c], (mate, at))

    def chunk(c, carry):
        its_side = (side + c // 2) % 2
        its_head = (me + 2 * (c % 2)) % 4
        pair = its_side * 4 + its_head - its_head % 2

        @pl.when(c == 0)
        def _():
            near.wait_recv()

        @pl.when(c == 1)
        def _():
            far.wait_recv()
            far_on.start()
            corner_top.start()
            across.wait_recv()
            across_on.start()
            corner_low.start()
            far_on.wait_recv()

        @pl.when(c == 2)
        def _():
            corner_top.wait_recv()
            corner_low.wait_recv()
            corner_on.start()
            across_on.wait_recv()

        @pl.when(c == 3)
        def _():
            corner_on.wait_recv()

        for first, size in SPANS:
            block = acts[pl.ds(pair, 2)].reshape(2 * rows, width)
            gate = nn(block, w_gu[:, first : first + size])
            up = nn(block, w_gu[:, units + first : units + first + size])
            grad = nt(
                tops[pl.ds(pair, 2)].reshape(2 * rows, width), w_dn[first : first + size, :]
            )
            sig = jax.nn.sigmoid(gate)
            silu = gate * sig
            shape = (2, rows, size)
            hidden[pl.ds(pair, 2), :, first : first + size] = (
                (silu * up).astype(BF).reshape(shape)
            )
            grad_gu[pl.ds(pair, 2), :, first : first + size] = (
                (grad * up * sig * (1 + gate * (1 - sig))).astype(BF).reshape(shape)
            )
            grad_gu[pl.ds(pair, 2), :, units + first : units + first + size] = (
                (grad * silu).astype(BF).reshape(shape)
            )

        def grad_cols(step, carry):
            span = pl.ds(pl.multiple_of(step * 256, 256), 256)
            block = grad_gu[pl.ds(pair, 2)].reshape(2 * rows, 2 * units)
            part = nt(block, w_gu[span, :])
            pairs[pl.ds(pl.multiple_of(2 * c * rows, 128), 2 * rows), span] = part.astype(BF)
            return carry

        lax.fori_loop(0, width // 256, grad_cols, 0)
        to_mate(c).start()

        @pl.when(c > 0)
        def _():
            keep_part(c - 1).wait()
            part_on(c - 1).wait_send()

        def out_cols(step, carry):
            span = pl.ds(pl.multiple_of(step * 256, 256), 256)
            block = hidden[pl.ds(pair, 2)].reshape(2 * rows, units)
            part = nn(block, w_dn[:, span])
            stage[:, :, span] = part.astype(BF).reshape(2, rows, 256)
            return carry

        lax.fori_loop(0, width // 256, out_cols, 0)
        keep_part(c).start()
        part_on(c).start()
        return carry

    lax.fori_loop(0, 4, chunk, 0)

    def add_rows(c, first, extra):
        def tile(step, carry):
            span = pl.ds(pl.multiple_of(first + step * 32, 32), 32)
            mine = pair_rows(2 * c + odd, first + step * 32, 32)
            total = pairs[mine, :].astype(F32) + got[c, span, :].astype(F32)
            for ref in extra:
                total = total + ref[pl.ds(pl.multiple_of(step * 32, 32), 32), :].astype(F32)
            pairs[mine, :] = total.astype(BF)
            return carry

        lax.fori_loop(0, half // 32, tile, 0)

    back_top = remote(
        BACK_TOP, pairs.at[pair_rows(6 + odd, 0, half)], in_top, (me, other)
    )
    back_low = remote(
        BACK_LOW, pairs.at[pair_rows(6 + odd, half, half)], in_low, (beside, at)
    )
    back_far = remote(BACK_FAR, pairs.at[pair_rows(2 + odd)], in_far, (beside, at))
    back_across = remote(BACK_ACROSS, pairs.at[pair_rows(4 + odd)], in_across, (me, other))
    to_mate(3).wait_recv()
    add_rows(3, 0, ())
    back_top.start()
    add_rows(3, half, ())
    back_low.start()
    to_mate(1).wait_recv()
    to_mate(2).wait_recv()
    add_rows(1, half, ())
    add_rows(2, 0, ())

    keep_part(3).wait()
    part_on(3).wait_send()

    def gu_rows(step, carry):
        span = pl.ds(pl.multiple_of(step * 256, 256), 256)
        turned[...] = transposed(acts[:, :, span].reshape(8 * rows, 256))
        buffer = step % 2

        @pl.when(step > 1)
        def _():
            local(base_sem + 5 + buffer, gu_stage.at[buffer], gu_out.at[pl.ds(0, 256)]).wait()

        for n in range(2 * units // 256):
            part = nn(
                turned[...],
                grad_gu[:, :, n * 256 : (n + 1) * 256].reshape(8 * rows, 256),
            )
            gu_stage[buffer, :, n * 256 : (n + 1) * 256] = part.astype(BF)
        local(base_sem + 5 + buffer, gu_stage.at[buffer], gu_out.at[span]).start()
        return carry

    lax.fori_loop(0, 5, gu_rows, 0)
    back_top.wait_recv()
    add_rows(1, 0, (in_top,))
    back_far.start()
    back_low.wait_recv()
    add_rows(2, half, (in_low,))
    back_across.start()
    lax.fori_loop(5, width // 256, gu_rows, 0)
    for buffer in range(2):
        local(base_sem + 5 + buffer, gu_stage.at[buffer], gu_out.at[pl.ds(0, 256)]).wait()

    target = (place + line - 1) % line
    sum_on = [
        remote(
            SUM_ON + h,
            gu_out.at[pl.ds(pl.multiple_of((h * line + target) * slab_rows, 16), slab_rows)],
            gu_next.at[h],
            (me, after),
        )
        for h in range(4)
    ]
    for copy in sum_on:
        copy.start()

    for copy in (near, far, across, far_on, across_on, corner_on, corner_top, corner_low):
        copy.wait_send()
    load_again = [
        local(1 + i, w_out_ref.at[pl.ds(i * rows, rows)], acts.at[i]) for i in range(6)
    ]
    for copy in load_again:
        copy.start()

    for i, (first, size) in enumerate(SPANS):
        turned[0:size, :] = transposed(
            hidden[:, :, first : first + size].reshape(8 * rows, size)
        )
        buffer = i % 2
        if i > 1:
            local(base_sem + 7, stage.at[0], down_out.at[pl.ds(0, rows)]).wait()

        def down_cols(step, carry):
            span = pl.ds(pl.multiple_of(step * 256, 256), 256)
            part = nn(turned[0:size, :], tops[:, :, span].reshape(8 * rows, 256))
            stage[buffer, 0:size, span] = part.astype(BF)
            return carry

        lax.fori_loop(0, width // 256, down_cols, 0)
        local(
            base_sem + 7 + buffer,
            stage.at[buffer, pl.ds(0, size)],
            down_out.at[pl.ds(first, size)],
        ).start()

    to_mate(0).wait_recv()
    back_far.wait_recv()
    back_across.wait_recv()
    keep_resid.wait()
    gain_out[...] = jnp.zeros_like(gain_out)
    low = got.at[0]

    def norm_back(step, carry):
        tile = pl.ds(pl.multiple_of(step * 32, 32), 32)
        grad = (
            pairs[pair_rows(odd, step * 32, 32), :].astype(F32)
            + got[0, tile, :].astype(F32)
            + in_far[tile, :].astype(F32)
            + in_across[tile, :].astype(F32)
        )
        block = resid[tile, :]
        scale = lax.rsqrt(jnp.mean(block * block, axis=1, keepdims=True) + EPS)
        gain_out[...] += jnp.sum(grad * block * scale, axis=0, keepdims=True)
        inner = grad * gain_ref[...]
        mean = jnp.mean(inner * block, axis=1, keepdims=True)
        total = (
            tops[slot, tile, :].astype(F32)
            + scale * inner
            - block * (scale * scale * scale * mean)
        )
        resid[tile, :] = total
        low[tile, :] = total.astype(BF)
        return carry

    lax.fori_loop(0, rows // 32, norm_back, 0)
    keep_grad = local(base_sem + 3, resid, grad_out)
    keep_grad.start()
    keep_low = local(base_sem + 4, low, grad_low_out)
    keep_low.start()
    keep_mixed.wait()
    for copy in load_again:
        copy.wait()

    def heads_cols(step, carry):
        span = pl.ds(pl.multiple_of(step * 256, 256), 256)
        mixed[:, span] = nt(low[...], acts[step]).astype(BF)
        return carry

    lax.fori_loop(0, 6, heads_cols, 0)
    heads_on = [
        remote(HEADS_BACK + i, mixed_cols(to), heads_out.at[me], (to, at))
        for i, to in enumerate((mate, beside, corner))
    ]
    for copy in heads_on:
        copy.start()
    own_back = local(0, mixed_cols(me), heads_out.at[me])
    own_back.start()

    own_back.wait()
    keep_grad.wait()
    keep_low.wait()
    local(base_sem + 7, stage.at[0, pl.ds(0, SPANS[2][1])], down_out.at[pl.ds(0, SPANS[2][1])]).wait()
    local(base_sem + 8, stage.at[1], down_out.at[pl.ds(0, rows)]).wait()
    for copy in heads_on + sum_on:
        copy.wait()
    for copy in heads + slab_on:
        copy.wait_send()
    for copy in weight_on + top_on:
        copy.wait_send()
    for c in range(4):
        to_mate(c).wait_send()
        part_on(c).wait_recv()
    for copy in (back_top, back_low, back_far, back_across):
        copy.wait_send()


def middle(attn_out, tokens, w_own, w_far, gain, tops, slabs, downs):
    rows, width = tokens.shape
    units = sum(block.shape[0] for block in downs)
    cols = attn_out.shape[2]
    line = lax.axis_size("blk") // 2
    slab_shape = slabs[0].shape
    anywhere = pl.BlockSpec(memory_space=pl.ANY)
    vmem = pl.BlockSpec(memory_space=pltpu.VMEM)
    shape = jax.ShapeDtypeStruct
    eight, four = (8, rows, width), (4, rows, width)
    return pl.pallas_call(
        functools.partial(middle_kernel, len(slabs), len(downs), line),
        out_shape=(
            shape((rows, width), F32),
            shape((rows, width), F32),
            shape((rows, width), BF),
            shape((rows, 4 * cols), BF),
            shape(attn_out.shape, BF),
            shape(four, BF),
            shape(four, BF),
            shape((4 * cols, width), BF),
            shape((width, 2 * units), BF),
            shape(slab_shape, BF),
            shape((units, width), BF),
            shape((1, width), F32),
        ),
        in_specs=[anywhere, vmem, anywhere, anywhere, vmem]
        + [anywhere] * (len(tops) + len(slabs) + len(downs)),
        out_specs=(anywhere,) * 11 + (vmem,),
        scratch_shapes=[
            pltpu.VMEM((rows, 4 * cols), BF),
            pltpu.VMEM(eight, BF),
            pltpu.VMEM(eight, BF),
            pltpu.VMEM((width, 2 * units), BF),
            pltpu.VMEM((units, width), BF),
            pltpu.VMEM((8, rows, units), BF),
            pltpu.VMEM((8, rows, 2 * units), BF),
            pltpu.VMEM((8 * rows, width), BF),
            pltpu.VMEM(four, BF),
            pltpu.VMEM((2, rows, width), BF),
            pltpu.VMEM((rows, width), BF),
            pltpu.VMEM((rows, width), BF),
            pltpu.VMEM((rows // 2, width), BF),
            pltpu.VMEM((rows // 2, width), BF),
            pltpu.VMEM((rows, width), F32),
            pltpu.VMEM((256, 8 * rows), BF),
            pltpu.VMEM((2, 256, 2 * units), BF),
            pltpu.SemaphoreType.DMA((TRANSFERS,)),
            pltpu.SemaphoreType.DMA((TRANSFERS,)),
            pltpu.SemaphoreType.DMA((24 + 4 * len(slabs) + len(downs),)),
        ],
        compiler_params=pltpu.CompilerParams(
            collective_id=1, has_side_effects=True, vmem_limit_bytes=60 << 20
        ),
        cost_estimate=pl.CostEstimate(
            flops=60_000_000_000, bytes_accessed=100_000_000, transcendentals=2_000_000
        ),
        name="middle",
    )(attn_out, tokens, w_own, w_far, gain, *tops, *slabs, *downs)


TOK_NEAR, TOK_FAR, TOK_ON, IN_QUERY, IN_REST = 0, 1, 2, 3, 6
TOP_FAR, TOP_ACROSS = 9, 10
UNITS_MOVE, SLAB_ON, DOWN_MOVE, DOWN_ONE, DOWN_TWO = 17, 31, 32, 33, 34
KV_ONE, KV_TWO, KV_PAIR_ONE, KV_PAIR_TWO, FIRST_TRANSFERS = 35, 36, 37, 38, 39
COLS_Q = QHEADS // 4 * HEAD
COLS_IN = COLS_Q + 4 * HEAD


def head_scale(block):
    low = lanes(block.shape) < HEAD
    square = block * block
    first = jnp.sum(jnp.where(low, square, 0.0), axis=1, keepdims=True)
    second = jnp.sum(jnp.where(low, 0.0, square), axis=1, keepdims=True)
    return jnp.where(
        low, lax.rsqrt(first / HEAD + EPS), lax.rsqrt(second / HEAD + EPS)
    )


def swap_halves(block):
    low = lanes(block.shape) % HEAD < HEAD // 2
    return jnp.where(low, pltpu.roll(block, 96, 1), pltpu.roll(block, 32, 1))


def first_kernel(
    line,
    tokens_ref,
    query_ref,
    rest_ref,
    gate_ref,
    up_ref,
    down_ref,
    w_out_ref,
    top_ref,
    cos_ref,
    sin_ref,
    query_gain_ref,
    key_gain_ref,
    wide_out,
    query_out,
    kv_out,
    raw_out,
    normed_out,
    w_in_out,
    top_far_out,
    top_across_out,
    w_out_all,
    slab_out,
    slab_next,
    down_out,
    down_one,
    down_two,
    toks_out,
    gain_out,
    toks,
    normed,
    w_in,
    raw,
    wide,
    query,
    kv_own,
    sends,
    recvs,
    ring_sends,
    ring_recvs,
    swap_sends,
    swap_recvs,
    out_ring_sends,
    out_ring_recvs,
    out_swap_sends,
    out_swap_recvs,
    locals_,
):
    me, at = lax.axis_index("head"), lax.axis_index("blk")
    count = lax.axis_size("blk")
    side, place = at % 2, at // 2
    odd = me % 2
    mate, beside, corner = me + 1 - 2 * odd, (me + 2) % 4, (me + 3 - 2 * odd) % 4
    other = at + 1 - 2 * side
    after, before = (at + 2) % count, (at + count - 2) % count
    rows, width = tokens_ref.shape
    half = rows // 2
    w_rows = query_ref.shape[0]
    units = slab_out.shape[2] // 2
    piece_to = 2 * (at % line) + at // line
    piece_from = (at % 2) * line + at // 2
    stays = piece_to == at

    barrier = pltpu.get_barrier_semaphore()
    peers = [(mate, at), (beside, at), (corner, at), (me, after), (me, before)]
    peers += [(head, other) for head in (me, mate, beside, corner)]
    for peer in peers:
        pl.semaphore_signal(barrier, inc=1, device_id=peer, device_id_type=MESH)

    @pl.when(jnp.logical_not(stays))
    def _():
        for peer in ((me, piece_to), (me, piece_from)):
            pl.semaphore_signal(barrier, inc=1, device_id=peer, device_id_type=MESH)

    pl.semaphore_wait(barrier, jnp.where(stays, len(peers), len(peers) + 2))

    def remote(index, source, target, device, send=sends, recv=recvs):
        return pltpu.make_async_remote_copy(
            src_ref=source,
            dst_ref=target,
            send_sem=send.at[index],
            recv_sem=recv.at[index],
            device_id=device,
            device_id_type=MESH,
        )

    def local(index, source, target):
        return pltpu.make_async_copy(source, target, locals_.at[index])

    def cols_of(ref, start, size):
        return ref.at[:, pl.ds(pl.multiple_of(start, 128), size)]

    own_q = w_in.at[me, at, :, pl.ds(0, COLS_Q)]
    own_rest = w_in.at[me, at, :, pl.ds(COLS_Q, COLS_Q)]
    split = []
    for i, to in enumerate((mate, beside, corner)):
        split.append(
            remote(IN_QUERY + i, cols_of(query_ref, to * COLS_Q, COLS_Q), own_q, (to, at))
        )
        split.append(remote(IN_REST + i, rest_ref.at[to], own_rest, (to, at)))
    for copy in split:
        copy.start()
    own = [
        local(0, cols_of(query_ref, me * COLS_Q, COLS_Q), own_q),
        local(1, rest_ref.at[me], own_rest),
        local(2, tokens_ref, toks.at[me]),
        local(3, w_out_ref, w_out_all.at[at]),
    ]
    for copy in own:
        copy.start()
    tok_near = remote(TOK_NEAR, tokens_ref, toks.at[me], (mate, at))
    tok_far = remote(TOK_FAR, tokens_ref, toks.at[me], (beside, at))
    tok_on = remote(TOK_ON, toks.at[beside], toks.at[beside], (mate, at))
    tok_far.start()
    tok_near.start()
    down_move = remote(DOWN_MOVE, down_ref, down_out, (me, piece_to))
    down_stay = local(4, down_ref, down_out)

    @pl.when(jnp.logical_not(stays))
    def _():
        down_move.start()

    @pl.when(stays)
    def _():
        down_stay.start()

    def units_at(ref, to_side, to_head):
        return cols_of(ref, (to_head * 2 + to_side) * units, units)

    slab_rows = pl.ds(pl.multiple_of(side * w_rows, 16), w_rows)
    targets = [(side, mate), (side, beside), (side, corner)]
    targets += [(1 - side, head) for head in (me, mate, beside, corner)]
    spread = []
    for i, (to_side, to_head) in enumerate(targets):
        device = (to_head, at if i < 3 else other)
        for j, ref in enumerate((gate_ref, up_ref)):
            spread.append(
                remote(
                    UNITS_MOVE + 2 * i + j,
                    units_at(ref, to_side, to_head),
                    slab_out.at[me, slab_rows, pl.ds(j * units, units)],
                    device,
                )
            )
    for copy in spread:
        copy.start()
    own_units = [
        local(
            5 + j,
            units_at(ref, side, me),
            slab_out.at[me, slab_rows, pl.ds(j * units, units)],
        )
        for j, ref in enumerate((gate_ref, up_ref))
    ]
    for copy in own_units:
        copy.start()

    def ring_copy(step):
        block = w_in.at[:, (at + count - 2 * (step - 1)) % count]
        return remote(step, block, block, (me, after), ring_sends, ring_recvs)

    def swap_copy(step):
        block = w_in.at[:, (at + count - 2 * step) % count]
        return remote(step, block, block, (me, other), swap_sends, swap_recvs)

    def out_ring(step):
        index = (at + count - 2 * (step - 1)) % count
        source = w_out_ref if step == 1 else w_out_all.at[index]
        return remote(
            step, source, w_out_all.at[index], (me, after), out_ring_sends, out_ring_recvs
        )

    def out_swap(step):
        index = (at + count - 2 * step) % count
        source = w_out_ref if step == 0 else w_out_all.at[index]
        return remote(
            step, source, w_out_all.at[index], (me, other), out_swap_sends, out_swap_recvs
        )

    out_ring(1).start()
    out_swap(0).start()
    for copy in split:
        copy.wait_recv()
    own[0].wait()
    own[1].wait()
    ring_copy(1).start()
    swap_copy(0).start()
    tok_far.wait_recv()
    tok_on.start()
    top_far = remote(TOP_FAR, top_ref, top_far_out, (beside, at))
    top_across = remote(TOP_ACROSS, top_ref, top_across_out, (me, other))
    top_far.start()
    for step in range(1, line):
        ring_copy(step).wait_recv()
        if step < line - 1:
            ring_copy(step + 1).start()
        swap_copy(step).start()
        out_ring(step).wait_recv()
        if step < line - 1:
            out_ring(step + 1).start()

    @pl.when(jnp.logical_not(stays))
    def _():
        down_move.wait_recv()

    @pl.when(stays)
    def _():
        down_stay.wait()

    down_on = remote(DOWN_ONE, down_out, down_one, (me, after))
    down_on.start()
    for copy in spread:
        copy.wait_recv()
    for copy in own_units:
        copy.wait()
    slab_on = remote(SLAB_ON, slab_out, slab_next, (me, after))
    slab_on.start()
    tok_near.wait_recv()
    tok_on.wait_recv()
    own[2].wait()
    own[3].wait()
    for step in range(line):
        swap_copy(step).wait_recv()
    for step in range(1, line):
        out_swap(step).start()
    top_across.start()
    keep_in = [
        local(7 + h, w_in.at[h], w_in_out.at[h]) for h in range(4)
    ]
    for copy in keep_in:
        copy.start()

    gains = w_in[:, :, :, COLS_IN : COLS_IN + 128].reshape(width, 128).astype(F32)
    gain_out[...] = transposed(gains)[0:8, :]

    def norm_tile(step, carry):
        head, tile = step // (rows // 32), pl.ds(pl.multiple_of(step % (rows // 32) * 32, 32), 32)
        block = toks[head, tile, :].astype(F32)
        scale = lax.rsqrt(jnp.mean(block * block, axis=1, keepdims=True) + EPS)
        normed[pl.ds(pl.multiple_of(step * 32, 32), 32), :] = (
            block * scale * gain_out[0:1, :]
        ).astype(BF)
        return carry

    lax.fori_loop(0, 4 * rows // 32, norm_tile, 0)
    keep_normed = local(11, normed, normed_out)
    keep_normed.start()
    keep_toks = local(16, toks, toks_out)
    keep_toks.start()

    def project(step, carry):
        tile = pl.ds(pl.multiple_of(step * 256, 256), 256)
        for first, size in SPANS:
            weight = w_in[:, :, :, first : first + size].reshape(width, size)
            raw[tile, first : first + size] = nn(normed[tile, :], weight)
        return carry

    lax.fori_loop(0, 4 * rows // 256, project, 0)
    keep_raw = local(12, raw.at[:, pl.ds(0, COLS_Q + 128)], raw_out)
    keep_raw.start()

    def rotated(block, gain, tile):
        block = block * head_scale(block) * gain
        return block * cos_ref[tile, :] + swap_halves(block) * sin_ref[tile, :]

    def prepare(step, carry):
        tile = pl.ds(pl.multiple_of(step * 64, 64), 64)
        first_half = lanes((64, 128)) < HEAD
        for t in range(QHEADS // 4 // 2):
            block = rotated(raw[tile, t * 128 : (t + 1) * 128], query_gain_ref[...], tile)
            block = block.astype(BF).astype(F32)
            moved = pltpu.roll(block, HEAD, 1)
            query[2 * t, tile, :] = jnp.where(first_half, block, 0.0).astype(BF)
            query[2 * t + 1, tile, :] = jnp.where(first_half, moved, 0.0).astype(BF)
            scaled = block * (SCALE * LOG2E)
            upper = scaled.astype(BF).astype(F32)
            lower = scaled - upper
            wide[2 * t, tile, :] = jnp.where(
                first_half, upper, pltpu.roll(lower, HEAD, 1)
            ).astype(BF)
            wide[2 * t + 1, tile, :] = jnp.where(
                first_half, pltpu.roll(upper, HEAD, 1), lower
            ).astype(BF)
        keys = rotated(raw[tile, COLS_Q : COLS_Q + 128], key_gain_ref[...], tile)
        values = raw[tile, COLS_Q + 128 : COLS_Q + 256]
        kv_own[0, tile, :] = jnp.where(
            first_half, keys, pltpu.roll(values, HEAD, 1)
        ).astype(BF)
        kv_own[1, tile, :] = jnp.where(
            first_half, pltpu.roll(keys, HEAD, 1), values
        ).astype(BF)
        return carry

    lax.fori_loop(0, 4 * rows // 64, prepare, 0)

    kv_one = remote(KV_ONE, kv_own, kv_out.at[2], (me, after))
    kv_two = remote(KV_TWO, kv_out.at[2], kv_out.at[0], (me, after))
    pair_one_even = remote(KV_PAIR_ONE, kv_own, kv_out.at[3], (me, other))
    pair_one_odd = remote(KV_PAIR_ONE, kv_out.at[2], kv_out.at[3], (me, other))
    pair_two_even = remote(KV_PAIR_TWO, kv_out.at[2], kv_out.at[1], (me, other))
    pair_two_odd = remote(KV_PAIR_TWO, kv_out.at[0], kv_out.at[1], (me, other))
    kv_one.start()

    @pl.when(side == 0)
    def _():
        pair_one_even.start()

    keep = [
        local(13, kv_own, kv_out.at[4]),
        local(14, wide, wide_out),
        local(15, query, query_out),
    ]
    for copy in keep:
        copy.start()
    kv_one.wait_recv()
    kv_two.start()

    @pl.when(side == 0)
    def _():
        pair_two_even.start()

    @pl.when(side == 1)
    def _():
        pair_one_odd.start()

    down_on.wait_recv()
    kv_two.wait_recv()

    @pl.when(side == 1)
    def _():
        pair_two_odd.start()

    down_last = remote(DOWN_TWO, down_one, down_two, (me, after))
    down_last.start()
    pair_one_even.wait_recv()
    pair_two_even.wait_recv()
    down_last.wait_recv()
    slab_on.wait_recv()
    for copy in (top_far, top_across):
        copy.wait_recv()
    for copy in keep + keep_in + [keep_normed, keep_raw, keep_toks]:
        copy.wait()
    for copy in split + spread:
        copy.wait_send()
    for copy in (tok_near, tok_far, tok_on, top_far, top_across):
        copy.wait_send()
    for copy in (slab_on, down_on, down_last, kv_one, kv_two):
        copy.wait_send()
    pair_one_even.wait_send()
    pair_two_even.wait_send()

    @pl.when(jnp.logical_not(stays))
    def _():
        down_move.wait_send()

    for step in range(line):
        swap_copy(step).wait_send()
        out_swap(step).wait()
        if step:
            ring_copy(step).wait_send()
            out_ring(step).wait_send()


def first(
    tokens, w_query, rest, w_gate, w_up, w_down, w_out, cotangent, cosine, sine, query_gain, key_gain
):
    rows, width = tokens.shape
    count = lax.axis_size("blk")
    w_rows, ff = w_gate.shape
    units = ff // 8
    block = 4 * rows
    anywhere = pl.BlockSpec(memory_space=pl.ANY)
    vmem = pl.BlockSpec(memory_space=pltpu.VMEM)
    shape = jax.ShapeDtypeStruct
    heads = QHEADS // 4
    slab = shape((4, 2 * w_rows, 2 * units), BF)
    dma = pltpu.SemaphoreType.DMA
    return pl.pallas_call(
        functools.partial(first_kernel, count // 2),
        out_shape=(
            shape((heads, block, 128), BF),
            shape((heads, block, 128), BF),
            shape((BACK + 1, 2, block, 128), BF),
            shape((block, COLS_Q + 128), F32),
            shape((block, width), BF),
            shape((4, count, w_rows, 2 * COLS_Q), BF),
            shape((rows, width), BF),
            shape((rows, width), BF),
            shape((count,) + w_out.shape, BF),
            slab,
            slab,
            shape(w_down.shape, BF),
            shape(w_down.shape, BF),
            shape(w_down.shape, BF),
            shape((4, rows, width), BF),
            shape((8, width), F32),
        ),
        in_specs=[anywhere] * 8 + [vmem] * 4,
        out_specs=(anywhere,) * 15 + (vmem,),
        scratch_shapes=[
            pltpu.VMEM((4, rows, width), BF),
            pltpu.VMEM((block, width), BF),
            pltpu.VMEM((4, count, w_rows, 2 * COLS_Q), BF),
            pltpu.VMEM((block, COLS_IN), F32),
            pltpu.VMEM((heads, block, 128), BF),
            pltpu.VMEM((heads, block, 128), BF),
            pltpu.VMEM((2, block, 128), BF),
            dma((FIRST_TRANSFERS,)),
            dma((FIRST_TRANSFERS,)),
            dma((count // 2,)),
            dma((count // 2,)),
            dma((count // 2,)),
            dma((count // 2,)),
            dma((count // 2,)),
            dma((count // 2,)),
            dma((count // 2,)),
            dma((count // 2,)),
            dma((17,)),
        ],
        compiler_params=pltpu.CompilerParams(
            collective_id=2, has_side_effects=True, vmem_limit_bytes=48 << 20
        ),
        cost_estimate=pl.CostEstimate(
            flops=60_000_000_000, bytes_accessed=60_000_000, transcendentals=1_000_000
        ),
        name="first",
    )(
        tokens, w_query, rest, w_gate, w_up, w_down, w_out, cotangent, cosine, sine,
        query_gain, key_gain,
    )


THREE, ONE, FOUR_ON, TWO_ON = 0, 2, 4, 6
UNITS_HOME, DOWN_ON, DOWN_HOME = 8, 15, 16
PART_MATE, PART_CORNER, PART_FAR, QUERY_HOME, REST_HOME = 17, 18, 19, 20, 23
LAST_TRANSFERS = 26


def head_means(block):
    low = lanes(block.shape) < HEAD
    first = jnp.sum(jnp.where(low, block, 0.0), axis=1, keepdims=True)
    second = jnp.sum(jnp.where(low, 0.0, block), axis=1, keepdims=True)
    return jnp.where(low, first, second) * (1.0 / HEAD)


class LineSum:
    def __init__(self, part, got, hold, arrive, sems, places, remote):
        self.part, self.got, self.hold, self.arrive = part, got, hold, arrive
        self.swap_sems, self.ring_sems = sems
        self.side, self.place, self.line, self.other, self.after = places
        self.remote = remote

    def target(self, step):
        return (self.place + self.line - step) % self.line

    def swap(self, step):
        to = self.target(step)
        return self.remote(
            step - 1,
            self.part(2 * to + 1 - self.side),
            self.got.at[to],
            self.other,
            *self.swap_sems,
        )

    def pass_on(self, step):
        return self.remote(
            step - 1, self.hold.at[step - 1], self.arrive.at[step - 1], self.after, *self.ring_sems
        )

    def start(self):
        for step in range(1, self.line + 1):
            self.swap(step).start()

    def step(self, step, out=None):
        to = self.target(step)
        self.swap(step).wait_recv()
        total = self.part(2 * to + self.side)[...].astype(F32) + self.got[to].astype(F32)
        if step > 1:
            self.pass_on(step - 1).wait_recv()
            total = total + self.arrive[step - 2].astype(F32)
        if step < self.line:
            self.hold[step - 1] = total.astype(BF)
            self.pass_on(step).start()
        else:
            out[...] = total.astype(out.dtype)

    def drain(self):
        for step in range(1, self.line + 1):
            self.swap(step).wait_send()
            if step < self.line:
                self.pass_on(step).wait_send()


def last_kernel(
    line,
    dq_four_ref,
    dq_two_ref,
    low_four_ref,
    low_two_ref,
    own_four_ref,
    own_two_ref,
    raw_ref,
    cos_ref,
    sin_ref,
    query_gain_ref,
    key_gain_ref,
    normed_ref,
    w_in_ref,
    toks_ref,
    gain_ref,
    gain_two_ref,
    units_ref,
    down_ref,
    down_parts_ref,
    slab_ref,
    dx_out,
    query_out,
    rest_out,
    units_out,
    down_out,
    w_out_out,
    gains_out,
    low,
    three,
    one,
    four_in,
    two_in,
    raw,
    normed,
    turned,
    w_in,
    toks,
    scales,
    grads,
    query_part,
    rest_part,
    query_got,
    rest_got,
    query_hold,
    rest_hold,
    query_arrive,
    rest_arrive,
    query_sum,
    rest_sum,
    slab,
    slab_got,
    slab_hold,
    slab_arrive,
    down_own,
    down_in,
    parts,
    part_got,
    part_far,
    gain_rows,
    head_gains,
    gains_in,
    sends,
    recvs,
    line_sems,
    gain_sends,
    gain_recvs,
    locals_,
):
    me, at = lax.axis_index("head"), lax.axis_index("blk")
    count = lax.axis_size("blk")
    side, place = at % 2, at // 2
    odd = me % 2
    mate, beside, corner = me + 1 - 2 * odd, (me + 2) % 4, (me + 3 - 2 * odd) % 4
    other = at + 1 - 2 * side
    after, before = (at + 2) % count, (at + count - 2) % count
    rows, width = dx_out.shape
    block = 4 * rows
    w_rows = w_in_ref.shape[2]
    piece_from = (at % 2) * line + at // 2
    piece_to = 2 * (at % line) + at // line
    stays = piece_to == at

    rounds = [(mate, at), (beside, at), (me, other)]
    bit = 1
    while bit < line:
        rounds.append((me, at + 2 * bit * (1 - 2 * ((place // bit) % 2))))
        bit *= 2
    barrier = pltpu.get_barrier_semaphore()
    peers = [(corner, at), (me, after), (me, before)]
    peers += [(head, other) for head in (mate, beside, corner)] + rounds
    for peer in peers:
        pl.semaphore_signal(barrier, inc=1, device_id=peer, device_id_type=MESH)

    @pl.when(jnp.logical_not(stays))
    def _():
        for peer in ((me, piece_to), (me, piece_from)):
            pl.semaphore_signal(barrier, inc=1, device_id=peer, device_id_type=MESH)

    pl.semaphore_wait(barrier, jnp.where(stays, len(peers), len(peers) + 2))

    def remote(index, source, target, device, send=sends, recv=recvs):
        return pltpu.make_async_remote_copy(
            src_ref=source,
            dst_ref=target,
            send_sem=send.at[index],
            recv_sem=recv.at[index],
            device_id=device,
            device_id_type=MESH,
        )

    def local(index, source, target):
        return pltpu.make_async_copy(source, target, locals_.at[index])

    low_refs, own_refs = (low_four_ref, low_two_ref), (own_four_ref, own_two_ref)
    three_on = [remote(THREE + g, low_refs[g].at[1], three.at[g], (me, other)) for g in (0, 1)]
    one_on = [remote(ONE + g, low_refs[g].at[3], one.at[g], (me, other)) for g in (0, 1)]
    for copy in three_on + one_on:
        copy.start()
    loads = [
        local(0, normed_ref, normed),
        local(1, raw_ref, raw),
        local(2, w_in_ref, w_in),
        local(3, toks_ref, toks),
        local(4, slab_ref, slab),
        local(5, down_parts_ref.at[place], down_own),
    ]
    for copy in loads:
        copy.start()
    low_loads = [
        local(6 + 2 * g + i, low_refs[g].at[2 * i], low.at[g, i]) for g in (0, 1) for i in (0, 1)
    ]
    for copy in low_loads:
        copy.start()
    down_on = remote(DOWN_ON, down_ref, down_in, (me, after))
    down_on.start()
    targets = [(side, mate), (side, beside), (side, corner)]
    targets += [(1 - side, head) for head in (me, mate, beside, corner)]
    homes = []
    for i, (to_side, to_head) in enumerate(targets):
        device = (to_head, at if i < 3 else other)
        source = units_ref.at[to_head, pl.ds(pl.multiple_of(to_side * w_rows, 16), w_rows)]
        homes.append(remote(UNITS_HOME + i, source, units_out.at[side * 4 + me], device))
    units_own = local(
        10,
        units_ref.at[me, pl.ds(pl.multiple_of(side * w_rows, 16), w_rows)],
        units_out.at[side * 4 + me],
    )

    places = (side, place, line, (me, other), (me, after))

    def line_sum(which, part, got, hold, arrive):
        sems = [(line_sems.at[which, i, 0], line_sems.at[which, i, 1]) for i in (0, 1)]
        return LineSum(part, got, hold, arrive, sems, places, remote)

    query_line = line_sum(
        0, lambda b: query_part.at[:, b], query_got, query_hold, query_arrive
    )
    rest_line = line_sum(1, lambda b: rest_part.at[:, b], rest_got, rest_hold, rest_arrive)
    slab_line = line_sum(2, lambda b: slab.at[b], slab_got, slab_hold, slab_arrive)

    head_gains[...] = jnp.zeros_like(head_gains)
    gain_rows[...] = jnp.zeros_like(gain_rows)
    loads[0].wait()
    loads[1].wait()

    def head_back(out, cols, tile, gain_tile, gain_row):
        value = raw[tile, cols]
        scale = head_scale(value)
        grad = out * cos_ref[tile, :] + swap_halves(out * sin_ref[tile, :])
        head_gains[0, gain_row : gain_row + 1, :] += jnp.sum(
            grad * value * scale, axis=0, keepdims=True
        )
        inner = grad * gain_tile
        mean = head_means(inner * value)
        return (scale * inner - value * (scale * scale * scale * mean)).astype(BF)

    def query_rows(step, carry):
        tile = pl.ds(pl.multiple_of(step * 64, 64), 64)
        for i in range(3):
            t = odd + i if i < 2 else 2 * (1 - odd)
            cols = pl.ds(pl.multiple_of(t * 128, 128), 128)
            if i < 2:
                out = dq_four_ref[tile, i * 128 : (i + 1) * 128]
            else:
                out = dq_two_ref[tile, :]
            grads[tile, cols] = head_back(out, cols, tile, query_gain_ref[...], 0)
        return carry

    lax.fori_loop(0, block // 64, query_rows, 0)
    per_tile = 256 // w_rows
    tiles_per_head = count // per_tile

    def query_weights(step, carry):
        span = pl.ds(pl.multiple_of(step * 256, 256), 256)
        turned[span, :] = transposed(normed[:, span])
        first = pl.ds(step % tiles_per_head * per_tile, per_tile)
        part = nn(turned[span, :], grads[:, 0:COLS_Q])
        query_part[step // tiles_per_head, first] = part.astype(BF).reshape(
            per_tile, w_rows, COLS_Q
        )
        return carry

    lax.fori_loop(0, width // 256, query_weights, 0)
    query_line.start()
    for copy in low_loads:
        copy.wait()

    for copy in three_on + one_on:
        copy.wait_recv()

    def add_pair(step, carry):
        tile = pl.ds(pl.multiple_of(step * 128, 128), 128)
        for g in (0, 1):
            got_three, got_one = three[g, tile, :].astype(F32), one[g, tile, :].astype(F32)
            to_four = jnp.where(side == 0, 0.0, got_three)
            to_two = jnp.where(side == 0, got_three, got_one)
            low[g, 0, tile, :] = (low[g, 0, tile, :].astype(F32) + to_four).astype(BF)
            low[g, 1, tile, :] = (low[g, 1, tile, :].astype(F32) + to_two).astype(BF)
        return carry

    lax.fori_loop(0, block // 128, add_pair, 0)
    four_on = [remote(FOUR_ON + g, low.at[g, 0], four_in.at[g], (me, before)) for g in (0, 1)]
    two_on = [remote(TWO_ON + g, low.at[g, 1], two_in.at[g], (me, before)) for g in (0, 1)]
    for copy in four_on:
        copy.start()
    loads[4].wait()
    slab_line.start()

    loads[3].wait()

    def token_scales(step, carry):
        tile = pl.ds(pl.multiple_of(step % (rows // 32) * 32, 32), 32)
        value = toks[step // (rows // 32), tile, :].astype(F32)
        scales[pl.ds(pl.multiple_of(step * 32, 32), 32), :] = lax.rsqrt(
            jnp.mean(value * value, axis=1, keepdims=True) + EPS
        )
        return carry

    lax.fori_loop(0, block // 32, token_scales, 0)
    for copy in four_on:
        copy.wait_recv()

    def add_four(step, carry):
        tile = pl.ds(pl.multiple_of(step * 128, 128), 128)
        for g in (0, 1):
            low[g, 1, tile, :] = (
                low[g, 1, tile, :].astype(F32) + four_in[g, tile, :].astype(F32)
            ).astype(BF)
        return carry

    lax.fori_loop(0, block // 128, add_four, 0)
    for copy in two_on:
        copy.start()
    loads[5].wait()
    down_on.wait_recv()

    def add_down(step, carry):
        span = pl.ds(pl.multiple_of(step * 256, 256), 256)
        down_own[:, span] = (
            down_own[:, span].astype(F32) + down_in[:, span].astype(F32)
        ).astype(BF)
        return carry

    lax.fori_loop(0, width // 256, add_down, 0)
    down_home = remote(DOWN_HOME, down_own, down_out, (me, piece_from))
    down_stay = local(11, down_own, down_out)

    @pl.when(jnp.logical_not(stays))
    def _():
        down_home.start()

    @pl.when(stays)
    def _():
        down_stay.start()

    for copy in homes:
        copy.start()
    units_own.start()
    query_line.step(1)
    slab_line.step(1)
    query_line.step(2)
    for copy in two_on:
        copy.wait_recv()

    def key_rows(step, carry):
        tile = pl.ds(pl.multiple_of(step * 64, 64), 64)
        first_half = lanes((64, 128)) < HEAD
        both = []
        for g in (0, 1):
            from_pair = jnp.where(side == 0, one[g, tile, :].astype(F32), 0.0)
            both.append(own_refs[g][tile, :] + from_pair + two_in[g, tile, :].astype(F32))
        zero = jnp.where(odd == 0, both[0], both[1])
        unit = jnp.where(odd == 0, both[1], both[0])
        keys = jnp.where(first_half, zero, pltpu.roll(unit, HEAD, 1))
        values = jnp.where(first_half, pltpu.roll(zero, HEAD, 1), unit)
        cols = pl.ds(COLS_Q, 128)
        grads[tile, cols] = head_back(keys, cols, tile, key_gain_ref[...], 1)
        grads[tile, COLS_Q + 128 : COLS_Q + 256] = values.astype(BF)
        return carry

    lax.fori_loop(0, block // 64, key_rows, 0)

    loads[2].wait()

    def token_cols(step, carry):
        span = pl.ds(pl.multiple_of(step * 256, 256), 256)
        first = pl.ds(step % tiles_per_head * per_tile, per_tile)
        weight = w_in[step // tiles_per_head, first, :, 0:COLS_IN].reshape(256, COLS_IN)
        part = nt(grads[...], weight)
        parts[:, :, span] = part.astype(BF).reshape(4, rows, 256)
        value = toks[:, :, span].reshape(block, 256).astype(F32)
        gain_rows[0:1, span] = jnp.sum(part * value * scales[...], axis=0, keepdims=True)
        return carry

    lax.fori_loop(0, width // 256, token_cols, 0)
    to_mate = [
        remote(PART_CORNER, parts.at[corner], part_got.at[1], (mate, at)),
        remote(PART_MATE, parts.at[mate], part_got.at[0], (mate, at)),
    ]
    for copy in to_mate:
        copy.start()
    gain_rows[1:2, :] = gain_two_ref[...]

    def rest_weights(step, carry):
        span = pl.ds(pl.multiple_of(step * 256, 256), 256)
        first = pl.ds(step % tiles_per_head * per_tile, per_tile)
        head = step // tiles_per_head
        part = nn(turned[span, :], grads[:, COLS_Q : COLS_Q + 256])
        rest_part[head, first, :, 0:256] = part.astype(BF).reshape(per_tile, w_rows, 256)
        gain_cols = transposed(gain_rows[:, span])
        rest_part[head, first, :, 256:384] = gain_cols.astype(BF).reshape(per_tile, w_rows, 128)
        return carry

    lax.fori_loop(0, width // 256, rest_weights, 0)
    rest_line.start()

    for step in range(3, line + 1):
        query_line.step(step, query_sum)
    query_home = [
        remote(QUERY_HOME + i, query_sum.at[to], query_out.at[me], (to, at))
        for i, to in enumerate((mate, beside, corner))
    ]
    query_own = local(12, query_sum.at[me], query_out.at[me])
    for copy in query_home:
        copy.start()
    query_own.start()
    to_mate[0].wait_recv()

    def add_part(step, carry):
        tile = pl.ds(pl.multiple_of(step * 32, 32), 32)
        parts[beside, tile, :] = (
            parts[beside, tile, :].astype(F32) + part_got[1, tile, :].astype(F32)
        ).astype(BF)
        return carry

    lax.fori_loop(0, rows // 32, add_part, 0)
    part_on = remote(PART_FAR, parts.at[beside], part_far, (beside, at))
    part_on.start()

    def gain_round(i):
        return remote(i, head_gains.at[i], gains_in.at[i], rounds[i], gain_sends, gain_recvs)

    rest_line.step(1)
    for i in range(len(rounds)):
        gain_round(i).start()
        gain_round(i).wait_recv()
        head_gains[i + 1] = head_gains[i] + gains_in[i]
        if i + 2 <= line:
            slab_line.step(i + 2, w_out_out)
            rest_line.step(i + 2, rest_sum)
    for step in range(len(rounds) + 2, line + 1):
        slab_line.step(step, w_out_out)
        rest_line.step(step, rest_sum)
    gains_out[...] = head_gains[len(rounds)]
    rest_home = [
        remote(REST_HOME + i, rest_sum.at[to], rest_out.at[me], (to, at))
        for i, to in enumerate((mate, beside, corner))
    ]
    rest_own = local(13, rest_sum.at[me], rest_out.at[me])
    for copy in rest_home:
        copy.start()
    rest_own.start()

    to_mate[1].wait_recv()
    part_on.wait_recv()

    def norm_back(step, carry):
        tile = pl.ds(pl.multiple_of(step * 32, 32), 32)
        grad = (
            parts[me, tile, :].astype(F32)
            + part_got[0, tile, :].astype(F32)
            + part_far[tile, :].astype(F32)
        )
        value = toks[me, tile, :].astype(F32)
        scale = lax.rsqrt(jnp.mean(value * value, axis=1, keepdims=True) + EPS)
        inner = grad * gain_ref[0:1, :]
        mean = jnp.mean(inner * value, axis=1, keepdims=True)
        dx_out[tile, :] = scale * inner - value * (scale * scale * scale * mean)
        return carry

    lax.fori_loop(0, rows // 32, norm_back, 0)

    for copy in homes + query_home + rest_home:
        copy.wait()
    for copy in (units_own, query_own, rest_own):
        copy.wait()
    for copy in three_on + one_on + four_on + two_on + to_mate + [down_on, part_on]:
        copy.wait_send()

    @pl.when(jnp.logical_not(stays))
    def _():
        down_home.wait()

    @pl.when(stays)
    def _():
        down_stay.wait()

    for total in (query_line, rest_line, slab_line):
        total.drain()
    for i in range(len(rounds)):
        gain_round(i).wait_send()


def last(
    dq, dkv_low, dkv_own, raw, cosine, sine, query_gain, key_gain, normed, w_in, toks, gains,
    gain_two, units, down, down_parts, slab,
):
    _, rows, width = toks.shape
    _, count, w_rows, _ = w_in.shape
    line = count // 2
    block = 4 * rows
    anywhere = pl.BlockSpec(memory_space=pl.ANY)
    vmem = pl.BlockSpec(memory_space=pltpu.VMEM)
    shape = jax.ShapeDtypeStruct
    dma = pltpu.SemaphoreType.DMA
    rounds = 3 + int(math.log2(line))
    part = (4, w_rows, COLS_Q)
    out_rows = slab.shape[1]
    return pl.pallas_call(
        functools.partial(last_kernel, line),
        out_shape=(
            shape((rows, width), F32),
            shape(part, BF),
            shape(part, BF),
            shape((8, w_rows, units.shape[2]), BF),
            shape(down.shape, BF),
            shape((out_rows, width), F32),
            shape((8, 128), F32),
        ),
        in_specs=[vmem] * 2 + [anywhere] * 2 + [vmem] * 2 + [anywhere] + [vmem] * 4
        + [anywhere] * 3 + [vmem] * 2 + [anywhere] * 4,
        out_specs=(vmem,) + (anywhere,) * 4 + (vmem,) * 2,
        scratch_shapes=[
            pltpu.VMEM((2, 2, block, 128), BF),
            pltpu.VMEM((2, block, 128), BF),
            pltpu.VMEM((2, block, 128), BF),
            pltpu.VMEM((2, block, 128), BF),
            pltpu.VMEM((2, block, 128), BF),
            pltpu.VMEM((block, COLS_Q + 128), F32),
            pltpu.VMEM((block, width), BF),
            pltpu.VMEM((width, block), BF),
            pltpu.VMEM(w_in.shape, BF),
            pltpu.VMEM(toks.shape, BF),
            pltpu.VMEM((block, 1), F32),
            pltpu.VMEM((block, COLS_IN), BF),
            pltpu.VMEM((4, count, w_rows, COLS_Q), BF),
            pltpu.VMEM((4, count, w_rows, COLS_Q), BF),
            pltpu.VMEM((line,) + part, BF),
            pltpu.VMEM((line,) + part, BF),
            pltpu.VMEM((line - 1,) + part, BF),
            pltpu.VMEM((line - 1,) + part, BF),
            pltpu.VMEM((line - 1,) + part, BF),
            pltpu.VMEM((line - 1,) + part, BF),
            pltpu.VMEM(part, BF),
            pltpu.VMEM(part, BF),
            pltpu.VMEM(slab.shape, BF),
            pltpu.VMEM((line,) + slab.shape[1:], BF),
            pltpu.VMEM((line - 1,) + slab.shape[1:], BF),
            pltpu.VMEM((line - 1,) + slab.shape[1:], BF),
            pltpu.VMEM(down.shape, BF),
            pltpu.VMEM(down.shape, BF),
            pltpu.VMEM((4, rows, width), BF),
            pltpu.VMEM((2, rows, width), BF),
            pltpu.VMEM((rows, width), BF),
            pltpu.VMEM((128, width), F32),
            pltpu.VMEM((rounds + 1, 8, 128), F32),
            pltpu.VMEM((rounds, 8, 128), F32),
            dma((LAST_TRANSFERS,)),
            dma((LAST_TRANSFERS,)),
            dma((3, 2, 2, line)),
            dma((rounds,)),
            dma((rounds,)),
            dma((14,)),
        ],
        compiler_params=pltpu.CompilerParams(
            collective_id=3, has_side_effects=True, vmem_limit_bytes=58 << 20
        ),
        cost_estimate=pl.CostEstimate(
            flops=60_000_000_000, bytes_accessed=60_000_000, transcendentals=1_000_000
        ),
        name="last",
    )(
        *dq, *dkv_low, *dkv_own, raw, cosine, sine, query_gain, key_gain, normed, w_in, toks, gains,
        gain_two, units, down, down_parts, slab,
    )


def shards(
    tokens,
    doc_lengths,
    norm1_gain,
    w_query,
    w_key,
    w_value,
    query_gain,
    key_gain,
    w_out,
    norm2_gain,
    w_gate,
    w_up,
    w_down,
    cotangent,
):
    tok_rows, width = tokens.shape
    blocks = lax.axis_size("blk")
    groups = lax.axis_size("head")
    group_id = lax.axis_index("head")
    blk_place = lax.axis_index("blk")
    block_len = groups * tok_rows
    per_group = QHEADS // groups
    head_ratio = QHEADS // KVHEADS
    w_rows = w_query.shape[0]
    line = blocks // 2
    side = blk_place % 2
    ff_rows = w_down.shape[0]
    ff_cols = line * ff_rows
    q_cols = per_group * HEAD
    firsts = [g * per_group // head_ratio for g in range(groups)]
    odd = group_id % 2

    starts = jnp.cumsum(doc_lengths) - doc_lengths
    offsets = jnp.arange(block_len, dtype=jnp.int32)
    token_pos = blk_place * block_len + offsets
    inside = starts[None, :] <= token_pos[:, None]
    token_start = jnp.max(jnp.where(inside, starts[None, :], 0), axis=1)
    in_doc = token_pos - token_start
    rope_freq = jnp.exp(-math.log(10000.0) * jnp.arange(HEAD // 2, dtype=F32) / (HEAD // 2))
    rope_angle = in_doc.astype(F32)[:, None] * rope_freq[None, :]
    cosine, sine = jnp.cos(rope_angle), jnp.sin(rope_angle)
    cosine = jnp.concatenate([cosine] * 4, axis=1)
    sine = jnp.concatenate([-sine, sine] * 2, axis=1)
    window_start = token_start - (blk_place - BACK) * block_len
    tiles = block_len // TILE
    edges = jnp.stack(
        [window_start[::TILE], window_start[TILE - 1 :: TILE]], axis=1
    ).reshape(2 * tiles)
    meta = jnp.concatenate([odd[None].astype(jnp.int32), edges.astype(jnp.int32)])

    rest = []
    for g in range(groups):
        kv = slice(firsts[g] * HEAD, (firsts[g] + 2) * HEAD)
        rest += [
            w_key[:, kv],
            w_value[:, kv],
            norm1_gain[:, None],
            norm2_gain[:, None],
            jnp.zeros((w_rows, 126), BF),
        ]
    rest = jnp.concatenate(rest, axis=1).reshape(w_rows, groups, COLS_Q)
    rest = jnp.swapaxes(rest, 0, 1)
    query_row = jnp.concatenate([query_gain, query_gain]).astype(F32)[None, :]
    key_row = jnp.concatenate([key_gain, key_gain]).astype(F32)[None, :]
    (
        wide,
        queries,
        kv_window,
        raw,
        normed_one,
        w_in,
        top_far,
        top_across,
        w_blk,
        slab,
        slab_next,
        down_own,
        down_one,
        down_two,
        toks,
        gains,
    ) = first(
        tokens,
        w_query,
        rest,
        w_gate,
        w_up,
        w_down,
        w_out,
        cotangent,
        cosine,
        sine,
        query_row,
        key_row,
    )
    slabs, downs = [slab, slab_next], [down_own, down_one, down_two]
    for _ in range(line - 4):
        slabs.append(ring(slabs[-1], 2))
        downs.append(ring(downs[-1], 2))
    w_own = w_blk.reshape(q_cols, width)
    slabs, downs, w_own, top_far, top_across, queries = sync(
        slabs, downs, w_own, top_far, top_across, queries
    )
    slabs.append(ring(slabs[-1], 2))
    downs.append(ring(downs[-1], 2))
    w_far = swap(w_own, "head", 2)
    half = tok_rows // 2
    top_high = swap(top_far[:half], "blk", 1)
    top_low = swap(top_across[half:], "head", 2)
    kept, attn_out = attend(meta, wide, kv_window, window_start[:, None])
    kept, attn_out, slabs, downs, w_far, top_high, top_low = sync(
        kept, attn_out, slabs, downs, w_far, top_high, top_low
    )
    if ff_rows % 16:
        w_d = jnp.zeros((line, ff_rows, width), BF)
        for step, part in enumerate(downs):
            w_d = put(w_d, part, (blk_place // 2 - step) % line)
        downs = [w_d.reshape(ff_cols, width)]
    attn_out = attn_out.reshape(groups, tok_rows, q_cols)

    (
        resid,
        grad_resid,
        grad_attn,
        mixed,
        grad_mix,
        out_mine,
        out_got,
        w_o,
        gu_parts,
        gu_moved,
        down_parts,
        grad_gain_two,
    ) = middle(
        attn_out,
        tokens,
        w_own,
        w_far,
        gains[1:2],
        (cotangent, top_far, top_across, top_high, top_low),
        slabs,
        downs,
    )
    down_parts = down_parts.reshape(line, ff_rows, width)
    gu_parts = gu_parts.reshape(groups, line, 2 * w_rows, 2 * ff_cols)
    down_sum = LineScatter(lambda p: take(down_parts, p))
    gu_sum = LineScatter(lambda p: take(gu_parts, p, 1))
    gu_sum.total = gu_moved
    gu_sum.add()
    out_parts = matmul_tn(mixed, grad_attn).astype(BF).reshape(groups, -1, width)
    down_sum.ahead(line - 4)
    gu_sum.ahead(line - 4)
    down_moved, gu_moved = down_sum.send(), gu_sum.send()

    def out_sum(i):
        return out_mine[i].astype(F32) + out_got[i].astype(F32)

    corner = out_sum(3).astype(BF)
    out_top = swap(corner[:half], "blk", 1)
    out_low = swap(corner[half:], "head", 2)
    near_parts = [swap(take(out_parts, group_id ^ bit), "head", 1) for bit in (1, 3)]
    back = functools.partial(
        attend_back,
        meta=meta,
        wide=wide,
        queries=queries,
        kv=kv_window,
        kept=kept,
        grads=grad_mix.reshape(block_len, q_cols),
        starts=window_start[None, :],
    )
    four = back(0)
    four, down_moved, gu_moved, out_top, out_low, near_parts, kv_window = sync(
        four, down_moved, gu_moved, out_top, out_low, near_parts, kv_window
    )
    down_sum.total, gu_sum.total = down_moved, gu_moved
    down_sum.add()
    gu_sum.add()
    down_moved, gu_moved = down_sum.send(), gu_sum.send()
    none = jnp.zeros((half, width), F32)
    out_far = out_sum(1) + jnp.concatenate([out_top.astype(F32), none], axis=0)
    out_across = out_sum(2) + jnp.concatenate([none, out_low.astype(F32)], axis=0)
    out_far = swap(out_far.astype(BF), "head", 2)
    out_across = swap(out_across.astype(BF), "blk", 1)
    far_parts = take(out_parts, group_id ^ 2).astype(F32) + near_parts[1].astype(F32)
    far_parts = swap(far_parts.astype(BF), "head", 2)
    two = back(1, kv=kv_window)
    four, two, down_moved, gu_moved, out_far, out_across, far_parts = sync(
        four, two, down_moved, gu_moved, out_far, out_across, far_parts
    )
    out_act = resid + out_sum(0) + out_far.astype(F32) + out_across.astype(F32)
    out_act = out_act.astype(BF)
    out_slab = take(out_parts, group_id).astype(F32) + near_parts[0].astype(F32)
    out_slab = (out_slab + far_parts.astype(F32)).astype(BF)
    out_slab = out_slab.reshape(blocks, w_out.shape[0], width)
    down_sum.total, gu_sum.total = down_moved, gu_moved
    down_sum.add()
    gu_sum.add()
    token_part, query_owned, rest_owned, units_owned, down_owned, d_w_out, head_gains = last(
        (four[0], two[0]),
        (four[1], two[1]),
        (four[2], two[2]),
        raw,
        cosine,
        sine,
        query_row,
        key_row,
        normed_one,
        w_in,
        toks,
        gains,
        grad_gain_two,
        gu_sum.total.astype(BF),
        down_sum.total.astype(BF),
        down_parts,
        out_slab,
    )
    d_tokens = grad_resid + token_part
    d_w_down = down_owned.astype(F32)
    units = units_owned.reshape(2, groups, w_rows, 2, ff_cols).astype(F32)
    units = jnp.transpose(units, (3, 2, 1, 0, 4)).reshape((2,) + w_gate.shape)
    d_w_gate, d_w_up = units[0], units[1]
    gain_sums = head_gains[:2, :HEAD] + head_gains[:2, HEAD:]
    owned = jnp.concatenate([query_owned, rest_owned], axis=2).astype(F32)
    owned = jnp.swapaxes(owned, 0, 1)
    d_w_query = owned[:, :, :q_cols].reshape(w_rows, QHEADS * HEAD)
    key_heads, value_heads = [], []
    for head_id in range(KVHEADS):
        keys_of, values_of = [], []
        for g in range(groups):
            for slot in range(2):
                if firsts[g] + slot == head_id:
                    at = q_cols + slot * HEAD
                    keys_of.append(owned[:, g, at : at + HEAD])
                    at += 2 * HEAD
                    values_of.append(owned[:, g, at : at + HEAD])
        key_heads.append(functools.reduce(jnp.add, keys_of))
        value_heads.append(functools.reduce(jnp.add, values_of))
    d_w_key = jnp.concatenate(key_heads, axis=1)
    d_w_value = jnp.concatenate(value_heads, axis=1)
    d_norm1_gain = jnp.sum(owned[:, :, q_cols + 4 * HEAD], axis=1)
    d_norm2_gain = jnp.sum(owned[:, :, q_cols + 4 * HEAD + 1], axis=1)
    return (
        out_act,
        d_tokens,
        d_norm1_gain,
        d_w_query,
        d_w_key,
        d_w_value,
        gain_sums[0],
        gain_sums[1],
        d_w_out,
        d_norm2_gain,
        d_w_gate,
        d_w_up,
        d_w_down,
    )


def solution(mesh):
    by_token = P(("blk", "head"), None)
    by_row = P(("head", "blk"), None)
    by_entry = P(("head", "blk"))
    in_specs = (
        by_token,
        P(),
        by_entry,
        by_row,
        by_row,
        by_row,
        P(),
        P(),
        by_row,
        by_entry,
        by_row,
        by_row,
        by_row,
        by_token,
    )
    out_specs = (
        by_token,
        by_token,
        by_entry,
        by_row,
        by_row,
        by_row,
        P(),
        P(),
        by_row,
        by_entry,
        by_row,
        by_row,
        by_row,
    )
    return jax.shard_map(shards, mesh=mesh, in_specs=in_specs, out_specs=out_specs, check_vma=False)
```

```python
import functools
import math

import jax
import jax.numpy as jnp
from jax import lax
from jax.experimental import pallas as pl
from jax.experimental.pallas import tpu as pltpu
from jax.sharding import PartitionSpec as P

QHEADS = 24
KVHEADS = 6
HEAD = 64
MAXDOC = 4096

EPS = 1e-06
SCALE = 0.125
LOG2E = 1.4426950408889634
NEG = -1e30
TILE = 256
BACK = 4
BF = jnp.bfloat16
F32 = jnp.float32


def matmul(left_side, right_side):
    return jnp.dot(left_side, right_side, preferred_element_type=F32)


def matmul_tn(left_side, right_side):
    return lax.dot_general(
        left_side, right_side, (((0,), (0,)), ((), ())), preferred_element_type=F32
    )


def matmul_nt(left_side, right_side):
    return lax.dot_general(
        left_side, right_side, (((1,), (1,)), ((), ())), preferred_element_type=F32
    )


def swap(block, axis, bit):
    count = lax.axis_size(axis)
    return lax.ppermute(block, axis, [(i, i ^ bit) for i in range(count)])


def ring(block, step):
    count = lax.axis_size("blk")
    return lax.ppermute(block, "blk", [(i, (i + step) % count) for i in range(count)])


def put(full, part, index, axis=0):
    return lax.dynamic_update_index_in_dim(full, part, index, axis)


def take(full, index, axis=0):
    return lax.dynamic_index_in_dim(full, index, axis, keepdims=False)


def place_of():
    at = lax.axis_index("blk")
    return at // 2, at % 2, lax.axis_size("blk") // 2


class LineScatter:
    def __init__(self, chunk):
        self.place, _, self.line = place_of()
        self.chunk = chunk
        self.step = 1
        self.total = chunk((self.place - 1) % self.line)

    def send(self):
        self.total = ring(self.total.astype(BF), 2)
        return self.total

    def add(self):
        self.step += 1
        mine = self.chunk((self.place - self.step) % self.line)
        self.total = self.total.astype(F32) + mine.astype(F32)

    def ahead(self, steps):
        for _ in range(steps):
            self.send()
            self.add()


def gather_blk(part, axis=0):
    place, side, line = place_of()
    shape = part.shape[:axis] + (line, 2) + part.shape[axis:]
    full = jnp.zeros(shape, part.dtype)
    held = part

    def store(full, block, source, side):
        block = block.reshape(block.shape[:axis] + (1, 1) + block.shape[axis:])
        at = [0] * full.ndim
        at[axis], at[axis + 1] = source, side
        return lax.dynamic_update_slice(full, block, at)

    for step in range(line):
        if step:
            held = ring(held, 2)
        other = swap(held, "blk", 1)
        source = (place - step) % line
        full = store(full, held, source, side)
        full = store(full, other, source, 1 - side)
    return full


def sync(*trees):
    return lax.optimization_barrier(trees)


def nt(left_side, right_side):
    return lax.dot_general(
        left_side, right_side, (((1,), (1,)), ((), ())), preferred_element_type=F32
    )


def nn(left_side, right_side):
    return lax.dot_general(
        left_side, right_side, (((1,), (0,)), ((), ())), preferred_element_type=F32
    )


def lanes(shape):
    return lax.broadcasted_iota(jnp.int32, shape, len(shape) - 1)


def transposed(block):
    return jnp.swapaxes(block, 0, 1)


def head_groups(meta_ref):
    odd = meta_ref[0]
    return ((4, 2 * odd, odd), (2, 4 * (1 - odd), 1 - odd))


def split_window(kv_ref, keys, values, step, slot):
    per_block = kv_ref.shape[2] // TILE
    block, part = step // per_block, step % per_block
    source = pl.ds(pl.multiple_of(part * TILE, TILE), TILE)
    target = pl.ds(pl.multiple_of(step * TILE, TILE), TILE)
    low = lanes((TILE, 128)) < HEAD
    both = kv_ref[block, slot, source, :].astype(F32)
    moved = pltpu.roll(both, HEAD, 1)
    keys[target, 0:128] = jnp.where(low, both, moved).astype(BF)
    values[target, :] = jnp.where(low, moved, 1.0).astype(BF)
    return target


def attend_kernel(
    meta_ref, query_ref, kv_ref, start_ref, out_ref, low_ref, acc_ref, keys, values
):
    heads, rows, _ = query_ref.shape
    base = keys.shape[1] - rows
    lane = lanes((TILE, 128))

    def fill(step, carry):
        for slot in range(2):
            split_window(kv_ref, keys.at[slot], values.at[slot], step, slot)
        return carry

    lax.fori_loop(0, keys.shape[1] // TILE, fill, 0)
    for count, first, slot in head_groups(meta_ref):
        for tile in range(rows // TILE):
            q_at = tile * TILE
            low, high = meta_ref[1 + 2 * tile], meta_ref[2 + 2 * tile]
            queries = query_ref[pl.ds(first, count), q_at : q_at + TILE, :].reshape(
                count * TILE, 2 * HEAD
            )
            acc = acc_ref.at[pl.ds(0, count * TILE)]
            acc[...] = jnp.zeros((count * TILE, 2 * HEAD), F32)
            start_col = start_ref[q_at : q_at + TILE, :]
            q_pos = base + q_at + lax.broadcasted_iota(jnp.int32, (TILE, 1), 0)

            def step(at, carry, masked, size=TILE):
                k_at = pl.multiple_of(at * TILE, TILE)
                scores = nt(queries, keys[slot, pl.ds(k_at, size), :])
                if masked:
                    k_pos = k_at + lax.broadcasted_iota(jnp.int32, (1, TILE), 1)
                    allowed = (start_col <= k_pos) & (k_pos <= q_pos)
                    scores = jnp.where(
                        allowed[None], scores.reshape(count, TILE, TILE), NEG
                    ).reshape(count * TILE, TILE)
                weights = jnp.exp2(scores).astype(BF)
                acc[...] += nn(weights, values[slot, pl.ds(k_at, size), :])
                return carry

            begin = low // TILE
            last = (base + q_at) // TILE
            clear = jnp.minimum((high + TILE - 1) // TILE, last)
            lax.fori_loop(begin, clear, functools.partial(step, masked=True), 0)
            pairs = (last - clear) // 4

            def wide_step(i, carry):
                return step(clear + 4 * i, carry, False, 4 * TILE)

            lax.fori_loop(0, pairs, wide_step, 0)
            lax.fori_loop(
                clear + 4 * pairs, last, functools.partial(step, masked=False), 0
            )
            step(last, 0, True)
            for j in range(count):
                part = acc_ref[j * TILE : (j + 1) * TILE, :]
                total = part[:, HEAD : HEAD + 1]
                out_ref[first + j, q_at : q_at + TILE, :] = jnp.where(
                    lane < HEAD, part / total, jnp.log2(total)
                )

    def lay(step, carry):
        tile = pl.ds(pl.multiple_of(step * TILE, TILE), TILE)
        for t in range(heads // 2):
            pair = jnp.where(
                lane < HEAD, out_ref[2 * t, tile, :], pltpu.roll(out_ref[2 * t + 1, tile, :], HEAD, 1)
            )
            low_ref[tile, t * 128 : (t + 1) * 128] = pair.astype(BF)
        return carry

    lax.fori_loop(0, rows // TILE, lay, 0)


def attend(meta, queries, kv, starts):
    heads, rows, _ = queries.shape
    window = kv.shape[0] * rows
    vmem = pl.BlockSpec(memory_space=pltpu.VMEM)
    return pl.pallas_call(
        attend_kernel,
        out_shape=(
            jax.ShapeDtypeStruct((heads, rows, 2 * HEAD), F32),
            jax.ShapeDtypeStruct((rows, heads * HEAD), BF),
        ),
        in_specs=[pl.BlockSpec(memory_space=pltpu.SMEM)] + [vmem] * 3,
        out_specs=(vmem, vmem),
        scratch_shapes=[
            pltpu.VMEM((4 * TILE, 2 * HEAD), F32),
            pltpu.VMEM((2, window, 2 * HEAD), BF),
            pltpu.VMEM((2, window, 2 * HEAD), BF),
        ],
        compiler_params=pltpu.CompilerParams(vmem_limit_bytes=48 << 20),
        cost_estimate=pl.CostEstimate(
            flops=60_000_000_000, bytes_accessed=20_000_000, transcendentals=20_000_000
        ),
        name="attend",
    )(meta, queries, kv, starts)


def attend_back_kernel(
    which,
    meta_ref,
    wide_ref,
    query_ref,
    kv_ref,
    out_ref,
    grad_ref,
    start_ref,
    dq_ref,
    low_ref,
    own_ref,
    keys,
    values,
    keys_t,
    query_t,
    grad_t,
    grads,
    dq,
    dkv,
):
    rows = query_ref.shape[1]
    window = keys.shape[0]
    base = window - rows
    lane = lanes((TILE, 128))
    low_lane = lane < HEAD
    count, first, slot = head_groups(meta_ref)[which]

    def fill(step, carry):
        target = split_window(kv_ref, keys, values, step, slot)
        keys[target, 128:256] = jnp.ones((TILE, 128), BF)
        keys_t[:, target] = transposed(keys[target, 0:128])[0:HEAD, :]
        dkv[target, :] = jnp.zeros((TILE, 128), F32)
        return carry

    lax.fori_loop(0, window // TILE, fill, 0)

    def low_terms(value, first):
        out = jnp.zeros_like(value)
        for i in range(3):
            term = value.astype(BF).astype(F32)
            out = jnp.where(lane == first + i, term, out)
            value = value - term
        return out

    def turn(step, carry):
        tile = pl.ds(pl.multiple_of(step * TILE, TILE), TILE)
        for j in range(count):
            query_t[j, 0:128, tile] = transposed(wide_ref[first + j, tile, :])
            kept = out_ref[first + j, tile, :]
            query_t[j, 128:256, tile] = transposed(low_terms(-kept, HEAD).astype(BF))
            pair = pl.ds(pl.multiple_of((first // 2 + j // 2) * 128, 128), 128)
            grad = grad_ref[tile, pair].astype(F32)
            moved = pltpu.roll(grad, HEAD, 1)
            if j % 2:
                grad, moved = moved, grad
            dots = jnp.sum(jnp.where(low_lane, grad * kept, 0.0), axis=1, keepdims=True)
            dots = jnp.broadcast_to(-dots, (TILE, 128))
            block = jnp.where(low_lane, grad, low_terms(dots, HEAD))
            grad_t[j, :, tile] = transposed(block.astype(BF))
            grads[j, tile, :] = jnp.where(low_lane, 0.0, moved).astype(BF)
            dq[j, :, tile] = jnp.zeros((HEAD, TILE), F32)
        return carry

    lax.fori_loop(0, rows // TILE, turn, 0)
    for tile in range(rows // TILE):
        q_at = tile * TILE
        q_cols = slice(q_at, q_at + TILE)
        low, high = meta_ref[1 + 2 * tile], meta_ref[2 + 2 * tile]
        start_row = start_ref[:, q_cols]
        q_pos = base + q_at + lax.broadcasted_iota(jnp.int32, (1, TILE), 1)

        def step(at, carry, masked, size=TILE):
            k_at = pl.multiple_of(at * TILE, TILE)
            k_rows = pl.ds(k_at, size)
            key_block = keys[k_rows, :]
            value_block = values[k_rows, :]
            key_t = keys_t[:, k_rows]
            if masked:
                k_pos = k_at + lax.broadcasted_iota(jnp.int32, (TILE, 1), 0)
                allowed = (start_row <= k_pos) & (k_pos <= q_pos)
            total = dkv[k_rows, :]
            for j in range(count):
                scores = nn(key_block, query_t[j, :, q_cols])
                if masked:
                    scores = jnp.where(allowed, scores, NEG)
                probs = jnp.exp2(scores)
                diff = nn(value_block, grad_t[j, :, q_cols])
                grad_score = (probs * diff).astype(BF)
                total = (
                    total
                    + nn(probs.astype(BF), grads[j, q_cols, :])
                    + nn(grad_score, query_ref[first + j, q_cols, :])
                )
                dq[j, :, q_cols] += nn(key_t, grad_score)
            dkv[k_rows, :] = total
            return carry

        begin = low // TILE
        last = (base + q_at) // TILE
        clear = jnp.minimum((high + TILE - 1) // TILE, last)
        lax.fori_loop(begin, clear, functools.partial(step, masked=True), 0)
        pairs = (last - clear) // 4

        def wide_step(i, carry):
            return step(clear + 4 * i, carry, False, 4 * TILE)

        lax.fori_loop(0, pairs, wide_step, 0)
        lax.fori_loop(
            clear + 4 * pairs, last, functools.partial(step, masked=False), 0
        )
        step(last, 0, True)

    def finish(step, carry):
        tile = pl.ds(pl.multiple_of(step * TILE, TILE), TILE)
        for t in range(count // 2):
            pair = jnp.concatenate([dq[2 * t, :, tile], dq[2 * t + 1, :, tile]], axis=0)
            dq_ref[tile, t * 128 : (t + 1) * 128] = transposed(pair) * SCALE
        for block in range(BACK + 1):
            source = pl.ds(pl.multiple_of(block * rows + step * TILE, TILE), TILE)
            part = dkv[source, :]
            part = jnp.where(low_lane, part * SCALE, part)
            if block < BACK:
                low_ref[block, tile, :] = part.astype(BF)
            else:
                own_ref[tile, :] = part
        return carry

    lax.fori_loop(0, rows // TILE, finish, 0)


def attend_back(which, meta, wide, queries, kv, kept, grads, starts):
    _, rows, _ = queries.shape
    window = kv.shape[0] * rows
    count = (4, 2)[which]
    vmem = pl.BlockSpec(memory_space=pltpu.VMEM)
    shape = jax.ShapeDtypeStruct
    return pl.pallas_call(
        functools.partial(attend_back_kernel, which),
        out_shape=(
            shape((rows, count * HEAD), F32),
            shape((BACK, rows, 128), BF),
            shape((rows, 128), F32),
        ),
        in_specs=[pl.BlockSpec(memory_space=pltpu.SMEM)] + [vmem] * 6,
        out_specs=(vmem,) * 3,
        scratch_shapes=[
            pltpu.VMEM((window, 256), BF),
            pltpu.VMEM((window, 128), BF),
            pltpu.VMEM((HEAD, window), BF),
            pltpu.VMEM((count, 256, rows), BF),
            pltpu.VMEM((count, 128, rows), BF),
            pltpu.VMEM((count, rows, 128), BF),
            pltpu.VMEM((count, HEAD, rows), F32),
            pltpu.VMEM((window, 128), F32),
        ],
        compiler_params=pltpu.CompilerParams(vmem_limit_bytes=48 << 20),
        cost_estimate=pl.CostEstimate(
            flops=count * 20_000_000_000, bytes_accessed=40_000_000, transcendentals=20_000_000
        ),
        name=("attend_back_four", "attend_back_two")[which],
    )(meta, wide, queries, kv, kept, grads, starts)


MESH = pl.DeviceIdType.MESH
HEADS_OUT, SLAB, NEAR, FAR, ACROSS, FAR_ON, ACROSS_ON = 0, 3, 7, 8, 9, 10, 11
CORNER_TOP, CORNER_LOW, CORNER_ON, TO_MATE = 12, 13, 14, 15
BACK_TOP, BACK_LOW, BACK_FAR, BACK_ACROSS, HEADS_BACK, SUM_ON = 19, 20, 21, 22, 23, 26
WEIGHT_ON, TOP_ON, OUT_MATE, DOWN_LAST, TRANSFERS = 30, 32, 37, 41, 42
SPANS = ((0, 256), (256, 256), (512, 128))


def middle_kernel(
    slabs,
    downs,
    line,
    attn_ref,
    tokens_ref,
    w_own_ref,
    w_far_ref,
    gain_ref,
    top_ref,
    top_far_ref,
    top_across_ref,
    top_high_ref,
    top_low_ref,
    *refs,
):
    slab_refs, down_refs = refs[:slabs], refs[slabs : slabs + downs]
    (
        resid_out,
        grad_out,
        grad_low_out,
        mixed_out,
        heads_out,
        part_out,
        part_in,
        w_out_ref,
        gu_out,
        gu_next,
        down_out,
        gain_out,
        mixed,
        acts,
        tops,
        w_gu,
        w_dn,
        hidden,
        grad_gu,
        pairs,
        got,
        stage,
        in_far,
        in_across,
        in_top,
        in_low,
        resid,
        turned,
        gu_stage,
        sends,
        recvs,
        locals_,
    ) = refs[slabs + downs :]
    me, at = lax.axis_index("head"), lax.axis_index("blk")
    count = lax.axis_size("blk")
    side, place = at % 2, at // 2
    odd = me % 2
    mate, beside, corner = me + 1 - 2 * odd, (me + 2) % 4, (me + 3 - 2 * odd) % 4
    other = at + 1 - 2 * side
    after, before = (at + 2) % count, (at + count - 2) % count
    rows, width = tokens_ref.shape
    half = rows // 2
    cols = mixed.shape[1] // 4
    units = w_dn.shape[0]
    slab_rows = slab_refs[0].shape[1]

    barrier = pltpu.get_barrier_semaphore()
    peers = ((mate, at), (beside, at), (corner, at), (me, other), (me, after), (me, before))
    for peer in peers:
        pl.semaphore_signal(barrier, inc=1, device_id=peer, device_id_type=MESH)
    pl.semaphore_wait(barrier, len(peers))

    def remote(index, source, target, device):
        return pltpu.make_async_remote_copy(
            src_ref=source,
            dst_ref=target,
            send_sem=sends.at[index],
            recv_sem=recvs.at[index],
            device_id=device,
            device_id_type=MESH,
        )

    def local(index, source, target):
        return pltpu.make_async_copy(source, target, locals_.at[index])

    def mixed_cols(head):
        return mixed.at[:, pl.ds(pl.multiple_of(head * cols, 128), cols)]

    heads = [
        remote(HEADS_OUT + i, attn_ref.at[to], mixed_cols(me), (to, at))
        for i, to in enumerate((mate, beside, corner))
    ]
    for copy in heads:
        copy.start()
    own_heads = local(0, attn_ref.at[me], mixed_cols(me))
    own_heads.start()

    def w_rows_of(head):
        return pairs.at[pl.ds(pl.multiple_of(head * cols, 128), cols)]

    weight_on = [
        remote(WEIGHT_ON, w_own_ref, w_rows_of(me), (mate, at)),
        remote(WEIGHT_ON + 1, w_far_ref, w_rows_of(beside), (mate, at)),
    ]
    for copy in weight_on:
        copy.start()
    load_out = [
        local(1, w_own_ref, w_rows_of(me)),
        local(2, w_far_ref, w_rows_of(beside)),
    ]
    for copy in load_out:
        copy.start()

    def slab_at(head, source):
        start = pl.multiple_of((head * line + source) * slab_rows, 16)
        return w_gu.at[pl.ds(start, slab_rows)]

    last = (place + line - (slabs - 1)) % line
    slab_on = [
        remote(SLAB + h, slab_refs[-1].at[h], slab_at(h, last), (me, after)) for h in range(4)
    ]
    for copy in slab_on:
        copy.start()
    load_slabs = [
        local(7 + 4 * i + h, ref.at[h], slab_at(h, (place + line - i) % line))
        for i, ref in enumerate(slab_refs)
        for h in range(4)
    ]
    for copy in load_slabs:
        copy.start()
    base_sem = 14 + 4 * slabs + downs
    if downs == 1:
        load_down = [local(14 + 4 * slabs, down_refs[0], w_dn)]
        down_last = []
    else:
        part_rows = units // line

        def down_at(source):
            return w_dn.at[pl.ds(pl.multiple_of(source * part_rows, 16), part_rows)]

        load_down = [
            local(14 + 4 * slabs + i, ref, down_at((place + line - i) % line))
            for i, ref in enumerate(down_refs)
        ]
        down_last = [remote(DOWN_LAST, down_refs[-1], down_at(last), (me, after))]
    for copy in down_last:
        copy.start()
    slot = side * 4 + me
    far_slot, across_slot = side * 4 + beside, (1 - side) * 4 + me
    corner_slot = (1 - side) * 4 + beside
    top_parts = (
        (top_ref, tops.at[slot]),
        (top_far_ref, tops.at[far_slot]),
        (top_across_ref, tops.at[across_slot]),
        (top_high_ref, tops.at[corner_slot, pl.ds(0, half)]),
        (top_low_ref, tops.at[corner_slot, pl.ds(half, half)]),
    )
    load_top = [
        local(7 + 4 * slabs + i, source, target) for i, (source, target) in enumerate(top_parts)
    ]
    for copy in load_down + load_top:
        copy.start()

    for copy in heads + weight_on:
        copy.wait_recv()
    own_heads.wait()
    for copy in load_out:
        copy.wait()
    top_on = [
        remote(TOP_ON + i, source, target, (mate, at))
        for i, (source, target) in enumerate(top_parts)
    ]
    for copy in top_on:
        copy.start()
    keep_weight = local(base_sem, pairs.at[pl.ds(0, 4 * cols)], w_out_ref)
    keep_weight.start()
    keep_mixed = local(base_sem + 2, mixed, mixed_out)
    keep_mixed.start()

    def resid_cols(step, carry):
        span = pl.ds(pl.multiple_of(step * 256, 256), 256)
        weight = pairs[0 : 4 * cols, span]
        resid[:, span] = tokens_ref[:, span].astype(F32) + nn(mixed[...], weight)
        return carry

    lax.fori_loop(0, width // 256, resid_cols, 0)

    def norm_tile(step, carry):
        tile = pl.ds(pl.multiple_of(step * 32, 32), 32)
        block = resid[tile, :]
        scale = lax.rsqrt(jnp.mean(block * block, axis=1, keepdims=True) + EPS)
        acts[slot, tile, :] = (block * scale * gain_ref[...]).astype(BF)
        return carry

    lax.fori_loop(0, rows // 32, norm_tile, 0)
    keep_resid = local(base_sem + 3, resid, resid_out)
    keep_resid.start()

    near = remote(NEAR, acts.at[slot], acts.at[slot], (mate, at))
    far = remote(FAR, acts.at[slot], acts.at[slot], (beside, at))
    across = remote(ACROSS, acts.at[slot], acts.at[slot], (me, other))
    far_on = remote(FAR_ON, acts.at[far_slot], acts.at[far_slot], (mate, at))
    across_on = remote(ACROSS_ON, acts.at[across_slot], acts.at[across_slot], (mate, at))
    corner_on = remote(CORNER_ON, acts.at[corner_slot], acts.at[corner_slot], (mate, at))
    far_top = acts.at[far_slot, pl.ds(0, half)]
    across_low = acts.at[across_slot, pl.ds(half, half)]
    corner_top = remote(CORNER_TOP, far_top, far_top, (me, other))
    corner_low = remote(CORNER_LOW, across_low, across_low, (beside, at))
    near.start()
    far.start()
    across.start()
    for copy in load_slabs:
        copy.wait()
    for copy in slab_on + down_last:
        copy.wait_recv()
    for copy in load_down + load_top + [keep_weight]:
        copy.wait()
    for copy in top_on:
        copy.wait_recv()

    def pair_rows(index, first=0, size=rows):
        return pl.ds(pl.multiple_of(index * rows + first, 16), size)

    def to_mate(c):
        return remote(
            TO_MATE + c, pairs.at[pair_rows(2 * c + 1 - odd)], got.at[c], (mate, at)
        )

    def keep_part(c):
        return local(base_sem + 4, stage.at[odd], part_out.at[c])

    def part_on(c):
        return remote(OUT_MATE + c, stage.at[1 - odd], part_in.at[c], (mate, at))

    def chunk(c, carry):
        its_side = (side + c // 2) % 2
        its_head = (me + 2 * (c % 2)) % 4
        pair = its_side * 4 + its_head - its_head % 2

        @pl.when(c == 0)
        def _():
            near.wait_recv()

        @pl.when(c == 1)
        def _():
            far.wait_recv()
            far_on.start()
            corner_top.start()
            across.wait_recv()
            across_on.start()
            corner_low.start()
            far_on.wait_recv()

        @pl.when(c == 2)
        def _():
            corner_top.wait_recv()
            corner_low.wait_recv()
            corner_on.start()
            across_on.wait_recv()

        @pl.when(c == 3)
        def _():
            corner_on.wait_recv()

        for first, size in SPANS:
            block = acts[pl.ds(pair, 2)].reshape(2 * rows, width)
            gate = nn(block, w_gu[:, first : first + size])
            up = nn(block, w_gu[:, units + first : units + first + size])
            grad = nt(
                tops[pl.ds(pair, 2)].reshape(2 * rows, width), w_dn[first : first + size, :]
            )
            sig = jax.nn.sigmoid(gate)
            silu = gate * sig
            shape = (2, rows, size)
            hidden[pl.ds(pair, 2), :, first : first + size] = (
                (silu * up).astype(BF).reshape(shape)
            )
            grad_gu[pl.ds(pair, 2), :, first : first + size] = (
                (grad * up * sig * (1 + gate * (1 - sig))).astype(BF).reshape(shape)
            )
            grad_gu[pl.ds(pair, 2), :, units + first : units + first + size] = (
                (grad * silu).astype(BF).reshape(shape)
            )

        def grad_cols(step, carry):
            span = pl.ds(pl.multiple_of(step * 256, 256), 256)
            block = grad_gu[pl.ds(pair, 2)].reshape(2 * rows, 2 * units)
            part = nt(block, w_gu[span, :])
            pairs[pl.ds(pl.multiple_of(2 * c * rows, 128), 2 * rows), span] = part.astype(BF)
            return carry

        lax.fori_loop(0, width // 256, grad_cols, 0)
        to_mate(c).start()

        @pl.when(c > 0)
        def _():
            keep_part(c - 1).wait()
            part_on(c - 1).wait_send()

        def out_cols(step, carry):
            span = pl.ds(pl.multiple_of(step * 256, 256), 256)
            block = hidden[pl.ds(pair, 2)].reshape(2 * rows, units)
            part = nn(block, w_dn[:, span])
            stage[:, :, span] = part.astype(BF).reshape(2, rows, 256)
            return carry

        lax.fori_loop(0, width // 256, out_cols, 0)
        keep_part(c).start()
        part_on(c).start()
        return carry

    lax.fori_loop(0, 4, chunk, 0)

    def add_rows(c, first, extra):
        def tile(step, carry):
            span = pl.ds(pl.multiple_of(first + step * 32, 32), 32)
            mine = pair_rows(2 * c + odd, first + step * 32, 32)
            total = pairs[mine, :].astype(F32) + got[c, span, :].astype(F32)
            for ref in extra:
                total = total + ref[pl.ds(pl.multiple_of(step * 32, 32), 32), :].astype(F32)
            pairs[mine, :] = total.astype(BF)
            return carry

        lax.fori_loop(0, half // 32, tile, 0)

    back_top = remote(
        BACK_TOP, pairs.at[pair_rows(6 + odd, 0, half)], in_top, (me, other)
    )
    back_low = remote(
        BACK_LOW, pairs.at[pair_rows(6 + odd, half, half)], in_low, (beside, at)
    )
    back_far = remote(BACK_FAR, pairs.at[pair_rows(2 + odd)], in_far, (beside, at))
    back_across = remote(BACK_ACROSS, pairs.at[pair_rows(4 + odd)], in_across, (me, other))
    to_mate(3).wait_recv()
    add_rows(3, 0, ())
    back_top.start()
    add_rows(3, half, ())
    back_low.start()
    to_mate(1).wait_recv()
    to_mate(2).wait_recv()
    add_rows(1, half, ())
    add_rows(2, 0, ())

    keep_part(3).wait()
    part_on(3).wait_send()

    def gu_rows(step, carry):
        span = pl.ds(pl.multiple_of(step * 256, 256), 256)
        turned[...] = transposed(acts[:, :, span].reshape(8 * rows, 256))
        buffer = step % 2

        @pl.when(step > 1)
        def _():
            local(base_sem + 5 + buffer, gu_stage.at[buffer], gu_out.at[pl.ds(0, 256)]).wait()

        for n in range(2 * units // 256):
            part = nn(
                turned[...],
                grad_gu[:, :, n * 256 : (n + 1) * 256].reshape(8 * rows, 256),
            )
            gu_stage[buffer, :, n * 256 : (n + 1) * 256] = part.astype(BF)
        local(base_sem + 5 + buffer, gu_stage.at[buffer], gu_out.at[span]).start()
        return carry

    lax.fori_loop(0, 5, gu_rows, 0)
    back_top.wait_recv()
    add_rows(1, 0, (in_top,))
    back_far.start()
    back_low.wait_recv()
    add_rows(2, half, (in_low,))
    back_across.start()
    lax.fori_loop(5, width // 256, gu_rows, 0)
    for buffer in range(2):
        local(base_sem + 5 + buffer, gu_stage.at[buffer], gu_out.at[pl.ds(0, 256)]).wait()

    target = (place + line - 1) % line
    sum_on = [
        remote(
            SUM_ON + h,
            gu_out.at[pl.ds(pl.multiple_of((h * line + target) * slab_rows, 16), slab_rows)],
            gu_next.at[h],
            (me, after),
        )
        for h in range(4)
    ]
    for copy in sum_on:
        copy.start()

    for copy in (near, far, across, far_on, across_on, corner_on, corner_top, corner_low):
        copy.wait_send()
    load_again = [
        local(1 + i, w_out_ref.at[pl.ds(i * rows, rows)], acts.at[i]) for i in range(6)
    ]
    for copy in load_again:
        copy.start()

    for i, (first, size) in enumerate(SPANS):
        turned[0:size, :] = transposed(
            hidden[:, :, first : first + size].reshape(8 * rows, size)
        )
        buffer = i % 2
        if i > 1:
            local(base_sem + 7, stage.at[0], down_out.at[pl.ds(0, rows)]).wait()

        def down_cols(step, carry):
            span = pl.ds(pl.multiple_of(step * 256, 256), 256)
            part = nn(turned[0:size, :], tops[:, :, span].reshape(8 * rows, 256))
            stage[buffer, 0:size, span] = part.astype(BF)
            return carry

        lax.fori_loop(0, width // 256, down_cols, 0)
        local(
            base_sem + 7 + buffer,
            stage.at[buffer, pl.ds(0, size)],
            down_out.at[pl.ds(first, size)],
        ).start()

    to_mate(0).wait_recv()
    back_far.wait_recv()
    back_across.wait_recv()
    keep_resid.wait()
    gain_out[...] = jnp.zeros_like(gain_out)
    low = got.at[0]

    def norm_back(step, carry):
        tile = pl.ds(pl.multiple_of(step * 32, 32), 32)
        grad = (
            pairs[pair_rows(odd, step * 32, 32), :].astype(F32)
            + got[0, tile, :].astype(F32)
            + in_far[tile, :].astype(F32)
            + in_across[tile, :].astype(F32)
        )
        block = resid[tile, :]
        scale = lax.rsqrt(jnp.mean(block * block, axis=1, keepdims=True) + EPS)
        gain_out[...] += jnp.sum(grad * block * scale, axis=0, keepdims=True)
        inner = grad * gain_ref[...]
        mean = jnp.mean(inner * block, axis=1, keepdims=True)
        total = (
            tops[slot, tile, :].astype(F32)
            + scale * inner
            - block * (scale * scale * scale * mean)
        )
        resid[tile, :] = total
        low[tile, :] = total.astype(BF)
        return carry

    lax.fori_loop(0, rows // 32, norm_back, 0)
    keep_grad = local(base_sem + 3, resid, grad_out)
    keep_grad.start()
    keep_low = local(base_sem + 4, low, grad_low_out)
    keep_low.start()
    keep_mixed.wait()
    for copy in load_again:
        copy.wait()

    def heads_cols(step, carry):
        span = pl.ds(pl.multiple_of(step * 256, 256), 256)
        mixed[:, span] = nt(low[...], acts[step]).astype(BF)
        return carry

    lax.fori_loop(0, 6, heads_cols, 0)
    heads_on = [
        remote(HEADS_BACK + i, mixed_cols(to), heads_out.at[me], (to, at))
        for i, to in enumerate((mate, beside, corner))
    ]
    for copy in heads_on:
        copy.start()
    own_back = local(0, mixed_cols(me), heads_out.at[me])
    own_back.start()

    own_back.wait()
    keep_grad.wait()
    keep_low.wait()
    local(base_sem + 7, stage.at[0, pl.ds(0, SPANS[2][1])], down_out.at[pl.ds(0, SPANS[2][1])]).wait()
    local(base_sem + 8, stage.at[1], down_out.at[pl.ds(0, rows)]).wait()
    for copy in heads_on + sum_on:
        copy.wait()
    for copy in heads + slab_on + down_last:
        copy.wait_send()
    for copy in weight_on + top_on:
        copy.wait_send()
    for c in range(4):
        to_mate(c).wait_send()
        part_on(c).wait_recv()
    for copy in (back_top, back_low, back_far, back_across):
        copy.wait_send()


def middle(attn_out, tokens, w_own, w_far, gain, tops, slabs, downs):
    rows, width = tokens.shape
    units = slabs[0].shape[2] // 2
    cols = attn_out.shape[2]
    line = lax.axis_size("blk") // 2
    slab_shape = slabs[0].shape
    anywhere = pl.BlockSpec(memory_space=pl.ANY)
    vmem = pl.BlockSpec(memory_space=pltpu.VMEM)
    shape = jax.ShapeDtypeStruct
    eight, four = (8, rows, width), (4, rows, width)
    return pl.pallas_call(
        functools.partial(middle_kernel, len(slabs), len(downs), line),
        out_shape=(
            shape((rows, width), F32),
            shape((rows, width), F32),
            shape((rows, width), BF),
            shape((rows, 4 * cols), BF),
            shape(attn_out.shape, BF),
            shape(four, BF),
            shape(four, BF),
            shape((4 * cols, width), BF),
            shape((width, 2 * units), BF),
            shape(slab_shape, BF),
            shape((units, width), BF),
            shape((1, width), F32),
        ),
        in_specs=[anywhere, vmem, anywhere, anywhere, vmem]
        + [anywhere] * (len(tops) + len(slabs) + len(downs)),
        out_specs=(anywhere,) * 11 + (vmem,),
        scratch_shapes=[
            pltpu.VMEM((rows, 4 * cols), BF),
            pltpu.VMEM(eight, BF),
            pltpu.VMEM(eight, BF),
            pltpu.VMEM((width, 2 * units), BF),
            pltpu.VMEM((units, width), BF),
            pltpu.VMEM((8, rows, units), BF),
            pltpu.VMEM((8, rows, 2 * units), BF),
            pltpu.VMEM((8 * rows, width), BF),
            pltpu.VMEM(four, BF),
            pltpu.VMEM((2, rows, width), BF),
            pltpu.VMEM((rows, width), BF),
            pltpu.VMEM((rows, width), BF),
            pltpu.VMEM((rows // 2, width), BF),
            pltpu.VMEM((rows // 2, width), BF),
            pltpu.VMEM((rows, width), F32),
            pltpu.VMEM((256, 8 * rows), BF),
            pltpu.VMEM((2, 256, 2 * units), BF),
            pltpu.SemaphoreType.DMA((TRANSFERS,)),
            pltpu.SemaphoreType.DMA((TRANSFERS,)),
            pltpu.SemaphoreType.DMA((24 + 4 * len(slabs) + len(downs),)),
        ],
        compiler_params=pltpu.CompilerParams(
            collective_id=1, has_side_effects=True, vmem_limit_bytes=60 << 20
        ),
        cost_estimate=pl.CostEstimate(
            flops=60_000_000_000, bytes_accessed=100_000_000, transcendentals=2_000_000
        ),
        name="middle",
    )(attn_out, tokens, w_own, w_far, gain, *tops, *slabs, *downs)


TOK_NEAR, TOK_FAR, TOK_ON, IN_QUERY, IN_REST = 0, 1, 2, 3, 6
TOP_FAR, TOP_ACROSS = 9, 10
UNITS_MOVE, SLAB_ON, DOWN_ON = 11, 18, 19
KV_ONE, KV_TWO, KV_PAIR_ONE, KV_PAIR_TWO, FIRST_TRANSFERS = 20, 21, 22, 23, 24
COLS_Q = QHEADS // 4 * HEAD
COLS_IN = COLS_Q + 4 * HEAD


def head_scale(block):
    low = lanes(block.shape) < HEAD
    square = block * block
    first = jnp.sum(jnp.where(low, square, 0.0), axis=1, keepdims=True)
    second = jnp.sum(jnp.where(low, 0.0, square), axis=1, keepdims=True)
    return jnp.where(
        low, lax.rsqrt(first / HEAD + EPS), lax.rsqrt(second / HEAD + EPS)
    )


def swap_halves(block):
    low = lanes(block.shape) % HEAD < HEAD // 2
    return jnp.where(low, pltpu.roll(block, 96, 1), pltpu.roll(block, 32, 1))


def first_kernel(
    line,
    tokens_ref,
    query_ref,
    rest_ref,
    gate_ref,
    up_ref,
    down_ref,
    w_out_ref,
    top_ref,
    cos_ref,
    sin_ref,
    query_gain_ref,
    key_gain_ref,
    wide_out,
    query_out,
    kv_out,
    raw_out,
    normed_out,
    w_in_out,
    top_far_out,
    top_across_out,
    w_out_all,
    slab_out,
    slab_next,
    down_next,
    toks_out,
    gain_out,
    toks,
    normed,
    w_in,
    raw,
    wide,
    query,
    kv_own,
    gate,
    up,
    blocks,
    sends,
    recvs,
    ring_sends,
    ring_recvs,
    swap_sends,
    swap_recvs,
    out_ring_sends,
    out_ring_recvs,
    out_swap_sends,
    out_swap_recvs,
    locals_,
):
    me, at = lax.axis_index("head"), lax.axis_index("blk")
    count = lax.axis_size("blk")
    side, place = at % 2, at // 2
    odd = me % 2
    mate, beside, corner = me + 1 - 2 * odd, (me + 2) % 4, (me + 3 - 2 * odd) % 4
    other = at + 1 - 2 * side
    after, before = (at + 2) % count, (at + count - 2) % count
    rows, width = tokens_ref.shape
    half = rows // 2
    w_rows = query_ref.shape[0]
    units = slab_out.shape[2] // 2

    barrier = pltpu.get_barrier_semaphore()
    peers = [(mate, at), (beside, at), (corner, at), (me, after), (me, before)]
    peers += [(head, other) for head in (me, mate, beside, corner)]
    for peer in peers:
        pl.semaphore_signal(barrier, inc=1, device_id=peer, device_id_type=MESH)
    pl.semaphore_wait(barrier, len(peers))

    def remote(index, source, target, device, send=sends, recv=recvs):
        return pltpu.make_async_remote_copy(
            src_ref=source,
            dst_ref=target,
            send_sem=send.at[index],
            recv_sem=recv.at[index],
            device_id=device,
            device_id_type=MESH,
        )

    def local(index, source, target):
        return pltpu.make_async_copy(source, target, locals_.at[index])

    def cols_of(ref, start, size):
        return ref.at[:, pl.ds(pl.multiple_of(start, 128), size)]

    own_q = w_in.at[me, at, :, pl.ds(0, COLS_Q)]
    own_rest = w_in.at[me, at, :, pl.ds(COLS_Q, COLS_Q)]
    split = []
    for i, to in enumerate((mate, beside, corner)):
        split.append(
            remote(IN_QUERY + i, cols_of(query_ref, to * COLS_Q, COLS_Q), own_q, (to, at))
        )
        split.append(remote(IN_REST + i, rest_ref.at[to], own_rest, (to, at)))
    for copy in split:
        copy.start()
    own = [
        local(0, cols_of(query_ref, me * COLS_Q, COLS_Q), own_q),
        local(1, rest_ref.at[me], own_rest),
        local(2, tokens_ref, toks.at[me]),
        local(3, w_out_ref, w_out_all.at[at]),
    ]
    for copy in own:
        copy.start()
    tok_near = remote(TOK_NEAR, tokens_ref, toks.at[me], (mate, at))
    tok_far = remote(TOK_FAR, tokens_ref, toks.at[me], (beside, at))
    tok_on = remote(TOK_ON, toks.at[beside], toks.at[beside], (mate, at))
    tok_far.start()
    tok_near.start()
    down_on = remote(DOWN_ON, down_ref, down_next, (me, after))
    down_on.start()
    own_units = [local(4, gate_ref, gate), local(5, up_ref, up)]
    for copy in own_units:
        copy.start()

    def ring_copy(step):
        block = w_in.at[:, (at + count - 2 * (step - 1)) % count]
        return remote(step, block, block, (me, after), ring_sends, ring_recvs)

    def swap_copy(step):
        block = w_in.at[:, (at + count - 2 * step) % count]
        return remote(step, block, block, (me, other), swap_sends, swap_recvs)

    def out_ring(step):
        index = (at + count - 2 * (step - 1)) % count
        source = w_out_ref if step == 1 else w_out_all.at[index]
        return remote(
            step, source, w_out_all.at[index], (me, after), out_ring_sends, out_ring_recvs
        )

    def out_swap(step):
        index = (at + count - 2 * step) % count
        source = w_out_ref if step == 0 else w_out_all.at[index]
        return remote(
            step, source, w_out_all.at[index], (me, other), out_swap_sends, out_swap_recvs
        )

    out_ring(1).start()
    out_swap(0).start()

    for copy in own_units:
        copy.wait()
    ff_rows = units // line
    for j, ref in enumerate((gate, up)):
        for head in range(4):
            columns = ref[:, 2 * units * head : 2 * units * (head + 1)].astype(F32)
            for to_side in range(2):
                chosen = [
                    columns[:, (2 * z + to_side) * ff_rows : (2 * z + to_side + 1) * ff_rows]
                    for z in range(line)
                ]
                blocks[to_side, head, :, j * units : (j + 1) * units] = jnp.concatenate(
                    chosen, axis=1
                ).astype(BF)
    slab_rows = pl.ds(pl.multiple_of(side * w_rows, 16), w_rows)
    targets = [(side, mate), (side, beside), (side, corner)]
    targets += [(1 - side, head) for head in (me, mate, beside, corner)]
    spread = [
        remote(
            UNITS_MOVE + i,
            blocks.at[to_side, to_head],
            slab_out.at[me, slab_rows],
            (to_head, at if i < 3 else other),
        )
        for i, (to_side, to_head) in enumerate(targets)
    ]
    for copy in spread:
        copy.start()
    own_block = local(6, blocks.at[side, me], slab_out.at[me, slab_rows])
    own_block.start()
    for copy in split:
        copy.wait_recv()
    own[0].wait()
    own[1].wait()
    ring_copy(1).start()
    swap_copy(0).start()
    tok_far.wait_recv()
    tok_on.start()
    top_far = remote(TOP_FAR, top_ref, top_far_out, (beside, at))
    top_across = remote(TOP_ACROSS, top_ref, top_across_out, (me, other))
    top_far.start()
    for step in range(1, line):
        ring_copy(step).wait_recv()
        if step < line - 1:
            ring_copy(step + 1).start()
        swap_copy(step).start()
        out_ring(step).wait_recv()
        if step < line - 1:
            out_ring(step + 1).start()

    for copy in spread:
        copy.wait_recv()
    own_block.wait()
    slab_on = remote(SLAB_ON, slab_out, slab_next, (me, after))
    slab_on.start()
    tok_near.wait_recv()
    tok_on.wait_recv()
    own[2].wait()
    own[3].wait()
    for step in range(line):
        swap_copy(step).wait_recv()
    for step in range(1, line):
        out_swap(step).start()
    top_across.start()
    keep_in = [
        local(7 + h, w_in.at[h], w_in_out.at[h]) for h in range(4)
    ]
    for copy in keep_in:
        copy.start()

    gains = w_in[:, :, :, COLS_IN : COLS_IN + 128].reshape(width, 128).astype(F32)
    gain_out[...] = transposed(gains)[0:8, :]

    def norm_tile(step, carry):
        head, tile = step // (rows // 32), pl.ds(pl.multiple_of(step % (rows // 32) * 32, 32), 32)
        block = toks[head, tile, :].astype(F32)
        scale = lax.rsqrt(jnp.mean(block * block, axis=1, keepdims=True) + EPS)
        normed[pl.ds(pl.multiple_of(step * 32, 32), 32), :] = (
            block * scale * gain_out[0:1, :]
        ).astype(BF)
        return carry

    lax.fori_loop(0, 4 * rows // 32, norm_tile, 0)
    keep_normed = local(11, normed, normed_out)
    keep_normed.start()
    keep_toks = local(16, toks, toks_out)
    keep_toks.start()

    def project(step, carry):
        tile = pl.ds(pl.multiple_of(step * 256, 256), 256)
        for first, size in SPANS:
            weight = w_in[:, :, :, first : first + size].reshape(width, size)
            raw[tile, first : first + size] = nn(normed[tile, :], weight)
        return carry

    lax.fori_loop(0, 4 * rows // 256, project, 0)
    keep_raw = local(12, raw.at[:, pl.ds(0, COLS_Q + 128)], raw_out)
    keep_raw.start()

    def rotated(block, gain, tile):
        block = block * head_scale(block) * gain
        return block * cos_ref[tile, :] + swap_halves(block) * sin_ref[tile, :]

    def prepare(step, carry):
        tile = pl.ds(pl.multiple_of(step * 64, 64), 64)
        first_half = lanes((64, 128)) < HEAD
        for t in range(QHEADS // 4 // 2):
            block = rotated(raw[tile, t * 128 : (t + 1) * 128], query_gain_ref[...], tile)
            block = block.astype(BF).astype(F32)
            moved = pltpu.roll(block, HEAD, 1)
            query[2 * t, tile, :] = jnp.where(first_half, block, 0.0).astype(BF)
            query[2 * t + 1, tile, :] = jnp.where(first_half, moved, 0.0).astype(BF)
            scaled = block * (SCALE * LOG2E)
            upper = scaled.astype(BF).astype(F32)
            lower = scaled - upper
            wide[2 * t, tile, :] = jnp.where(
                first_half, upper, pltpu.roll(lower, HEAD, 1)
            ).astype(BF)
            wide[2 * t + 1, tile, :] = jnp.where(
                first_half, pltpu.roll(upper, HEAD, 1), lower
            ).astype(BF)
        keys = rotated(raw[tile, COLS_Q : COLS_Q + 128], key_gain_ref[...], tile)
        values = raw[tile, COLS_Q + 128 : COLS_Q + 256]
        kv_own[0, tile, :] = jnp.where(
            first_half, keys, pltpu.roll(values, HEAD, 1)
        ).astype(BF)
        kv_own[1, tile, :] = jnp.where(
            first_half, pltpu.roll(keys, HEAD, 1), values
        ).astype(BF)
        return carry

    lax.fori_loop(0, 4 * rows // 64, prepare, 0)

    kv_one = remote(KV_ONE, kv_own, kv_out.at[2], (me, after))
    kv_two = remote(KV_TWO, kv_out.at[2], kv_out.at[0], (me, after))
    pair_one_even = remote(KV_PAIR_ONE, kv_own, kv_out.at[3], (me, other))
    pair_one_odd = remote(KV_PAIR_ONE, kv_out.at[2], kv_out.at[3], (me, other))
    pair_two_even = remote(KV_PAIR_TWO, kv_out.at[2], kv_out.at[1], (me, other))
    pair_two_odd = remote(KV_PAIR_TWO, kv_out.at[0], kv_out.at[1], (me, other))
    kv_one.start()

    @pl.when(side == 0)
    def _():
        pair_one_even.start()

    keep = [
        local(13, kv_own, kv_out.at[4]),
        local(14, wide, wide_out),
        local(15, query, query_out),
    ]
    for copy in keep:
        copy.start()
    kv_one.wait_recv()
    kv_two.start()

    @pl.when(side == 0)
    def _():
        pair_two_even.start()

    @pl.when(side == 1)
    def _():
        pair_one_odd.start()

    kv_two.wait_recv()

    @pl.when(side == 1)
    def _():
        pair_two_odd.start()

    pair_one_even.wait_recv()
    pair_two_even.wait_recv()
    down_on.wait_recv()
    slab_on.wait_recv()
    for copy in (top_far, top_across):
        copy.wait_recv()
    for copy in keep + keep_in + [keep_normed, keep_raw, keep_toks]:
        copy.wait()
    for copy in split + spread:
        copy.wait_send()
    for copy in (tok_near, tok_far, tok_on, top_far, top_across):
        copy.wait_send()
    for copy in (slab_on, down_on, kv_one, kv_two):
        copy.wait_send()
    pair_one_even.wait_send()
    pair_two_even.wait_send()

    for step in range(line):
        swap_copy(step).wait_send()
        out_swap(step).wait()
        if step:
            ring_copy(step).wait_send()
            out_ring(step).wait_send()


def first(
    tokens, w_query, rest, w_gate, w_up, w_down, w_out, cotangent, cosine, sine, query_gain, key_gain
):
    rows, width = tokens.shape
    count = lax.axis_size("blk")
    w_rows, ff = w_gate.shape
    units = ff // 8
    block = 4 * rows
    anywhere = pl.BlockSpec(memory_space=pl.ANY)
    vmem = pl.BlockSpec(memory_space=pltpu.VMEM)
    shape = jax.ShapeDtypeStruct
    heads = QHEADS // 4
    slab = shape((4, 2 * w_rows, 2 * units), BF)
    dma = pltpu.SemaphoreType.DMA
    return pl.pallas_call(
        functools.partial(first_kernel, count // 2),
        out_shape=(
            shape((heads, block, 128), BF),
            shape((heads, block, 128), BF),
            shape((BACK + 1, 2, block, 128), BF),
            shape((block, COLS_Q + 128), F32),
            shape((block, width), BF),
            shape((4, count, w_rows, 2 * COLS_Q), BF),
            shape((rows, width), BF),
            shape((rows, width), BF),
            shape((count,) + w_out.shape, BF),
            slab,
            slab,
            shape(w_down.shape, BF),
            shape((4, rows, width), BF),
            shape((8, width), F32),
        ),
        in_specs=[anywhere] * 8 + [vmem] * 4,
        out_specs=(anywhere,) * 13 + (vmem,),
        scratch_shapes=[
            pltpu.VMEM((4, rows, width), BF),
            pltpu.VMEM((block, width), BF),
            pltpu.VMEM((4, count, w_rows, 2 * COLS_Q), BF),
            pltpu.VMEM((block, COLS_IN), F32),
            pltpu.VMEM((heads, block, 128), BF),
            pltpu.VMEM((heads, block, 128), BF),
            pltpu.VMEM((2, block, 128), BF),
            pltpu.VMEM(w_gate.shape, BF),
            pltpu.VMEM(w_up.shape, BF),
            pltpu.VMEM((2, 4, w_rows, 2 * units), BF),
            dma((FIRST_TRANSFERS,)),
            dma((FIRST_TRANSFERS,)),
            dma((count // 2,)),
            dma((count // 2,)),
            dma((count // 2,)),
            dma((count // 2,)),
            dma((count // 2,)),
            dma((count // 2,)),
            dma((count // 2,)),
            dma((count // 2,)),
            dma((17,)),
        ],
        compiler_params=pltpu.CompilerParams(
            collective_id=2, has_side_effects=True, vmem_limit_bytes=48 << 20
        ),
        cost_estimate=pl.CostEstimate(
            flops=60_000_000_000, bytes_accessed=60_000_000, transcendentals=1_000_000
        ),
        name="first",
    )(
        tokens, w_query, rest, w_gate, w_up, w_down, w_out, cotangent, cosine, sine,
        query_gain, key_gain,
    )


THREE, ONE, FOUR_ON, TWO_ON = 0, 2, 4, 6
UNITS_HOME, DOWN_STEP = 8, 15
PART_MATE, PART_CORNER, PART_FAR, QUERY_HOME, REST_HOME = 17, 18, 19, 20, 23
LAST_TRANSFERS = 26


def head_means(block):
    low = lanes(block.shape) < HEAD
    first = jnp.sum(jnp.where(low, block, 0.0), axis=1, keepdims=True)
    second = jnp.sum(jnp.where(low, 0.0, block), axis=1, keepdims=True)
    return jnp.where(low, first, second) * (1.0 / HEAD)


class LineSum:
    def __init__(self, part, got, hold, arrive, sems, places, remote):
        self.part, self.got, self.hold, self.arrive = part, got, hold, arrive
        self.swap_sems, self.ring_sems = sems
        self.side, self.place, self.line, self.other, self.after = places
        self.remote = remote

    def target(self, step):
        return (self.place + self.line - step) % self.line

    def swap(self, step):
        to = self.target(step)
        return self.remote(
            step - 1,
            self.part(2 * to + 1 - self.side),
            self.got.at[to],
            self.other,
            *self.swap_sems,
        )

    def pass_on(self, step):
        return self.remote(
            step - 1, self.hold.at[step - 1], self.arrive.at[step - 1], self.after, *self.ring_sems
        )

    def start(self):
        for step in range(1, self.line + 1):
            self.swap(step).start()

    def step(self, step, out=None):
        to = self.target(step)
        self.swap(step).wait_recv()
        total = self.part(2 * to + self.side)[...].astype(F32) + self.got[to].astype(F32)
        if step > 1:
            self.pass_on(step - 1).wait_recv()
            total = total + self.arrive[step - 2].astype(F32)
        if step < self.line:
            self.hold[step - 1] = total.astype(BF)
            self.pass_on(step).start()
        else:
            out[...] = total.astype(out.dtype)

    def drain(self):
        for step in range(1, self.line + 1):
            self.swap(step).wait_send()
            if step < self.line:
                self.pass_on(step).wait_send()


def last_kernel(
    line,
    dq_four_ref,
    dq_two_ref,
    low_four_ref,
    low_two_ref,
    own_four_ref,
    own_two_ref,
    three_four_ref,
    one_four_ref,
    raw_ref,
    cos_ref,
    sin_ref,
    query_gain_ref,
    key_gain_ref,
    normed_ref,
    w_in_ref,
    toks_ref,
    gain_ref,
    gain_two_ref,
    units_ref,
    down_ref,
    down_parts_ref,
    slab_ref,
    grad_ref,
    dx_out,
    query_out,
    key_out,
    value_out,
    norm_out,
    gate_out,
    up_out,
    down_out,
    w_out_out,
    gains_out,
    low,
    three,
    one,
    four_in,
    two_in,
    raw,
    normed,
    turned,
    w_in,
    toks,
    scales,
    grads,
    query_part,
    rest_part,
    query_got,
    rest_got,
    query_hold,
    rest_hold,
    query_arrive,
    rest_arrive,
    query_sum,
    rest_sum,
    slab,
    slab_got,
    slab_hold,
    slab_arrive,
    units_in,
    query_in,
    rest_in,
    down_own,
    down_in,
    parts,
    part_got,
    part_far,
    gain_rows,
    head_gains,
    gains_in,
    sends,
    recvs,
    line_sems,
    gain_sends,
    gain_recvs,
    locals_,
):
    me, at = lax.axis_index("head"), lax.axis_index("blk")
    count = lax.axis_size("blk")
    side, place = at % 2, at // 2
    odd = me % 2
    mate, beside, corner = me + 1 - 2 * odd, (me + 2) % 4, (me + 3 - 2 * odd) % 4
    other = at + 1 - 2 * side
    after, before = (at + 2) % count, (at + count - 2) % count
    rows, width = dx_out.shape
    block = 4 * rows
    w_rows = w_in_ref.shape[2]

    rounds = [(mate, at), (beside, at), (me, other)]
    bit = 1
    while bit < line:
        rounds.append((me, at + 2 * bit * (1 - 2 * ((place // bit) % 2))))
        bit *= 2
    barrier = pltpu.get_barrier_semaphore()
    peers = [(corner, at), (me, after), (me, before)]
    peers += [(head, other) for head in (mate, beside, corner)] + rounds
    for peer in peers:
        pl.semaphore_signal(barrier, inc=1, device_id=peer, device_id_type=MESH)

    pl.semaphore_wait(barrier, len(peers))

    def remote(index, source, target, device, send=sends, recv=recvs):
        return pltpu.make_async_remote_copy(
            src_ref=source,
            dst_ref=target,
            send_sem=send.at[index],
            recv_sem=recv.at[index],
            device_id=device,
            device_id_type=MESH,
        )

    def local(index, source, target):
        return pltpu.make_async_copy(source, target, locals_.at[index])

    low_refs, own_refs = (low_four_ref, low_two_ref), (own_four_ref, own_two_ref)
    three_on = [remote(THREE, low_refs[1].at[1], three.at[1], (me, other))]
    one_on = [remote(ONE, low_refs[1].at[3], one.at[1], (me, other))]
    for copy in three_on + one_on:
        copy.start()
    pair_loads = [local(11, three_four_ref, three.at[0]), local(12, one_four_ref, one.at[0])]
    for copy in pair_loads:
        copy.start()
    loads = [
        local(0, normed_ref, normed),
        local(1, raw_ref, raw),
        local(2, w_in_ref, w_in),
        local(3, toks_ref, toks),
        local(4, slab_ref, slab),
        local(5, down_parts_ref.at[(place + 1) % line], down_own.at[0]),
        local(15, down_parts_ref.at[place], down_own.at[1]),
        local(16, grad_ref, dx_out),
    ]
    for copy in loads:
        copy.start()
    low_loads = [
        local(6 + 2 * g + i, low_refs[g].at[2 * i], low.at[g, i]) for g in (0, 1) for i in (0, 1)
    ]
    for copy in low_loads:
        copy.start()
    down_on = remote(DOWN_STEP, down_ref, down_in.at[0], (me, after))
    down_on.start()
    down_last = remote(DOWN_STEP + 1, down_own.at[0], down_in.at[1], (me, after))
    targets = [(side, mate), (side, beside), (side, corner)]
    targets += [(1 - side, head) for head in (me, mate, beside, corner)]
    homes = []
    for i, (to_side, to_head) in enumerate(targets):
        device = (to_head, at if i < 3 else other)
        source = units_ref.at[to_head, pl.ds(pl.multiple_of(to_side * w_rows, 16), w_rows)]
        homes.append(remote(UNITS_HOME + i, source, units_in.at[side * 4 + me], device))
    units_own = local(
        10,
        units_ref.at[me, pl.ds(pl.multiple_of(side * w_rows, 16), w_rows)],
        units_in.at[side * 4 + me],
    )

    places = (side, place, line, (me, other), (me, after))

    def line_sum(which, part, got, hold, arrive):
        sems = [(line_sems.at[which, i, 0], line_sems.at[which, i, 1]) for i in (0, 1)]
        return LineSum(part, got, hold, arrive, sems, places, remote)

    query_line = line_sum(
        0, lambda b: query_part.at[:, b], query_got, query_hold, query_arrive
    )
    rest_line = line_sum(1, lambda b: rest_part.at[:, b], rest_got, rest_hold, rest_arrive)
    slab_line = line_sum(2, lambda b: slab.at[b], slab_got, slab_hold, slab_arrive)

    head_gains[...] = jnp.zeros_like(head_gains)
    gain_rows[...] = jnp.zeros_like(gain_rows)
    loads[0].wait()
    loads[1].wait()

    def head_back(out, cols, tile, gain_tile, gain_row):
        value = raw[tile, cols]
        scale = head_scale(value)
        grad = out * cos_ref[tile, :] + swap_halves(out * sin_ref[tile, :])
        head_gains[0, gain_row : gain_row + 1, :] += jnp.sum(
            grad * value * scale, axis=0, keepdims=True
        )
        inner = grad * gain_tile
        mean = head_means(inner * value)
        return (scale * inner - value * (scale * scale * scale * mean)).astype(BF)

    def query_rows(step, carry):
        tile = pl.ds(pl.multiple_of(step * 64, 64), 64)
        for i in range(3):
            t = odd + i if i < 2 else 2 * (1 - odd)
            cols = pl.ds(pl.multiple_of(t * 128, 128), 128)
            if i < 2:
                out = dq_four_ref[tile, i * 128 : (i + 1) * 128]
            else:
                out = dq_two_ref[tile, :]
            grads[tile, cols] = head_back(out, cols, tile, query_gain_ref[...], 0)
        return carry

    lax.fori_loop(0, block // 64, query_rows, 0)
    per_tile = 256 // w_rows
    tiles_per_head = count // per_tile

    def query_weights(step, carry):
        span = pl.ds(pl.multiple_of(step * 256, 256), 256)
        turned[span, :] = transposed(normed[:, span])
        first = pl.ds(step % tiles_per_head * per_tile, per_tile)
        part = nn(turned[span, :], grads[:, 0:COLS_Q])
        query_part[step // tiles_per_head, first] = part.astype(BF).reshape(
            per_tile, w_rows, COLS_Q
        )
        return carry

    lax.fori_loop(0, width // 256, query_weights, 0)
    query_line.start()
    for copy in low_loads:
        copy.wait()

    for copy in three_on + one_on:
        copy.wait_recv()
    for copy in pair_loads:
        copy.wait()

    def add_pair(step, carry):
        tile = pl.ds(pl.multiple_of(step * 128, 128), 128)
        for g in (0, 1):
            got_three, got_one = three[g, tile, :].astype(F32), one[g, tile, :].astype(F32)
            to_four = jnp.where(side == 0, 0.0, got_three)
            to_two = jnp.where(side == 0, got_three, got_one)
            low[g, 0, tile, :] = (low[g, 0, tile, :].astype(F32) + to_four).astype(BF)
            low[g, 1, tile, :] = (low[g, 1, tile, :].astype(F32) + to_two).astype(BF)
        return carry

    lax.fori_loop(0, block // 128, add_pair, 0)
    four_on = [remote(FOUR_ON + g, low.at[g, 0], four_in.at[g], (me, before)) for g in (0, 1)]
    two_on = [remote(TWO_ON + g, low.at[g, 1], two_in.at[g], (me, before)) for g in (0, 1)]
    for copy in four_on:
        copy.start()
    loads[4].wait()
    slab_line.start()

    loads[3].wait()

    def token_scales(step, carry):
        tile = pl.ds(pl.multiple_of(step % (rows // 32) * 32, 32), 32)
        value = toks[step // (rows // 32), tile, :].astype(F32)
        scales[pl.ds(pl.multiple_of(step * 32, 32), 32), :] = lax.rsqrt(
            jnp.mean(value * value, axis=1, keepdims=True) + EPS
        )
        return carry

    lax.fori_loop(0, block // 32, token_scales, 0)
    for copy in four_on:
        copy.wait_recv()

    def add_four(step, carry):
        tile = pl.ds(pl.multiple_of(step * 128, 128), 128)
        for g in (0, 1):
            low[g, 1, tile, :] = (
                low[g, 1, tile, :].astype(F32) + four_in[g, tile, :].astype(F32)
            ).astype(BF)
        return carry

    lax.fori_loop(0, block // 128, add_four, 0)
    for copy in two_on:
        copy.start()
    loads[5].wait()
    down_on.wait_recv()

    def add_down(step, carry):
        span = pl.ds(pl.multiple_of(step * 256, 256), 256)
        down_own[0, :, span] = (
            down_own[0, :, span].astype(F32) + down_in[0, :, span].astype(F32)
        ).astype(BF)
        return carry

    lax.fori_loop(0, width // 256, add_down, 0)
    down_last.start()
    for copy in homes:
        copy.start()
    units_own.start()
    query_line.step(1)
    slab_line.step(1)
    query_line.step(2)
    for copy in two_on:
        copy.wait_recv()

    def key_rows(step, carry):
        tile = pl.ds(pl.multiple_of(step * 64, 64), 64)
        first_half = lanes((64, 128)) < HEAD
        both = []
        for g in (0, 1):
            from_pair = jnp.where(side == 0, one[g, tile, :].astype(F32), 0.0)
            both.append(own_refs[g][tile, :] + from_pair + two_in[g, tile, :].astype(F32))
        zero = jnp.where(odd == 0, both[0], both[1])
        unit = jnp.where(odd == 0, both[1], both[0])
        keys = jnp.where(first_half, zero, pltpu.roll(unit, HEAD, 1))
        values = jnp.where(first_half, pltpu.roll(zero, HEAD, 1), unit)
        cols = pl.ds(COLS_Q, 128)
        grads[tile, cols] = head_back(keys, cols, tile, key_gain_ref[...], 1)
        grads[tile, COLS_Q + 128 : COLS_Q + 256] = values.astype(BF)
        return carry

    lax.fori_loop(0, block // 64, key_rows, 0)

    loads[2].wait()

    def token_cols(step, carry):
        span = pl.ds(pl.multiple_of(step * 256, 256), 256)
        first = pl.ds(step % tiles_per_head * per_tile, per_tile)
        weight = w_in[step // tiles_per_head, first, :, 0:COLS_IN].reshape(256, COLS_IN)
        part = nt(grads[...], weight)
        parts[:, :, span] = part.astype(BF).reshape(4, rows, 256)
        value = toks[:, :, span].reshape(block, 256).astype(F32)
        gain_rows[0:1, span] = jnp.sum(part * value * scales[...], axis=0, keepdims=True)
        return carry

    lax.fori_loop(0, width // 256, token_cols, 0)
    to_mate = [
        remote(PART_CORNER, parts.at[corner], part_got.at[1], (mate, at)),
        remote(PART_MATE, parts.at[mate], part_got.at[0], (mate, at)),
    ]
    for copy in to_mate:
        copy.start()
    gain_rows[1:2, :] = gain_two_ref[...]

    def rest_weights(step, carry):
        span = pl.ds(pl.multiple_of(step * 256, 256), 256)
        first = pl.ds(step % tiles_per_head * per_tile, per_tile)
        head = step // tiles_per_head
        part = nn(turned[span, :], grads[:, COLS_Q : COLS_Q + 256])
        rest_part[head, first, :, 0:256] = part.astype(BF).reshape(per_tile, w_rows, 256)
        gain_cols = transposed(gain_rows[:, span])
        rest_part[head, first, :, 256:384] = gain_cols.astype(BF).reshape(per_tile, w_rows, 128)
        return carry

    lax.fori_loop(0, width // 256, rest_weights, 0)
    rest_line.start()

    for step in range(3, line + 1):
        query_line.step(step, query_sum)
    query_home = [
        remote(QUERY_HOME + i, query_sum.at[to], query_in.at[me], (to, at))
        for i, to in enumerate((mate, beside, corner))
    ]
    query_own = local(13, query_sum.at[me], query_in.at[me])
    for copy in query_home:
        copy.start()
    query_own.start()
    to_mate[0].wait_recv()

    def add_part(step, carry):
        tile = pl.ds(pl.multiple_of(step * 32, 32), 32)
        parts[beside, tile, :] = (
            parts[beside, tile, :].astype(F32) + part_got[1, tile, :].astype(F32)
        ).astype(BF)
        return carry

    lax.fori_loop(0, rows // 32, add_part, 0)
    part_on = remote(PART_FAR, parts.at[beside], part_far, (beside, at))
    part_on.start()

    def gain_round(i):
        return remote(i, head_gains.at[i], gains_in.at[i], rounds[i], gain_sends, gain_recvs)

    rest_line.step(1)
    for i in range(len(rounds)):
        gain_round(i).start()
        gain_round(i).wait_recv()
        head_gains[i + 1] = head_gains[i] + gains_in[i]
        if i + 2 <= line:
            slab_line.step(i + 2, w_out_out)
            rest_line.step(i + 2, rest_sum)
    for step in range(len(rounds) + 2, line + 1):
        slab_line.step(step, w_out_out)
        rest_line.step(step, rest_sum)
    gains_out[...] = head_gains[len(rounds)]
    rest_home = [
        remote(REST_HOME + i, rest_sum.at[to], rest_in.at[me], (to, at))
        for i, to in enumerate((mate, beside, corner))
    ]
    rest_own = local(14, rest_sum.at[me], rest_in.at[me])
    for copy in rest_home:
        copy.start()
    rest_own.start()

    to_mate[1].wait_recv()
    part_on.wait_recv()
    loads[7].wait()

    def norm_back(step, carry):
        tile = pl.ds(pl.multiple_of(step * 32, 32), 32)
        grad = (
            parts[me, tile, :].astype(F32)
            + part_got[0, tile, :].astype(F32)
            + part_far[tile, :].astype(F32)
        )
        value = toks[me, tile, :].astype(F32)
        scale = lax.rsqrt(jnp.mean(value * value, axis=1, keepdims=True) + EPS)
        inner = grad * gain_ref[0:1, :]
        mean = jnp.mean(inner * value, axis=1, keepdims=True)
        dx_out[tile, :] += scale * inner - value * (scale * scale * scale * mean)
        return carry

    lax.fori_loop(0, rows // 32, norm_back, 0)

    loads[6].wait()
    down_last.wait_recv()

    def down_rows(step, carry):
        span = pl.ds(pl.multiple_of(step * 256, 256), 256)
        down_out[:, span] = down_own[1, :, span].astype(F32) + down_in[1, :, span].astype(F32)
        return carry

    lax.fori_loop(0, width // 256, down_rows, 0)
    for copy in homes:
        copy.wait()
    units_own.wait()
    units = units_ref.shape[2] // 2
    ff_rows = units // line
    for j, out in enumerate((gate_out, up_out)):
        for head in range(4):
            sides = [
                units_in[4 * of_side + head, :, j * units : (j + 1) * units].astype(F32)
                for of_side in range(2)
            ]
            pieces = [
                sides[p % 2][:, p // 2 * ff_rows : (p // 2 + 1) * ff_rows]
                for p in range(2 * line)
            ]
            out[:, 2 * units * head : 2 * units * (head + 1)] = jnp.concatenate(pieces, axis=1)
    for copy in query_home:
        copy.wait()
    query_own.wait()
    for g in range(4):
        query_out[:, g * COLS_Q : (g + 1) * COLS_Q] = query_in[g].astype(F32)
    for copy in rest_home:
        copy.wait()
    rest_own.wait()
    first_half = lanes((w_rows, 128)) < HEAD
    for j, out in enumerate((key_out, value_out)):
        tiles = [rest_in[g, :, j * 128 : (j + 1) * 128].astype(F32) for g in range(4)]
        moved = [pltpu.roll(tile, HEAD, 1) for tile in tiles]
        out[:, 0:128] = tiles[0] + jnp.where(first_half, 0.0, moved[1])
        out[:, 128:256] = jnp.where(first_half, moved[1], moved[2])
        out[:, 256:384] = tiles[3] + jnp.where(first_half, moved[2], 0.0)
    norm_out[...] = (
        rest_in[0, :, 256:384].astype(F32)
        + rest_in[1, :, 256:384].astype(F32)
        + rest_in[2, :, 256:384].astype(F32)
        + rest_in[3, :, 256:384].astype(F32)
    )
    for copy in three_on + one_on + four_on + two_on + to_mate:
        copy.wait_send()
    for copy in (down_on, down_last, part_on):
        copy.wait_send()
    for total in (query_line, rest_line, slab_line):
        total.drain()
    for i in range(len(rounds)):
        gain_round(i).wait_send()


def last(
    dq, dkv_low, dkv_own, pair_four, raw, cosine, sine, query_gain, key_gain, normed, w_in, toks,
    gains, gain_two, units, down, down_parts, slab, grad,
):
    _, rows, width = toks.shape
    _, count, w_rows, _ = w_in.shape
    line = count // 2
    block = 4 * rows
    anywhere = pl.BlockSpec(memory_space=pl.ANY)
    vmem = pl.BlockSpec(memory_space=pltpu.VMEM)
    shape = jax.ShapeDtypeStruct
    dma = pltpu.SemaphoreType.DMA
    rounds = 3 + int(math.log2(line))
    part = (4, w_rows, COLS_Q)
    out_rows = slab.shape[1]
    return pl.pallas_call(
        functools.partial(last_kernel, line),
        out_shape=(
            shape((rows, width), F32),
            shape((w_rows, 4 * COLS_Q), F32),
            shape((w_rows, KVHEADS * HEAD), F32),
            shape((w_rows, KVHEADS * HEAD), F32),
            shape((w_rows, 128), F32),
            shape((w_rows, 4 * units.shape[2]), F32),
            shape((w_rows, 4 * units.shape[2]), F32),
            shape(down.shape, F32),
            shape((out_rows, width), F32),
            shape((8, 128), F32),
        ),
        in_specs=[vmem] * 2 + [anywhere] * 2 + [vmem] * 2 + [anywhere] * 3 + [vmem] * 4
        + [anywhere] * 3 + [vmem] * 2 + [anywhere] * 5,
        out_specs=(vmem,) * 10,
        scratch_shapes=[
            pltpu.VMEM((2, 2, block, 128), BF),
            pltpu.VMEM((2, block, 128), BF),
            pltpu.VMEM((2, block, 128), BF),
            pltpu.VMEM((2, block, 128), BF),
            pltpu.VMEM((2, block, 128), BF),
            pltpu.VMEM((block, COLS_Q + 128), F32),
            pltpu.VMEM((block, width), BF),
            pltpu.VMEM((width, block), BF),
            pltpu.VMEM(w_in.shape, BF),
            pltpu.VMEM(toks.shape, BF),
            pltpu.VMEM((block, 1), F32),
            pltpu.VMEM((block, COLS_IN), BF),
            pltpu.VMEM((4, count, w_rows, COLS_Q), BF),
            pltpu.VMEM((4, count, w_rows, COLS_Q), BF),
            pltpu.VMEM((line,) + part, BF),
            pltpu.VMEM((line,) + part, BF),
            pltpu.VMEM((line - 1,) + part, BF),
            pltpu.VMEM((line - 1,) + part, BF),
            pltpu.VMEM((line - 1,) + part, BF),
            pltpu.VMEM((line - 1,) + part, BF),
            pltpu.VMEM(part, BF),
            pltpu.VMEM(part, BF),
            pltpu.VMEM(slab.shape, BF),
            pltpu.VMEM((line,) + slab.shape[1:], BF),
            pltpu.VMEM((line - 1,) + slab.shape[1:], BF),
            pltpu.VMEM((line - 1,) + slab.shape[1:], BF),
            pltpu.VMEM((8, w_rows, units.shape[2]), BF),
            pltpu.VMEM(part, BF),
            pltpu.VMEM(part, BF),
            pltpu.VMEM((2,) + down.shape, BF),
            pltpu.VMEM((2,) + down.shape, BF),
            pltpu.VMEM((4, rows, width), BF),
            pltpu.VMEM((2, rows, width), BF),
            pltpu.VMEM((rows, width), BF),
            pltpu.VMEM((128, width), F32),
            pltpu.VMEM((rounds + 1, 8, 128), F32),
            pltpu.VMEM((rounds, 8, 128), F32),
            dma((LAST_TRANSFERS,)),
            dma((LAST_TRANSFERS,)),
            dma((3, 2, 2, line)),
            dma((rounds,)),
            dma((rounds,)),
            dma((17,)),
        ],
        compiler_params=pltpu.CompilerParams(
            collective_id=3, has_side_effects=True, vmem_limit_bytes=58 << 20
        ),
        cost_estimate=pl.CostEstimate(
            flops=60_000_000_000, bytes_accessed=60_000_000, transcendentals=1_000_000
        ),
        name="last",
    )(
        *dq, *dkv_low, *dkv_own, *pair_four, raw, cosine, sine, query_gain, key_gain, normed, w_in,
        toks, gains, gain_two, units, down, down_parts, slab, grad,
    )


def shards(
    tokens,
    doc_lengths,
    norm1_gain,
    w_query,
    w_key,
    w_value,
    query_gain,
    key_gain,
    w_out,
    norm2_gain,
    w_gate,
    w_up,
    w_down,
    cotangent,
):
    tok_rows, width = tokens.shape
    blocks = lax.axis_size("blk")
    groups = lax.axis_size("head")
    group_id = lax.axis_index("head")
    blk_place = lax.axis_index("blk")
    block_len = groups * tok_rows
    per_group = QHEADS // groups
    head_ratio = QHEADS // KVHEADS
    w_rows = w_query.shape[0]
    line = blocks // 2
    side = blk_place % 2
    ff_rows = w_down.shape[0]
    ff_cols = line * ff_rows
    q_cols = per_group * HEAD
    firsts = [g * per_group // head_ratio for g in range(groups)]
    odd = group_id % 2

    starts = jnp.cumsum(doc_lengths) - doc_lengths
    offsets = jnp.arange(block_len, dtype=jnp.int32)
    token_pos = blk_place * block_len + offsets
    inside = starts[None, :] <= token_pos[:, None]
    token_start = jnp.max(jnp.where(inside, starts[None, :], 0), axis=1)
    in_doc = token_pos - token_start
    rope_freq = jnp.exp(-math.log(10000.0) * jnp.arange(HEAD // 2, dtype=F32) / (HEAD // 2))
    rope_angle = in_doc.astype(F32)[:, None] * rope_freq[None, :]
    cosine, sine = jnp.cos(rope_angle), jnp.sin(rope_angle)
    cosine = jnp.concatenate([cosine] * 4, axis=1)
    sine = jnp.concatenate([-sine, sine] * 2, axis=1)
    window_start = token_start - (blk_place - BACK) * block_len
    tiles = block_len // TILE
    edges = jnp.stack(
        [window_start[::TILE], window_start[TILE - 1 :: TILE]], axis=1
    ).reshape(2 * tiles)
    meta = jnp.concatenate([odd[None].astype(jnp.int32), edges.astype(jnp.int32)])

    rest = []
    for g in range(groups):
        kv = slice(firsts[g] * HEAD, (firsts[g] + 2) * HEAD)
        rest += [
            w_key[:, kv],
            w_value[:, kv],
            norm1_gain[:, None],
            norm2_gain[:, None],
            jnp.zeros((w_rows, 126), BF),
        ]
    rest = jnp.concatenate(rest, axis=1).reshape(w_rows, groups, COLS_Q)
    rest = jnp.swapaxes(rest, 0, 1)
    query_row = jnp.concatenate([query_gain, query_gain]).astype(F32)[None, :]
    key_row = jnp.concatenate([key_gain, key_gain]).astype(F32)[None, :]
    (
        wide,
        queries,
        kv_window,
        raw,
        normed_one,
        w_in,
        top_far,
        top_across,
        w_blk,
        slab,
        slab_next,
        down_next,
        toks,
        gains,
    ) = first(
        tokens,
        w_query,
        rest,
        w_gate,
        w_up,
        w_down,
        w_out,
        cotangent,
        cosine,
        sine,
        query_row,
        key_row,
    )
    slabs, downs = [slab, slab_next], [w_down, down_next]
    for _ in range(line - 4):
        slabs.append(ring(slabs[-1], 2))
        downs.append(ring(downs[-1], 2))
    w_own = w_blk.reshape(q_cols, width)
    slabs, downs, w_own, top_far, top_across, queries = sync(
        slabs, downs, w_own, top_far, top_across, queries
    )
    slabs.append(ring(slabs[-1], 2))
    downs.append(ring(downs[-1], 2))
    w_far = swap(w_own, "head", 2)
    half = tok_rows // 2
    top_high = swap(top_far[:half], "blk", 1)
    top_low = swap(top_across[half:], "head", 2)
    kept, attn_out = attend(meta, wide, kv_window, window_start[:, None])
    kept, attn_out, slabs, downs, w_far, top_high, top_low = sync(
        kept, attn_out, slabs, downs, w_far, top_high, top_low
    )
    if ff_rows % 16:
        downs.append(ring(downs[-1], 2))
        w_d = jnp.zeros((line, ff_rows, width), BF)
        for step, part in enumerate(downs):
            w_d = put(w_d, part, (blk_place // 2 - step) % line)
        downs = [w_d.reshape(ff_cols, width)]
    attn_out = attn_out.reshape(groups, tok_rows, q_cols)

    (
        resid,
        grad_resid,
        grad_attn,
        mixed,
        grad_mix,
        out_mine,
        out_got,
        w_o,
        gu_parts,
        gu_moved,
        down_parts,
        grad_gain_two,
    ) = middle(
        attn_out,
        tokens,
        w_own,
        w_far,
        gains[1:2],
        (cotangent, top_far, top_across, top_high, top_low),
        slabs,
        downs,
    )
    down_parts = down_parts.reshape(line, ff_rows, width)
    gu_parts = gu_parts.reshape(groups, line, 2 * w_rows, 2 * ff_cols)
    down_sum = LineScatter(lambda p: take(down_parts, p))
    gu_sum = LineScatter(lambda p: take(gu_parts, p, 1))
    gu_sum.total = gu_moved
    gu_sum.add()
    out_parts = matmul_tn(mixed, grad_attn).astype(BF).reshape(groups, -1, width)
    down_sum.ahead(line - 4)
    gu_sum.ahead(line - 4)
    down_moved, gu_moved = down_sum.send(), gu_sum.send()

    out_sum = (out_mine.astype(F32) + out_got.astype(F32)).astype(BF)
    out_far = swap(out_sum[1], "head", 2)
    out_across = swap(out_sum[2], "blk", 1)
    out_corner = lax.ppermute(
        out_sum[3],
        ("head", "blk"),
        [(i, (i // blocks ^ 2) * blocks + (i % blocks ^ 1)) for i in range(groups * blocks)],
    )
    near_parts = [swap(take(out_parts, group_id ^ bit), "head", 1) for bit in (1, 3)]
    back = functools.partial(
        attend_back,
        meta=meta,
        wide=wide,
        queries=queries,
        kv=kv_window,
        kept=kept,
        grads=grad_mix.reshape(block_len, q_cols),
        starts=window_start[None, :],
    )
    four = back(0)
    four, down_moved, gu_moved, out_far, out_across, out_corner, near_parts, kv_window = sync(
        four, down_moved, gu_moved, out_far, out_across, out_corner, near_parts, kv_window
    )
    down_sum.total, gu_sum.total = down_moved, gu_moved
    down_sum.add()
    gu_sum.add()
    gu_moved = gu_sum.send()
    pair_four = [swap(four[1][i], "blk", 1) for i in (1, 3)]
    far_parts = take(out_parts, group_id ^ 2).astype(F32) + near_parts[1].astype(F32)
    far_parts = swap(far_parts.astype(BF), "head", 2)
    two = back(1, kv=kv_window)
    four, two, gu_moved, pair_four, far_parts = sync(four, two, gu_moved, pair_four, far_parts)
    gu_sum.total = gu_moved
    gu_sum.add()
    out_act = (
        resid
        + out_sum[0].astype(F32)
        + out_far.astype(F32)
        + out_across.astype(F32)
        + out_corner.astype(F32)
    ).astype(BF)
    out_slab = take(out_parts, group_id).astype(F32) + near_parts[0].astype(F32)
    out_slab = (out_slab + far_parts.astype(F32)).astype(BF)
    out_slab = out_slab.reshape(blocks, w_out.shape[0], width)
    (
        d_tokens,
        d_w_query,
        d_w_key,
        d_w_value,
        norm_gains,
        d_w_gate,
        d_w_up,
        d_w_down,
        d_w_out,
        head_gains,
    ) = last(
        (four[0], two[0]),
        (four[1], two[1]),
        (four[2], two[2]),
        pair_four,
        raw,
        cosine,
        sine,
        query_row,
        key_row,
        normed_one,
        w_in,
        toks,
        gains,
        grad_gain_two,
        gu_sum.total.astype(BF),
        down_sum.total.astype(BF),
        down_parts,
        out_slab,
        grad_resid,
    )
    gain_sums = head_gains[:2, :HEAD] + head_gains[:2, HEAD:]
    d_norm1_gain, d_norm2_gain = norm_gains[:, 0], norm_gains[:, 1]
    return (
        out_act,
        d_tokens,
        d_norm1_gain,
        d_w_query,
        d_w_key,
        d_w_value,
        gain_sums[0],
        gain_sums[1],
        d_w_out,
        d_norm2_gain,
        d_w_gate,
        d_w_up,
        d_w_down,
    )


def solution(mesh):
    by_token = P(("blk", "head"), None)
    by_row = P(("head", "blk"), None)
    by_entry = P(("head", "blk"))
    in_specs = (
        by_token,
        P(),
        by_entry,
        by_row,
        by_row,
        by_row,
        P(),
        P(),
        by_row,
        by_entry,
        by_row,
        by_row,
        by_row,
        by_token,
    )
    out_specs = (
        by_token,
        by_token,
        by_entry,
        by_row,
        by_row,
        by_row,
        P(),
        P(),
        by_row,
        by_entry,
        by_row,
        by_row,
        by_row,
    )
    return jax.shard_map(shards, mesh=mesh, in_specs=in_specs, out_specs=out_specs, check_vma=False)
```

```python
import functools
import math

import jax
import jax.numpy as jnp
from jax import lax
from jax.experimental import pallas as pl
from jax.experimental.pallas import tpu as pltpu
from jax.sharding import PartitionSpec as P

QHEADS = 24
KVHEADS = 6
HEAD = 64
MAXDOC = 4096

EPS = 1e-06
SCALE = 0.125
LOG2E = 1.4426950408889634
NEG = -1e30
TILE = 256
BACK = 4
BF = jnp.bfloat16
F32 = jnp.float32


def matmul(left_side, right_side):
    return jnp.dot(left_side, right_side, preferred_element_type=F32)


def matmul_tn(left_side, right_side):
    return lax.dot_general(
        left_side, right_side, (((0,), (0,)), ((), ())), preferred_element_type=F32
    )


def matmul_nt(left_side, right_side):
    return lax.dot_general(
        left_side, right_side, (((1,), (1,)), ((), ())), preferred_element_type=F32
    )


def swap(block, axis, bit):
    count = lax.axis_size(axis)
    return lax.ppermute(block, axis, [(i, i ^ bit) for i in range(count)])


def ring(block, step):
    count = lax.axis_size("blk")
    return lax.ppermute(block, "blk", [(i, (i + step) % count) for i in range(count)])


def put(full, part, index, axis=0):
    return lax.dynamic_update_index_in_dim(full, part, index, axis)


def take(full, index, axis=0):
    return lax.dynamic_index_in_dim(full, index, axis, keepdims=False)


def place_of():
    at = lax.axis_index("blk")
    return at // 2, at % 2, lax.axis_size("blk") // 2


class LineScatter:
    def __init__(self, chunk):
        self.place, _, self.line = place_of()
        self.chunk = chunk
        self.step = 1
        self.total = chunk((self.place - 1) % self.line)

    def send(self):
        self.total = ring(self.total.astype(BF), 2)
        return self.total

    def add(self):
        self.step += 1
        mine = self.chunk((self.place - self.step) % self.line)
        self.total = self.total.astype(F32) + mine.astype(F32)

    def ahead(self, steps):
        for _ in range(steps):
            self.send()
            self.add()


def gather_blk(part, axis=0):
    place, side, line = place_of()
    shape = part.shape[:axis] + (line, 2) + part.shape[axis:]
    full = jnp.zeros(shape, part.dtype)
    held = part

    def store(full, block, source, side):
        block = block.reshape(block.shape[:axis] + (1, 1) + block.shape[axis:])
        at = [0] * full.ndim
        at[axis], at[axis + 1] = source, side
        return lax.dynamic_update_slice(full, block, at)

    for step in range(line):
        if step:
            held = ring(held, 2)
        other = swap(held, "blk", 1)
        source = (place - step) % line
        full = store(full, held, source, side)
        full = store(full, other, source, 1 - side)
    return full


def sync(*trees):
    return lax.optimization_barrier(trees)


def nt(left_side, right_side):
    return lax.dot_general(
        left_side, right_side, (((1,), (1,)), ((), ())), preferred_element_type=F32
    )


def nn(left_side, right_side):
    return lax.dot_general(
        left_side, right_side, (((1,), (0,)), ((), ())), preferred_element_type=F32
    )


def lanes(shape):
    return lax.broadcasted_iota(jnp.int32, shape, len(shape) - 1)


def transposed(block):
    return jnp.swapaxes(block, 0, 1)


def head_groups(meta_ref):
    odd = meta_ref[0]
    return ((4, 2 * odd, odd), (2, 4 * (1 - odd), 1 - odd))


def split_window(kv_ref, keys, values, step, slot):
    per_block = kv_ref.shape[2] // TILE
    block, part = step // per_block, step % per_block
    source = pl.ds(pl.multiple_of(part * TILE, TILE), TILE)
    target = pl.ds(pl.multiple_of(step * TILE, TILE), TILE)
    low = lanes((TILE, 128)) < HEAD
    both = kv_ref[block, slot, source, :].astype(F32)
    moved = pltpu.roll(both, HEAD, 1)
    keys[target, 0:128] = jnp.where(low, both, moved).astype(BF)
    values[target, :] = jnp.where(low, moved, 1.0).astype(BF)
    return target


def attend_kernel(
    meta_ref, query_ref, kv_ref, start_ref, out_ref, low_ref, acc_ref, keys, values
):
    heads, rows, _ = query_ref.shape
    base = keys.shape[1] - rows
    lane = lanes((TILE, 128))

    def fill(step, carry):
        for slot in range(2):
            split_window(kv_ref, keys.at[slot], values.at[slot], step, slot)
        return carry

    lax.fori_loop(0, keys.shape[1] // TILE, fill, 0)
    for count, first, slot in head_groups(meta_ref):
        for tile in range(rows // TILE):
            q_at = tile * TILE
            low, high = meta_ref[1 + 2 * tile], meta_ref[2 + 2 * tile]
            queries = query_ref[pl.ds(first, count), q_at : q_at + TILE, :].reshape(
                count * TILE, 2 * HEAD
            )
            acc = acc_ref.at[pl.ds(0, count * TILE)]
            acc[...] = jnp.zeros((count * TILE, 2 * HEAD), F32)
            start_col = start_ref[q_at : q_at + TILE, :]
            q_pos = base + q_at + lax.broadcasted_iota(jnp.int32, (TILE, 1), 0)

            def step(at, carry, masked, size=TILE):
                k_at = pl.multiple_of(at * TILE, TILE)
                scores = nt(queries, keys[slot, pl.ds(k_at, size), :])
                if masked:
                    k_pos = k_at + lax.broadcasted_iota(jnp.int32, (1, TILE), 1)
                    allowed = (start_col <= k_pos) & (k_pos <= q_pos)
                    scores = jnp.where(
                        allowed[None], scores.reshape(count, TILE, TILE), NEG
                    ).reshape(count * TILE, TILE)
                weights = jnp.exp2(scores).astype(BF)
                acc[...] += nn(weights, values[slot, pl.ds(k_at, size), :])
                return carry

            begin = low // TILE
            last = (base + q_at) // TILE
            clear = jnp.minimum((high + TILE - 1) // TILE, last)
            lax.fori_loop(begin, clear, functools.partial(step, masked=True), 0)
            pairs = (last - clear) // 4

            def wide_step(i, carry):
                return step(clear + 4 * i, carry, False, 4 * TILE)

            lax.fori_loop(0, pairs, wide_step, 0)
            lax.fori_loop(
                clear + 4 * pairs, last, functools.partial(step, masked=False), 0
            )
            step(last, 0, True)
            for j in range(count):
                part = acc_ref[j * TILE : (j + 1) * TILE, :]
                total = part[:, HEAD : HEAD + 1]
                out_ref[first + j, q_at : q_at + TILE, :] = jnp.where(
                    lane < HEAD, part / total, jnp.log2(total)
                )

    def lay(step, carry):
        tile = pl.ds(pl.multiple_of(step * TILE, TILE), TILE)
        for t in range(heads // 2):
            pair = jnp.where(
                lane < HEAD, out_ref[2 * t, tile, :], pltpu.roll(out_ref[2 * t + 1, tile, :], HEAD, 1)
            )
            low_ref[tile, t * 128 : (t + 1) * 128] = pair.astype(BF)
        return carry

    lax.fori_loop(0, rows // TILE, lay, 0)


def attend(meta, queries, kv, starts):
    heads, rows, _ = queries.shape
    window = kv.shape[0] * rows
    vmem = pl.BlockSpec(memory_space=pltpu.VMEM)
    return pl.pallas_call(
        attend_kernel,
        out_shape=(
            jax.ShapeDtypeStruct((heads, rows, 2 * HEAD), F32),
            jax.ShapeDtypeStruct((rows, heads * HEAD), BF),
        ),
        in_specs=[pl.BlockSpec(memory_space=pltpu.SMEM)] + [vmem] * 3,
        out_specs=(vmem, vmem),
        scratch_shapes=[
            pltpu.VMEM((4 * TILE, 2 * HEAD), F32),
            pltpu.VMEM((2, window, 2 * HEAD), BF),
            pltpu.VMEM((2, window, 2 * HEAD), BF),
        ],
        compiler_params=pltpu.CompilerParams(vmem_limit_bytes=48 << 20),
        cost_estimate=pl.CostEstimate(
            flops=60_000_000_000, bytes_accessed=20_000_000, transcendentals=20_000_000
        ),
        name="attend",
    )(meta, queries, kv, starts)


def attend_back_kernel(
    which,
    meta_ref,
    wide_ref,
    query_ref,
    kv_ref,
    out_ref,
    grad_ref,
    start_ref,
    dq_ref,
    low_ref,
    own_ref,
    keys,
    values,
    keys_t,
    query_t,
    grad_t,
    grads,
    dq,
    dkv,
):
    rows = query_ref.shape[1]
    window = keys.shape[0]
    base = window - rows
    lane = lanes((TILE, 128))
    low_lane = lane < HEAD
    count, first, slot = head_groups(meta_ref)[which]

    def fill(step, carry):
        target = split_window(kv_ref, keys, values, step, slot)
        keys[target, 128:256] = jnp.ones((TILE, 128), BF)
        keys_t[:, target] = transposed(keys[target, 0:128])[0:HEAD, :]
        dkv[target, :] = jnp.zeros((TILE, 128), F32)
        return carry

    lax.fori_loop(0, window // TILE, fill, 0)

    def low_terms(value, first):
        out = jnp.zeros_like(value)
        for i in range(3):
            term = value.astype(BF).astype(F32)
            out = jnp.where(lane == first + i, term, out)
            value = value - term
        return out

    def turn(step, carry):
        tile = pl.ds(pl.multiple_of(step * TILE, TILE), TILE)
        for j in range(count):
            query_t[j, 0:128, tile] = transposed(wide_ref[first + j, tile, :])
            kept = out_ref[first + j, tile, :]
            query_t[j, 128:256, tile] = transposed(low_terms(-kept, HEAD).astype(BF))
            pair = pl.ds(pl.multiple_of((first // 2 + j // 2) * 128, 128), 128)
            grad = grad_ref[tile, pair].astype(F32)
            moved = pltpu.roll(grad, HEAD, 1)
            if j % 2:
                grad, moved = moved, grad
            dots = jnp.sum(jnp.where(low_lane, grad * kept, 0.0), axis=1, keepdims=True)
            dots = jnp.broadcast_to(-dots, (TILE, 128))
            block = jnp.where(low_lane, grad, low_terms(dots, HEAD))
            grad_t[j, :, tile] = transposed(block.astype(BF))
            grads[j, tile, :] = jnp.where(low_lane, 0.0, moved).astype(BF)
            dq[j, :, tile] = jnp.zeros((HEAD, TILE), F32)
        return carry

    lax.fori_loop(0, rows // TILE, turn, 0)
    for tile in range(rows // TILE):
        q_at = tile * TILE
        q_cols = slice(q_at, q_at + TILE)
        low, high = meta_ref[1 + 2 * tile], meta_ref[2 + 2 * tile]
        start_row = start_ref[:, q_cols]
        q_pos = base + q_at + lax.broadcasted_iota(jnp.int32, (1, TILE), 1)

        def step(at, carry, masked, size=TILE):
            k_at = pl.multiple_of(at * TILE, TILE)
            k_rows = pl.ds(k_at, size)
            key_block = keys[k_rows, :]
            value_block = values[k_rows, :]
            key_t = keys_t[:, k_rows]
            if masked:
                k_pos = k_at + lax.broadcasted_iota(jnp.int32, (TILE, 1), 0)
                allowed = (start_row <= k_pos) & (k_pos <= q_pos)
            total = dkv[k_rows, :]
            for j in range(count):
                scores = nn(key_block, query_t[j, :, q_cols])
                if masked:
                    scores = jnp.where(allowed, scores, NEG)
                probs = jnp.exp2(scores)
                diff = nn(value_block, grad_t[j, :, q_cols])
                grad_score = (probs * diff).astype(BF)
                total = (
                    total
                    + nn(probs.astype(BF), grads[j, q_cols, :])
                    + nn(grad_score, query_ref[first + j, q_cols, :])
                )
                dq[j, :, q_cols] += nn(key_t, grad_score)
            dkv[k_rows, :] = total
            return carry

        begin = low // TILE
        last = (base + q_at) // TILE
        clear = jnp.minimum((high + TILE - 1) // TILE, last)
        lax.fori_loop(begin, clear, functools.partial(step, masked=True), 0)
        pairs = (last - clear) // 4

        def wide_step(i, carry):
            return step(clear + 4 * i, carry, False, 4 * TILE)

        lax.fori_loop(0, pairs, wide_step, 0)
        lax.fori_loop(
            clear + 4 * pairs, last, functools.partial(step, masked=False), 0
        )
        step(last, 0, True)

    def finish(step, carry):
        tile = pl.ds(pl.multiple_of(step * TILE, TILE), TILE)
        for t in range(count // 2):
            pair = jnp.concatenate([dq[2 * t, :, tile], dq[2 * t + 1, :, tile]], axis=0)
            dq_ref[tile, t * 128 : (t + 1) * 128] = transposed(pair) * SCALE
        for block in range(BACK + 1):
            source = pl.ds(pl.multiple_of(block * rows + step * TILE, TILE), TILE)
            part = dkv[source, :]
            part = jnp.where(low_lane, part * SCALE, part)
            if block < BACK:
                low_ref[(0, 2, 1, 3)[block], tile, :] = part.astype(BF)
            else:
                own_ref[tile, :] = part
        return carry

    lax.fori_loop(0, rows // TILE, finish, 0)


def attend_back(which, meta, wide, queries, kv, kept, grads, starts):
    _, rows, _ = queries.shape
    window = kv.shape[0] * rows
    count = (4, 2)[which]
    vmem = pl.BlockSpec(memory_space=pltpu.VMEM)
    shape = jax.ShapeDtypeStruct
    return pl.pallas_call(
        functools.partial(attend_back_kernel, which),
        out_shape=(
            shape((rows, count * HEAD), F32),
            shape((BACK, rows, 128), BF),
            shape((rows, 128), F32),
        ),
        in_specs=[pl.BlockSpec(memory_space=pltpu.SMEM)] + [vmem] * 6,
        out_specs=(vmem,) * 3,
        scratch_shapes=[
            pltpu.VMEM((window, 256), BF),
            pltpu.VMEM((window, 128), BF),
            pltpu.VMEM((HEAD, window), BF),
            pltpu.VMEM((count, 256, rows), BF),
            pltpu.VMEM((count, 128, rows), BF),
            pltpu.VMEM((count, rows, 128), BF),
            pltpu.VMEM((count, HEAD, rows), F32),
            pltpu.VMEM((window, 128), F32),
        ],
        compiler_params=pltpu.CompilerParams(vmem_limit_bytes=48 << 20),
        cost_estimate=pl.CostEstimate(
            flops=count * 20_000_000_000, bytes_accessed=40_000_000, transcendentals=20_000_000
        ),
        name=("attend_back_four", "attend_back_two")[which],
    )(meta, wide, queries, kv, kept, grads, starts)


MESH = pl.DeviceIdType.MESH
HEADS_OUT, SLAB, NEAR, FAR, ACROSS, FAR_ON, ACROSS_ON = 0, 3, 7, 8, 9, 10, 11
CORNER_TOP, CORNER_LOW, CORNER_ON, TO_MATE = 12, 13, 14, 15
BACK_TOP, BACK_LOW, BACK_FAR, BACK_ACROSS, HEADS_BACK, SUM_ON = 19, 20, 21, 22, 23, 26
WEIGHT_ON, TOP_ON, OUT_MATE, DOWN_LAST, WEIGHT_BACK, TRANSFERS = 30, 32, 36, 40, 41, 43
SPANS = ((0, 256), (256, 256), (512, 128))


def middle_kernel(
    slabs,
    downs,
    line,
    attn_ref,
    tokens_ref,
    w_own_ref,
    w_far_ref,
    gain_ref,
    top_ref,
    top_far_ref,
    top_across_ref,
    top_corner_ref,
    *refs,
):
    slab_refs, down_refs = refs[:slabs], refs[slabs : slabs + downs]
    (
        resid_out,
        grad_out,
        grad_low_out,
        mixed_out,
        heads_out,
        part_out,
        part_in,
        w_out_ref,
        gu_out,
        gu_next,
        down_out,
        weight_own,
        weight_in,
        sum_own,
        sum_far,
        sum_across,
        sum_corner,
        gain_out,
        mixed,
        acts,
        tops,
        w_gu,
        w_dn,
        hidden,
        grad_gu,
        pairs,
        got,
        stage,
        in_far,
        in_across,
        in_top,
        in_low,
        resid,
        turned,
        gu_stage,
        sends,
        recvs,
        locals_,
    ) = refs[slabs + downs :]
    me, at = lax.axis_index("head"), lax.axis_index("blk")
    count = lax.axis_size("blk")
    side, place = at % 2, at // 2
    odd = me % 2
    mate, beside, corner = me + 1 - 2 * odd, (me + 2) % 4, (me + 3 - 2 * odd) % 4
    other = at + 1 - 2 * side
    after, before = (at + 2) % count, (at + count - 2) % count
    rows, width = tokens_ref.shape
    half = rows // 2
    cols = mixed.shape[1] // 4
    units = w_dn.shape[0]
    slab_rows = slab_refs[0].shape[1]

    barrier = pltpu.get_barrier_semaphore()
    peers = ((mate, at), (beside, at), (corner, at), (me, other), (me, after), (me, before))
    for peer in peers:
        pl.semaphore_signal(barrier, inc=1, device_id=peer, device_id_type=MESH)
    pl.semaphore_wait(barrier, len(peers))

    def remote(index, source, target, device):
        return pltpu.make_async_remote_copy(
            src_ref=source,
            dst_ref=target,
            send_sem=sends.at[index],
            recv_sem=recvs.at[index],
            device_id=device,
            device_id_type=MESH,
        )

    def local(index, source, target):
        return pltpu.make_async_copy(source, target, locals_.at[index])

    def mixed_cols(head):
        return mixed.at[:, pl.ds(pl.multiple_of(head * cols, 128), cols)]

    heads = [
        remote(HEADS_OUT + i, attn_ref.at[to], mixed_cols(me), (to, at))
        for i, to in enumerate((mate, beside, corner))
    ]
    for copy in heads:
        copy.start()
    own_heads = local(0, attn_ref.at[me], mixed_cols(me))
    own_heads.start()

    def w_rows_of(head):
        return pairs.at[pl.ds(pl.multiple_of(head * cols, 128), cols)]

    weight_on = [
        remote(WEIGHT_ON, w_own_ref, w_rows_of(me), (mate, at)),
        remote(WEIGHT_ON + 1, w_far_ref, w_rows_of(beside), (mate, at)),
    ]
    for copy in weight_on:
        copy.start()
    load_out = [
        local(1, w_own_ref, w_rows_of(me)),
        local(2, w_far_ref, w_rows_of(beside)),
    ]
    for copy in load_out:
        copy.start()

    def slab_at(head, source):
        start = pl.multiple_of((head * line + source) * slab_rows, 16)
        return w_gu.at[pl.ds(start, slab_rows)]

    last = (place + line - (slabs - 1)) % line
    slab_on = [
        remote(SLAB + h, slab_refs[-1].at[h], slab_at(h, last), (me, after)) for h in range(4)
    ]
    for copy in slab_on:
        copy.start()
    load_slabs = [
        local(7 + 4 * i + h, ref.at[h], slab_at(h, (place + line - i) % line))
        for i, ref in enumerate(slab_refs)
        for h in range(4)
    ]
    for copy in load_slabs:
        copy.start()
    base_sem = 14 + 4 * slabs + downs
    if downs == 1:
        load_down = [local(14 + 4 * slabs, down_refs[0], w_dn)]
        down_last = []
    else:
        part_rows = units // line

        def down_at(source):
            return w_dn.at[pl.ds(pl.multiple_of(source * part_rows, 16), part_rows)]

        load_down = [
            local(14 + 4 * slabs + i, ref, down_at((place + line - i) % line))
            for i, ref in enumerate(down_refs)
        ]
        down_last = [remote(DOWN_LAST, down_refs[-1], down_at(last), (me, after))]
    for copy in down_last:
        copy.start()
    slot = side * 4 + me
    far_slot, across_slot = side * 4 + beside, (1 - side) * 4 + me
    corner_slot = (1 - side) * 4 + beside
    top_parts = (
        (top_ref, tops.at[slot]),
        (top_far_ref, tops.at[far_slot]),
        (top_across_ref, tops.at[across_slot]),
        (top_corner_ref, tops.at[corner_slot]),
    )
    load_top = [
        local(7 + 4 * slabs + i, source, target) for i, (source, target) in enumerate(top_parts)
    ]
    for copy in load_down + load_top:
        copy.start()

    for copy in heads + weight_on:
        copy.wait_recv()
    own_heads.wait()
    for copy in load_out:
        copy.wait()
    top_on = [
        remote(TOP_ON + i, source, target, (mate, at))
        for i, (source, target) in enumerate(top_parts)
    ]
    for copy in top_on:
        copy.start()
    keep_weight = local(base_sem, pairs.at[pl.ds(0, 4 * cols)], w_out_ref)
    keep_weight.start()
    keep_mixed = local(base_sem + 2, mixed, mixed_out)
    keep_mixed.start()

    def resid_cols(step, carry):
        span = pl.ds(pl.multiple_of(step * 256, 256), 256)
        weight = pairs[0 : 4 * cols, span]
        resid[:, span] = tokens_ref[:, span].astype(F32) + nn(mixed[...], weight)
        return carry

    lax.fori_loop(0, width // 256, resid_cols, 0)

    def norm_tile(step, carry):
        tile = pl.ds(pl.multiple_of(step * 32, 32), 32)
        block = resid[tile, :]
        scale = lax.rsqrt(jnp.mean(block * block, axis=1, keepdims=True) + EPS)
        acts[slot, tile, :] = (block * scale * gain_ref[...]).astype(BF)
        return carry

    lax.fori_loop(0, rows // 32, norm_tile, 0)
    keep_resid = local(base_sem + 3, resid, resid_out)
    keep_resid.start()

    near = remote(NEAR, acts.at[slot], acts.at[slot], (mate, at))
    far = remote(FAR, acts.at[slot], acts.at[slot], (beside, at))
    across = remote(ACROSS, acts.at[slot], acts.at[slot], (me, other))
    far_on = remote(FAR_ON, acts.at[far_slot], acts.at[far_slot], (mate, at))
    across_on = remote(ACROSS_ON, acts.at[across_slot], acts.at[across_slot], (mate, at))
    corner_on = remote(CORNER_ON, acts.at[corner_slot], acts.at[corner_slot], (mate, at))
    far_top = acts.at[far_slot, pl.ds(0, half)]
    across_low = acts.at[across_slot, pl.ds(half, half)]
    corner_top = remote(CORNER_TOP, far_top, far_top, (me, other))
    corner_low = remote(CORNER_LOW, across_low, across_low, (beside, at))
    near.start()
    far.start()
    across.start()
    far.wait_recv()
    far_on.start()
    corner_top.start()
    across.wait_recv()
    across_on.start()
    corner_low.start()
    for copy in load_slabs:
        copy.wait()
    for copy in slab_on + down_last:
        copy.wait_recv()
    for copy in load_down + load_top + [keep_weight]:
        copy.wait()
    for copy in top_on:
        copy.wait_recv()

    def pair_rows(index, first=0, size=rows):
        return pl.ds(pl.multiple_of(index * rows + first, 16), size)

    def to_mate(c):
        return remote(
            TO_MATE + c, pairs.at[pair_rows(2 * c + 1 - odd)], got.at[c], (mate, at)
        )

    def keep_part(c):
        return local(base_sem + 4, stage.at[odd], part_out.at[c])

    def part_on(c):
        return remote(OUT_MATE + c, stage.at[1 - odd], part_in.at[c], (mate, at))

    def chunk(c, carry):
        its_side = (side + c // 2) % 2
        its_head = (me + 2 * (c % 2)) % 4
        pair = its_side * 4 + its_head - its_head % 2

        @pl.when(c == 0)
        def _():
            near.wait_recv()

        @pl.when(c == 1)
        def _():
            far_on.wait_recv()

        @pl.when(c == 2)
        def _():
            corner_top.wait_recv()
            corner_low.wait_recv()
            corner_on.start()
            across_on.wait_recv()

        @pl.when(c == 3)
        def _():
            corner_on.wait_recv()

        for first, size in SPANS:
            block = acts[pl.ds(pair, 2)].reshape(2 * rows, width)
            gate = nn(block, w_gu[:, first : first + size])
            up = nn(block, w_gu[:, units + first : units + first + size])
            grad = nt(
                tops[pl.ds(pair, 2)].reshape(2 * rows, width), w_dn[first : first + size, :]
            )
            sig = jax.nn.sigmoid(gate)
            silu = gate * sig
            shape = (2, rows, size)
            hidden[pl.ds(pair, 2), :, first : first + size] = (
                (silu * up).astype(BF).reshape(shape)
            )
            grad_gu[pl.ds(pair, 2), :, first : first + size] = (
                (grad * up * sig * (1 + gate * (1 - sig))).astype(BF).reshape(shape)
            )
            grad_gu[pl.ds(pair, 2), :, units + first : units + first + size] = (
                (grad * silu).astype(BF).reshape(shape)
            )

        def grad_cols(step, carry):
            span = pl.ds(pl.multiple_of(step * 256, 256), 256)
            block = grad_gu[pl.ds(pair, 2)].reshape(2 * rows, 2 * units)
            part = nt(block, w_gu[span, :])
            pairs[pl.ds(pl.multiple_of(2 * c * rows, 128), 2 * rows), span] = part.astype(BF)
            return carry

        lax.fori_loop(0, width // 256, grad_cols, 0)
        to_mate(c).start()

        @pl.when(c > 0)
        def _():
            keep_part(c - 1).wait()
            part_on(c - 1).wait_send()

        def out_cols(step, carry):
            span = pl.ds(pl.multiple_of(step * 256, 256), 256)
            block = hidden[pl.ds(pair, 2)].reshape(2 * rows, units)
            part = nn(block, w_dn[:, span])
            stage[:, :, span] = part.astype(BF).reshape(2, rows, 256)
            return carry

        lax.fori_loop(0, width // 256, out_cols, 0)
        keep_part(c).start()
        part_on(c).start()
        return carry

    lax.fori_loop(0, 4, chunk, 0)

    def add_rows(c, first, extra):
        def tile(step, carry):
            span = pl.ds(pl.multiple_of(first + step * 32, 32), 32)
            mine = pair_rows(2 * c + odd, first + step * 32, 32)
            total = pairs[mine, :].astype(F32) + got[c, span, :].astype(F32)
            for ref in extra:
                total = total + ref[pl.ds(pl.multiple_of(step * 32, 32), 32), :].astype(F32)
            pairs[mine, :] = total.astype(BF)
            return carry

        lax.fori_loop(0, half // 32, tile, 0)

    back_top = remote(
        BACK_TOP, pairs.at[pair_rows(6 + odd, 0, half)], in_top, (me, other)
    )
    back_low = remote(
        BACK_LOW, pairs.at[pair_rows(6 + odd, half, half)], in_low, (beside, at)
    )
    back_far = remote(BACK_FAR, pairs.at[pair_rows(2 + odd)], in_far, (beside, at))
    back_across = remote(BACK_ACROSS, pairs.at[pair_rows(4 + odd)], in_across, (me, other))
    to_mate(3).wait_recv()
    add_rows(3, 0, ())
    back_top.start()
    add_rows(3, half, ())
    back_low.start()
    to_mate(1).wait_recv()
    to_mate(2).wait_recv()
    add_rows(1, half, ())
    add_rows(2, 0, ())

    keep_part(3).wait()
    part_on(3).wait_send()

    def gu_rows(step, carry):
        span = pl.ds(pl.multiple_of(step * 256, 256), 256)
        turned[...] = transposed(acts[:, :, span].reshape(8 * rows, 256))
        buffer = step % 2

        @pl.when(step > 1)
        def _():
            local(base_sem + 5 + buffer, gu_stage.at[buffer], gu_out.at[pl.ds(0, 256)]).wait()

        for n in range(2 * units // 256):
            part = nn(
                turned[...],
                grad_gu[:, :, n * 256 : (n + 1) * 256].reshape(8 * rows, 256),
            )
            gu_stage[buffer, :, n * 256 : (n + 1) * 256] = part.astype(BF)
        local(base_sem + 5 + buffer, gu_stage.at[buffer], gu_out.at[span]).start()
        return carry

    lax.fori_loop(0, 5, gu_rows, 0)
    back_top.wait_recv()
    add_rows(1, 0, (in_top,))
    back_far.start()
    back_low.wait_recv()
    add_rows(2, half, (in_low,))
    back_across.start()
    lax.fori_loop(5, width // 256, gu_rows, 0)
    for buffer in range(2):
        local(base_sem + 5 + buffer, gu_stage.at[buffer], gu_out.at[pl.ds(0, 256)]).wait()

    target = (place + line - 1) % line
    sum_on = [
        remote(
            SUM_ON + h,
            gu_out.at[pl.ds(pl.multiple_of((h * line + target) * slab_rows, 16), slab_rows)],
            gu_next.at[h],
            (me, after),
        )
        for h in range(4)
    ]
    for copy in sum_on:
        copy.start()

    for copy in (near, far, across, far_on, across_on, corner_on, corner_top, corner_low):
        copy.wait_send()
    load_again = [
        local(1 + i, w_out_ref.at[pl.ds(i * rows, rows)], acts.at[i]) for i in range(6)
    ]
    for copy in load_again:
        copy.start()

    for i, (first, size) in enumerate(SPANS):
        turned[0:size, :] = transposed(
            hidden[:, :, first : first + size].reshape(8 * rows, size)
        )
        buffer = i % 2
        if i > 1:
            local(base_sem + 7, stage.at[0], down_out.at[pl.ds(0, rows)]).wait()

        def down_cols(step, carry):
            span = pl.ds(pl.multiple_of(step * 256, 256), 256)
            part = nn(turned[0:size, :], tops[:, :, span].reshape(8 * rows, 256))
            stage[buffer, 0:size, span] = part.astype(BF)
            return carry

        lax.fori_loop(0, width // 256, down_cols, 0)
        local(
            base_sem + 7 + buffer,
            stage.at[buffer, pl.ds(0, size)],
            down_out.at[pl.ds(first, size)],
        ).start()

    to_mate(0).wait_recv()
    back_far.wait_recv()
    back_across.wait_recv()
    keep_resid.wait()
    gain_out[...] = jnp.zeros_like(gain_out)
    low = got.at[0]

    def norm_back(step, carry):
        tile = pl.ds(pl.multiple_of(step * 32, 32), 32)
        grad = (
            pairs[pair_rows(odd, step * 32, 32), :].astype(F32)
            + got[0, tile, :].astype(F32)
            + in_far[tile, :].astype(F32)
            + in_across[tile, :].astype(F32)
        )
        block = resid[tile, :]
        scale = lax.rsqrt(jnp.mean(block * block, axis=1, keepdims=True) + EPS)
        gain_out[...] += jnp.sum(grad * block * scale, axis=0, keepdims=True)
        inner = grad * gain_ref[...]
        mean = jnp.mean(inner * block, axis=1, keepdims=True)
        total = (
            tops[slot, tile, :].astype(F32)
            + scale * inner
            - block * (scale * scale * scale * mean)
        )
        resid[tile, :] = total
        low[tile, :] = total.astype(BF)
        return carry

    lax.fori_loop(0, rows // 32, norm_back, 0)
    keep_grad = local(base_sem + 3, resid, grad_out)
    keep_grad.start()
    keep_low = local(base_sem + 4, low, grad_low_out)
    keep_low.start()
    keep_mixed.wait()
    for copy in load_again:
        copy.wait()

    def heads_cols(step, carry):
        span = pl.ds(pl.multiple_of(step * 256, 256), 256)
        turned[:, span] = nt(low[...], acts[step]).astype(BF)
        return carry

    lax.fori_loop(0, 6, heads_cols, 0)

    def grad_cols_of(head):
        return turned.at[:, pl.ds(pl.multiple_of(head * cols, 128), cols)]

    heads_on = [
        remote(HEADS_BACK + i, grad_cols_of(to), heads_out.at[me], (to, at))
        for i, to in enumerate((mate, beside, corner))
    ]
    for copy in heads_on:
        copy.start()
    own_back = local(0, grad_cols_of(me), heads_out.at[me])
    own_back.start()

    for c in range(4):
        part_on(c).wait_recv()
    load_parts = [
        local(1, part_out, tops.at[pl.ds(0, 4)]),
        local(2, part_in, tops.at[pl.ds(4, 4)]),
    ]
    for copy in load_parts:
        copy.start()

    for c in range(4):
        to_mate(c).wait_send()
    for copy in (back_top, back_low, back_far, back_across):
        copy.wait_send()

    def weight_rows(step, carry):
        span = pl.ds(pl.multiple_of(step * 256, 256), 256)
        left = transposed(mixed[:, span])
        for n in range(width // 512):
            part = nn(left, low[:, n * 512 : (n + 1) * 512])
            pairs[span, n * 512 : (n + 1) * 512] = part.astype(BF)
        return carry

    lax.fori_loop(0, 6, weight_rows, 0)
    weight_back = [
        remote(WEIGHT_BACK, w_rows_of(mate), weight_in.at[0], (mate, at)),
        remote(WEIGHT_BACK + 1, w_rows_of(corner), weight_in.at[1], (mate, at)),
    ]
    keep_back = [
        local(3, w_rows_of(me), weight_own.at[0]),
        local(4, w_rows_of(beside), weight_own.at[1]),
    ]
    for copy in weight_back + keep_back:
        copy.start()
    for copy in load_parts:
        copy.wait()

    def add_out(step, carry):
        tile = pl.ds(pl.multiple_of(step % (rows // 32) * 32, 32), 32)
        c = step // (rows // 32)
        total = tops[c, tile, :].astype(F32) + tops[c + 4, tile, :].astype(F32)
        tops[c, tile, :] = total.astype(BF)
        return carry

    lax.fori_loop(0, 4 * rows // 32, add_out, 0)
    keep_sums = [
        local(7 + c, tops.at[c], ref)
        for c, ref in enumerate((sum_own, sum_far, sum_across, sum_corner))
    ]
    for copy in keep_sums:
        copy.start()
    for copy in weight_back + keep_back + keep_sums:
        copy.wait()

    own_back.wait()
    keep_grad.wait()
    keep_low.wait()
    local(base_sem + 7, stage.at[0, pl.ds(0, SPANS[2][1])], down_out.at[pl.ds(0, SPANS[2][1])]).wait()
    local(base_sem + 8, stage.at[1], down_out.at[pl.ds(0, rows)]).wait()
    for copy in heads_on + sum_on:
        copy.wait()
    for copy in heads + slab_on + down_last:
        copy.wait_send()
    for copy in weight_on + top_on:
        copy.wait_send()


def middle(attn_out, tokens, w_own, w_far, gain, tops, slabs, downs):
    rows, width = tokens.shape
    units = slabs[0].shape[2] // 2
    cols = attn_out.shape[2]
    line = lax.axis_size("blk") // 2
    slab_shape = slabs[0].shape
    anywhere = pl.BlockSpec(memory_space=pl.ANY)
    vmem = pl.BlockSpec(memory_space=pltpu.VMEM)
    shape = jax.ShapeDtypeStruct
    eight, four = (8, rows, width), (4, rows, width)
    return pl.pallas_call(
        functools.partial(middle_kernel, len(slabs), len(downs), line),
        out_shape=(
            shape((rows, width), F32),
            shape((rows, width), F32),
            shape((rows, width), BF),
            shape((rows, 4 * cols), BF),
            shape(attn_out.shape, BF),
            shape(four, BF),
            shape(four, BF),
            shape((4 * cols, width), BF),
            shape((width, 2 * units), BF),
            shape(slab_shape, BF),
            shape((units, width), BF),
            shape((2, cols, width), BF),
            shape((2, cols, width), BF),
            shape((rows, width), BF),
            shape((rows, width), BF),
            shape((rows, width), BF),
            shape((rows, width), BF),
            shape((1, width), F32),
        ),
        in_specs=[anywhere, vmem, anywhere, anywhere, vmem]
        + [anywhere] * (len(tops) + len(slabs) + len(downs)),
        out_specs=(anywhere,) * 17 + (vmem,),
        scratch_shapes=[
            pltpu.VMEM((rows, 4 * cols), BF),
            pltpu.VMEM(eight, BF),
            pltpu.VMEM(eight, BF),
            pltpu.VMEM((width, 2 * units), BF),
            pltpu.VMEM((units, width), BF),
            pltpu.VMEM((8, rows, units), BF),
            pltpu.VMEM((8, rows, 2 * units), BF),
            pltpu.VMEM((8 * rows, width), BF),
            pltpu.VMEM(four, BF),
            pltpu.VMEM((2, rows, width), BF),
            pltpu.VMEM((rows, width), BF),
            pltpu.VMEM((rows, width), BF),
            pltpu.VMEM((rows // 2, width), BF),
            pltpu.VMEM((rows // 2, width), BF),
            pltpu.VMEM((rows, width), F32),
            pltpu.VMEM((256, 8 * rows), BF),
            pltpu.VMEM((2, 256, 2 * units), BF),
            pltpu.SemaphoreType.DMA((TRANSFERS,)),
            pltpu.SemaphoreType.DMA((TRANSFERS,)),
            pltpu.SemaphoreType.DMA((24 + 4 * len(slabs) + len(downs),)),
        ],
        compiler_params=pltpu.CompilerParams(
            collective_id=1, has_side_effects=True, vmem_limit_bytes=60 << 20
        ),
        cost_estimate=pl.CostEstimate(
            flops=60_000_000_000, bytes_accessed=100_000_000, transcendentals=2_000_000
        ),
        name="middle",
    )(attn_out, tokens, w_own, w_far, gain, *tops, *slabs, *downs)


TOK_NEAR, TOK_FAR, TOK_ON, IN_QUERY, IN_REST = 0, 1, 2, 3, 6
TOP_FAR = 9
UNITS_MOVE, SLAB_ON, DOWN_ON = 11, 18, 19
KV_ONE, KV_TWO, KV_PAIR_ONE, KV_PAIR_TWO, FIRST_TRANSFERS = 20, 21, 22, 23, 24
COLS_Q = QHEADS // 4 * HEAD
COLS_IN = COLS_Q + 4 * HEAD


def head_scale(block):
    low = lanes(block.shape) < HEAD
    square = block * block
    first = jnp.sum(jnp.where(low, square, 0.0), axis=1, keepdims=True)
    second = jnp.sum(jnp.where(low, 0.0, square), axis=1, keepdims=True)
    return jnp.where(
        low, lax.rsqrt(first / HEAD + EPS), lax.rsqrt(second / HEAD + EPS)
    )


def swap_halves(block):
    low = lanes(block.shape) % HEAD < HEAD // 2
    return jnp.where(low, pltpu.roll(block, 96, 1), pltpu.roll(block, 32, 1))


def first_kernel(
    line,
    tokens_ref,
    query_ref,
    rest_ref,
    gate_ref,
    up_ref,
    down_ref,
    w_out_ref,
    top_ref,
    cos_ref,
    sin_ref,
    query_gain_ref,
    key_gain_ref,
    wide_out,
    query_out,
    kv_out,
    raw_out,
    normed_out,
    w_in_out,
    top_far_out,
    w_out_all,
    slab_out,
    slab_next,
    down_next,
    toks_out,
    gain_out,
    toks,
    normed,
    w_in,
    raw,
    wide,
    query,
    kv_own,
    gate,
    up,
    blocks,
    sends,
    recvs,
    ring_sends,
    ring_recvs,
    swap_sends,
    swap_recvs,
    out_ring_sends,
    out_ring_recvs,
    out_swap_sends,
    out_swap_recvs,
    locals_,
):
    me, at = lax.axis_index("head"), lax.axis_index("blk")
    count = lax.axis_size("blk")
    side, place = at % 2, at // 2
    odd = me % 2
    mate, beside, corner = me + 1 - 2 * odd, (me + 2) % 4, (me + 3 - 2 * odd) % 4
    other = at + 1 - 2 * side
    after, before = (at + 2) % count, (at + count - 2) % count
    rows, width = tokens_ref.shape
    half = rows // 2
    w_rows = query_ref.shape[0]
    units = slab_out.shape[2] // 2

    barrier = pltpu.get_barrier_semaphore()
    peers = [(mate, at), (beside, at), (corner, at), (me, after), (me, before)]
    peers += [(head, other) for head in (me, mate, beside, corner)]
    for peer in peers:
        pl.semaphore_signal(barrier, inc=1, device_id=peer, device_id_type=MESH)
    pl.semaphore_wait(barrier, len(peers))

    def remote(index, source, target, device, send=sends, recv=recvs):
        return pltpu.make_async_remote_copy(
            src_ref=source,
            dst_ref=target,
            send_sem=send.at[index],
            recv_sem=recv.at[index],
            device_id=device,
            device_id_type=MESH,
        )

    def local(index, source, target):
        return pltpu.make_async_copy(source, target, locals_.at[index])

    def cols_of(ref, start, size):
        return ref.at[:, pl.ds(pl.multiple_of(start, 128), size)]

    own_q = w_in.at[me, at, :, pl.ds(0, COLS_Q)]
    own_rest = w_in.at[me, at, :, pl.ds(COLS_Q, COLS_Q)]
    split = []
    for i, to in enumerate((mate, beside, corner)):
        split.append(
            remote(IN_QUERY + i, cols_of(query_ref, to * COLS_Q, COLS_Q), own_q, (to, at))
        )
        split.append(remote(IN_REST + i, rest_ref.at[to], own_rest, (to, at)))
    for copy in split:
        copy.start()
    own = [
        local(0, cols_of(query_ref, me * COLS_Q, COLS_Q), own_q),
        local(1, rest_ref.at[me], own_rest),
        local(2, tokens_ref, toks.at[me]),
        local(3, w_out_ref, w_out_all.at[at]),
    ]
    for copy in own:
        copy.start()
    tok_near = remote(TOK_NEAR, tokens_ref, toks.at[me], (mate, at))
    tok_far = remote(TOK_FAR, tokens_ref, toks.at[me], (beside, at))
    tok_on = remote(TOK_ON, toks.at[beside], toks.at[beside], (mate, at))
    tok_far.start()
    tok_near.start()
    down_on = remote(DOWN_ON, down_ref, down_next, (me, after))
    down_on.start()
    own_units = [local(4, gate_ref, gate), local(5, up_ref, up)]
    for copy in own_units:
        copy.start()

    def ring_copy(step):
        block = w_in.at[:, (at + count - 2 * (step - 1)) % count]
        return remote(step, block, block, (me, after), ring_sends, ring_recvs)

    def swap_copy(step):
        block = w_in.at[:, (at + count - 2 * step) % count]
        return remote(step, block, block, (me, other), swap_sends, swap_recvs)

    def out_ring(step):
        index = (at + count - 2 * (step - 1)) % count
        source = w_out_ref if step == 1 else w_out_all.at[index]
        return remote(
            step, source, w_out_all.at[index], (me, after), out_ring_sends, out_ring_recvs
        )

    def out_swap(step):
        index = (at + count - 2 * step) % count
        source = w_out_ref if step == 0 else w_out_all.at[index]
        return remote(
            step, source, w_out_all.at[index], (me, other), out_swap_sends, out_swap_recvs
        )

    out_ring(1).start()
    out_swap(0).start()

    for copy in own_units:
        copy.wait()
    ff_rows = units // line
    for j, ref in enumerate((gate, up)):
        for head in range(4):
            columns = ref[:, 2 * units * head : 2 * units * (head + 1)].astype(F32)
            for to_side in range(2):
                chosen = [
                    columns[:, (2 * z + to_side) * ff_rows : (2 * z + to_side + 1) * ff_rows]
                    for z in range(line)
                ]
                blocks[to_side, head, :, j * units : (j + 1) * units] = jnp.concatenate(
                    chosen, axis=1
                ).astype(BF)
    slab_rows = pl.ds(pl.multiple_of(side * w_rows, 16), w_rows)
    targets = [(side, mate), (side, beside), (side, corner)]
    targets += [(1 - side, head) for head in (me, mate, beside, corner)]
    spread = [
        remote(
            UNITS_MOVE + i,
            blocks.at[to_side, to_head],
            slab_out.at[me, slab_rows],
            (to_head, at if i < 3 else other),
        )
        for i, (to_side, to_head) in enumerate(targets)
    ]
    for copy in spread:
        copy.start()
    own_block = local(6, blocks.at[side, me], slab_out.at[me, slab_rows])
    own_block.start()
    for copy in split:
        copy.wait_recv()
    own[0].wait()
    own[1].wait()
    ring_copy(1).start()
    swap_copy(0).start()
    tok_far.wait_recv()
    tok_on.start()
    top_far = remote(TOP_FAR, top_ref, top_far_out, (beside, at))
    top_far.start()
    for step in range(1, line):
        ring_copy(step).wait_recv()
        if step < line - 1:
            ring_copy(step + 1).start()
        swap_copy(step).start()
        out_ring(step).wait_recv()
        if step < line - 1:
            out_ring(step + 1).start()

    for copy in spread:
        copy.wait_recv()
    own_block.wait()
    slab_on = remote(SLAB_ON, slab_out, slab_next, (me, after))
    slab_on.start()
    tok_near.wait_recv()
    tok_on.wait_recv()
    own[2].wait()
    own[3].wait()
    for step in range(line):
        swap_copy(step).wait_recv()
    for step in range(1, line):
        out_swap(step).start()
    keep_in = [
        local(7 + h, w_in.at[h], w_in_out.at[h]) for h in range(4)
    ]
    for copy in keep_in:
        copy.start()

    gains = w_in[:, :, :, COLS_IN : COLS_IN + 128].reshape(width, 128).astype(F32)
    gain_out[...] = transposed(gains)[0:8, :]

    def norm_tile(step, carry):
        head, tile = step // (rows // 32), pl.ds(pl.multiple_of(step % (rows // 32) * 32, 32), 32)
        block = toks[head, tile, :].astype(F32)
        scale = lax.rsqrt(jnp.mean(block * block, axis=1, keepdims=True) + EPS)
        normed[pl.ds(pl.multiple_of(step * 32, 32), 32), :] = (
            block * scale * gain_out[0:1, :]
        ).astype(BF)
        return carry

    lax.fori_loop(0, 4 * rows // 32, norm_tile, 0)
    keep_normed = local(11, normed, normed_out)
    keep_normed.start()
    keep_toks = local(16, toks, toks_out)
    keep_toks.start()

    def project(step, carry):
        tile = pl.ds(pl.multiple_of(step * 256, 256), 256)
        for first, size in SPANS:
            weight = w_in[:, :, :, first : first + size].reshape(width, size)
            raw[tile, first : first + size] = nn(normed[tile, :], weight)
        return carry

    lax.fori_loop(0, 4 * rows // 256, project, 0)
    keep_raw = local(12, raw.at[:, pl.ds(0, COLS_Q + 128)], raw_out)
    keep_raw.start()

    def rotated(block, gain, tile):
        block = block * head_scale(block) * gain
        return block * cos_ref[tile, :] + swap_halves(block) * sin_ref[tile, :]

    def prepare(step, carry):
        tile = pl.ds(pl.multiple_of(step * 64, 64), 64)
        first_half = lanes((64, 128)) < HEAD
        for t in range(QHEADS // 4 // 2):
            block = rotated(raw[tile, t * 128 : (t + 1) * 128], query_gain_ref[...], tile)
            block = block.astype(BF).astype(F32)
            moved = pltpu.roll(block, HEAD, 1)
            query[2 * t, tile, :] = jnp.where(first_half, block, 0.0).astype(BF)
            query[2 * t + 1, tile, :] = jnp.where(first_half, moved, 0.0).astype(BF)
            scaled = block * (SCALE * LOG2E)
            upper = scaled.astype(BF).astype(F32)
            lower = scaled - upper
            wide[2 * t, tile, :] = jnp.where(
                first_half, upper, pltpu.roll(lower, HEAD, 1)
            ).astype(BF)
            wide[2 * t + 1, tile, :] = jnp.where(
                first_half, pltpu.roll(upper, HEAD, 1), lower
            ).astype(BF)
        keys = rotated(raw[tile, COLS_Q : COLS_Q + 128], key_gain_ref[...], tile)
        values = raw[tile, COLS_Q + 128 : COLS_Q + 256]
        kv_own[0, tile, :] = jnp.where(
            first_half, keys, pltpu.roll(values, HEAD, 1)
        ).astype(BF)
        kv_own[1, tile, :] = jnp.where(
            first_half, pltpu.roll(keys, HEAD, 1), values
        ).astype(BF)
        return carry

    lax.fori_loop(0, 4 * rows // 64, prepare, 0)

    kv_one = remote(KV_ONE, kv_own, kv_out.at[2], (me, after))
    kv_two = remote(KV_TWO, kv_out.at[2], kv_out.at[0], (me, after))
    pair_one_even = remote(KV_PAIR_ONE, kv_own, kv_out.at[3], (me, other))
    pair_one_odd = remote(KV_PAIR_ONE, kv_out.at[2], kv_out.at[3], (me, other))
    pair_two_even = remote(KV_PAIR_TWO, kv_out.at[2], kv_out.at[1], (me, other))
    pair_two_odd = remote(KV_PAIR_TWO, kv_out.at[0], kv_out.at[1], (me, other))
    kv_one.start()

    @pl.when(side == 0)
    def _():
        pair_one_even.start()

    keep = [
        local(13, kv_own, kv_out.at[4]),
        local(14, wide, wide_out),
        local(15, query, query_out),
    ]
    for copy in keep:
        copy.start()
    kv_one.wait_recv()
    kv_two.start()

    @pl.when(side == 0)
    def _():
        pair_two_even.start()

    @pl.when(side == 1)
    def _():
        pair_one_odd.start()

    kv_two.wait_recv()

    @pl.when(side == 1)
    def _():
        pair_two_odd.start()

    pair_one_even.wait_recv()
    pair_two_even.wait_recv()
    down_on.wait_recv()
    slab_on.wait_recv()
    top_far.wait_recv()
    for copy in keep + keep_in + [keep_normed, keep_raw, keep_toks]:
        copy.wait()
    for copy in split + spread:
        copy.wait_send()
    for copy in (tok_near, tok_far, tok_on, top_far):
        copy.wait_send()
    for copy in (slab_on, down_on, kv_one, kv_two):
        copy.wait_send()
    pair_one_even.wait_send()
    pair_two_even.wait_send()

    for step in range(line):
        swap_copy(step).wait_send()
        out_swap(step).wait()
        if step:
            ring_copy(step).wait_send()
            out_ring(step).wait_send()


def first(
    tokens, w_query, rest, w_gate, w_up, w_down, w_out, cotangent, cosine, sine, query_gain, key_gain
):
    rows, width = tokens.shape
    count = lax.axis_size("blk")
    w_rows, ff = w_gate.shape
    units = ff // 8
    block = 4 * rows
    anywhere = pl.BlockSpec(memory_space=pl.ANY)
    vmem = pl.BlockSpec(memory_space=pltpu.VMEM)
    shape = jax.ShapeDtypeStruct
    heads = QHEADS // 4
    slab = shape((4, 2 * w_rows, 2 * units), BF)
    dma = pltpu.SemaphoreType.DMA
    return pl.pallas_call(
        functools.partial(first_kernel, count // 2),
        out_shape=(
            shape((heads, block, 128), BF),
            shape((heads, block, 128), BF),
            shape((BACK + 1, 2, block, 128), BF),
            shape((block, COLS_Q + 128), F32),
            shape((block, width), BF),
            shape((4, count, w_rows, 2 * COLS_Q), BF),
            shape((rows, width), BF),
            shape((count,) + w_out.shape, BF),
            slab,
            slab,
            shape(w_down.shape, BF),
            shape((4, rows, width), BF),
            shape((8, width), F32),
        ),
        in_specs=[anywhere] * 8 + [vmem] * 4,
        out_specs=(anywhere,) * 12 + (vmem,),
        scratch_shapes=[
            pltpu.VMEM((4, rows, width), BF),
            pltpu.VMEM((block, width), BF),
            pltpu.VMEM((4, count, w_rows, 2 * COLS_Q), BF),
            pltpu.VMEM((block, COLS_IN), F32),
            pltpu.VMEM((heads, block, 128), BF),
            pltpu.VMEM((heads, block, 128), BF),
            pltpu.VMEM((2, block, 128), BF),
            pltpu.VMEM(w_gate.shape, BF),
            pltpu.VMEM(w_up.shape, BF),
            pltpu.VMEM((2, 4, w_rows, 2 * units), BF),
            dma((FIRST_TRANSFERS,)),
            dma((FIRST_TRANSFERS,)),
            dma((count // 2,)),
            dma((count // 2,)),
            dma((count // 2,)),
            dma((count // 2,)),
            dma((count // 2,)),
            dma((count // 2,)),
            dma((count // 2,)),
            dma((count // 2,)),
            dma((17,)),
        ],
        compiler_params=pltpu.CompilerParams(
            collective_id=2, has_side_effects=True, vmem_limit_bytes=48 << 20
        ),
        cost_estimate=pl.CostEstimate(
            flops=60_000_000_000, bytes_accessed=60_000_000, transcendentals=1_000_000
        ),
        name="first",
    )(
        tokens, w_query, rest, w_gate, w_up, w_down, w_out, cotangent, cosine, sine,
        query_gain, key_gain,
    )


THREE, ONE, FOUR_ON, TWO_ON = 0, 2, 4, 6
UNITS_HOME, DOWN_STEP = 8, 15
PART_MATE, PART_CORNER, PART_FAR, QUERY_HOME, REST_HOME = 17, 18, 19, 20, 23
LAST_TRANSFERS = 26


def head_means(block):
    low = lanes(block.shape) < HEAD
    first = jnp.sum(jnp.where(low, block, 0.0), axis=1, keepdims=True)
    second = jnp.sum(jnp.where(low, 0.0, block), axis=1, keepdims=True)
    return jnp.where(low, first, second) * (1.0 / HEAD)


class LineSum:
    def __init__(self, part, got, hold, arrive, sems, places, remote):
        self.part, self.got, self.hold, self.arrive = part, got, hold, arrive
        self.swap_sems, self.ring_sems = sems
        self.side, self.place, self.line, self.other, self.after = places
        self.remote = remote

    def target(self, step):
        return (self.place + self.line - step) % self.line

    def swap(self, step):
        to = self.target(step)
        return self.remote(
            step - 1,
            self.part(2 * to + 1 - self.side),
            self.got.at[to],
            self.other,
            *self.swap_sems,
        )

    def pass_on(self, step):
        return self.remote(
            step - 1, self.hold.at[step - 1], self.arrive.at[step - 1], self.after, *self.ring_sems
        )

    def start(self):
        for step in range(1, self.line + 1):
            self.swap(step).start()

    def step(self, step, out=None):
        to = self.target(step)
        self.swap(step).wait_recv()
        total = self.part(2 * to + self.side)[...].astype(F32) + self.got[to].astype(F32)
        if step > 1:
            self.pass_on(step - 1).wait_recv()
            total = total + self.arrive[step - 2].astype(F32)
        if step < self.line:
            self.hold[step - 1] = total.astype(BF)
            self.pass_on(step).start()
        else:
            out[...] = total.astype(out.dtype)

    def drain(self):
        for step in range(1, self.line + 1):
            self.swap(step).wait_send()
            if step < self.line:
                self.pass_on(step).wait_send()


def last_kernel(
    line,
    dq_four_ref,
    dq_two_ref,
    low_four_ref,
    low_two_ref,
    own_four_ref,
    own_two_ref,
    pair_four_ref,
    raw_ref,
    cos_ref,
    sin_ref,
    query_gain_ref,
    key_gain_ref,
    normed_ref,
    w_in_ref,
    toks_ref,
    gain_ref,
    gain_two_ref,
    units_ref,
    units_parts_ref,
    down_ref,
    down_parts_ref,
    slab_ref,
    grad_ref,
    dx_out,
    query_out,
    key_out,
    value_out,
    norm_out,
    gate_out,
    up_out,
    down_out,
    w_out_out,
    gains_out,
    low,
    three,
    one,
    four_in,
    two_in,
    raw,
    normed,
    turned,
    w_in,
    toks,
    scales,
    grads,
    query_part,
    rest_part,
    query_got,
    rest_got,
    query_hold,
    rest_hold,
    query_arrive,
    rest_arrive,
    query_sum,
    rest_sum,
    slab,
    slab_got,
    slab_hold,
    slab_arrive,
    units_sum,
    units_in,
    query_in,
    rest_in,
    down_own,
    down_in,
    parts,
    part_got,
    part_far,
    gain_rows,
    head_gains,
    gains_in,
    sends,
    recvs,
    line_sems,
    gain_sends,
    gain_recvs,
    locals_,
):
    me, at = lax.axis_index("head"), lax.axis_index("blk")
    count = lax.axis_size("blk")
    side, place = at % 2, at // 2
    odd = me % 2
    mate, beside, corner = me + 1 - 2 * odd, (me + 2) % 4, (me + 3 - 2 * odd) % 4
    other = at + 1 - 2 * side
    after, before = (at + 2) % count, (at + count - 2) % count
    rows, width = dx_out.shape
    block = 4 * rows
    w_rows = w_in_ref.shape[2]

    rounds = [(mate, at), (beside, at), (me, other)]
    bit = 1
    while bit < line:
        rounds.append((me, at + 2 * bit * (1 - 2 * ((place // bit) % 2))))
        bit *= 2
    barrier = pltpu.get_barrier_semaphore()
    peers = [(corner, at), (me, after), (me, before)]
    peers += [(head, other) for head in (mate, beside, corner)] + rounds
    for peer in peers:
        pl.semaphore_signal(barrier, inc=1, device_id=peer, device_id_type=MESH)

    pl.semaphore_wait(barrier, len(peers))

    def remote(index, source, target, device, send=sends, recv=recvs):
        return pltpu.make_async_remote_copy(
            src_ref=source,
            dst_ref=target,
            send_sem=send.at[index],
            recv_sem=recv.at[index],
            device_id=device,
            device_id_type=MESH,
        )

    def local(index, source, target):
        return pltpu.make_async_copy(source, target, locals_.at[index])

    units_own_part = parts.at[:, pl.ds(0, 2 * w_rows), pl.ds(0, units_ref.shape[2])]
    low_refs, own_refs = (low_four_ref, low_two_ref), (own_four_ref, own_two_ref)
    three_on = remote(THREE, low_refs[1].at[2], three.at[1], (me, other))
    one_on = remote(ONE, low_refs[1].at[3], one.at[1], (me, other))
    three_on.start()
    one_on.start()
    low_loads = [local(6 + g, low_refs[g].at[pl.ds(0, 2)], low.at[g]) for g in (0, 1)]
    pair_loads = [
        local(11, pair_four_ref.at[0], three.at[0]),
        local(12, pair_four_ref.at[1], one.at[0]),
    ]
    for copy in low_loads + pair_loads:
        copy.start()
    loads = [
        local(0, normed_ref, normed),
        local(1, raw_ref, raw),
        local(2, w_in_ref, w_in),
        local(3, toks_ref, toks),
        local(4, slab_ref, slab),
        local(5, down_parts_ref.at[(place + 1) % line], down_own.at[0]),
        local(15, down_parts_ref.at[place], down_own.at[1]),
        local(16, grad_ref, dx_out),
        local(8, units_ref, units_sum),
        local(9, units_parts_ref.at[:, place], units_own_part),
    ]
    for copy in loads:
        copy.start()
    down_on = remote(DOWN_STEP, down_ref, down_in.at[0], (me, after))
    down_on.start()
    down_last = remote(DOWN_STEP + 1, down_own.at[0], down_in.at[1], (me, after))
    targets = [(side, mate), (side, beside), (side, corner)]
    targets += [(1 - side, head) for head in (me, mate, beside, corner)]
    homes = []
    for i, (to_side, to_head) in enumerate(targets):
        device = (to_head, at if i < 3 else other)
        source = units_sum.at[
            to_head, pl.ds(pl.multiple_of(to_side * w_rows, 16), w_rows)
        ]
        homes.append(remote(UNITS_HOME + i, source, units_in.at[side * 4 + me], device))
    units_own = local(
        10,
        units_sum.at[me, pl.ds(pl.multiple_of(side * w_rows, 16), w_rows)],
        units_in.at[side * 4 + me],
    )

    places = (side, place, line, (me, other), (me, after))

    def line_sum(which, part, got, hold, arrive):
        sems = [(line_sems.at[which, i, 0], line_sems.at[which, i, 1]) for i in (0, 1)]
        return LineSum(part, got, hold, arrive, sems, places, remote)

    query_line = line_sum(
        0, lambda b: query_part.at[:, b], query_got, query_hold, query_arrive
    )
    rest_line = line_sum(1, lambda b: rest_part.at[:, b], rest_got, rest_hold, rest_arrive)
    slab_line = line_sum(2, lambda b: slab.at[b], slab_got, slab_hold, slab_arrive)

    four_on = [remote(FOUR_ON + g, low.at[g, 0], four_in.at[g], (me, before)) for g in (0, 1)]
    two_on = [remote(TWO_ON + g, low.at[g, 1], two_in.at[g], (me, before)) for g in (0, 1)]

    def add_pair(g):
        def tile_of(step, carry):
            tile = pl.ds(pl.multiple_of(step * 128, 128), 128)
            got_three, got_one = three[g, tile, :].astype(F32), one[g, tile, :].astype(F32)
            to_four = jnp.where(side == 0, 0.0, got_three)
            to_two = jnp.where(side == 0, got_three, got_one)
            low[g, 0, tile, :] = (low[g, 0, tile, :].astype(F32) + to_four).astype(BF)
            low[g, 1, tile, :] = (low[g, 1, tile, :].astype(F32) + to_two).astype(BF)
            return carry

        lax.fori_loop(0, block // 128, tile_of, 0)
        four_on[g].start()

    def add_four(g):
        def tile_of(step, carry):
            tile = pl.ds(pl.multiple_of(step * 128, 128), 128)
            low[g, 1, tile, :] = (
                low[g, 1, tile, :].astype(F32) + four_in[g, tile, :].astype(F32)
            ).astype(BF)
            return carry

        four_on[g].wait_recv()
        lax.fori_loop(0, block // 128, tile_of, 0)
        two_on[g].start()

    for copy in low_loads + pair_loads:
        copy.wait()
    add_pair(0)

    head_gains[...] = jnp.zeros_like(head_gains)
    gain_rows[...] = jnp.zeros_like(gain_rows)
    loads[0].wait()
    loads[1].wait()

    def head_back(out, cols, tile, gain_tile, gain_row):
        value = raw[tile, cols]
        scale = head_scale(value)
        grad = out * cos_ref[tile, :] + swap_halves(out * sin_ref[tile, :])
        head_gains[0, gain_row : gain_row + 1, :] += jnp.sum(
            grad * value * scale, axis=0, keepdims=True
        )
        inner = grad * gain_tile
        mean = head_means(inner * value)
        return (scale * inner - value * (scale * scale * scale * mean)).astype(BF)

    def query_rows(step, carry):
        tile = pl.ds(pl.multiple_of(step * 64, 64), 64)
        for i in range(3):
            t = odd + i if i < 2 else 2 * (1 - odd)
            cols = pl.ds(pl.multiple_of(t * 128, 128), 128)
            if i < 2:
                out = dq_four_ref[tile, i * 128 : (i + 1) * 128]
            else:
                out = dq_two_ref[tile, :]
            grads[tile, cols] = head_back(out, cols, tile, query_gain_ref[...], 0)
        return carry

    lax.fori_loop(0, block // 64, query_rows, 0)
    three_on.wait_recv()
    one_on.wait_recv()
    add_pair(1)
    add_four(0)
    per_tile = 256 // w_rows
    tiles_per_head = count // per_tile

    def query_weights(step, carry):
        span = pl.ds(pl.multiple_of(step * 256, 256), 256)
        turned[span, :] = transposed(normed[:, span])
        first = pl.ds(step % tiles_per_head * per_tile, per_tile)
        part = nn(turned[span, :], grads[:, 0:COLS_Q])
        query_part[step // tiles_per_head, first] = part.astype(BF).reshape(
            per_tile, w_rows, COLS_Q
        )
        return carry

    lax.fori_loop(0, width // 256, query_weights, 0)
    query_line.start()
    add_four(1)
    loads[4].wait()
    slab_line.start()

    loads[3].wait()

    def token_scales(step, carry):
        tile = pl.ds(pl.multiple_of(step % (rows // 32) * 32, 32), 32)
        value = toks[step // (rows // 32), tile, :].astype(F32)
        scales[pl.ds(pl.multiple_of(step * 32, 32), 32), :] = lax.rsqrt(
            jnp.mean(value * value, axis=1, keepdims=True) + EPS
        )
        return carry

    lax.fori_loop(0, block // 32, token_scales, 0)
    loads[5].wait()
    down_on.wait_recv()

    def add_down(step, carry):
        span = pl.ds(pl.multiple_of(step * 256, 256), 256)
        down_own[0, :, span] = (
            down_own[0, :, span].astype(F32) + down_in[0, :, span].astype(F32)
        ).astype(BF)
        return carry

    lax.fori_loop(0, width // 256, add_down, 0)
    down_last.start()
    loads[8].wait()
    loads[9].wait()

    def add_units(step, carry):
        head, tile = step // (2 * w_rows // 16), step % (2 * w_rows // 16)
        tile = pl.ds(pl.multiple_of(tile * 16, 16), 16)
        total = units_sum[head, tile, :].astype(F32) + units_own_part[head, tile, :].astype(F32)
        units_sum[head, tile, :] = total.astype(BF)
        return carry

    lax.fori_loop(0, 8 * w_rows // 16, add_units, 0)
    query_line.step(1)
    for copy in two_on:
        copy.wait_recv()

    def key_rows(step, carry):
        tile = pl.ds(pl.multiple_of(step * 64, 64), 64)
        first_half = lanes((64, 128)) < HEAD
        both = []
        for g in (0, 1):
            from_pair = jnp.where(side == 0, one[g, tile, :].astype(F32), 0.0)
            both.append(own_refs[g][tile, :] + from_pair + two_in[g, tile, :].astype(F32))
        zero = jnp.where(odd == 0, both[0], both[1])
        unit = jnp.where(odd == 0, both[1], both[0])
        keys = jnp.where(first_half, zero, pltpu.roll(unit, HEAD, 1))
        values = jnp.where(first_half, pltpu.roll(zero, HEAD, 1), unit)
        cols = pl.ds(COLS_Q, 128)
        grads[tile, cols] = head_back(keys, cols, tile, key_gain_ref[...], 1)
        grads[tile, COLS_Q + 128 : COLS_Q + 256] = values.astype(BF)
        return carry

    lax.fori_loop(0, block // 64, key_rows, 0)

    loads[2].wait()

    def token_cols(step, carry):
        span = pl.ds(pl.multiple_of(step * 256, 256), 256)
        first = pl.ds(step % tiles_per_head * per_tile, per_tile)
        weight = w_in[step // tiles_per_head, first, :, 0:COLS_IN].reshape(256, COLS_IN)
        part = nt(grads[...], weight)
        parts[:, :, span] = part.astype(BF).reshape(4, rows, 256)
        value = toks[:, :, span].reshape(block, 256).astype(F32)
        gain_rows[0:1, span] = jnp.sum(part * value * scales[...], axis=0, keepdims=True)
        return carry

    lax.fori_loop(0, width // 256, token_cols, 0)
    to_mate = [
        remote(PART_CORNER, parts.at[corner], part_got.at[1], (mate, at)),
        remote(PART_MATE, parts.at[mate], part_got.at[0], (mate, at)),
    ]
    for copy in to_mate:
        copy.start()
    gain_rows[1:2, :] = gain_two_ref[...]

    def rest_weights(step, carry):
        span = pl.ds(pl.multiple_of(step * 256, 256), 256)
        first = pl.ds(step % tiles_per_head * per_tile, per_tile)
        head = step // tiles_per_head
        part = nn(turned[span, :], grads[:, COLS_Q : COLS_Q + 256])
        rest_part[head, first, :, 0:256] = part.astype(BF).reshape(per_tile, w_rows, 256)
        gain_cols = transposed(gain_rows[:, span])
        rest_part[head, first, :, 256:384] = gain_cols.astype(BF).reshape(per_tile, w_rows, 128)
        return carry

    lax.fori_loop(0, width // 256, rest_weights, 0)
    rest_line.start()
    for copy in homes:
        copy.start()
    units_own.start()
    slab_line.step(1)
    for step in range(2, line + 1):
        query_line.step(step, query_sum)
    query_home = [
        remote(QUERY_HOME + i, query_sum.at[to], query_in.at[me], (to, at))
        for i, to in enumerate((mate, beside, corner))
    ]
    query_own = local(13, query_sum.at[me], query_in.at[me])
    for copy in query_home:
        copy.start()
    query_own.start()
    to_mate[0].wait_recv()

    def add_part(step, carry):
        tile = pl.ds(pl.multiple_of(step * 32, 32), 32)
        parts[beside, tile, :] = (
            parts[beside, tile, :].astype(F32) + part_got[1, tile, :].astype(F32)
        ).astype(BF)
        return carry

    lax.fori_loop(0, rows // 32, add_part, 0)
    part_on = remote(PART_FAR, parts.at[beside], part_far, (beside, at))
    part_on.start()

    def gain_round(i):
        return remote(i, head_gains.at[i], gains_in.at[i], rounds[i], gain_sends, gain_recvs)

    rest_line.step(1)
    for i in range(len(rounds)):
        gain_round(i).start()
        gain_round(i).wait_recv()
        head_gains[i + 1] = head_gains[i] + gains_in[i]
        if i + 2 <= line:
            slab_line.step(i + 2, w_out_out)
            rest_line.step(i + 2, rest_sum)
    for step in range(len(rounds) + 2, line + 1):
        slab_line.step(step, w_out_out)
        rest_line.step(step, rest_sum)
    gains_out[...] = head_gains[len(rounds)]
    rest_home = [
        remote(REST_HOME + i, rest_sum.at[to], rest_in.at[me], (to, at))
        for i, to in enumerate((mate, beside, corner))
    ]
    rest_own = local(14, rest_sum.at[me], rest_in.at[me])
    for copy in rest_home:
        copy.start()
    rest_own.start()

    to_mate[1].wait_recv()
    part_on.wait_recv()
    loads[7].wait()

    def norm_back(step, carry):
        tile = pl.ds(pl.multiple_of(step * 32, 32), 32)
        grad = (
            parts[me, tile, :].astype(F32)
            + part_got[0, tile, :].astype(F32)
            + part_far[tile, :].astype(F32)
        )
        value = toks[me, tile, :].astype(F32)
        scale = lax.rsqrt(jnp.mean(value * value, axis=1, keepdims=True) + EPS)
        inner = grad * gain_ref[0:1, :]
        mean = jnp.mean(inner * value, axis=1, keepdims=True)
        dx_out[tile, :] += scale * inner - value * (scale * scale * scale * mean)
        return carry

    lax.fori_loop(0, rows // 32, norm_back, 0)

    loads[6].wait()
    down_last.wait_recv()

    def down_rows(step, carry):
        span = pl.ds(pl.multiple_of(step * 256, 256), 256)
        down_out[:, span] = down_own[1, :, span].astype(F32) + down_in[1, :, span].astype(F32)
        return carry

    lax.fori_loop(0, width // 256, down_rows, 0)
    for copy in homes:
        copy.wait()
    units_own.wait()
    units = units_ref.shape[2] // 2
    ff_rows = units // line
    for j, out in enumerate((gate_out, up_out)):
        for head in range(4):
            sides = [
                units_in[4 * of_side + head, :, j * units : (j + 1) * units].astype(F32)
                for of_side in range(2)
            ]
            pieces = [
                sides[p % 2][:, p // 2 * ff_rows : (p // 2 + 1) * ff_rows]
                for p in range(2 * line)
            ]
            out[:, 2 * units * head : 2 * units * (head + 1)] = jnp.concatenate(pieces, axis=1)
    for copy in query_home:
        copy.wait()
    query_own.wait()
    for g in range(4):
        query_out[:, g * COLS_Q : (g + 1) * COLS_Q] = query_in[g].astype(F32)
    for copy in rest_home:
        copy.wait()
    rest_own.wait()
    first_half = lanes((w_rows, 128)) < HEAD
    for j, out in enumerate((key_out, value_out)):
        tiles = [rest_in[g, :, j * 128 : (j + 1) * 128].astype(F32) for g in range(4)]
        moved = [pltpu.roll(tile, HEAD, 1) for tile in tiles]
        out[:, 0:128] = tiles[0] + jnp.where(first_half, 0.0, moved[1])
        out[:, 128:256] = jnp.where(first_half, moved[1], moved[2])
        out[:, 256:384] = tiles[3] + jnp.where(first_half, moved[2], 0.0)
    norm_out[...] = (
        rest_in[0, :, 256:384].astype(F32)
        + rest_in[1, :, 256:384].astype(F32)
        + rest_in[2, :, 256:384].astype(F32)
        + rest_in[3, :, 256:384].astype(F32)
    )
    for copy in four_on + two_on + to_mate:
        copy.wait_send()
    for copy in (three_on, one_on, down_on, down_last, part_on):
        copy.wait_send()
    for total in (query_line, rest_line, slab_line):
        total.drain()
    for i in range(len(rounds)):
        gain_round(i).wait_send()


def last(
    dq, dkv_low, dkv_own, pair_four, raw, cosine, sine, query_gain, key_gain, normed, w_in, toks,
    gains, gain_two, units, units_parts, down, down_parts, slab, grad,
):
    _, rows, width = toks.shape
    _, count, w_rows, _ = w_in.shape
    line = count // 2
    block = 4 * rows
    anywhere = pl.BlockSpec(memory_space=pl.ANY)
    vmem = pl.BlockSpec(memory_space=pltpu.VMEM)
    shape = jax.ShapeDtypeStruct
    dma = pltpu.SemaphoreType.DMA
    rounds = 3 + int(math.log2(line))
    part = (4, w_rows, COLS_Q)
    out_rows = slab.shape[1]
    return pl.pallas_call(
        functools.partial(last_kernel, line),
        out_shape=(
            shape((rows, width), F32),
            shape((w_rows, 4 * COLS_Q), F32),
            shape((w_rows, KVHEADS * HEAD), F32),
            shape((w_rows, KVHEADS * HEAD), F32),
            shape((w_rows, 128), F32),
            shape((w_rows, 4 * units.shape[2]), F32),
            shape((w_rows, 4 * units.shape[2]), F32),
            shape(down.shape, F32),
            shape((out_rows, width), F32),
            shape((8, 128), F32),
        ),
        in_specs=[vmem] * 2 + [anywhere] * 2 + [vmem] * 2 + [anywhere] * 2 + [vmem] * 4
        + [anywhere] * 3 + [vmem] * 2 + [anywhere] * 6,
        out_specs=(vmem,) * 10,
        scratch_shapes=[
            pltpu.VMEM((2, 2, block, 128), BF),
            pltpu.VMEM((2, block, 128), BF),
            pltpu.VMEM((2, block, 128), BF),
            pltpu.VMEM((2, block, 128), BF),
            pltpu.VMEM((2, block, 128), BF),
            pltpu.VMEM((block, COLS_Q + 128), F32),
            pltpu.VMEM((block, width), BF),
            pltpu.VMEM((width, block), BF),
            pltpu.VMEM(w_in.shape, BF),
            pltpu.VMEM(toks.shape, BF),
            pltpu.VMEM((block, 1), F32),
            pltpu.VMEM((block, COLS_IN), BF),
            pltpu.VMEM((4, count, w_rows, COLS_Q), BF),
            pltpu.VMEM((4, count, w_rows, COLS_Q), BF),
            pltpu.VMEM((line,) + part, BF),
            pltpu.VMEM((line,) + part, BF),
            pltpu.VMEM((line - 1,) + part, BF),
            pltpu.VMEM((line - 1,) + part, BF),
            pltpu.VMEM((line - 1,) + part, BF),
            pltpu.VMEM((line - 1,) + part, BF),
            pltpu.VMEM(part, BF),
            pltpu.VMEM(part, BF),
            pltpu.VMEM(slab.shape, BF),
            pltpu.VMEM((line,) + slab.shape[1:], BF),
            pltpu.VMEM((line - 1,) + slab.shape[1:], BF),
            pltpu.VMEM((line - 1,) + slab.shape[1:], BF),
            pltpu.VMEM(units.shape, BF),
            pltpu.VMEM((8, w_rows, units.shape[2]), BF),
            pltpu.VMEM(part, BF),
            pltpu.VMEM(part, BF),
            pltpu.VMEM((2,) + down.shape, BF),
            pltpu.VMEM((2,) + down.shape, BF),
            pltpu.VMEM((4, rows, width), BF),
            pltpu.VMEM((2, rows, width), BF),
            pltpu.VMEM((rows, width), BF),
            pltpu.VMEM((128, width), F32),
            pltpu.VMEM((rounds + 1, 8, 128), F32),
            pltpu.VMEM((rounds, 8, 128), F32),
            dma((LAST_TRANSFERS,)),
            dma((LAST_TRANSFERS,)),
            dma((3, 2, 2, line)),
            dma((rounds,)),
            dma((rounds,)),
            dma((17,)),
        ],
        compiler_params=pltpu.CompilerParams(
            collective_id=3, has_side_effects=True, vmem_limit_bytes=58 << 20
        ),
        cost_estimate=pl.CostEstimate(
            flops=60_000_000_000, bytes_accessed=60_000_000, transcendentals=1_000_000
        ),
        name="last",
    )(
        *dq, *dkv_low, *dkv_own, pair_four, raw, cosine, sine, query_gain, key_gain, normed, w_in,
        toks, gains, gain_two, units, units_parts, down, down_parts, slab, grad,
    )


def shards(
    tokens,
    doc_lengths,
    norm1_gain,
    w_query,
    w_key,
    w_value,
    query_gain,
    key_gain,
    w_out,
    norm2_gain,
    w_gate,
    w_up,
    w_down,
    cotangent,
):
    tok_rows, width = tokens.shape
    blocks = lax.axis_size("blk")
    groups = lax.axis_size("head")
    group_id = lax.axis_index("head")
    blk_place = lax.axis_index("blk")
    block_len = groups * tok_rows
    per_group = QHEADS // groups
    head_ratio = QHEADS // KVHEADS
    w_rows = w_query.shape[0]
    line = blocks // 2
    side = blk_place % 2
    ff_rows = w_down.shape[0]
    ff_cols = line * ff_rows
    q_cols = per_group * HEAD
    firsts = [g * per_group // head_ratio for g in range(groups)]
    odd = group_id % 2

    starts = jnp.cumsum(doc_lengths) - doc_lengths
    offsets = jnp.arange(block_len, dtype=jnp.int32)
    token_pos = blk_place * block_len + offsets
    inside = starts[None, :] <= token_pos[:, None]
    token_start = jnp.max(jnp.where(inside, starts[None, :], 0), axis=1)
    in_doc = token_pos - token_start
    rope_freq = jnp.exp(-math.log(10000.0) * jnp.arange(HEAD // 2, dtype=F32) / (HEAD // 2))
    rope_angle = in_doc.astype(F32)[:, None] * rope_freq[None, :]
    cosine, sine = jnp.cos(rope_angle), jnp.sin(rope_angle)
    cosine = jnp.concatenate([cosine] * 4, axis=1)
    sine = jnp.concatenate([-sine, sine] * 2, axis=1)
    window_start = token_start - (blk_place - BACK) * block_len
    tiles = block_len // TILE
    edges = jnp.stack(
        [window_start[::TILE], window_start[TILE - 1 :: TILE]], axis=1
    ).reshape(2 * tiles)
    meta = jnp.concatenate([odd[None].astype(jnp.int32), edges.astype(jnp.int32)])

    rest = []
    for g in range(groups):
        kv = slice(firsts[g] * HEAD, (firsts[g] + 2) * HEAD)
        rest += [
            w_key[:, kv],
            w_value[:, kv],
            norm1_gain[:, None],
            norm2_gain[:, None],
            jnp.zeros((w_rows, 126), BF),
        ]
    rest = jnp.concatenate(rest, axis=1).reshape(w_rows, groups, COLS_Q)
    rest = jnp.swapaxes(rest, 0, 1)
    query_row = jnp.concatenate([query_gain, query_gain]).astype(F32)[None, :]
    key_row = jnp.concatenate([key_gain, key_gain]).astype(F32)[None, :]
    (
        wide,
        queries,
        kv_window,
        raw,
        normed_one,
        w_in,
        top_far,
        w_blk,
        slab,
        slab_next,
        down_next,
        toks,
        gains,
    ) = first(
        tokens,
        w_query,
        rest,
        w_gate,
        w_up,
        w_down,
        w_out,
        cotangent,
        cosine,
        sine,
        query_row,
        key_row,
    )
    slabs, downs = [slab, slab_next], [w_down, down_next]
    for _ in range(line - 4):
        slabs.append(ring(slabs[-1], 2))
        downs.append(ring(downs[-1], 2))
    w_own = w_blk.reshape(q_cols, width)
    slabs, downs, w_own, top_far, top_own, queries = sync(
        slabs, downs, w_own, top_far, cotangent, queries
    )
    slabs.append(ring(slabs[-1], 2))
    downs.append(ring(downs[-1], 2))
    w_far = swap(w_own, "head", 2)
    top_across = swap(top_own, "blk", 1)
    top_corner = swap(top_far, "blk", 1)
    kept, attn_out = attend(meta, wide, kv_window, window_start[:, None])
    kept, attn_out, slabs, downs, w_far, top_across, top_corner = sync(
        kept, attn_out, slabs, downs, w_far, top_across, top_corner
    )
    if ff_rows % 16:
        downs.append(ring(downs[-1], 2))
        w_d = jnp.zeros((line, ff_rows, width), BF)
        for step, part in enumerate(downs):
            w_d = put(w_d, part, (blk_place // 2 - step) % line)
        downs = [w_d.reshape(ff_cols, width)]
    attn_out = attn_out.reshape(groups, tok_rows, q_cols)

    (
        resid,
        grad_resid,
        grad_attn,
        mixed,
        grad_mix,
        _,
        _,
        _,
        gu_parts,
        gu_moved,
        down_parts,
        weight_own,
        weight_in,
        out_own,
        out_far,
        out_across,
        out_corner,
        grad_gain_two,
    ) = middle(
        attn_out,
        tokens,
        w_own,
        w_far,
        gains[1:2],
        (cotangent, top_far, top_across, top_corner),
        slabs,
        downs,
    )
    down_parts = down_parts.reshape(line, ff_rows, width)
    gu_parts = gu_parts.reshape(groups, line, 2 * w_rows, 2 * ff_cols)
    down_sum = LineScatter(lambda p: take(down_parts, p))
    gu_sum = LineScatter(lambda p: take(gu_parts, p, 1))
    gu_sum.total = gu_moved
    gu_sum.add()
    down_sum.ahead(line - 4)
    gu_sum.ahead(line - 4)
    down_moved, gu_moved = down_sum.send(), gu_sum.send()

    out_far = swap(out_far, "head", 2)
    out_across = swap(out_across, "blk", 1)
    out_corner = lax.ppermute(
        out_corner,
        ("head", "blk"),
        [(i, (i // blocks ^ 2) * blocks + (i % blocks ^ 1)) for i in range(groups * blocks)],
    )
    back = functools.partial(
        attend_back,
        meta=meta,
        wide=wide,
        queries=queries,
        kv=kv_window,
        kept=kept,
        grads=grad_mix.reshape(block_len, q_cols),
        starts=window_start[None, :],
    )
    four = back(0)
    four, down_moved, gu_moved, out_far, out_across, out_corner, kv_window = sync(
        four, down_moved, gu_moved, out_far, out_across, out_corner, kv_window
    )
    down_sum.total, gu_sum.total = down_moved, gu_moved
    down_sum.add()
    gu_sum.add()
    gu_moved = gu_sum.send()
    pair_four = swap(four[1][2:], "blk", 1)
    slab_far = swap((weight_own[1].astype(F32) + weight_in[1].astype(F32)).astype(BF), "head", 2)
    two = back(1, kv=kv_window)
    four, two, gu_moved, pair_four, slab_far = sync(four, two, gu_moved, pair_four, slab_far)
    out_act = (
        resid
        + out_own.astype(F32)
        + out_far.astype(F32)
        + out_across.astype(F32)
        + out_corner.astype(F32)
    ).astype(BF)
    out_slab = weight_own[0].astype(F32) + weight_in[0].astype(F32) + slab_far.astype(F32)
    out_slab = out_slab.astype(BF).reshape(blocks, w_out.shape[0], width)
    (
        d_tokens,
        d_w_query,
        d_w_key,
        d_w_value,
        norm_gains,
        d_w_gate,
        d_w_up,
        d_w_down,
        d_w_out,
        head_gains,
    ) = last(
        (four[0], two[0]),
        (four[1], two[1]),
        (four[2], two[2]),
        pair_four,
        raw,
        cosine,
        sine,
        query_row,
        key_row,
        normed_one,
        w_in,
        toks,
        gains,
        grad_gain_two,
        gu_moved,
        gu_parts,
        down_sum.total.astype(BF),
        down_parts,
        out_slab,
        grad_resid,
    )
    gain_sums = head_gains[:2, :HEAD] + head_gains[:2, HEAD:]
    d_norm1_gain, d_norm2_gain = norm_gains[:, 0], norm_gains[:, 1]
    return (
        out_act,
        d_tokens,
        d_norm1_gain,
        d_w_query,
        d_w_key,
        d_w_value,
        gain_sums[0],
        gain_sums[1],
        d_w_out,
        d_norm2_gain,
        d_w_gate,
        d_w_up,
        d_w_down,
    )


def solution(mesh):
    by_token = P(("blk", "head"), None)
    by_row = P(("head", "blk"), None)
    by_entry = P(("head", "blk"))
    in_specs = (
        by_token,
        P(),
        by_entry,
        by_row,
        by_row,
        by_row,
        P(),
        P(),
        by_row,
        by_entry,
        by_row,
        by_row,
        by_row,
        by_token,
    )
    out_specs = (
        by_token,
        by_token,
        by_entry,
        by_row,
        by_row,
        by_row,
        P(),
        P(),
        by_row,
        by_entry,
        by_row,
        by_row,
        by_row,
    )
    return jax.shard_map(shards, mesh=mesh, in_specs=in_specs, out_specs=out_specs, check_vma=False)
```

```python
import functools
import math

import jax
import jax.numpy as jnp
from jax import lax
from jax.experimental import pallas as pl
from jax.experimental.pallas import tpu as pltpu
from jax.sharding import PartitionSpec as P

QHEADS = 24
KVHEADS = 6
HEAD = 64
MAXDOC = 4096

EPS = 1e-06
SCALE = 0.125
LOG2E = 1.4426950408889634
NEG = -1e30
TILE = 256
BACK = 4
BF = jnp.bfloat16
F32 = jnp.float32


def matmul(left_side, right_side):
    return jnp.dot(left_side, right_side, preferred_element_type=F32)


def matmul_tn(left_side, right_side):
    return lax.dot_general(
        left_side, right_side, (((0,), (0,)), ((), ())), preferred_element_type=F32
    )


def matmul_nt(left_side, right_side):
    return lax.dot_general(
        left_side, right_side, (((1,), (1,)), ((), ())), preferred_element_type=F32
    )


def swap(block, axis, bit):
    count = lax.axis_size(axis)
    return lax.ppermute(block, axis, [(i, i ^ bit) for i in range(count)])


def ring(block, step):
    count = lax.axis_size("blk")
    return lax.ppermute(block, "blk", [(i, (i + step) % count) for i in range(count)])


def put(full, part, index, axis=0):
    return lax.dynamic_update_index_in_dim(full, part, index, axis)


def take(full, index, axis=0):
    return lax.dynamic_index_in_dim(full, index, axis, keepdims=False)


def place_of():
    at = lax.axis_index("blk")
    return at // 2, at % 2, lax.axis_size("blk") // 2


class LineScatter:
    def __init__(self, chunk):
        self.place, _, self.line = place_of()
        self.chunk = chunk
        self.step = 1
        self.total = chunk((self.place - 1) % self.line)

    def send(self):
        self.total = ring(self.total.astype(BF), 2)
        return self.total

    def add(self):
        self.step += 1
        mine = self.chunk((self.place - self.step) % self.line)
        self.total = self.total.astype(F32) + mine.astype(F32)

    def ahead(self, steps):
        for _ in range(steps):
            self.send()
            self.add()


def gather_blk(part, axis=0):
    place, side, line = place_of()
    shape = part.shape[:axis] + (line, 2) + part.shape[axis:]
    full = jnp.zeros(shape, part.dtype)
    held = part

    def store(full, block, source, side):
        block = block.reshape(block.shape[:axis] + (1, 1) + block.shape[axis:])
        at = [0] * full.ndim
        at[axis], at[axis + 1] = source, side
        return lax.dynamic_update_slice(full, block, at)

    for step in range(line):
        if step:
            held = ring(held, 2)
        other = swap(held, "blk", 1)
        source = (place - step) % line
        full = store(full, held, source, side)
        full = store(full, other, source, 1 - side)
    return full


def sync(*trees):
    return lax.optimization_barrier(trees)


def nt(left_side, right_side):
    return lax.dot_general(
        left_side, right_side, (((1,), (1,)), ((), ())), preferred_element_type=F32
    )


def nn(left_side, right_side):
    return lax.dot_general(
        left_side, right_side, (((1,), (0,)), ((), ())), preferred_element_type=F32
    )


def lanes(shape):
    return lax.broadcasted_iota(jnp.int32, shape, len(shape) - 1)


def transposed(block):
    return jnp.swapaxes(block, 0, 1)


def head_groups(meta_ref):
    odd = meta_ref[0]
    return ((4, 2 * odd, odd), (2, 4 * (1 - odd), 1 - odd))


def split_window(kv_ref, keys, values, step, slot):
    per_block = kv_ref.shape[2] // TILE
    block, part = step // per_block, step % per_block
    source = pl.ds(pl.multiple_of(part * TILE, TILE), TILE)
    target = pl.ds(pl.multiple_of(step * TILE, TILE), TILE)
    low = lanes((TILE, 128)) < HEAD
    both = kv_ref[block, slot, source, :].astype(F32)
    moved = pltpu.roll(both, HEAD, 1)
    keys[target, 0:128] = jnp.where(low, both, moved).astype(BF)
    values[target, :] = jnp.where(low, moved, 1.0).astype(BF)
    return target


def attend_kernel(
    meta_ref, query_ref, kv_ref, start_ref, out_ref, low_ref, acc_ref, keys, values
):
    heads, rows, _ = query_ref.shape
    base = keys.shape[1] - rows
    lane = lanes((TILE, 128))

    def fill(step, carry):
        for slot in range(2):
            split_window(kv_ref, keys.at[slot], values.at[slot], step, slot)
        return carry

    lax.fori_loop(0, keys.shape[1] // TILE, fill, 0)
    for count, first, slot in head_groups(meta_ref):
        for tile in range(rows // TILE):
            q_at = tile * TILE
            low, high = meta_ref[1 + 2 * tile], meta_ref[2 + 2 * tile]
            queries = query_ref[pl.ds(first, count), q_at : q_at + TILE, :].reshape(
                count * TILE, 2 * HEAD
            )
            acc = acc_ref.at[pl.ds(0, count * TILE)]
            acc[...] = jnp.zeros((count * TILE, 2 * HEAD), F32)
            start_col = start_ref[q_at : q_at + TILE, :]
            q_pos = base + q_at + lax.broadcasted_iota(jnp.int32, (TILE, 1), 0)

            def step(at, carry, masked, size=TILE):
                k_at = pl.multiple_of(at * TILE, TILE)
                scores = nt(queries, keys[slot, pl.ds(k_at, size), :])
                if masked:
                    k_pos = k_at + lax.broadcasted_iota(jnp.int32, (1, TILE), 1)
                    allowed = (start_col <= k_pos) & (k_pos <= q_pos)
                    scores = jnp.where(
                        allowed[None], scores.reshape(count, TILE, TILE), NEG
                    ).reshape(count * TILE, TILE)
                weights = jnp.exp2(scores).astype(BF)
                acc[...] += nn(weights, values[slot, pl.ds(k_at, size), :])
                return carry

            begin = low // TILE
            last = (base + q_at) // TILE
            clear = jnp.minimum((high + TILE - 1) // TILE, last)
            lax.fori_loop(begin, clear, functools.partial(step, masked=True), 0)
            pairs = (last - clear) // 4

            def wide_step(i, carry):
                return step(clear + 4 * i, carry, False, 4 * TILE)

            lax.fori_loop(0, pairs, wide_step, 0)
            lax.fori_loop(
                clear + 4 * pairs, last, functools.partial(step, masked=False), 0
            )
            step(last, 0, True)
            for j in range(count):
                part = acc_ref[j * TILE : (j + 1) * TILE, :]
                total = part[:, HEAD : HEAD + 1]
                out_ref[first + j, q_at : q_at + TILE, :] = jnp.where(
                    lane < HEAD, part / total, jnp.log2(total)
                )

    def lay(step, carry):
        tile = pl.ds(pl.multiple_of(step * TILE, TILE), TILE)
        for t in range(heads // 2):
            pair = jnp.where(
                lane < HEAD, out_ref[2 * t, tile, :], pltpu.roll(out_ref[2 * t + 1, tile, :], HEAD, 1)
            )
            low_ref[tile, t * 128 : (t + 1) * 128] = pair.astype(BF)
        return carry

    lax.fori_loop(0, rows // TILE, lay, 0)


def attend(meta, queries, kv, starts):
    heads, rows, _ = queries.shape
    window = kv.shape[0] * rows
    vmem = pl.BlockSpec(memory_space=pltpu.VMEM)
    return pl.pallas_call(
        attend_kernel,
        out_shape=(
            jax.ShapeDtypeStruct((heads, rows, 2 * HEAD), F32),
            jax.ShapeDtypeStruct((rows, heads * HEAD), BF),
        ),
        in_specs=[pl.BlockSpec(memory_space=pltpu.SMEM)] + [vmem] * 3,
        out_specs=(vmem, vmem),
        scratch_shapes=[
            pltpu.VMEM((4 * TILE, 2 * HEAD), F32),
            pltpu.VMEM((2, window, 2 * HEAD), BF),
            pltpu.VMEM((2, window, 2 * HEAD), BF),
        ],
        compiler_params=pltpu.CompilerParams(vmem_limit_bytes=48 << 20),
        cost_estimate=pl.CostEstimate(
            flops=60_000_000_000, bytes_accessed=20_000_000, transcendentals=20_000_000
        ),
        name="attend",
    )(meta, queries, kv, starts)


def attend_back_kernel(
    which,
    meta_ref,
    wide_ref,
    query_ref,
    kv_ref,
    out_ref,
    grad_ref,
    start_ref,
    dq_ref,
    low_ref,
    pair_ref,
    own_ref,
    keys,
    values,
    keys_t,
    query_t,
    grad_t,
    grads,
    dq,
    dkv,
):
    rows = query_ref.shape[1]
    window = keys.shape[0]
    base = window - rows
    lane = lanes((TILE, 128))
    low_lane = lane < HEAD
    count, first, slot = head_groups(meta_ref)[which]

    def fill(step, carry):
        target = split_window(kv_ref, keys, values, step, slot)
        keys[target, 128:256] = jnp.ones((TILE, 128), BF)
        keys_t[:, target] = transposed(keys[target, 0:128])[0:HEAD, :]
        dkv[target, :] = jnp.zeros((TILE, 128), F32)
        return carry

    lax.fori_loop(0, window // TILE, fill, 0)

    def low_terms(value, first):
        out = jnp.zeros_like(value)
        for i in range(3):
            term = value.astype(BF).astype(F32)
            out = jnp.where(lane == first + i, term, out)
            value = value - term
        return out

    def turn(step, carry):
        tile = pl.ds(pl.multiple_of(step * TILE, TILE), TILE)
        for j in range(count):
            query_t[j, 0:128, tile] = transposed(wide_ref[first + j, tile, :])
            kept = out_ref[first + j, tile, :]
            query_t[j, 128:256, tile] = transposed(low_terms(-kept, HEAD).astype(BF))
            pair = pl.ds(pl.multiple_of((first // 2 + j // 2) * 128, 128), 128)
            grad = grad_ref[tile, pair].astype(F32)
            moved = pltpu.roll(grad, HEAD, 1)
            if j % 2:
                grad, moved = moved, grad
            dots = jnp.sum(jnp.where(low_lane, grad * kept, 0.0), axis=1, keepdims=True)
            dots = jnp.broadcast_to(-dots, (TILE, 128))
            block = jnp.where(low_lane, grad, low_terms(dots, HEAD))
            grad_t[j, :, tile] = transposed(block.astype(BF))
            grads[j, tile, :] = jnp.where(low_lane, 0.0, moved).astype(BF)
            dq[j, :, tile] = jnp.zeros((HEAD, TILE), F32)
        return carry

    lax.fori_loop(0, rows // TILE, turn, 0)
    for tile in range(rows // TILE):
        q_at = tile * TILE
        q_cols = slice(q_at, q_at + TILE)
        low, high = meta_ref[1 + 2 * tile], meta_ref[2 + 2 * tile]
        start_row = start_ref[:, q_cols]
        q_pos = base + q_at + lax.broadcasted_iota(jnp.int32, (1, TILE), 1)

        def step(at, carry, masked, size=TILE):
            k_at = pl.multiple_of(at * TILE, TILE)
            k_rows = pl.ds(k_at, size)
            key_block = keys[k_rows, :]
            value_block = values[k_rows, :]
            key_t = keys_t[:, k_rows]
            if masked:
                k_pos = k_at + lax.broadcasted_iota(jnp.int32, (TILE, 1), 0)
                allowed = (start_row <= k_pos) & (k_pos <= q_pos)
            total = dkv[k_rows, :]
            for j in range(count):
                scores = nn(key_block, query_t[j, :, q_cols])
                if masked:
                    scores = jnp.where(allowed, scores, NEG)
                probs = jnp.exp2(scores)
                diff = nn(value_block, grad_t[j, :, q_cols])
                grad_score = (probs * diff).astype(BF)
                total = (
                    total
                    + nn(probs.astype(BF), grads[j, q_cols, :])
                    + nn(grad_score, query_ref[first + j, q_cols, :])
                )
                dq[j, :, q_cols] += nn(key_t, grad_score)
            dkv[k_rows, :] = total
            return carry

        begin = low // TILE
        last = (base + q_at) // TILE
        clear = jnp.minimum((high + TILE - 1) // TILE, last)
        lax.fori_loop(begin, clear, functools.partial(step, masked=True), 0)
        pairs = (last - clear) // 4

        def wide_step(i, carry):
            return step(clear + 4 * i, carry, False, 4 * TILE)

        lax.fori_loop(0, pairs, wide_step, 0)
        lax.fori_loop(
            clear + 4 * pairs, last, functools.partial(step, masked=False), 0
        )
        step(last, 0, True)

    def finish(step, carry):
        tile = pl.ds(pl.multiple_of(step * TILE, TILE), TILE)
        for t in range(count // 2):
            pair = jnp.concatenate([dq[2 * t, :, tile], dq[2 * t + 1, :, tile]], axis=0)
            dq_ref[tile, t * 128 : (t + 1) * 128] = transposed(pair) * SCALE
        for block in range(BACK + 1):
            source = pl.ds(pl.multiple_of(block * rows + step * TILE, TILE), TILE)
            part = dkv[source, :]
            part = jnp.where(low_lane, part * SCALE, part)
            if block < BACK:
                target = pair_ref if block % 2 else low_ref
                target[block // 2, tile, :] = part.astype(BF)
            else:
                own_ref[tile, :] = part
        return carry

    lax.fori_loop(0, rows // TILE, finish, 0)


def attend_back(which, meta, wide, queries, kv, kept, grads, starts):
    _, rows, _ = queries.shape
    window = kv.shape[0] * rows
    count = (4, 2)[which]
    vmem = pl.BlockSpec(memory_space=pltpu.VMEM)
    shape = jax.ShapeDtypeStruct
    return pl.pallas_call(
        functools.partial(attend_back_kernel, which),
        out_shape=(
            shape((rows, count * HEAD), F32),
            shape((BACK // 2, rows, 128), BF),
            shape((BACK // 2, rows, 128), BF),
            shape((rows, 128), F32),
        ),
        in_specs=[pl.BlockSpec(memory_space=pltpu.SMEM)] + [vmem] * 6,
        out_specs=(vmem,) * 4,
        scratch_shapes=[
            pltpu.VMEM((window, 256), BF),
            pltpu.VMEM((window, 128), BF),
            pltpu.VMEM((HEAD, window), BF),
            pltpu.VMEM((count, 256, rows), BF),
            pltpu.VMEM((count, 128, rows), BF),
            pltpu.VMEM((count, rows, 128), BF),
            pltpu.VMEM((count, HEAD, rows), F32),
            pltpu.VMEM((window, 128), F32),
        ],
        compiler_params=pltpu.CompilerParams(vmem_limit_bytes=48 << 20),
        cost_estimate=pl.CostEstimate(
            flops=count * 20_000_000_000, bytes_accessed=40_000_000, transcendentals=20_000_000
        ),
        name=("attend_back_four", "attend_back_two")[which],
    )(meta, wide, queries, kv, kept, grads, starts)


MESH = pl.DeviceIdType.MESH
HEADS_OUT, SLAB, NEAR, FAR, ACROSS, FAR_ON, ACROSS_ON = 0, 3, 7, 8, 9, 10, 11
CORNER_TOP, CORNER_LOW, CORNER_ON, TO_MATE = 12, 13, 14, 15
BACK_TOP, BACK_LOW, BACK_FAR, BACK_ACROSS, HEADS_BACK, SUM_ON = 19, 20, 21, 22, 23, 26
WEIGHT_ON, TOP_ON, OUT_MATE, DOWN_LAST, WEIGHT_BACK, TRANSFERS = 30, 32, 36, 40, 41, 43
SPANS = ((0, 256), (256, 256), (512, 128))


def middle_kernel(
    slabs,
    downs,
    line,
    attn_ref,
    tokens_ref,
    w_own_ref,
    w_far_ref,
    gain_ref,
    top_ref,
    top_far_ref,
    top_across_ref,
    top_corner_ref,
    *refs,
):
    slab_refs, down_refs = refs[:slabs], refs[slabs : slabs + downs]
    (
        resid_out,
        grad_out,
        grad_low_out,
        mixed_out,
        heads_out,
        part_out,
        part_in,
        w_out_ref,
        gu_out,
        gu_next,
        down_out,
        weight_own,
        weight_in,
        sum_own,
        sum_far,
        sum_across,
        sum_corner,
        gain_out,
        mixed,
        acts,
        tops,
        w_gu,
        w_dn,
        hidden,
        grad_gu,
        pairs,
        got,
        stage,
        in_far,
        in_across,
        in_top,
        in_low,
        resid,
        turned,
        gu_stage,
        sends,
        recvs,
        locals_,
    ) = refs[slabs + downs :]
    me, at = lax.axis_index("head"), lax.axis_index("blk")
    count = lax.axis_size("blk")
    side, place = at % 2, at // 2
    odd = me % 2
    mate, beside, corner = me + 1 - 2 * odd, (me + 2) % 4, (me + 3 - 2 * odd) % 4
    other = at + 1 - 2 * side
    after, before = (at + 2) % count, (at + count - 2) % count
    rows, width = tokens_ref.shape
    half = rows // 2
    cols = mixed.shape[1] // 4
    units = w_dn.shape[0]
    slab_rows = slab_refs[0].shape[1]

    barrier = pltpu.get_barrier_semaphore()
    peers = ((mate, at), (beside, at), (corner, at), (me, other), (me, after), (me, before))
    for peer in peers:
        pl.semaphore_signal(barrier, inc=1, device_id=peer, device_id_type=MESH)
    pl.semaphore_wait(barrier, len(peers))

    def remote(index, source, target, device):
        return pltpu.make_async_remote_copy(
            src_ref=source,
            dst_ref=target,
            send_sem=sends.at[index],
            recv_sem=recvs.at[index],
            device_id=device,
            device_id_type=MESH,
        )

    def local(index, source, target):
        return pltpu.make_async_copy(source, target, locals_.at[index])

    def mixed_cols(head):
        return mixed.at[:, pl.ds(pl.multiple_of(head * cols, 128), cols)]

    heads = [
        remote(HEADS_OUT + i, attn_ref.at[to], mixed_cols(me), (to, at))
        for i, to in enumerate((mate, beside, corner))
    ]
    for copy in heads:
        copy.start()
    own_heads = local(0, attn_ref.at[me], mixed_cols(me))
    own_heads.start()

    def w_rows_of(head):
        return pairs.at[pl.ds(pl.multiple_of(head * cols, 128), cols)]

    weight_on = [
        remote(WEIGHT_ON, w_own_ref, w_rows_of(me), (mate, at)),
        remote(WEIGHT_ON + 1, w_far_ref, w_rows_of(beside), (mate, at)),
    ]
    for copy in weight_on:
        copy.start()
    load_out = [
        local(1, w_own_ref, w_rows_of(me)),
        local(2, w_far_ref, w_rows_of(beside)),
    ]
    for copy in load_out:
        copy.start()

    def slab_at(head, source):
        start = pl.multiple_of((head * line + source) * slab_rows, 16)
        return w_gu.at[pl.ds(start, slab_rows)]

    last = (place + line - (slabs - 1)) % line
    slab_on = [
        remote(SLAB + h, slab_refs[-1].at[h], slab_at(h, last), (me, after)) for h in range(4)
    ]
    load_slabs = [
        local(7 + 4 * i + h, ref.at[h], slab_at(h, (place + line - i) % line))
        for i, ref in enumerate(slab_refs)
        for h in range(4)
    ]
    for copy in load_slabs:
        copy.start()
    base_sem = 14 + 4 * slabs + downs
    if downs == 1:
        load_down = [local(14 + 4 * slabs, down_refs[0], w_dn)]
        down_last = []
    else:
        part_rows = units // line

        def down_at(source):
            return w_dn.at[pl.ds(pl.multiple_of(source * part_rows, 16), part_rows)]

        load_down = [
            local(14 + 4 * slabs + i, ref, down_at((place + line - i) % line))
            for i, ref in enumerate(down_refs)
        ]
        down_last = [remote(DOWN_LAST, down_refs[-1], down_at(last), (me, after))]
    for copy in down_last + slab_on:
        copy.start()
    slot = side * 4 + me
    far_slot, across_slot = side * 4 + beside, (1 - side) * 4 + me
    corner_slot = (1 - side) * 4 + beside
    top_parts = (
        (top_ref, tops.at[slot]),
        (top_far_ref, tops.at[far_slot]),
        (top_across_ref, tops.at[across_slot]),
        (top_corner_ref, tops.at[corner_slot]),
    )
    load_top = [
        local(7 + 4 * slabs + i, source, target) for i, (source, target) in enumerate(top_parts)
    ]
    for copy in load_down + load_top:
        copy.start()

    for copy in heads + weight_on:
        copy.wait_recv()
    own_heads.wait()
    for copy in load_out:
        copy.wait()
    top_on = [
        remote(TOP_ON + i, source, target, (mate, at))
        for i, (source, target) in enumerate(top_parts)
    ]
    for copy in top_on:
        copy.start()
    keep_weight = local(base_sem, pairs.at[pl.ds(0, 4 * cols)], w_out_ref)
    keep_weight.start()
    keep_mixed = local(base_sem + 2, mixed, mixed_out)
    keep_mixed.start()

    def resid_cols(step, carry):
        span = pl.ds(pl.multiple_of(step * 256, 256), 256)
        weight = pairs[0 : 4 * cols, span]
        resid[:, span] = tokens_ref[:, span].astype(F32) + nn(mixed[...], weight)
        return carry

    lax.fori_loop(0, width // 256, resid_cols, 0)

    def norm_tile(step, carry):
        tile = pl.ds(pl.multiple_of(step * 32, 32), 32)
        block = resid[tile, :]
        scale = lax.rsqrt(jnp.mean(block * block, axis=1, keepdims=True) + EPS)
        acts[slot, tile, :] = (block * scale * gain_ref[...]).astype(BF)
        return carry

    lax.fori_loop(0, rows // 32, norm_tile, 0)
    keep_resid = local(base_sem + 3, resid, resid_out)
    keep_resid.start()

    near = remote(NEAR, acts.at[slot], acts.at[slot], (mate, at))
    far = remote(FAR, acts.at[slot], acts.at[slot], (beside, at))
    across = remote(ACROSS, acts.at[slot], acts.at[slot], (me, other))
    far_on = remote(FAR_ON, acts.at[far_slot], acts.at[far_slot], (mate, at))
    across_on = remote(ACROSS_ON, acts.at[across_slot], acts.at[across_slot], (mate, at))
    corner_on = remote(CORNER_ON, acts.at[corner_slot], acts.at[corner_slot], (mate, at))
    far_top = acts.at[far_slot, pl.ds(0, half)]
    across_low = acts.at[across_slot, pl.ds(half, half)]
    corner_top = remote(CORNER_TOP, far_top, far_top, (me, other))
    corner_low = remote(CORNER_LOW, across_low, across_low, (beside, at))
    near.start()
    far.start()
    across.start()
    for copy in load_down + load_top + [keep_weight]:
        copy.wait()
    for copy in down_last + top_on:
        copy.wait_recv()

    def hidden_back(step, carry):
        for first, size in SPANS:
            grad = nt(
                tops[pl.ds(2 * step, 2)].reshape(2 * rows, width),
                w_dn[first : first + size, :],
            )
            grad_gu[pl.ds(2 * step, 2), :, units + first : units + first + size] = (
                grad.astype(BF).reshape(2, rows, size)
            )
        return carry

    lax.fori_loop(0, 4, hidden_back, 0)
    far.wait_recv()
    far_on.start()
    corner_top.start()
    across.wait_recv()
    across_on.start()
    corner_low.start()
    for copy in load_slabs:
        copy.wait()
    for copy in slab_on:
        copy.wait_recv()

    def pair_rows(index, first=0, size=rows):
        return pl.ds(pl.multiple_of(index * rows + first, 16), size)

    def to_mate(c):
        return remote(
            TO_MATE + c, pairs.at[pair_rows(2 * c + 1 - odd)], got.at[c], (mate, at)
        )

    def keep_part(c):
        return local(base_sem + 4, stage.at[odd], part_out.at[c])

    def part_on(c):
        return remote(OUT_MATE + c, stage.at[1 - odd], part_in.at[c], (mate, at))

    def chunk(c, carry):
        its_side = (side + c // 2) % 2
        its_head = (me + 2 * (c % 2)) % 4
        pair = its_side * 4 + its_head - its_head % 2

        @pl.when(c == 0)
        def _():
            near.wait_recv()

        @pl.when(c == 1)
        def _():
            far_on.wait_recv()

        @pl.when(c == 2)
        def _():
            corner_top.wait_recv()
            corner_low.wait_recv()
            corner_on.start()
            across_on.wait_recv()

        @pl.when(c == 3)
        def _():
            corner_on.wait_recv()

        for first, size in SPANS:
            block = acts[pl.ds(pair, 2)].reshape(2 * rows, width)
            gate = nn(block, w_gu[:, first : first + size])
            up = nn(block, w_gu[:, units + first : units + first + size])
            grad = grad_gu[pl.ds(pair, 2), :, units + first : units + first + size]
            grad = grad.reshape(2 * rows, size).astype(F32)
            sig = jax.nn.sigmoid(gate)
            silu = gate * sig
            shape = (2, rows, size)
            hidden[pl.ds(pair, 2), :, first : first + size] = (
                (silu * up).astype(BF).reshape(shape)
            )
            grad_gu[pl.ds(pair, 2), :, first : first + size] = (
                (grad * up * sig * (1 + gate * (1 - sig))).astype(BF).reshape(shape)
            )
            grad_gu[pl.ds(pair, 2), :, units + first : units + first + size] = (
                (grad * silu).astype(BF).reshape(shape)
            )

        def grad_cols(step, carry):
            span = pl.ds(pl.multiple_of(step * 256, 256), 256)
            block = grad_gu[pl.ds(pair, 2)].reshape(2 * rows, 2 * units)
            part = nt(block, w_gu[span, :])
            pairs[pl.ds(pl.multiple_of(2 * c * rows, 128), 2 * rows), span] = part.astype(BF)
            return carry

        lax.fori_loop(0, width // 256, grad_cols, 0)
        to_mate(c).start()

        @pl.when(c > 0)
        def _():
            keep_part(c - 1).wait()
            part_on(c - 1).wait_send()

        def out_cols(step, carry):
            span = pl.ds(pl.multiple_of(step * 256, 256), 256)
            block = hidden[pl.ds(pair, 2)].reshape(2 * rows, units)
            part = nn(block, w_dn[:, span])
            stage[:, :, span] = part.astype(BF).reshape(2, rows, 256)
            return carry

        lax.fori_loop(0, width // 256, out_cols, 0)
        keep_part(c).start()
        part_on(c).start()
        return carry

    lax.fori_loop(0, 4, chunk, 0)

    def add_rows(c, first, extra):
        def tile(step, carry):
            span = pl.ds(pl.multiple_of(first + step * 32, 32), 32)
            mine = pair_rows(2 * c + odd, first + step * 32, 32)
            total = pairs[mine, :].astype(F32) + got[c, span, :].astype(F32)
            for ref in extra:
                total = total + ref[pl.ds(pl.multiple_of(step * 32, 32), 32), :].astype(F32)
            pairs[mine, :] = total.astype(BF)
            return carry

        lax.fori_loop(0, half // 32, tile, 0)

    back_top = remote(
        BACK_TOP, pairs.at[pair_rows(6 + odd, 0, half)], in_top, (me, other)
    )
    back_low = remote(
        BACK_LOW, pairs.at[pair_rows(6 + odd, half, half)], in_low, (beside, at)
    )
    back_far = remote(BACK_FAR, pairs.at[pair_rows(2 + odd)], in_far, (beside, at))
    back_across = remote(BACK_ACROSS, pairs.at[pair_rows(4 + odd)], in_across, (me, other))
    to_mate(3).wait_recv()
    add_rows(3, 0, ())
    back_top.start()
    add_rows(3, half, ())
    back_low.start()
    to_mate(1).wait_recv()
    to_mate(2).wait_recv()
    add_rows(1, half, ())
    add_rows(2, 0, ())

    keep_part(3).wait()
    part_on(3).wait_send()

    def gu_rows(step, carry):
        span = pl.ds(pl.multiple_of(step * 256, 256), 256)
        turned[...] = transposed(acts[:, :, span].reshape(8 * rows, 256))
        buffer = step % 2

        @pl.when(step > 1)
        def _():
            local(base_sem + 5 + buffer, gu_stage.at[buffer], gu_out.at[pl.ds(0, 256)]).wait()

        for n in range(2 * units // 256):
            part = nn(
                turned[...],
                grad_gu[:, :, n * 256 : (n + 1) * 256].reshape(8 * rows, 256),
            )
            gu_stage[buffer, :, n * 256 : (n + 1) * 256] = part.astype(BF)
        local(base_sem + 5 + buffer, gu_stage.at[buffer], gu_out.at[span]).start()
        return carry

    lax.fori_loop(0, 5, gu_rows, 0)
    back_top.wait_recv()
    add_rows(1, 0, (in_top,))
    back_far.start()
    back_low.wait_recv()
    add_rows(2, half, (in_low,))
    back_across.start()
    lax.fori_loop(5, width // 256, gu_rows, 0)
    for buffer in range(2):
        local(base_sem + 5 + buffer, gu_stage.at[buffer], gu_out.at[pl.ds(0, 256)]).wait()

    target = (place + line - 1) % line
    sum_on = [
        remote(
            SUM_ON + h,
            gu_out.at[pl.ds(pl.multiple_of((h * line + target) * slab_rows, 16), slab_rows)],
            gu_next.at[h],
            (me, after),
        )
        for h in range(4)
    ]
    for copy in sum_on:
        copy.start()

    for copy in (near, far, across, far_on, across_on, corner_on, corner_top, corner_low):
        copy.wait_send()
    load_again = [
        local(1 + i, w_out_ref.at[pl.ds(i * rows, rows)], acts.at[i]) for i in range(6)
    ]
    for copy in load_again:
        copy.start()

    for i, (first, size) in enumerate(SPANS):
        turned[0:size, :] = transposed(
            hidden[:, :, first : first + size].reshape(8 * rows, size)
        )
        buffer = i % 2
        if i > 1:
            local(base_sem + 7, stage.at[0], down_out.at[pl.ds(0, rows)]).wait()

        def down_cols(step, carry):
            span = pl.ds(pl.multiple_of(step * 256, 256), 256)
            part = nn(turned[0:size, :], tops[:, :, span].reshape(8 * rows, 256))
            stage[buffer, 0:size, span] = part.astype(BF)
            return carry

        lax.fori_loop(0, width // 256, down_cols, 0)
        local(
            base_sem + 7 + buffer,
            stage.at[buffer, pl.ds(0, size)],
            down_out.at[pl.ds(first, size)],
        ).start()

    to_mate(0).wait_recv()
    back_far.wait_recv()
    back_across.wait_recv()
    keep_resid.wait()
    gain_out[...] = jnp.zeros_like(gain_out)
    low = got.at[0]

    def norm_back(step, carry):
        tile = pl.ds(pl.multiple_of(step * 32, 32), 32)
        grad = (
            pairs[pair_rows(odd, step * 32, 32), :].astype(F32)
            + got[0, tile, :].astype(F32)
            + in_far[tile, :].astype(F32)
            + in_across[tile, :].astype(F32)
        )
        block = resid[tile, :]
        scale = lax.rsqrt(jnp.mean(block * block, axis=1, keepdims=True) + EPS)
        gain_out[...] += jnp.sum(grad * block * scale, axis=0, keepdims=True)
        inner = grad * gain_ref[...]
        mean = jnp.mean(inner * block, axis=1, keepdims=True)
        total = (
            tops[slot, tile, :].astype(F32)
            + scale * inner
            - block * (scale * scale * scale * mean)
        )
        resid[tile, :] = total
        low[tile, :] = total.astype(BF)
        return carry

    lax.fori_loop(0, rows // 32, norm_back, 0)
    keep_grad = local(base_sem + 3, resid, grad_out)
    keep_grad.start()
    keep_low = local(base_sem + 4, low, grad_low_out)
    keep_low.start()
    keep_mixed.wait()
    for copy in load_again:
        copy.wait()

    def heads_cols(step, carry):
        span = pl.ds(pl.multiple_of(step * 256, 256), 256)
        turned[:, span] = nt(low[...], acts[step]).astype(BF)
        return carry

    lax.fori_loop(0, 6, heads_cols, 0)

    def grad_cols_of(head):
        return turned.at[:, pl.ds(pl.multiple_of(head * cols, 128), cols)]

    heads_on = [
        remote(HEADS_BACK + i, grad_cols_of(to), heads_out.at[me], (to, at))
        for i, to in enumerate((mate, beside, corner))
    ]
    for copy in heads_on:
        copy.start()
    own_back = local(0, grad_cols_of(me), heads_out.at[me])
    own_back.start()

    for c in range(4):
        part_on(c).wait_recv()
    load_parts = [
        local(1, part_out, tops.at[pl.ds(0, 4)]),
        local(2, part_in, tops.at[pl.ds(4, 4)]),
    ]
    for copy in load_parts:
        copy.start()

    for c in range(4):
        to_mate(c).wait_send()
    for copy in (back_top, back_low, back_far, back_across):
        copy.wait_send()

    def weight_rows(step, carry):
        span = pl.ds(pl.multiple_of(step * 256, 256), 256)
        left = transposed(mixed[:, span])
        for n in range(width // 512):
            part = nn(left, low[:, n * 512 : (n + 1) * 512])
            pairs[span, n * 512 : (n + 1) * 512] = part.astype(BF)
        return carry

    lax.fori_loop(0, 6, weight_rows, 0)
    weight_back = [
        remote(WEIGHT_BACK, w_rows_of(mate), weight_in.at[0], (mate, at)),
        remote(WEIGHT_BACK + 1, w_rows_of(corner), weight_in.at[1], (mate, at)),
    ]
    keep_back = [
        local(3, w_rows_of(me), weight_own.at[0]),
        local(4, w_rows_of(beside), weight_own.at[1]),
    ]
    for copy in weight_back + keep_back:
        copy.start()
    for copy in load_parts:
        copy.wait()

    def add_out(step, carry):
        tile = pl.ds(pl.multiple_of(step % (rows // 32) * 32, 32), 32)
        c = step // (rows // 32)
        total = tops[c, tile, :].astype(F32) + tops[c + 4, tile, :].astype(F32)
        tops[c, tile, :] = total.astype(BF)
        return carry

    lax.fori_loop(0, 4 * rows // 32, add_out, 0)
    keep_sums = [
        local(7 + c, tops.at[c], ref)
        for c, ref in enumerate((sum_own, sum_far, sum_across, sum_corner))
    ]
    for copy in keep_sums:
        copy.start()
    for copy in weight_back + keep_back + keep_sums:
        copy.wait()

    own_back.wait()
    keep_grad.wait()
    keep_low.wait()
    local(base_sem + 7, stage.at[0, pl.ds(0, SPANS[2][1])], down_out.at[pl.ds(0, SPANS[2][1])]).wait()
    local(base_sem + 8, stage.at[1], down_out.at[pl.ds(0, rows)]).wait()
    for copy in heads_on + sum_on:
        copy.wait()
    for copy in heads + slab_on + down_last:
        copy.wait_send()
    for copy in weight_on + top_on:
        copy.wait_send()


def middle(attn_out, tokens, w_own, w_far, gain, tops, slabs, downs):
    rows, width = tokens.shape
    units = slabs[0].shape[2] // 2
    cols = attn_out.shape[2]
    line = lax.axis_size("blk") // 2
    slab_shape = slabs[0].shape
    anywhere = pl.BlockSpec(memory_space=pl.ANY)
    vmem = pl.BlockSpec(memory_space=pltpu.VMEM)
    shape = jax.ShapeDtypeStruct
    eight, four = (8, rows, width), (4, rows, width)
    return pl.pallas_call(
        functools.partial(middle_kernel, len(slabs), len(downs), line),
        out_shape=(
            shape((rows, width), F32),
            shape((rows, width), F32),
            shape((rows, width), BF),
            shape((rows, 4 * cols), BF),
            shape(attn_out.shape, BF),
            shape(four, BF),
            shape(four, BF),
            shape((4 * cols, width), BF),
            shape((width, 2 * units), BF),
            shape(slab_shape, BF),
            shape((units, width), BF),
            shape((2, cols, width), BF),
            shape((2, cols, width), BF),
            shape((rows, width), BF),
            shape((rows, width), BF),
            shape((rows, width), BF),
            shape((rows, width), BF),
            shape((1, width), F32),
        ),
        in_specs=[anywhere, vmem, anywhere, anywhere, vmem]
        + [anywhere] * (len(tops) + len(slabs) + len(downs)),
        out_specs=(anywhere,) * 17 + (vmem,),
        scratch_shapes=[
            pltpu.VMEM((rows, 4 * cols), BF),
            pltpu.VMEM(eight, BF),
            pltpu.VMEM(eight, BF),
            pltpu.VMEM((width, 2 * units), BF),
            pltpu.VMEM((units, width), BF),
            pltpu.VMEM((8, rows, units), BF),
            pltpu.VMEM((8, rows, 2 * units), BF),
            pltpu.VMEM((8 * rows, width), BF),
            pltpu.VMEM(four, BF),
            pltpu.VMEM((2, rows, width), BF),
            pltpu.VMEM((rows, width), BF),
            pltpu.VMEM((rows, width), BF),
            pltpu.VMEM((rows // 2, width), BF),
            pltpu.VMEM((rows // 2, width), BF),
            pltpu.VMEM((rows, width), F32),
            pltpu.VMEM((256, 8 * rows), BF),
            pltpu.VMEM((2, 256, 2 * units), BF),
            pltpu.SemaphoreType.DMA((TRANSFERS,)),
            pltpu.SemaphoreType.DMA((TRANSFERS,)),
            pltpu.SemaphoreType.DMA((24 + 4 * len(slabs) + len(downs),)),
        ],
        compiler_params=pltpu.CompilerParams(
            collective_id=1, has_side_effects=True, vmem_limit_bytes=60 << 20
        ),
        cost_estimate=pl.CostEstimate(
            flops=60_000_000_000, bytes_accessed=100_000_000, transcendentals=2_000_000
        ),
        name="middle",
    )(attn_out, tokens, w_own, w_far, gain, *tops, *slabs, *downs)


TOK_NEAR, TOK_FAR, TOK_ON, IN_QUERY, IN_REST = 0, 1, 2, 3, 6
TOP_FAR = 9
UNITS_MOVE, SLAB_ON, DOWN_ON = 11, 18, 19
KV_ONE, KV_TWO, KV_PAIR_ONE, KV_PAIR_TWO, FIRST_TRANSFERS = 20, 22, 24, 26, 28
COLS_Q = QHEADS // 4 * HEAD
COLS_IN = COLS_Q + 4 * HEAD


def head_scale(block):
    low = lanes(block.shape) < HEAD
    square = block * block
    first = jnp.sum(jnp.where(low, square, 0.0), axis=1, keepdims=True)
    second = jnp.sum(jnp.where(low, 0.0, square), axis=1, keepdims=True)
    return jnp.where(
        low, lax.rsqrt(first / HEAD + EPS), lax.rsqrt(second / HEAD + EPS)
    )


def swap_halves(block):
    low = lanes(block.shape) % HEAD < HEAD // 2
    return jnp.where(low, pltpu.roll(block, 96, 1), pltpu.roll(block, 32, 1))


def first_kernel(
    line,
    tokens_ref,
    query_ref,
    rest_ref,
    gate_ref,
    up_ref,
    down_ref,
    w_out_ref,
    top_ref,
    cos_ref,
    sin_ref,
    query_gain_ref,
    key_gain_ref,
    wide_out,
    query_out,
    kv_out,
    raw_out,
    normed_out,
    w_in_out,
    top_far_out,
    w_out_all,
    slab_out,
    slab_next,
    down_next,
    toks_out,
    gain_out,
    toks,
    normed,
    w_in,
    raw,
    wide,
    query,
    kv_own,
    gate,
    up,
    blocks,
    sends,
    recvs,
    ring_sends,
    ring_recvs,
    swap_sends,
    swap_recvs,
    out_ring_sends,
    out_ring_recvs,
    out_swap_sends,
    out_swap_recvs,
    locals_,
):
    me, at = lax.axis_index("head"), lax.axis_index("blk")
    count = lax.axis_size("blk")
    side, place = at % 2, at // 2
    odd = me % 2
    mate, beside, corner = me + 1 - 2 * odd, (me + 2) % 4, (me + 3 - 2 * odd) % 4
    other = at + 1 - 2 * side
    after, before = (at + 2) % count, (at + count - 2) % count
    rows, width = tokens_ref.shape
    half = rows // 2
    w_rows = query_ref.shape[0]
    units = slab_out.shape[2] // 2

    barrier = pltpu.get_barrier_semaphore()
    peers = [(mate, at), (beside, at), (corner, at), (me, after), (me, before)]
    peers += [(head, other) for head in (me, mate, beside, corner)]
    for peer in peers:
        pl.semaphore_signal(barrier, inc=1, device_id=peer, device_id_type=MESH)
    pl.semaphore_wait(barrier, len(peers))

    def remote(index, source, target, device, send=sends, recv=recvs):
        return pltpu.make_async_remote_copy(
            src_ref=source,
            dst_ref=target,
            send_sem=send.at[index],
            recv_sem=recv.at[index],
            device_id=device,
            device_id_type=MESH,
        )

    def local(index, source, target):
        return pltpu.make_async_copy(source, target, locals_.at[index])

    def cols_of(ref, start, size):
        return ref.at[:, pl.ds(pl.multiple_of(start, 128), size)]

    own_q = w_in.at[me, at, :, pl.ds(0, COLS_Q)]
    own_rest = w_in.at[me, at, :, pl.ds(COLS_Q, COLS_Q)]
    split = []
    for i, to in enumerate((mate, beside, corner)):
        split.append(
            remote(IN_QUERY + i, cols_of(query_ref, to * COLS_Q, COLS_Q), own_q, (to, at))
        )
        split.append(remote(IN_REST + i, rest_ref.at[to], own_rest, (to, at)))
    for copy in split:
        copy.start()
    own = [
        local(0, cols_of(query_ref, me * COLS_Q, COLS_Q), own_q),
        local(1, rest_ref.at[me], own_rest),
        local(2, tokens_ref, toks.at[me]),
        local(3, w_out_ref, w_out_all.at[at]),
    ]
    for copy in own:
        copy.start()
    tok_near = remote(TOK_NEAR, tokens_ref, toks.at[me], (mate, at))
    tok_far = remote(TOK_FAR, tokens_ref, toks.at[me], (beside, at))
    tok_on = remote(TOK_ON, toks.at[beside], toks.at[beside], (mate, at))
    tok_far.start()
    tok_near.start()
    down_on = remote(DOWN_ON, down_ref, down_next, (me, after))
    down_on.start()
    own_units = [local(4, gate_ref, gate), local(5, up_ref, up)]
    for copy in own_units:
        copy.start()

    def ring_copy(step):
        block = w_in.at[:, (at + count - 2 * (step - 1)) % count]
        return remote(step, block, block, (me, after), ring_sends, ring_recvs)

    def swap_copy(step):
        block = w_in.at[:, (at + count - 2 * step) % count]
        return remote(step, block, block, (me, other), swap_sends, swap_recvs)

    def out_ring(step):
        index = (at + count - 2 * (step - 1)) % count
        source = w_out_ref if step == 1 else w_out_all.at[index]
        return remote(
            step, source, w_out_all.at[index], (me, after), out_ring_sends, out_ring_recvs
        )

    def out_swap(step):
        index = (at + count - 2 * step) % count
        source = w_out_ref if step == 0 else w_out_all.at[index]
        return remote(
            step, source, w_out_all.at[index], (me, other), out_swap_sends, out_swap_recvs
        )

    out_ring(1).start()
    out_swap(0).start()

    for copy in own_units:
        copy.wait()
    ff_rows = units // line
    for j, ref in enumerate((gate, up)):
        for head in range(4):
            columns = ref[:, 2 * units * head : 2 * units * (head + 1)].astype(F32)
            for to_side in range(2):
                chosen = [
                    columns[:, (2 * z + to_side) * ff_rows : (2 * z + to_side + 1) * ff_rows]
                    for z in range(line)
                ]
                blocks[to_side, head, :, j * units : (j + 1) * units] = jnp.concatenate(
                    chosen, axis=1
                ).astype(BF)
    slab_rows = pl.ds(pl.multiple_of(side * w_rows, 16), w_rows)
    targets = [(side, mate), (side, beside), (side, corner)]
    targets += [(1 - side, head) for head in (me, mate, beside, corner)]
    spread = [
        remote(
            UNITS_MOVE + i,
            blocks.at[to_side, to_head],
            slab_out.at[me, slab_rows],
            (to_head, at if i < 3 else other),
        )
        for i, (to_side, to_head) in enumerate(targets)
    ]
    for copy in spread:
        copy.start()
    own_block = local(6, blocks.at[side, me], slab_out.at[me, slab_rows])
    own_block.start()
    for copy in split:
        copy.wait_recv()
    own[0].wait()
    own[1].wait()
    ring_copy(1).start()
    swap_copy(0).start()
    tok_far.wait_recv()
    tok_on.start()
    top_far = remote(TOP_FAR, top_ref, top_far_out, (beside, at))
    top_far.start()
    for step in range(1, line):
        ring_copy(step).wait_recv()
        if step < line - 1:
            ring_copy(step + 1).start()
        swap_copy(step).start()
        out_ring(step).wait_recv()
        if step < line - 1:
            out_ring(step + 1).start()

    for copy in spread:
        copy.wait_recv()
    own_block.wait()
    slab_on = remote(SLAB_ON, slab_out, slab_next, (me, after))
    slab_on.start()
    tok_near.wait_recv()
    tok_on.wait_recv()
    own[2].wait()
    own[3].wait()
    for step in range(line):
        swap_copy(step).wait_recv()
    for step in range(1, line):
        out_swap(step).start()
    keep_in = [
        local(7 + h, w_in.at[h], w_in_out.at[h]) for h in range(4)
    ]
    for copy in keep_in:
        copy.start()

    gains = w_in[:, :, :, COLS_IN : COLS_IN + 128].reshape(width, 128).astype(F32)
    gain_out[...] = transposed(gains)[0:8, :]

    def norm_tile(step, carry):
        head, tile = step // (rows // 32), pl.ds(pl.multiple_of(step % (rows // 32) * 32, 32), 32)
        block = toks[head, tile, :].astype(F32)
        scale = lax.rsqrt(jnp.mean(block * block, axis=1, keepdims=True) + EPS)
        normed[pl.ds(pl.multiple_of(step * 32, 32), 32), :] = (
            block * scale * gain_out[0:1, :]
        ).astype(BF)
        return carry

    lax.fori_loop(0, 4 * rows // 32, norm_tile, 0)
    keep_normed = local(11, normed, normed_out)
    keep_normed.start()
    keep_toks = local(16, toks, toks_out)
    keep_toks.start()

    def project(spans):
        def tile_of(step, carry):
            tile = pl.ds(pl.multiple_of(step * 256, 256), 256)
            for first, size in spans:
                weight = w_in[:, :, :, first : first + size].reshape(width, size)
                raw[tile, first : first + size] = nn(normed[tile, :], weight)
            return carry

        lax.fori_loop(0, 4 * rows // 256, tile_of, 0)

    def rotated(block, gain, tile):
        block = block * head_scale(block) * gain
        return block * cos_ref[tile, :] + swap_halves(block) * sin_ref[tile, :]

    def prepare_keys(step, carry):
        tile = pl.ds(pl.multiple_of(step * 64, 64), 64)
        first_half = lanes((64, 128)) < HEAD
        keys = rotated(raw[tile, COLS_Q : COLS_Q + 128], key_gain_ref[...], tile)
        values = raw[tile, COLS_Q + 128 : COLS_Q + 256]
        kv_own[0, tile, :] = jnp.where(
            first_half, keys, pltpu.roll(values, HEAD, 1)
        ).astype(BF)
        kv_own[1, tile, :] = jnp.where(
            first_half, pltpu.roll(keys, HEAD, 1), values
        ).astype(BF)
        return carry

    def prepare_queries(step, carry):
        tile = pl.ds(pl.multiple_of(step * 64, 64), 64)
        first_half = lanes((64, 128)) < HEAD
        for t in range(QHEADS // 4 // 2):
            block = rotated(raw[tile, t * 128 : (t + 1) * 128], query_gain_ref[...], tile)
            block = block.astype(BF).astype(F32)
            moved = pltpu.roll(block, HEAD, 1)
            query[2 * t, tile, :] = jnp.where(first_half, block, 0.0).astype(BF)
            query[2 * t + 1, tile, :] = jnp.where(first_half, moved, 0.0).astype(BF)
            scaled = block * (SCALE * LOG2E)
            upper = scaled.astype(BF).astype(F32)
            lower = scaled - upper
            wide[2 * t, tile, :] = jnp.where(
                first_half, upper, pltpu.roll(lower, HEAD, 1)
            ).astype(BF)
            wide[2 * t + 1, tile, :] = jnp.where(
                first_half, pltpu.roll(upper, HEAD, 1), lower
            ).astype(BF)
        return carry

    project(((COLS_Q, 256),))
    lax.fori_loop(0, 4 * rows // 64, prepare_keys, 0)

    def kv_copies(index, source, target, device):
        return [remote(index + g, source(g), kv_out.at[target, g], device) for g in (0, 1)]

    def kv_from(block):
        return lambda g: kv_out.at[block, g]

    def kv_mine(g):
        return kv_own.at[g]

    kv_one = kv_copies(KV_ONE, kv_mine, 2, (me, after))
    kv_two = kv_copies(KV_TWO, kv_from(2), 0, (me, after))
    pair_one_even = kv_copies(KV_PAIR_ONE, kv_mine, 3, (me, other))
    pair_one_odd = kv_copies(KV_PAIR_ONE, kv_from(2), 3, (me, other))
    pair_two_even = kv_copies(KV_PAIR_TWO, kv_from(2), 1, (me, other))
    pair_two_odd = kv_copies(KV_PAIR_TWO, kv_from(0), 1, (me, other))
    for g in (0, 1):
        kv_one[g].start()

    @pl.when(side == 0)
    def _():
        for g in (0, 1):
            pair_one_even[g].start()

    project(((0, 256), (256, 128)))
    keep_raw = local(12, raw.at[:, pl.ds(0, COLS_Q + 128)], raw_out)
    keep_raw.start()
    for g in (0, 1):
        kv_one[g].wait_recv()
        kv_two[g].start()

        @pl.when(side == 0)
        def _(g=g):
            pair_two_even[g].start()

        @pl.when(side == 1)
        def _(g=g):
            pair_one_odd[g].start()

    lax.fori_loop(0, 4 * rows // 64, prepare_queries, 0)
    keep = [
        local(13, kv_own, kv_out.at[4]),
        local(14, wide, wide_out),
        local(15, query, query_out),
    ]
    for copy in keep:
        copy.start()
    for g in (0, 1):
        kv_two[g].wait_recv()

        @pl.when(side == 1)
        def _(g=g):
            pair_two_odd[g].start()

    for g in (0, 1):
        pair_one_even[g].wait_recv()
        pair_two_even[g].wait_recv()
    down_on.wait_recv()
    slab_on.wait_recv()
    top_far.wait_recv()
    for copy in keep + keep_in + [keep_normed, keep_raw, keep_toks]:
        copy.wait()
    for copy in split + spread:
        copy.wait_send()
    for copy in (tok_near, tok_far, tok_on, top_far):
        copy.wait_send()
    for copy in [slab_on, down_on] + kv_one + kv_two + pair_one_even + pair_two_even:
        copy.wait_send()

    for step in range(line):
        swap_copy(step).wait_send()
        out_swap(step).wait()
        if step:
            ring_copy(step).wait_send()
            out_ring(step).wait_send()


def first(
    tokens, w_query, rest, w_gate, w_up, w_down, w_out, cotangent, cosine, sine, query_gain, key_gain
):
    rows, width = tokens.shape
    count = lax.axis_size("blk")
    w_rows, ff = w_gate.shape
    units = ff // 8
    block = 4 * rows
    anywhere = pl.BlockSpec(memory_space=pl.ANY)
    vmem = pl.BlockSpec(memory_space=pltpu.VMEM)
    shape = jax.ShapeDtypeStruct
    heads = QHEADS // 4
    slab = shape((4, 2 * w_rows, 2 * units), BF)
    dma = pltpu.SemaphoreType.DMA
    return pl.pallas_call(
        functools.partial(first_kernel, count // 2),
        out_shape=(
            shape((heads, block, 128), BF),
            shape((heads, block, 128), BF),
            shape((BACK + 1, 2, block, 128), BF),
            shape((block, COLS_Q + 128), F32),
            shape((block, width), BF),
            shape((4, count, w_rows, 2 * COLS_Q), BF),
            shape((rows, width), BF),
            shape((count,) + w_out.shape, BF),
            slab,
            slab,
            shape(w_down.shape, BF),
            shape((4, rows, width), BF),
            shape((8, width), F32),
        ),
        in_specs=[anywhere] * 8 + [vmem] * 4,
        out_specs=(anywhere,) * 12 + (vmem,),
        scratch_shapes=[
            pltpu.VMEM((4, rows, width), BF),
            pltpu.VMEM((block, width), BF),
            pltpu.VMEM((4, count, w_rows, 2 * COLS_Q), BF),
            pltpu.VMEM((block, COLS_IN), F32),
            pltpu.VMEM((heads, block, 128), BF),
            pltpu.VMEM((heads, block, 128), BF),
            pltpu.VMEM((2, block, 128), BF),
            pltpu.VMEM(w_gate.shape, BF),
            pltpu.VMEM(w_up.shape, BF),
            pltpu.VMEM((2, 4, w_rows, 2 * units), BF),
            dma((FIRST_TRANSFERS,)),
            dma((FIRST_TRANSFERS,)),
            dma((count // 2,)),
            dma((count // 2,)),
            dma((count // 2,)),
            dma((count // 2,)),
            dma((count // 2,)),
            dma((count // 2,)),
            dma((count // 2,)),
            dma((count // 2,)),
            dma((17,)),
        ],
        compiler_params=pltpu.CompilerParams(
            collective_id=2, has_side_effects=True, vmem_limit_bytes=48 << 20
        ),
        cost_estimate=pl.CostEstimate(
            flops=60_000_000_000, bytes_accessed=60_000_000, transcendentals=1_000_000
        ),
        name="first",
    )(
        tokens, w_query, rest, w_gate, w_up, w_down, w_out, cotangent, cosine, sine,
        query_gain, key_gain,
    )


THREE, ONE, FOUR_ON, TWO_ON = 0, 2, 4, 6
UNITS_HOME, DOWN_STEP = 8, 15
PART_MATE, PART_CORNER, PART_FAR, QUERY_HOME, REST_HOME = 17, 18, 19, 20, 23
LAST_TRANSFERS = 26


def head_means(block):
    low = lanes(block.shape) < HEAD
    first = jnp.sum(jnp.where(low, block, 0.0), axis=1, keepdims=True)
    second = jnp.sum(jnp.where(low, 0.0, block), axis=1, keepdims=True)
    return jnp.where(low, first, second) * (1.0 / HEAD)


class LineSum:
    def __init__(self, part, got, hold, arrive, sems, places, remote):
        self.part, self.got, self.hold, self.arrive = part, got, hold, arrive
        self.swap_sems, self.ring_sems = sems
        self.side, self.place, self.line, self.other, self.after = places
        self.remote = remote

    def target(self, step):
        return (self.place + self.line - step) % self.line

    def swap(self, step):
        to = self.target(step)
        return self.remote(
            step - 1,
            self.part(2 * to + 1 - self.side),
            self.got.at[to],
            self.other,
            *self.swap_sems,
        )

    def pass_on(self, step):
        return self.remote(
            step - 1, self.hold.at[step - 1], self.arrive.at[step - 1], self.after, *self.ring_sems
        )

    def start(self):
        for step in range(1, self.line + 1):
            self.swap(step).start()

    def step(self, step, out=None):
        to = self.target(step)
        self.swap(step).wait_recv()
        total = self.part(2 * to + self.side)[...].astype(F32) + self.got[to].astype(F32)
        if step > 1:
            self.pass_on(step - 1).wait_recv()
            total = total + self.arrive[step - 2].astype(F32)
        if step < self.line:
            self.hold[step - 1] = total.astype(BF)
            self.pass_on(step).start()
        else:
            out[...] = total.astype(out.dtype)

    def drain(self):
        for step in range(1, self.line + 1):
            self.swap(step).wait_send()
            if step < self.line:
                self.pass_on(step).wait_send()


def last_kernel(
    line,
    dq_four_ref,
    dq_two_ref,
    low_four_ref,
    low_two_ref,
    pair_two_ref,
    own_four_ref,
    own_two_ref,
    pair_four_ref,
    raw_ref,
    cos_ref,
    sin_ref,
    query_gain_ref,
    key_gain_ref,
    normed_ref,
    w_in_ref,
    toks_ref,
    gain_ref,
    gain_two_ref,
    units_ref,
    units_parts_ref,
    down_ref,
    down_parts_ref,
    slab_ref,
    grad_ref,
    dx_out,
    query_out,
    key_out,
    value_out,
    norm_out,
    gate_out,
    up_out,
    down_out,
    w_out_out,
    gains_out,
    low,
    three,
    one,
    four_in,
    two_in,
    raw,
    normed,
    turned,
    w_in,
    toks,
    scales,
    grads,
    query_part,
    rest_part,
    query_got,
    rest_got,
    query_hold,
    rest_hold,
    query_arrive,
    rest_arrive,
    query_sum,
    rest_sum,
    slab,
    slab_got,
    slab_hold,
    slab_arrive,
    units_sum,
    units_in,
    query_in,
    rest_in,
    down_own,
    down_in,
    parts,
    part_got,
    part_far,
    gain_rows,
    head_gains,
    gains_in,
    sends,
    recvs,
    line_sems,
    gain_sends,
    gain_recvs,
    locals_,
):
    me, at = lax.axis_index("head"), lax.axis_index("blk")
    count = lax.axis_size("blk")
    side, place = at % 2, at // 2
    odd = me % 2
    mate, beside, corner = me + 1 - 2 * odd, (me + 2) % 4, (me + 3 - 2 * odd) % 4
    other = at + 1 - 2 * side
    after, before = (at + 2) % count, (at + count - 2) % count
    rows, width = dx_out.shape
    block = 4 * rows
    w_rows = w_in_ref.shape[2]

    rounds = [(mate, at), (beside, at), (me, other)]
    bit = 1
    while bit < line:
        rounds.append((me, at + 2 * bit * (1 - 2 * ((place // bit) % 2))))
        bit *= 2
    barrier = pltpu.get_barrier_semaphore()
    peers = [(corner, at), (me, after), (me, before)]
    peers += [(head, other) for head in (mate, beside, corner)] + rounds
    for peer in peers:
        pl.semaphore_signal(barrier, inc=1, device_id=peer, device_id_type=MESH)

    pl.semaphore_wait(barrier, len(peers))

    def remote(index, source, target, device, send=sends, recv=recvs):
        return pltpu.make_async_remote_copy(
            src_ref=source,
            dst_ref=target,
            send_sem=send.at[index],
            recv_sem=recv.at[index],
            device_id=device,
            device_id_type=MESH,
        )

    def local(index, source, target):
        return pltpu.make_async_copy(source, target, locals_.at[index])

    units_own_part = parts.at[:, pl.ds(0, 2 * w_rows), pl.ds(0, units_ref.shape[2])]
    low_refs, own_refs = (low_four_ref, low_two_ref), (own_four_ref, own_two_ref)
    three_on = remote(THREE, pair_two_ref.at[0], three.at[1], (me, other))
    one_on = remote(ONE, pair_two_ref.at[1], one.at[1], (me, other))
    three_on.start()
    one_on.start()
    low_loads = [local(6 + g, low_refs[g], low.at[g]) for g in (0, 1)]
    pair_loads = [
        local(11, pair_four_ref.at[0], three.at[0]),
        local(12, pair_four_ref.at[1], one.at[0]),
    ]
    for copy in low_loads + pair_loads:
        copy.start()
    loads = [
        local(0, normed_ref, normed),
        local(1, raw_ref, raw),
        local(2, w_in_ref, w_in),
        local(3, toks_ref, toks),
        local(4, slab_ref, slab),
        local(5, down_parts_ref.at[(place + 1) % line], down_own.at[0]),
        local(15, down_parts_ref.at[place], down_own.at[1]),
        local(16, grad_ref, dx_out),
        local(8, units_ref, units_sum),
        local(9, units_parts_ref.at[:, place], units_own_part),
    ]
    for copy in loads:
        copy.start()
    down_on = remote(DOWN_STEP, down_ref, down_in.at[0], (me, after))
    down_on.start()
    down_last = remote(DOWN_STEP + 1, down_own.at[0], down_in.at[1], (me, after))
    targets = [(side, mate), (side, beside), (side, corner)]
    targets += [(1 - side, head) for head in (me, mate, beside, corner)]
    homes = []
    for i, (to_side, to_head) in enumerate(targets):
        device = (to_head, at if i < 3 else other)
        source = units_sum.at[
            to_head, pl.ds(pl.multiple_of(to_side * w_rows, 16), w_rows)
        ]
        homes.append(remote(UNITS_HOME + i, source, units_in.at[side * 4 + me], device))
    units_own = local(
        10,
        units_sum.at[me, pl.ds(pl.multiple_of(side * w_rows, 16), w_rows)],
        units_in.at[side * 4 + me],
    )

    places = (side, place, line, (me, other), (me, after))

    def line_sum(which, part, got, hold, arrive):
        sems = [(line_sems.at[which, i, 0], line_sems.at[which, i, 1]) for i in (0, 1)]
        return LineSum(part, got, hold, arrive, sems, places, remote)

    query_line = line_sum(
        0, lambda b: query_part.at[b], query_got, query_hold, query_arrive
    )
    rest_line = line_sum(1, lambda b: rest_part.at[b], rest_got, rest_hold, rest_arrive)
    slab_line = line_sum(2, lambda b: slab.at[b], slab_got, slab_hold, slab_arrive)

    four_on = [remote(FOUR_ON + g, low.at[g, 0], four_in.at[g], (me, before)) for g in (0, 1)]
    two_on = [remote(TWO_ON + g, low.at[g, 1], two_in.at[g], (me, before)) for g in (0, 1)]

    def add_pair(g):
        def tile_of(step, carry):
            tile = pl.ds(pl.multiple_of(step * 128, 128), 128)
            got_three, got_one = three[g, tile, :].astype(F32), one[g, tile, :].astype(F32)
            to_four = jnp.where(side == 0, 0.0, got_three)
            to_two = jnp.where(side == 0, got_three, got_one)
            low[g, 0, tile, :] = (low[g, 0, tile, :].astype(F32) + to_four).astype(BF)
            low[g, 1, tile, :] = (low[g, 1, tile, :].astype(F32) + to_two).astype(BF)
            return carry

        lax.fori_loop(0, block // 128, tile_of, 0)
        four_on[g].start()

    def add_four(g):
        def tile_of(step, carry):
            tile = pl.ds(pl.multiple_of(step * 128, 128), 128)
            low[g, 1, tile, :] = (
                low[g, 1, tile, :].astype(F32) + four_in[g, tile, :].astype(F32)
            ).astype(BF)
            return carry

        four_on[g].wait_recv()
        lax.fori_loop(0, block // 128, tile_of, 0)
        two_on[g].start()

    for copy in low_loads + pair_loads:
        copy.wait()
    add_pair(0)
    loads[8].wait()
    loads[9].wait()

    def add_units(step, carry):
        head, tile = step // (2 * w_rows // 16), step % (2 * w_rows // 16)
        tile = pl.ds(pl.multiple_of(tile * 16, 16), 16)
        total = units_sum[head, tile, :].astype(F32) + units_own_part[head, tile, :].astype(F32)
        units_sum[head, tile, :] = total.astype(BF)
        return carry

    lax.fori_loop(0, 8 * w_rows // 16, add_units, 0)
    for copy in homes:
        copy.start()
    units_own.start()
    loads[4].wait()
    slab_line.start()

    head_gains[...] = jnp.zeros_like(head_gains)
    gain_rows[...] = jnp.zeros_like(gain_rows)
    loads[0].wait()
    loads[1].wait()

    def head_back(out, cols, tile, gain_tile, gain_row):
        value = raw[tile, cols]
        scale = head_scale(value)
        grad = out * cos_ref[tile, :] + swap_halves(out * sin_ref[tile, :])
        head_gains[0, gain_row : gain_row + 1, :] += jnp.sum(
            grad * value * scale, axis=0, keepdims=True
        )
        inner = grad * gain_tile
        mean = head_means(inner * value)
        return (scale * inner - value * (scale * scale * scale * mean)).astype(BF)

    def query_rows(step, carry):
        tile = pl.ds(pl.multiple_of(step * 64, 64), 64)
        for i in range(3):
            t = odd + i if i < 2 else 2 * (1 - odd)
            cols = pl.ds(pl.multiple_of(t * 128, 128), 128)
            if i < 2:
                out = dq_four_ref[tile, i * 128 : (i + 1) * 128]
            else:
                out = dq_two_ref[tile, :]
            grads[tile, cols] = head_back(out, cols, tile, query_gain_ref[...], 0)
        return carry

    lax.fori_loop(0, block // 64, query_rows, 0)
    three_on.wait_recv()
    one_on.wait_recv()
    add_pair(1)
    add_four(0)
    per_tile = 256 // w_rows
    tiles_per_head = count // per_tile

    def query_weights(step, carry):
        span = pl.ds(pl.multiple_of(step * 256, 256), 256)
        turned[span, :] = transposed(normed[:, span])
        first = pl.ds(step % tiles_per_head * per_tile, per_tile)
        part = nn(turned[span, :], grads[:, 0:COLS_Q])
        query_part[first, step // tiles_per_head] = part.astype(BF).reshape(
            per_tile, w_rows, COLS_Q
        )
        return carry

    lax.fori_loop(0, width // 256, query_weights, 0)
    query_line.start()
    add_four(1)
    slab_line.step(1)

    loads[3].wait()

    def token_scales(step, carry):
        tile = pl.ds(pl.multiple_of(step % (rows // 32) * 32, 32), 32)
        value = toks[step // (rows // 32), tile, :].astype(F32)
        scales[pl.ds(pl.multiple_of(step * 32, 32), 32), :] = lax.rsqrt(
            jnp.mean(value * value, axis=1, keepdims=True) + EPS
        )
        return carry

    lax.fori_loop(0, block // 32, token_scales, 0)
    loads[5].wait()
    down_on.wait_recv()

    def add_down(step, carry):
        span = pl.ds(pl.multiple_of(step * 256, 256), 256)
        down_own[0, :, span] = (
            down_own[0, :, span].astype(F32) + down_in[0, :, span].astype(F32)
        ).astype(BF)
        return carry

    lax.fori_loop(0, width // 256, add_down, 0)
    down_last.start()
    query_line.step(1)
    for copy in two_on:
        copy.wait_recv()

    def key_rows(step, carry):
        tile = pl.ds(pl.multiple_of(step * 64, 64), 64)
        first_half = lanes((64, 128)) < HEAD
        both = []
        for g in (0, 1):
            from_pair = jnp.where(side == 0, one[g, tile, :].astype(F32), 0.0)
            both.append(own_refs[g][tile, :] + from_pair + two_in[g, tile, :].astype(F32))
        zero = jnp.where(odd == 0, both[0], both[1])
        unit = jnp.where(odd == 0, both[1], both[0])
        keys = jnp.where(first_half, zero, pltpu.roll(unit, HEAD, 1))
        values = jnp.where(first_half, pltpu.roll(zero, HEAD, 1), unit)
        cols = pl.ds(COLS_Q, 128)
        grads[tile, cols] = head_back(keys, cols, tile, key_gain_ref[...], 1)
        grads[tile, COLS_Q + 128 : COLS_Q + 256] = values.astype(BF)
        return carry

    lax.fori_loop(0, block // 64, key_rows, 0)

    def gain_round(i):
        return remote(i, head_gains.at[i], gains_in.at[i], rounds[i], gain_sends, gain_recvs)

    def gain_step(i):
        if 0 <= i < len(rounds):
            gain_round(i).wait_recv()
            head_gains[i + 1] = head_gains[i] + gains_in[i]
        if i + 1 < len(rounds):
            gain_round(i + 1).start()

    gain_step(-1)

    loads[2].wait()

    def token_cols(step, carry):
        span = pl.ds(pl.multiple_of(step * 256, 256), 256)
        first = pl.ds(step % tiles_per_head * per_tile, per_tile)
        weight = w_in[step // tiles_per_head, first, :, 0:COLS_IN].reshape(256, COLS_IN)
        part = nt(grads[...], weight)
        parts[:, :, span] = part.astype(BF).reshape(4, rows, 256)
        value = toks[:, :, span].reshape(block, 256).astype(F32)
        gain_rows[0:1, span] = jnp.sum(part * value * scales[...], axis=0, keepdims=True)
        return carry

    lax.fori_loop(0, width // 256, token_cols, 0)
    to_mate = [
        remote(PART_CORNER, parts.at[corner], part_got.at[1], (mate, at)),
        remote(PART_MATE, parts.at[mate], part_got.at[0], (mate, at)),
    ]
    for copy in to_mate:
        copy.start()
    gain_rows[1:2, :] = gain_two_ref[...]

    def rest_weights(step, carry):
        span = pl.ds(pl.multiple_of(step * 256, 256), 256)
        first = pl.ds(step % tiles_per_head * per_tile, per_tile)
        head = step // tiles_per_head
        part = nn(turned[span, :], grads[:, COLS_Q : COLS_Q + 256])
        rest_part[first, head, :, 0:256] = part.astype(BF).reshape(per_tile, w_rows, 256)
        gain_cols = transposed(gain_rows[:, span])
        rest_part[first, head, :, 256:384] = gain_cols.astype(BF).reshape(per_tile, w_rows, 128)
        return carry

    lax.fori_loop(0, width // 256, rest_weights, 0)
    rest_line.start()
    gain_step(0)
    to_mate[0].wait_recv()

    def add_part(step, carry):
        tile = pl.ds(pl.multiple_of(step * 32, 32), 32)
        parts[beside, tile, :] = (
            parts[beside, tile, :].astype(F32) + part_got[1, tile, :].astype(F32)
        ).astype(BF)
        return carry

    lax.fori_loop(0, rows // 32, add_part, 0)
    part_on = remote(PART_FAR, parts.at[beside], part_far, (beside, at))
    part_on.start()

    query_line.step(2, query_sum)
    slab_line.step(2, w_out_out)

    loads[6].wait()
    down_last.wait_recv()

    def down_rows(step, carry):
        span = pl.ds(pl.multiple_of(step * 256, 256), 256)
        down_out[:, span] = down_own[1, :, span].astype(F32) + down_in[1, :, span].astype(F32)
        return carry

    lax.fori_loop(0, width // 256, down_rows, 0)
    gain_step(1)
    for step in range(3, line + 1):
        query_line.step(step, query_sum)
    query_home = [
        remote(QUERY_HOME + i, query_sum.at[to], query_in.at[me], (to, at))
        for i, to in enumerate((mate, beside, corner))
    ]
    query_own = local(13, query_sum.at[me], query_in.at[me])
    for copy in query_home:
        copy.start()
    query_own.start()
    for copy in homes:
        copy.wait()
    units_own.wait()
    units = units_ref.shape[2] // 2
    ff_rows = units // line
    for j, out in enumerate((gate_out, up_out)):
        for head in range(4):
            sides = [
                units_in[4 * of_side + head, :, j * units : (j + 1) * units].astype(F32)
                for of_side in range(2)
            ]
            pieces = [
                sides[p % 2][:, p // 2 * ff_rows : (p // 2 + 1) * ff_rows]
                for p in range(2 * line)
            ]
            out[:, 2 * units * head : 2 * units * (head + 1)] = jnp.concatenate(pieces, axis=1)
    gain_step(2)
    rest_line.step(1)
    for step in range(2, line + 1):
        if step > 2:
            slab_line.step(step, w_out_out)
        rest_line.step(step, rest_sum)
        gain_step(step + 1)
    rest_home = [
        remote(REST_HOME + i, rest_sum.at[to], rest_in.at[me], (to, at))
        for i, to in enumerate((mate, beside, corner))
    ]
    rest_own = local(14, rest_sum.at[me], rest_in.at[me])
    for copy in rest_home:
        copy.start()
    rest_own.start()
    for i in range(line + 2, len(rounds)):
        gain_step(i)
    gains_out[...] = head_gains[len(rounds)]

    to_mate[1].wait_recv()
    part_on.wait_recv()
    loads[7].wait()

    def norm_back(step, carry):
        tile = pl.ds(pl.multiple_of(step * 32, 32), 32)
        grad = (
            parts[me, tile, :].astype(F32)
            + part_got[0, tile, :].astype(F32)
            + part_far[tile, :].astype(F32)
        )
        value = toks[me, tile, :].astype(F32)
        scale = lax.rsqrt(jnp.mean(value * value, axis=1, keepdims=True) + EPS)
        inner = grad * gain_ref[0:1, :]
        mean = jnp.mean(inner * value, axis=1, keepdims=True)
        dx_out[tile, :] += scale * inner - value * (scale * scale * scale * mean)
        return carry

    lax.fori_loop(0, rows // 32, norm_back, 0)

    for copy in query_home:
        copy.wait()
    query_own.wait()
    for g in range(4):
        query_out[:, g * COLS_Q : (g + 1) * COLS_Q] = query_in[g].astype(F32)
    for copy in rest_home:
        copy.wait()
    rest_own.wait()
    first_half = lanes((w_rows, 128)) < HEAD
    for j, out in enumerate((key_out, value_out)):
        tiles = [rest_in[g, :, j * 128 : (j + 1) * 128].astype(F32) for g in range(4)]
        moved = [pltpu.roll(tile, HEAD, 1) for tile in tiles]
        out[:, 0:128] = tiles[0] + jnp.where(first_half, 0.0, moved[1])
        out[:, 128:256] = jnp.where(first_half, moved[1], moved[2])
        out[:, 256:384] = tiles[3] + jnp.where(first_half, moved[2], 0.0)
    norm_out[...] = (
        rest_in[0, :, 256:384].astype(F32)
        + rest_in[1, :, 256:384].astype(F32)
        + rest_in[2, :, 256:384].astype(F32)
        + rest_in[3, :, 256:384].astype(F32)
    )
    for copy in four_on + two_on + to_mate:
        copy.wait_send()
    for copy in (three_on, one_on, down_on, down_last, part_on):
        copy.wait_send()
    for total in (query_line, rest_line, slab_line):
        total.drain()
    for i in range(len(rounds)):
        gain_round(i).wait_send()


def last(
    dq, dkv_low, pair_two, dkv_own, pair_four, raw, cosine, sine, query_gain, key_gain, normed, w_in, toks,
    gains, gain_two, units, units_parts, down, down_parts, slab, grad,
):
    _, rows, width = toks.shape
    _, count, w_rows, _ = w_in.shape
    line = count // 2
    block = 4 * rows
    anywhere = pl.BlockSpec(memory_space=pl.ANY)
    vmem = pl.BlockSpec(memory_space=pltpu.VMEM)
    shape = jax.ShapeDtypeStruct
    dma = pltpu.SemaphoreType.DMA
    rounds = 3 + int(math.log2(line))
    part = (4, w_rows, COLS_Q)
    out_rows = slab.shape[1]
    return pl.pallas_call(
        functools.partial(last_kernel, line),
        out_shape=(
            shape((rows, width), F32),
            shape((w_rows, 4 * COLS_Q), F32),
            shape((w_rows, KVHEADS * HEAD), F32),
            shape((w_rows, KVHEADS * HEAD), F32),
            shape((w_rows, 128), F32),
            shape((w_rows, 4 * units.shape[2]), F32),
            shape((w_rows, 4 * units.shape[2]), F32),
            shape(down.shape, F32),
            shape((out_rows, width), F32),
            shape((8, 128), F32),
        ),
        in_specs=[vmem] * 2 + [anywhere] * 3 + [vmem] * 2 + [anywhere] * 2 + [vmem] * 4
        + [anywhere] * 3 + [vmem] * 2 + [anywhere] * 6,
        out_specs=(vmem,) * 10,
        scratch_shapes=[
            pltpu.VMEM((2, 2, block, 128), BF),
            pltpu.VMEM((2, block, 128), BF),
            pltpu.VMEM((2, block, 128), BF),
            pltpu.VMEM((2, block, 128), BF),
            pltpu.VMEM((2, block, 128), BF),
            pltpu.VMEM((block, COLS_Q + 128), F32),
            pltpu.VMEM((block, width), BF),
            pltpu.VMEM((width, block), BF),
            pltpu.VMEM(w_in.shape, BF),
            pltpu.VMEM(toks.shape, BF),
            pltpu.VMEM((block, 1), F32),
            pltpu.VMEM((block, COLS_IN), BF),
            pltpu.VMEM((count, 4, w_rows, COLS_Q), BF),
            pltpu.VMEM((count, 4, w_rows, COLS_Q), BF),
            pltpu.VMEM((line,) + part, BF),
            pltpu.VMEM((line,) + part, BF),
            pltpu.VMEM((line - 1,) + part, BF),
            pltpu.VMEM((line - 1,) + part, BF),
            pltpu.VMEM((line - 1,) + part, BF),
            pltpu.VMEM((line - 1,) + part, BF),
            pltpu.VMEM(part, BF),
            pltpu.VMEM(part, BF),
            pltpu.VMEM(slab.shape, BF),
            pltpu.VMEM((line,) + slab.shape[1:], BF),
            pltpu.VMEM((line - 1,) + slab.shape[1:], BF),
            pltpu.VMEM((line - 1,) + slab.shape[1:], BF),
            pltpu.VMEM(units.shape, BF),
            pltpu.VMEM((8, w_rows, units.shape[2]), BF),
            pltpu.VMEM(part, BF),
            pltpu.VMEM(part, BF),
            pltpu.VMEM((2,) + down.shape, BF),
            pltpu.VMEM((2,) + down.shape, BF),
            pltpu.VMEM((4, rows, width), BF),
            pltpu.VMEM((2, rows, width), BF),
            pltpu.VMEM((rows, width), BF),
            pltpu.VMEM((128, width), F32),
            pltpu.VMEM((rounds + 1, 8, 128), F32),
            pltpu.VMEM((rounds, 8, 128), F32),
            dma((LAST_TRANSFERS,)),
            dma((LAST_TRANSFERS,)),
            dma((3, 2, 2, line)),
            dma((rounds,)),
            dma((rounds,)),
            dma((17,)),
        ],
        compiler_params=pltpu.CompilerParams(
            collective_id=3, has_side_effects=True, vmem_limit_bytes=58 << 20
        ),
        cost_estimate=pl.CostEstimate(
            flops=60_000_000_000, bytes_accessed=60_000_000, transcendentals=1_000_000
        ),
        name="last",
    )(
        *dq, *dkv_low, pair_two, *dkv_own, pair_four, raw, cosine, sine, query_gain, key_gain, normed, w_in,
        toks, gains, gain_two, units, units_parts, down, down_parts, slab, grad,
    )


def shards(
    tokens,
    doc_lengths,
    norm1_gain,
    w_query,
    w_key,
    w_value,
    query_gain,
    key_gain,
    w_out,
    norm2_gain,
    w_gate,
    w_up,
    w_down,
    cotangent,
):
    tok_rows, width = tokens.shape
    blocks = lax.axis_size("blk")
    groups = lax.axis_size("head")
    group_id = lax.axis_index("head")
    blk_place = lax.axis_index("blk")
    block_len = groups * tok_rows
    per_group = QHEADS // groups
    head_ratio = QHEADS // KVHEADS
    w_rows = w_query.shape[0]
    line = blocks // 2
    side = blk_place % 2
    ff_rows = w_down.shape[0]
    ff_cols = line * ff_rows
    q_cols = per_group * HEAD
    firsts = [g * per_group // head_ratio for g in range(groups)]
    odd = group_id % 2

    starts = jnp.cumsum(doc_lengths) - doc_lengths
    offsets = jnp.arange(block_len, dtype=jnp.int32)
    token_pos = blk_place * block_len + offsets
    inside = starts[None, :] <= token_pos[:, None]
    token_start = jnp.max(jnp.where(inside, starts[None, :], 0), axis=1)
    in_doc = token_pos - token_start
    rope_freq = jnp.exp(-math.log(10000.0) * jnp.arange(HEAD // 2, dtype=F32) / (HEAD // 2))
    rope_angle = in_doc.astype(F32)[:, None] * rope_freq[None, :]
    cosine, sine = jnp.cos(rope_angle), jnp.sin(rope_angle)
    cosine = jnp.concatenate([cosine] * 4, axis=1)
    sine = jnp.concatenate([-sine, sine] * 2, axis=1)
    window_start = token_start - (blk_place - BACK) * block_len
    tiles = block_len // TILE
    edges = jnp.stack(
        [window_start[::TILE], window_start[TILE - 1 :: TILE]], axis=1
    ).reshape(2 * tiles)
    meta = jnp.concatenate([odd[None].astype(jnp.int32), edges.astype(jnp.int32)])

    rest = []
    for g in range(groups):
        kv = slice(firsts[g] * HEAD, (firsts[g] + 2) * HEAD)
        rest += [
            w_key[:, kv],
            w_value[:, kv],
            norm1_gain[:, None],
            norm2_gain[:, None],
            jnp.zeros((w_rows, 126), BF),
        ]
    rest = jnp.concatenate(rest, axis=1).reshape(w_rows, groups, COLS_Q)
    rest = jnp.swapaxes(rest, 0, 1)
    query_row = jnp.concatenate([query_gain, query_gain]).astype(F32)[None, :]
    key_row = jnp.concatenate([key_gain, key_gain]).astype(F32)[None, :]
    (
        wide,
        queries,
        kv_window,
        raw,
        normed_one,
        w_in,
        top_far,
        w_blk,
        slab,
        slab_next,
        down_next,
        toks,
        gains,
    ) = first(
        tokens,
        w_query,
        rest,
        w_gate,
        w_up,
        w_down,
        w_out,
        cotangent,
        cosine,
        sine,
        query_row,
        key_row,
    )
    slabs, downs = [slab, slab_next], [w_down, down_next]
    for _ in range(line - 4):
        slabs.append(ring(slabs[-1], 2))
        downs.append(ring(downs[-1], 2))
    w_own = w_blk.reshape(q_cols, width)
    slabs, downs, w_own, top_far, top_own, queries = sync(
        slabs, downs, w_own, top_far, cotangent, queries
    )
    slabs.append(ring(slabs[-1], 2))
    downs.append(ring(downs[-1], 2))
    w_far = swap(w_own, "head", 2)
    top_across = swap(top_own, "blk", 1)
    top_corner = swap(top_far, "blk", 1)
    kept, attn_out = attend(meta, wide, kv_window, window_start[:, None])
    kept, attn_out, slabs, downs, w_far, top_across, top_corner = sync(
        kept, attn_out, slabs, downs, w_far, top_across, top_corner
    )
    if ff_rows % 16:
        downs.append(ring(downs[-1], 2))
        w_d = jnp.zeros((line, ff_rows, width), BF)
        for step, part in enumerate(downs):
            w_d = put(w_d, part, (blk_place // 2 - step) % line)
        downs = [w_d.reshape(ff_cols, width)]
    attn_out = attn_out.reshape(groups, tok_rows, q_cols)

    (
        resid,
        grad_resid,
        grad_attn,
        mixed,
        grad_mix,
        _,
        _,
        _,
        gu_parts,
        gu_moved,
        down_parts,
        weight_own,
        weight_in,
        out_own,
        out_far,
        out_across,
        out_corner,
        grad_gain_two,
    ) = middle(
        attn_out,
        tokens,
        w_own,
        w_far,
        gains[1:2],
        (cotangent, top_far, top_across, top_corner),
        slabs,
        downs,
    )
    down_parts = down_parts.reshape(line, ff_rows, width)
    gu_parts = gu_parts.reshape(groups, line, 2 * w_rows, 2 * ff_cols)
    down_sum = LineScatter(lambda p: take(down_parts, p))
    gu_sum = LineScatter(lambda p: take(gu_parts, p, 1))
    gu_sum.total = gu_moved
    gu_sum.add()
    down_sum.ahead(line - 4)
    gu_sum.ahead(line - 4)
    down_moved, gu_moved = down_sum.send(), gu_sum.send()

    out_far = swap(out_far, "head", 2)
    out_across = swap(out_across, "blk", 1)
    out_corner = lax.ppermute(
        out_corner,
        ("head", "blk"),
        [(i, (i // blocks ^ 2) * blocks + (i % blocks ^ 1)) for i in range(groups * blocks)],
    )
    back = functools.partial(
        attend_back,
        meta=meta,
        wide=wide,
        queries=queries,
        kv=kv_window,
        kept=kept,
        grads=grad_mix.reshape(block_len, q_cols),
        starts=window_start[None, :],
    )
    four = back(0)
    four, down_moved, gu_moved, out_far, out_across, out_corner, kv_window = sync(
        four, down_moved, gu_moved, out_far, out_across, out_corner, kv_window
    )
    down_sum.total, gu_sum.total = down_moved, gu_moved
    down_sum.add()
    gu_sum.add()
    gu_moved = gu_sum.send()
    pair_four = swap(four[2], "blk", 1)
    slab_far = swap((weight_own[1].astype(F32) + weight_in[1].astype(F32)).astype(BF), "head", 2)
    two = back(1, kv=kv_window)
    four, two, gu_moved, pair_four, slab_far = sync(four, two, gu_moved, pair_four, slab_far)
    out_act = (
        resid
        + out_own.astype(F32)
        + out_far.astype(F32)
        + out_across.astype(F32)
        + out_corner.astype(F32)
    ).astype(BF)
    out_slab = weight_own[0].astype(F32) + weight_in[0].astype(F32) + slab_far.astype(F32)
    out_slab = out_slab.astype(BF).reshape(blocks, w_out.shape[0], width)
    (
        d_tokens,
        d_w_query,
        d_w_key,
        d_w_value,
        norm_gains,
        d_w_gate,
        d_w_up,
        d_w_down,
        d_w_out,
        head_gains,
    ) = last(
        (four[0], two[0]),
        (four[1], two[1]),
        two[2],
        (four[3], two[3]),
        pair_four,
        raw,
        cosine,
        sine,
        query_row,
        key_row,
        normed_one,
        w_in,
        toks,
        gains,
        grad_gain_two,
        gu_moved,
        gu_parts,
        down_sum.total.astype(BF),
        down_parts,
        out_slab,
        grad_resid,
    )
    gain_sums = head_gains[:2, :HEAD] + head_gains[:2, HEAD:]
    d_norm1_gain, d_norm2_gain = norm_gains[:, 0], norm_gains[:, 1]
    return (
        out_act,
        d_tokens,
        d_norm1_gain,
        d_w_query,
        d_w_key,
        d_w_value,
        gain_sums[0],
        gain_sums[1],
        d_w_out,
        d_norm2_gain,
        d_w_gate,
        d_w_up,
        d_w_down,
    )


def solution(mesh):
    by_token = P(("blk", "head"), None)
    by_row = P(("head", "blk"), None)
    by_entry = P(("head", "blk"))
    in_specs = (
        by_token,
        P(),
        by_entry,
        by_row,
        by_row,
        by_row,
        P(),
        P(),
        by_row,
        by_entry,
        by_row,
        by_row,
        by_row,
        by_token,
    )
    out_specs = (
        by_token,
        by_token,
        by_entry,
        by_row,
        by_row,
        by_row,
        P(),
        P(),
        by_row,
        by_entry,
        by_row,
        by_row,
        by_row,
    )
    return jax.shard_map(shards, mesh=mesh, in_specs=in_specs, out_specs=out_specs, check_vma=False)
```

```python
import functools
import math

import jax
import jax.numpy as jnp
from jax import lax
from jax.experimental import pallas as pl
from jax.experimental.pallas import tpu as pltpu
from jax.sharding import PartitionSpec as P

QHEADS = 24
KVHEADS = 6
HEAD = 64
MAXDOC = 4096

EPS = 1e-06
SCALE = 0.125
LOG2E = 1.4426950408889634
NEG = -1e30
TILE = 256
BACK = 4
BF = jnp.bfloat16
F32 = jnp.float32


def matmul(left_side, right_side):
    return jnp.dot(left_side, right_side, preferred_element_type=F32)


def matmul_tn(left_side, right_side):
    return lax.dot_general(
        left_side, right_side, (((0,), (0,)), ((), ())), preferred_element_type=F32
    )


def matmul_nt(left_side, right_side):
    return lax.dot_general(
        left_side, right_side, (((1,), (1,)), ((), ())), preferred_element_type=F32
    )


def swap(block, axis, bit):
    count = lax.axis_size(axis)
    return lax.ppermute(block, axis, [(i, i ^ bit) for i in range(count)])


def ring(block, step):
    count = lax.axis_size("blk")
    return lax.ppermute(block, "blk", [(i, (i + step) % count) for i in range(count)])


def put(full, part, index, axis=0):
    return lax.dynamic_update_index_in_dim(full, part, index, axis)


def take(full, index, axis=0):
    return lax.dynamic_index_in_dim(full, index, axis, keepdims=False)


def place_of():
    at = lax.axis_index("blk")
    return at // 2, at % 2, lax.axis_size("blk") // 2


class LineScatter:
    def __init__(self, chunk):
        self.place, _, self.line = place_of()
        self.chunk = chunk
        self.step = 1
        self.total = chunk((self.place - 1) % self.line)

    def send(self):
        self.total = ring(self.total.astype(BF), 2)
        return self.total

    def add(self):
        self.step += 1
        mine = self.chunk((self.place - self.step) % self.line)
        self.total = self.total.astype(F32) + mine.astype(F32)

    def ahead(self, steps):
        for _ in range(steps):
            self.send()
            self.add()


def gather_blk(part, axis=0):
    place, side, line = place_of()
    shape = part.shape[:axis] + (line, 2) + part.shape[axis:]
    full = jnp.zeros(shape, part.dtype)
    held = part

    def store(full, block, source, side):
        block = block.reshape(block.shape[:axis] + (1, 1) + block.shape[axis:])
        at = [0] * full.ndim
        at[axis], at[axis + 1] = source, side
        return lax.dynamic_update_slice(full, block, at)

    for step in range(line):
        if step:
            held = ring(held, 2)
        other = swap(held, "blk", 1)
        source = (place - step) % line
        full = store(full, held, source, side)
        full = store(full, other, source, 1 - side)
    return full


def sync(*trees):
    return lax.optimization_barrier(trees)


def nt(left_side, right_side):
    return lax.dot_general(
        left_side, right_side, (((1,), (1,)), ((), ())), preferred_element_type=F32
    )


def nn(left_side, right_side):
    return lax.dot_general(
        left_side, right_side, (((1,), (0,)), ((), ())), preferred_element_type=F32
    )


def lanes(shape):
    return lax.broadcasted_iota(jnp.int32, shape, len(shape) - 1)


def transposed(block):
    return jnp.swapaxes(block, 0, 1)


def head_groups(meta_ref):
    odd = meta_ref[0]
    return ((4, 2 * odd, odd), (2, 4 * (1 - odd), 1 - odd))


def split_window(kv_ref, keys, values, step, slot):
    per_block = kv_ref.shape[2] // TILE
    block, part = step // per_block, step % per_block
    source = pl.ds(pl.multiple_of(part * TILE, TILE), TILE)
    target = pl.ds(pl.multiple_of(step * TILE, TILE), TILE)
    low = lanes((TILE, 128)) < HEAD
    both = kv_ref[block, slot, source, :].astype(F32)
    moved = pltpu.roll(both, HEAD, 1)
    keys[target, 0:128] = jnp.where(low, both, moved).astype(BF)
    values[target, :] = jnp.where(low, moved, 1.0).astype(BF)
    return target


def attend_kernel(
    meta_ref, query_ref, kv_ref, start_ref, out_ref, low_ref, acc_ref, keys, values
):
    heads, rows, _ = query_ref.shape
    base = keys.shape[1] - rows
    lane = lanes((TILE, 128))

    def fill(step, carry):
        for slot in range(2):
            split_window(kv_ref, keys.at[slot], values.at[slot], step, slot)
        return carry

    lax.fori_loop(meta_ref[1] // TILE, keys.shape[1] // TILE, fill, 0)
    for count, first, slot in head_groups(meta_ref):
        for tile in range(rows // TILE):
            q_at = tile * TILE
            low, high = meta_ref[1 + 2 * tile], meta_ref[2 + 2 * tile]
            queries = query_ref[pl.ds(first, count), q_at : q_at + TILE, :].reshape(
                count * TILE, 2 * HEAD
            )
            acc = acc_ref.at[pl.ds(0, count * TILE)]
            acc[...] = jnp.zeros((count * TILE, 2 * HEAD), F32)
            start_col = start_ref[q_at : q_at + TILE, :]
            q_pos = base + q_at + lax.broadcasted_iota(jnp.int32, (TILE, 1), 0)

            def step(at, carry, masked, size=TILE):
                k_at = pl.multiple_of(at * TILE, TILE)
                scores = nt(queries, keys[slot, pl.ds(k_at, size), :])
                if masked:
                    k_pos = k_at + lax.broadcasted_iota(jnp.int32, (1, TILE), 1)
                    allowed = (start_col <= k_pos) & (k_pos <= q_pos)
                    scores = jnp.where(
                        allowed[None], scores.reshape(count, TILE, TILE), NEG
                    ).reshape(count * TILE, TILE)
                weights = jnp.exp2(scores).astype(BF)
                acc[...] += nn(weights, values[slot, pl.ds(k_at, size), :])
                return carry

            begin = low // TILE
            last = (base + q_at) // TILE
            clear = jnp.minimum((high + TILE - 1) // TILE, last)
            lax.fori_loop(begin, clear, functools.partial(step, masked=True), 0)
            pairs = (last - clear) // 4

            def wide_step(i, carry):
                return step(clear + 4 * i, carry, False, 4 * TILE)

            lax.fori_loop(0, pairs, wide_step, 0)
            lax.fori_loop(
                clear + 4 * pairs, last, functools.partial(step, masked=False), 0
            )
            step(last, 0, True)
            for j in range(count):
                part = acc_ref[j * TILE : (j + 1) * TILE, :]
                total = part[:, HEAD : HEAD + 1]
                out_ref[first + j, q_at : q_at + TILE, :] = jnp.where(
                    lane < HEAD, part / total, jnp.log2(total)
                )

    def lay(step, carry):
        tile = pl.ds(pl.multiple_of(step * TILE, TILE), TILE)
        for t in range(heads // 2):
            pair = jnp.where(
                lane < HEAD, out_ref[2 * t, tile, :], pltpu.roll(out_ref[2 * t + 1, tile, :], HEAD, 1)
            )
            low_ref[tile, t * 128 : (t + 1) * 128] = pair.astype(BF)
        return carry

    lax.fori_loop(0, rows // TILE, lay, 0)


def attend(meta, queries, kv, starts):
    heads, rows, _ = queries.shape
    window = kv.shape[0] * rows
    vmem = pl.BlockSpec(memory_space=pltpu.VMEM)
    return pl.pallas_call(
        attend_kernel,
        out_shape=(
            jax.ShapeDtypeStruct((heads, rows, 2 * HEAD), F32),
            jax.ShapeDtypeStruct((rows, heads * HEAD), BF),
        ),
        in_specs=[pl.BlockSpec(memory_space=pltpu.SMEM)] + [vmem] * 3,
        out_specs=(vmem, vmem),
        scratch_shapes=[
            pltpu.VMEM((4 * TILE, 2 * HEAD), F32),
            pltpu.VMEM((2, window, 2 * HEAD), BF),
            pltpu.VMEM((2, window, 2 * HEAD), BF),
        ],
        compiler_params=pltpu.CompilerParams(vmem_limit_bytes=48 << 20),
        cost_estimate=pl.CostEstimate(
            flops=60_000_000_000, bytes_accessed=20_000_000, transcendentals=20_000_000
        ),
        name="attend",
    )(meta, queries, kv, starts)


def attend_back_kernel(
    which,
    meta_ref,
    wide_ref,
    query_ref,
    kv_ref,
    out_ref,
    grad_ref,
    start_ref,
    dq_ref,
    low_ref,
    pair_ref,
    own_ref,
    keys,
    values,
    keys_t,
    query_t,
    grad_t,
    grads,
    dq,
    dkv,
):
    rows = query_ref.shape[1]
    window = keys.shape[0]
    base = window - rows
    lane = lanes((TILE, 128))
    low_lane = lane < HEAD
    count, first, slot = head_groups(meta_ref)[which]

    def fill(step, carry):
        target = split_window(kv_ref, keys, values, step, slot)
        keys[target, 128:256] = jnp.ones((TILE, 128), BF)
        keys_t[:, target] = transposed(keys[target, 0:128])[0:HEAD, :]
        return carry

    def clear_sums(step, carry):
        dkv[pl.ds(pl.multiple_of(step * TILE, TILE), TILE), :] = jnp.zeros((TILE, 128), F32)
        return carry

    lax.fori_loop(0, window // TILE, clear_sums, 0)
    lax.fori_loop(meta_ref[1] // TILE, window // TILE, fill, 0)

    def low_terms(value, first):
        out = jnp.zeros_like(value)
        for i in range(3):
            term = value.astype(BF).astype(F32)
            out = jnp.where(lane == first + i, term, out)
            value = value - term
        return out

    def turn(step, carry):
        tile = pl.ds(pl.multiple_of(step * TILE, TILE), TILE)
        for j in range(count):
            query_t[j, 0:128, tile] = transposed(wide_ref[first + j, tile, :])
            kept = out_ref[first + j, tile, :]
            query_t[j, 128:256, tile] = transposed(low_terms(-kept, HEAD).astype(BF))
            pair = pl.ds(pl.multiple_of((first // 2 + j // 2) * 128, 128), 128)
            grad = grad_ref[tile, pair].astype(F32)
            moved = pltpu.roll(grad, HEAD, 1)
            if j % 2:
                grad, moved = moved, grad
            dots = jnp.sum(jnp.where(low_lane, grad * kept, 0.0), axis=1, keepdims=True)
            dots = jnp.broadcast_to(-dots, (TILE, 128))
            block = jnp.where(low_lane, grad, low_terms(dots, HEAD))
            grad_t[j, :, tile] = transposed(block.astype(BF))
            grads[j, tile, :] = jnp.where(low_lane, 0.0, moved).astype(BF)
            dq[j, :, tile] = jnp.zeros((HEAD, TILE), F32)
        return carry

    lax.fori_loop(0, rows // TILE, turn, 0)
    for tile in range(rows // TILE):
        q_at = tile * TILE
        q_cols = slice(q_at, q_at + TILE)
        low, high = meta_ref[1 + 2 * tile], meta_ref[2 + 2 * tile]
        start_row = start_ref[:, q_cols]
        q_pos = base + q_at + lax.broadcasted_iota(jnp.int32, (1, TILE), 1)

        def step(at, carry, masked, size=TILE):
            k_at = pl.multiple_of(at * TILE, TILE)
            k_rows = pl.ds(k_at, size)
            key_block = keys[k_rows, :]
            value_block = values[k_rows, :]
            key_t = keys_t[:, k_rows]
            if masked:
                k_pos = k_at + lax.broadcasted_iota(jnp.int32, (TILE, 1), 0)
                allowed = (start_row <= k_pos) & (k_pos <= q_pos)
            total = dkv[k_rows, :]
            for j in range(count):
                scores = nn(key_block, query_t[j, :, q_cols])
                if masked:
                    scores = jnp.where(allowed, scores, NEG)
                probs = jnp.exp2(scores)
                diff = nn(value_block, grad_t[j, :, q_cols])
                grad_score = (probs * diff).astype(BF)
                total = (
                    total
                    + nn(probs.astype(BF), grads[j, q_cols, :])
                    + nn(grad_score, query_ref[first + j, q_cols, :])
                )
                dq[j, :, q_cols] += nn(key_t, grad_score)
            dkv[k_rows, :] = total
            return carry

        begin = low // TILE
        last = (base + q_at) // TILE
        clear = jnp.minimum((high + TILE - 1) // TILE, last)
        lax.fori_loop(begin, clear, functools.partial(step, masked=True), 0)
        pairs = (last - clear) // 4

        def wide_step(i, carry):
            return step(clear + 4 * i, carry, False, 4 * TILE)

        lax.fori_loop(0, pairs, wide_step, 0)
        lax.fori_loop(
            clear + 4 * pairs, last, functools.partial(step, masked=False), 0
        )
        step(last, 0, True)

    def finish(step, carry):
        tile = pl.ds(pl.multiple_of(step * TILE, TILE), TILE)
        for t in range(count // 2):
            pair = jnp.concatenate([dq[2 * t, :, tile], dq[2 * t + 1, :, tile]], axis=0)
            dq_ref[tile, t * 128 : (t + 1) * 128] = transposed(pair) * SCALE
        for block in range(BACK + 1):
            source = pl.ds(pl.multiple_of(block * rows + step * TILE, TILE), TILE)
            part = dkv[source, :]
            part = jnp.where(low_lane, part * SCALE, part)
            if block < BACK:
                target = pair_ref if block % 2 else low_ref
                target[block // 2, tile, :] = part.astype(BF)
            else:
                own_ref[tile, :] = part
        return carry

    lax.fori_loop(0, rows // TILE, finish, 0)


def attend_back(which, meta, wide, queries, kv, kept, grads, starts):
    _, rows, _ = queries.shape
    window = kv.shape[0] * rows
    count = (4, 2)[which]
    vmem = pl.BlockSpec(memory_space=pltpu.VMEM)
    shape = jax.ShapeDtypeStruct
    return pl.pallas_call(
        functools.partial(attend_back_kernel, which),
        out_shape=(
            shape((rows, count * HEAD), F32),
            shape((BACK // 2, rows, 128), BF),
            shape((BACK // 2, rows, 128), BF),
            shape((rows, 128), F32),
        ),
        in_specs=[pl.BlockSpec(memory_space=pltpu.SMEM)] + [vmem] * 6,
        out_specs=(vmem,) * 4,
        scratch_shapes=[
            pltpu.VMEM((window, 256), BF),
            pltpu.VMEM((window, 128), BF),
            pltpu.VMEM((HEAD, window), BF),
            pltpu.VMEM((count, 256, rows), BF),
            pltpu.VMEM((count, 128, rows), BF),
            pltpu.VMEM((count, rows, 128), BF),
            pltpu.VMEM((count, HEAD, rows), F32),
            pltpu.VMEM((window, 128), F32),
        ],
        compiler_params=pltpu.CompilerParams(vmem_limit_bytes=48 << 20),
        cost_estimate=pl.CostEstimate(
            flops=count * 20_000_000_000, bytes_accessed=40_000_000, transcendentals=20_000_000
        ),
        name=("attend_back_four", "attend_back_two")[which],
    )(meta, wide, queries, kv, kept, grads, starts)


MESH = pl.DeviceIdType.MESH
HEADS_OUT, SLAB, NEAR, FAR, ACROSS, FAR_ON, ACROSS_ON = 0, 3, 7, 8, 9, 10, 11
CORNER_TOP, CORNER_LOW, CORNER_ON, TO_MATE = 12, 13, 14, 15
BACK_TOP, BACK_LOW, BACK_FAR, BACK_ACROSS, HEADS_BACK, SUM_ON = 19, 20, 21, 22, 23, 26
WEIGHT_ON, TOP_ON, OUT_MATE, DOWN_LAST, WEIGHT_BACK, TRANSFERS = 30, 32, 36, 40, 41, 43
SPANS = ((0, 256), (256, 256), (512, 128))


def middle_kernel(
    slabs,
    downs,
    line,
    attn_ref,
    tokens_ref,
    w_own_ref,
    w_far_ref,
    gain_ref,
    top_ref,
    top_far_ref,
    top_across_ref,
    top_corner_ref,
    *refs,
):
    slab_refs, down_refs = refs[:slabs], refs[slabs : slabs + downs]
    (
        resid_out,
        grad_out,
        grad_low_out,
        mixed_out,
        heads_out,
        part_out,
        part_in,
        w_out_ref,
        gu_out,
        gu_next,
        down_out,
        weight_own,
        weight_in,
        sum_own,
        sum_far,
        sum_across,
        sum_corner,
        gain_out,
        mixed,
        acts,
        tops,
        w_gu,
        w_dn,
        hidden,
        grad_gu,
        pairs,
        got,
        stage,
        in_far,
        in_across,
        in_top,
        in_low,
        resid,
        turned,
        gu_stage,
        sends,
        recvs,
        locals_,
    ) = refs[slabs + downs :]
    me, at = lax.axis_index("head"), lax.axis_index("blk")
    count = lax.axis_size("blk")
    side, place = at % 2, at // 2
    odd = me % 2
    mate, beside, corner = me + 1 - 2 * odd, (me + 2) % 4, (me + 3 - 2 * odd) % 4
    other = at + 1 - 2 * side
    after, before = (at + 2) % count, (at + count - 2) % count
    rows, width = tokens_ref.shape
    half = rows // 2
    cols = mixed.shape[1] // 4
    units = w_dn.shape[0]
    slab_rows = slab_refs[0].shape[1]

    barrier = pltpu.get_barrier_semaphore()
    peers = ((mate, at), (beside, at), (corner, at), (me, other), (me, after), (me, before))
    for peer in peers:
        pl.semaphore_signal(barrier, inc=1, device_id=peer, device_id_type=MESH)
    pl.semaphore_wait(barrier, len(peers))

    def remote(index, source, target, device):
        return pltpu.make_async_remote_copy(
            src_ref=source,
            dst_ref=target,
            send_sem=sends.at[index],
            recv_sem=recvs.at[index],
            device_id=device,
            device_id_type=MESH,
        )

    def local(index, source, target):
        return pltpu.make_async_copy(source, target, locals_.at[index])

    def mixed_cols(head):
        return mixed.at[:, pl.ds(pl.multiple_of(head * cols, 128), cols)]

    heads = [
        remote(HEADS_OUT + i, attn_ref.at[to], mixed_cols(me), (to, at))
        for i, to in enumerate((mate, beside, corner))
    ]
    for copy in heads:
        copy.start()
    own_heads = local(0, attn_ref.at[me], mixed_cols(me))
    own_heads.start()

    def w_rows_of(head):
        return pairs.at[pl.ds(pl.multiple_of(head * cols, 128), cols)]

    weight_on = [
        remote(WEIGHT_ON, w_own_ref, w_rows_of(me), (mate, at)),
        remote(WEIGHT_ON + 1, w_far_ref, w_rows_of(beside), (mate, at)),
    ]
    for copy in weight_on:
        copy.start()
    load_out = [
        local(1, w_own_ref, w_rows_of(me)),
        local(2, w_far_ref, w_rows_of(beside)),
    ]
    for copy in load_out:
        copy.start()

    def slab_at(head, source):
        start = pl.multiple_of((head * line + source) * slab_rows, 16)
        return w_gu.at[pl.ds(start, slab_rows)]

    last = (place + line - (slabs - 1)) % line
    slab_on = [
        remote(SLAB + h, slab_refs[-1].at[h], slab_at(h, last), (me, after)) for h in range(4)
    ]
    load_slabs = [
        local(7 + 4 * i + h, ref.at[h], slab_at(h, (place + line - i) % line))
        for i, ref in enumerate(slab_refs)
        for h in range(4)
    ]
    for copy in load_slabs:
        copy.start()
    base_sem = 14 + 4 * slabs + downs
    if downs == 1:
        load_down = [local(14 + 4 * slabs, down_refs[0], w_dn)]
        down_last = []
    else:
        part_rows = units // line

        def down_at(source):
            return w_dn.at[pl.ds(pl.multiple_of(source * part_rows, 16), part_rows)]

        load_down = [
            local(14 + 4 * slabs + i, ref, down_at((place + line - i) % line))
            for i, ref in enumerate(down_refs)
        ]
        down_last = [remote(DOWN_LAST, down_refs[-1], down_at(last), (me, after))]
    for copy in down_last + slab_on:
        copy.start()
    slot = side * 4 + me
    far_slot, across_slot = side * 4 + beside, (1 - side) * 4 + me
    corner_slot = (1 - side) * 4 + beside
    top_parts = (
        (top_ref, tops.at[slot]),
        (top_far_ref, tops.at[far_slot]),
        (top_across_ref, tops.at[across_slot]),
        (top_corner_ref, tops.at[corner_slot]),
    )
    load_top = [
        local(7 + 4 * slabs + i, source, target) for i, (source, target) in enumerate(top_parts)
    ]
    for copy in load_down + load_top:
        copy.start()

    for copy in heads + weight_on:
        copy.wait_recv()
    own_heads.wait()
    for copy in load_out:
        copy.wait()
    top_on = [
        remote(TOP_ON + i, source, target, (mate, at))
        for i, (source, target) in enumerate(top_parts)
    ]
    for copy in top_on:
        copy.start()
    keep_weight = local(base_sem, pairs.at[pl.ds(0, 4 * cols)], w_out_ref)
    keep_weight.start()
    keep_mixed = local(base_sem + 2, mixed, mixed_out)
    keep_mixed.start()

    def resid_cols(step, carry):
        span = pl.ds(pl.multiple_of(step * 256, 256), 256)
        weight = pairs[0 : 4 * cols, span]
        resid[:, span] = tokens_ref[:, span].astype(F32) + nn(mixed[...], weight)
        return carry

    lax.fori_loop(0, width // 256, resid_cols, 0)

    def norm_tile(step, carry):
        tile = pl.ds(pl.multiple_of(step * 32, 32), 32)
        block = resid[tile, :]
        scale = lax.rsqrt(jnp.mean(block * block, axis=1, keepdims=True) + EPS)
        acts[slot, tile, :] = (block * scale * gain_ref[...]).astype(BF)
        return carry

    lax.fori_loop(0, rows // 32, norm_tile, 0)
    keep_resid = local(base_sem + 3, resid, resid_out)
    keep_resid.start()

    near = remote(NEAR, acts.at[slot], acts.at[slot], (mate, at))
    far = remote(FAR, acts.at[slot], acts.at[slot], (beside, at))
    across = remote(ACROSS, acts.at[slot], acts.at[slot], (me, other))
    far_on = remote(FAR_ON, acts.at[far_slot], acts.at[far_slot], (mate, at))
    across_on = remote(ACROSS_ON, acts.at[across_slot], acts.at[across_slot], (mate, at))
    corner_on = remote(CORNER_ON, acts.at[corner_slot], acts.at[corner_slot], (mate, at))
    far_top = acts.at[far_slot, pl.ds(0, half)]
    across_low = acts.at[across_slot, pl.ds(half, half)]
    corner_top = remote(CORNER_TOP, far_top, far_top, (me, other))
    corner_low = remote(CORNER_LOW, across_low, across_low, (beside, at))
    near.start()
    far.start()
    across.start()
    for copy in load_down + load_top + [keep_weight]:
        copy.wait()
    for copy in down_last + top_on:
        copy.wait_recv()

    def hidden_back(step, carry):
        for first, size in SPANS:
            grad = nt(
                tops[pl.ds(2 * step, 2)].reshape(2 * rows, width),
                w_dn[first : first + size, :],
            )
            grad_gu[pl.ds(2 * step, 2), :, units + first : units + first + size] = (
                grad.astype(BF).reshape(2, rows, size)
            )
        return carry

    lax.fori_loop(0, 4, hidden_back, 0)
    far.wait_recv()
    far_on.start()
    corner_top.start()
    across.wait_recv()
    across_on.start()
    corner_low.start()
    for copy in load_slabs:
        copy.wait()
    for copy in slab_on:
        copy.wait_recv()

    def pair_rows(index, first=0, size=rows):
        return pl.ds(pl.multiple_of(index * rows + first, 16), size)

    def to_mate(c):
        return remote(
            TO_MATE + c, pairs.at[pair_rows(2 * c + 1 - odd)], got.at[c], (mate, at)
        )

    def keep_part(c):
        return local(base_sem + 4, stage.at[odd], part_out.at[c])

    def part_on(c):
        return remote(OUT_MATE + c, stage.at[1 - odd], part_in.at[c], (mate, at))

    def chunk(c, carry):
        its_side = (side + c // 2) % 2
        its_head = (me + 2 * (c % 2)) % 4
        pair = its_side * 4 + its_head - its_head % 2

        @pl.when(c == 0)
        def _():
            near.wait_recv()

        @pl.when(c == 1)
        def _():
            far_on.wait_recv()

        @pl.when(c == 2)
        def _():
            corner_top.wait_recv()
            corner_low.wait_recv()
            corner_on.start()
            across_on.wait_recv()

        @pl.when(c == 3)
        def _():
            corner_on.wait_recv()

        for first, size in SPANS:
            block = acts[pl.ds(pair, 2)].reshape(2 * rows, width)
            gate = nn(block, w_gu[:, first : first + size])
            up = nn(block, w_gu[:, units + first : units + first + size])
            grad = grad_gu[pl.ds(pair, 2), :, units + first : units + first + size]
            grad = grad.reshape(2 * rows, size).astype(F32)
            sig = jax.nn.sigmoid(gate)
            silu = gate * sig
            shape = (2, rows, size)
            hidden[pl.ds(pair, 2), :, first : first + size] = (
                (silu * up).astype(BF).reshape(shape)
            )
            grad_gu[pl.ds(pair, 2), :, first : first + size] = (
                (grad * up * sig * (1 + gate * (1 - sig))).astype(BF).reshape(shape)
            )
            grad_gu[pl.ds(pair, 2), :, units + first : units + first + size] = (
                (grad * silu).astype(BF).reshape(shape)
            )

        def grad_cols(step, carry):
            span = pl.ds(pl.multiple_of(step * 256, 256), 256)
            block = grad_gu[pl.ds(pair, 2)].reshape(2 * rows, 2 * units)
            part = nt(block, w_gu[span, :])
            pairs[pl.ds(pl.multiple_of(2 * c * rows, 128), 2 * rows), span] = part.astype(BF)
            return carry

        lax.fori_loop(0, width // 256, grad_cols, 0)
        to_mate(c).start()

        @pl.when(c > 0)
        def _():
            keep_part(c - 1).wait()
            part_on(c - 1).wait_send()

        def out_cols(step, carry):
            span = pl.ds(pl.multiple_of(step * 256, 256), 256)
            block = hidden[pl.ds(pair, 2)].reshape(2 * rows, units)
            part = nn(block, w_dn[:, span])
            stage[:, :, span] = part.astype(BF).reshape(2, rows, 256)
            return carry

        lax.fori_loop(0, width // 256, out_cols, 0)
        keep_part(c).start()
        part_on(c).start()
        return carry

    lax.fori_loop(0, 4, chunk, 0)

    def add_rows(c, first, extra):
        def tile(step, carry):
            span = pl.ds(pl.multiple_of(first + step * 32, 32), 32)
            mine = pair_rows(2 * c + odd, first + step * 32, 32)
            total = pairs[mine, :].astype(F32) + got[c, span, :].astype(F32)
            for ref in extra:
                total = total + ref[pl.ds(pl.multiple_of(step * 32, 32), 32), :].astype(F32)
            pairs[mine, :] = total.astype(BF)
            return carry

        lax.fori_loop(0, half // 32, tile, 0)

    back_top = remote(
        BACK_TOP, pairs.at[pair_rows(6 + odd, 0, half)], in_top, (me, other)
    )
    back_low = remote(
        BACK_LOW, pairs.at[pair_rows(6 + odd, half, half)], in_low, (beside, at)
    )
    back_far = remote(BACK_FAR, pairs.at[pair_rows(2 + odd)], in_far, (beside, at))
    back_across = remote(BACK_ACROSS, pairs.at[pair_rows(4 + odd)], in_across, (me, other))
    to_mate(3).wait_recv()
    add_rows(3, 0, ())
    back_top.start()
    add_rows(3, half, ())
    back_low.start()
    to_mate(1).wait_recv()
    to_mate(2).wait_recv()
    add_rows(1, half, ())
    add_rows(2, 0, ())

    keep_part(3).wait()
    part_on(3).wait_send()

    def gu_rows(step, carry):
        span = pl.ds(pl.multiple_of(step * 256, 256), 256)
        turned[...] = transposed(acts[:, :, span].reshape(8 * rows, 256))
        buffer = step % 2

        @pl.when(step > 1)
        def _():
            local(base_sem + 5 + buffer, gu_stage.at[buffer], gu_out.at[pl.ds(0, 256)]).wait()

        for n in range(2 * units // 256):
            part = nn(
                turned[...],
                grad_gu[:, :, n * 256 : (n + 1) * 256].reshape(8 * rows, 256),
            )
            gu_stage[buffer, :, n * 256 : (n + 1) * 256] = part.astype(BF)
        local(base_sem + 5 + buffer, gu_stage.at[buffer], gu_out.at[span]).start()
        return carry

    lax.fori_loop(0, 5, gu_rows, 0)
    back_top.wait_recv()
    add_rows(1, 0, (in_top,))
    back_far.start()
    back_low.wait_recv()
    add_rows(2, half, (in_low,))
    back_across.start()
    lax.fori_loop(5, width // 256, gu_rows, 0)
    for buffer in range(2):
        local(base_sem + 5 + buffer, gu_stage.at[buffer], gu_out.at[pl.ds(0, 256)]).wait()

    target = (place + line - 1) % line
    sum_on = [
        remote(
            SUM_ON + h,
            gu_out.at[pl.ds(pl.multiple_of((h * line + target) * slab_rows, 16), slab_rows)],
            gu_next.at[h],
            (me, after),
        )
        for h in range(4)
    ]
    for copy in sum_on:
        copy.start()

    for copy in (near, far, across, far_on, across_on, corner_on, corner_top, corner_low):
        copy.wait_send()
    load_again = [
        local(1 + i, w_out_ref.at[pl.ds(i * rows, rows)], acts.at[i]) for i in range(6)
    ]
    for copy in load_again:
        copy.start()

    for i, (first, size) in enumerate(SPANS):
        turned[0:size, :] = transposed(
            hidden[:, :, first : first + size].reshape(8 * rows, size)
        )
        buffer = i % 2
        if i > 1:
            local(base_sem + 7, stage.at[0], down_out.at[pl.ds(0, rows)]).wait()

        def down_cols(step, carry):
            span = pl.ds(pl.multiple_of(step * 256, 256), 256)
            part = nn(turned[0:size, :], tops[:, :, span].reshape(8 * rows, 256))
            stage[buffer, 0:size, span] = part.astype(BF)
            return carry

        lax.fori_loop(0, width // 256, down_cols, 0)
        local(
            base_sem + 7 + buffer,
            stage.at[buffer, pl.ds(0, size)],
            down_out.at[pl.ds(first, size)],
        ).start()

    to_mate(0).wait_recv()
    back_far.wait_recv()
    back_across.wait_recv()
    keep_resid.wait()
    gain_out[...] = jnp.zeros_like(gain_out)
    low = got.at[0]

    def norm_back(step, carry):
        tile = pl.ds(pl.multiple_of(step * 32, 32), 32)
        grad = (
            pairs[pair_rows(odd, step * 32, 32), :].astype(F32)
            + got[0, tile, :].astype(F32)
            + in_far[tile, :].astype(F32)
            + in_across[tile, :].astype(F32)
        )
        block = resid[tile, :]
        scale = lax.rsqrt(jnp.mean(block * block, axis=1, keepdims=True) + EPS)
        gain_out[...] += jnp.sum(grad * block * scale, axis=0, keepdims=True)
        inner = grad * gain_ref[...]
        mean = jnp.mean(inner * block, axis=1, keepdims=True)
        total = (
            tops[slot, tile, :].astype(F32)
            + scale * inner
            - block * (scale * scale * scale * mean)
        )
        resid[tile, :] = total
        low[tile, :] = total.astype(BF)
        return carry

    lax.fori_loop(0, rows // 32, norm_back, 0)
    keep_grad = local(base_sem + 3, resid, grad_out)
    keep_grad.start()
    keep_low = local(base_sem + 4, low, grad_low_out)
    keep_low.start()
    keep_mixed.wait()
    for copy in load_again:
        copy.wait()

    def heads_cols(step, carry):
        span = pl.ds(pl.multiple_of(step * 256, 256), 256)
        turned[:, span] = nt(low[...], acts[step]).astype(BF)
        return carry

    lax.fori_loop(0, 6, heads_cols, 0)

    def grad_cols_of(head):
        return turned.at[:, pl.ds(pl.multiple_of(head * cols, 128), cols)]

    heads_on = [
        remote(HEADS_BACK + i, grad_cols_of(to), heads_out.at[me], (to, at))
        for i, to in enumerate((mate, beside, corner))
    ]
    for copy in heads_on:
        copy.start()
    own_back = local(0, grad_cols_of(me), heads_out.at[me])
    own_back.start()

    for c in range(4):
        part_on(c).wait_recv()
    load_parts = [
        local(1, part_out, tops.at[pl.ds(0, 4)]),
        local(2, part_in, tops.at[pl.ds(4, 4)]),
    ]
    for copy in load_parts:
        copy.start()

    for c in range(4):
        to_mate(c).wait_send()
    for copy in (back_top, back_low, back_far, back_across):
        copy.wait_send()

    def weight_rows(step, carry):
        span = pl.ds(pl.multiple_of(step * 256, 256), 256)
        left = transposed(mixed[:, span])
        for n in range(width // 512):
            part = nn(left, low[:, n * 512 : (n + 1) * 512])
            pairs[span, n * 512 : (n + 1) * 512] = part.astype(BF)
        return carry

    lax.fori_loop(0, 6, weight_rows, 0)
    weight_back = [
        remote(WEIGHT_BACK, w_rows_of(mate), weight_in.at[0], (mate, at)),
        remote(WEIGHT_BACK + 1, w_rows_of(corner), weight_in.at[1], (mate, at)),
    ]
    keep_back = [
        local(3, w_rows_of(me), weight_own.at[0]),
        local(4, w_rows_of(beside), weight_own.at[1]),
    ]
    for copy in weight_back + keep_back:
        copy.start()
    for copy in load_parts:
        copy.wait()

    def add_out(step, carry):
        tile = pl.ds(pl.multiple_of(step % (rows // 32) * 32, 32), 32)
        c = step // (rows // 32)
        total = tops[c, tile, :].astype(F32) + tops[c + 4, tile, :].astype(F32)
        tops[c, tile, :] = total.astype(BF)
        return carry

    lax.fori_loop(0, 4 * rows // 32, add_out, 0)
    keep_sums = [
        local(7 + c, tops.at[c], ref)
        for c, ref in enumerate((sum_own, sum_far, sum_across, sum_corner))
    ]
    for copy in keep_sums:
        copy.start()
    for copy in weight_back + keep_back + keep_sums:
        copy.wait()

    own_back.wait()
    keep_grad.wait()
    keep_low.wait()
    local(base_sem + 7, stage.at[0, pl.ds(0, SPANS[2][1])], down_out.at[pl.ds(0, SPANS[2][1])]).wait()
    local(base_sem + 8, stage.at[1], down_out.at[pl.ds(0, rows)]).wait()
    for copy in heads_on + sum_on:
        copy.wait()
    for copy in heads + slab_on + down_last:
        copy.wait_send()
    for copy in weight_on + top_on:
        copy.wait_send()


def middle(attn_out, tokens, w_own, w_far, gain, tops, slabs, downs):
    rows, width = tokens.shape
    units = slabs[0].shape[2] // 2
    cols = attn_out.shape[2]
    line = lax.axis_size("blk") // 2
    slab_shape = slabs[0].shape
    anywhere = pl.BlockSpec(memory_space=pl.ANY)
    vmem = pl.BlockSpec(memory_space=pltpu.VMEM)
    shape = jax.ShapeDtypeStruct
    eight, four = (8, rows, width), (4, rows, width)
    return pl.pallas_call(
        functools.partial(middle_kernel, len(slabs), len(downs), line),
        out_shape=(
            shape((rows, width), F32),
            shape((rows, width), F32),
            shape((rows, width), BF),
            shape((rows, 4 * cols), BF),
            shape(attn_out.shape, BF),
            shape(four, BF),
            shape(four, BF),
            shape((4 * cols, width), BF),
            shape((width, 2 * units), BF),
            shape(slab_shape, BF),
            shape((units, width), BF),
            shape((2, cols, width), BF),
            shape((2, cols, width), BF),
            shape((rows, width), BF),
            shape((rows, width), BF),
            shape((rows, width), BF),
            shape((rows, width), BF),
            shape((1, width), F32),
        ),
        in_specs=[anywhere, vmem, anywhere, anywhere, vmem]
        + [anywhere] * (len(tops) + len(slabs) + len(downs)),
        out_specs=(anywhere,) * 17 + (vmem,),
        scratch_shapes=[
            pltpu.VMEM((rows, 4 * cols), BF),
            pltpu.VMEM(eight, BF),
            pltpu.VMEM(eight, BF),
            pltpu.VMEM((width, 2 * units), BF),
            pltpu.VMEM((units, width), BF),
            pltpu.VMEM((8, rows, units), BF),
            pltpu.VMEM((8, rows, 2 * units), BF),
            pltpu.VMEM((8 * rows, width), BF),
            pltpu.VMEM(four, BF),
            pltpu.VMEM((2, rows, width), BF),
            pltpu.VMEM((rows, width), BF),
            pltpu.VMEM((rows, width), BF),
            pltpu.VMEM((rows // 2, width), BF),
            pltpu.VMEM((rows // 2, width), BF),
            pltpu.VMEM((rows, width), F32),
            pltpu.VMEM((256, 8 * rows), BF),
            pltpu.VMEM((2, 256, 2 * units), BF),
            pltpu.SemaphoreType.DMA((TRANSFERS,)),
            pltpu.SemaphoreType.DMA((TRANSFERS,)),
            pltpu.SemaphoreType.DMA((24 + 4 * len(slabs) + len(downs),)),
        ],
        compiler_params=pltpu.CompilerParams(
            collective_id=1, has_side_effects=True, vmem_limit_bytes=60 << 20
        ),
        cost_estimate=pl.CostEstimate(
            flops=60_000_000_000, bytes_accessed=100_000_000, transcendentals=2_000_000
        ),
        name="middle",
    )(attn_out, tokens, w_own, w_far, gain, *tops, *slabs, *downs)


TOK_NEAR, TOK_FAR, TOK_ON, IN_QUERY, IN_REST = 0, 1, 2, 3, 6
TOP_FAR = 9
UNITS_MOVE, SLAB_ON, DOWN_ON = 11, 18, 19
KV_ONE, KV_TWO, KV_PAIR_ONE, KV_PAIR_TWO, FIRST_TRANSFERS = 20, 22, 24, 26, 28
COLS_Q = QHEADS // 4 * HEAD
COLS_IN = COLS_Q + 4 * HEAD


def head_scale(block):
    low = lanes(block.shape) < HEAD
    square = block * block
    first = jnp.sum(jnp.where(low, square, 0.0), axis=1, keepdims=True)
    second = jnp.sum(jnp.where(low, 0.0, square), axis=1, keepdims=True)
    return jnp.where(
        low, lax.rsqrt(first / HEAD + EPS), lax.rsqrt(second / HEAD + EPS)
    )


def swap_halves(block):
    low = lanes(block.shape) % HEAD < HEAD // 2
    return jnp.where(low, pltpu.roll(block, 96, 1), pltpu.roll(block, 32, 1))


def first_kernel(
    line,
    tokens_ref,
    query_ref,
    rest_ref,
    gate_ref,
    up_ref,
    down_ref,
    w_out_ref,
    top_ref,
    cos_ref,
    sin_ref,
    query_gain_ref,
    key_gain_ref,
    wide_out,
    query_out,
    kv_out,
    raw_out,
    normed_out,
    w_in_out,
    top_far_out,
    w_out_all,
    slab_out,
    slab_next,
    down_next,
    toks_out,
    gain_out,
    toks,
    normed,
    w_in,
    raw,
    wide,
    query,
    kv_own,
    gate,
    up,
    blocks,
    sends,
    recvs,
    ring_sends,
    ring_recvs,
    swap_sends,
    swap_recvs,
    out_ring_sends,
    out_ring_recvs,
    out_swap_sends,
    out_swap_recvs,
    locals_,
):
    me, at = lax.axis_index("head"), lax.axis_index("blk")
    count = lax.axis_size("blk")
    side, place = at % 2, at // 2
    odd = me % 2
    mate, beside, corner = me + 1 - 2 * odd, (me + 2) % 4, (me + 3 - 2 * odd) % 4
    other = at + 1 - 2 * side
    after, before = (at + 2) % count, (at + count - 2) % count
    rows, width = tokens_ref.shape
    half = rows // 2
    w_rows = query_ref.shape[0]
    units = slab_out.shape[2] // 2

    barrier = pltpu.get_barrier_semaphore()
    peers = [(mate, at), (beside, at), (corner, at), (me, after), (me, before)]
    peers += [(head, other) for head in (me, mate, beside, corner)]
    for peer in peers:
        pl.semaphore_signal(barrier, inc=1, device_id=peer, device_id_type=MESH)
    pl.semaphore_wait(barrier, len(peers))

    def remote(index, source, target, device, send=sends, recv=recvs):
        return pltpu.make_async_remote_copy(
            src_ref=source,
            dst_ref=target,
            send_sem=send.at[index],
            recv_sem=recv.at[index],
            device_id=device,
            device_id_type=MESH,
        )

    def local(index, source, target):
        return pltpu.make_async_copy(source, target, locals_.at[index])

    def cols_of(ref, start, size):
        return ref.at[:, pl.ds(pl.multiple_of(start, 128), size)]

    own_q = w_in.at[me, at, :, pl.ds(0, COLS_Q)]
    own_rest = w_in.at[me, at, :, pl.ds(COLS_Q, COLS_Q)]
    split = []
    for i, to in enumerate((mate, beside, corner)):
        split.append(
            remote(IN_QUERY + i, cols_of(query_ref, to * COLS_Q, COLS_Q), own_q, (to, at))
        )
        split.append(remote(IN_REST + i, rest_ref.at[to], own_rest, (to, at)))
    for copy in split:
        copy.start()
    own = [
        local(0, cols_of(query_ref, me * COLS_Q, COLS_Q), own_q),
        local(1, rest_ref.at[me], own_rest),
        local(2, tokens_ref, toks.at[me]),
        local(3, w_out_ref, w_out_all.at[at]),
    ]
    for copy in own:
        copy.start()
    tok_near = remote(TOK_NEAR, tokens_ref, toks.at[me], (mate, at))
    tok_far = remote(TOK_FAR, tokens_ref, toks.at[me], (beside, at))
    tok_on = remote(TOK_ON, toks.at[beside], toks.at[beside], (mate, at))
    tok_far.start()
    tok_near.start()
    down_on = remote(DOWN_ON, down_ref, down_next, (me, after))
    down_on.start()
    own_units = [local(4, gate_ref, gate), local(5, up_ref, up)]
    for copy in own_units:
        copy.start()

    def ring_copy(step):
        block = w_in.at[:, (at + count - 2 * (step - 1)) % count]
        return remote(step, block, block, (me, after), ring_sends, ring_recvs)

    def swap_copy(step):
        block = w_in.at[:, (at + count - 2 * step) % count]
        return remote(step, block, block, (me, other), swap_sends, swap_recvs)

    def out_ring(step):
        index = (at + count - 2 * (step - 1)) % count
        source = w_out_ref if step == 1 else w_out_all.at[index]
        return remote(
            step, source, w_out_all.at[index], (me, after), out_ring_sends, out_ring_recvs
        )

    def out_swap(step):
        index = (at + count - 2 * step) % count
        source = w_out_ref if step == 0 else w_out_all.at[index]
        return remote(
            step, source, w_out_all.at[index], (me, other), out_swap_sends, out_swap_recvs
        )

    out_ring(1).start()
    out_swap(0).start()

    for copy in own_units:
        copy.wait()
    ff_rows = units // line
    for j, ref in enumerate((gate, up)):
        for head in range(4):
            columns = ref[:, 2 * units * head : 2 * units * (head + 1)].astype(F32)
            for to_side in range(2):
                chosen = [
                    columns[:, (2 * z + to_side) * ff_rows : (2 * z + to_side + 1) * ff_rows]
                    for z in range(line)
                ]
                blocks[to_side, head, :, j * units : (j + 1) * units] = jnp.concatenate(
                    chosen, axis=1
                ).astype(BF)
    slab_rows = pl.ds(pl.multiple_of(side * w_rows, 16), w_rows)
    targets = [(side, mate), (side, beside), (side, corner)]
    targets += [(1 - side, head) for head in (me, mate, beside, corner)]
    spread = [
        remote(
            UNITS_MOVE + i,
            blocks.at[to_side, to_head],
            slab_out.at[me, slab_rows],
            (to_head, at if i < 3 else other),
        )
        for i, (to_side, to_head) in enumerate(targets)
    ]
    for copy in spread:
        copy.start()
    own_block = local(6, blocks.at[side, me], slab_out.at[me, slab_rows])
    own_block.start()
    for copy in split:
        copy.wait_recv()
    own[0].wait()
    own[1].wait()
    ring_copy(1).start()
    swap_copy(0).start()
    tok_far.wait_recv()
    tok_on.start()
    top_far = remote(TOP_FAR, top_ref, top_far_out, (beside, at))
    top_far.start()
    for step in range(1, line):
        ring_copy(step).wait_recv()
        if step < line - 1:
            ring_copy(step + 1).start()
        swap_copy(step).start()
        out_ring(step).wait_recv()
        if step < line - 1:
            out_ring(step + 1).start()

    for copy in spread:
        copy.wait_recv()
    own_block.wait()
    slab_on = remote(SLAB_ON, slab_out, slab_next, (me, after))
    slab_on.start()
    tok_near.wait_recv()
    tok_on.wait_recv()
    own[2].wait()
    own[3].wait()
    for step in range(line):
        swap_copy(step).wait_recv()
    for step in range(1, line):
        out_swap(step).start()
    keep_in = [
        local(7 + h, w_in.at[h], w_in_out.at[h]) for h in range(4)
    ]
    for copy in keep_in:
        copy.start()

    gains = w_in[:, :, :, COLS_IN : COLS_IN + 128].reshape(width, 128).astype(F32)
    gain_out[...] = transposed(gains)[0:8, :]

    def norm_tile(step, carry):
        head, tile = step // (rows // 32), pl.ds(pl.multiple_of(step % (rows // 32) * 32, 32), 32)
        block = toks[head, tile, :].astype(F32)
        scale = lax.rsqrt(jnp.mean(block * block, axis=1, keepdims=True) + EPS)
        normed[pl.ds(pl.multiple_of(step * 32, 32), 32), :] = (
            block * scale * gain_out[0:1, :]
        ).astype(BF)
        return carry

    lax.fori_loop(0, 4 * rows // 32, norm_tile, 0)
    keep_normed = local(11, normed, normed_out)
    keep_normed.start()
    keep_toks = local(16, toks, toks_out)
    keep_toks.start()

    def project(spans):
        def tile_of(step, carry):
            tile = pl.ds(pl.multiple_of(step * 256, 256), 256)
            for first, size in spans:
                weight = w_in[:, :, :, first : first + size].reshape(width, size)
                raw[tile, first : first + size] = nn(normed[tile, :], weight)
            return carry

        lax.fori_loop(0, 4 * rows // 256, tile_of, 0)

    def rotated(block, gain, tile):
        block = block * head_scale(block) * gain
        return block * cos_ref[tile, :] + swap_halves(block) * sin_ref[tile, :]

    def prepare_keys(step, carry):
        tile = pl.ds(pl.multiple_of(step * 64, 64), 64)
        first_half = lanes((64, 128)) < HEAD
        keys = rotated(raw[tile, COLS_Q : COLS_Q + 128], key_gain_ref[...], tile)
        values = raw[tile, COLS_Q + 128 : COLS_Q + 256]
        kv_own[0, tile, :] = jnp.where(
            first_half, keys, pltpu.roll(values, HEAD, 1)
        ).astype(BF)
        kv_own[1, tile, :] = jnp.where(
            first_half, pltpu.roll(keys, HEAD, 1), values
        ).astype(BF)
        return carry

    def prepare_queries(step, carry):
        tile = pl.ds(pl.multiple_of(step * 64, 64), 64)
        first_half = lanes((64, 128)) < HEAD
        for t in range(QHEADS // 4 // 2):
            block = rotated(raw[tile, t * 128 : (t + 1) * 128], query_gain_ref[...], tile)
            block = block.astype(BF).astype(F32)
            moved = pltpu.roll(block, HEAD, 1)
            query[2 * t, tile, :] = jnp.where(first_half, block, 0.0).astype(BF)
            query[2 * t + 1, tile, :] = jnp.where(first_half, moved, 0.0).astype(BF)
            scaled = block * (SCALE * LOG2E)
            upper = scaled.astype(BF).astype(F32)
            lower = scaled - upper
            wide[2 * t, tile, :] = jnp.where(
                first_half, upper, pltpu.roll(lower, HEAD, 1)
            ).astype(BF)
            wide[2 * t + 1, tile, :] = jnp.where(
                first_half, pltpu.roll(upper, HEAD, 1), lower
            ).astype(BF)
        return carry

    project(((COLS_Q, 256),))
    lax.fori_loop(0, 4 * rows // 64, prepare_keys, 0)

    def kv_copies(index, source, target, device):
        return [remote(index + g, source(g), kv_out.at[target, g], device) for g in (0, 1)]

    def kv_from(block):
        return lambda g: kv_out.at[block, g]

    def kv_mine(g):
        return kv_own.at[g]

    kv_one = kv_copies(KV_ONE, kv_mine, 2, (me, after))
    kv_two = kv_copies(KV_TWO, kv_from(2), 0, (me, after))
    pair_one_even = kv_copies(KV_PAIR_ONE, kv_mine, 3, (me, other))
    pair_one_odd = kv_copies(KV_PAIR_ONE, kv_from(2), 3, (me, other))
    pair_two_even = kv_copies(KV_PAIR_TWO, kv_from(2), 1, (me, other))
    pair_two_odd = kv_copies(KV_PAIR_TWO, kv_from(0), 1, (me, other))
    for g in (0, 1):
        kv_one[g].start()

    @pl.when(side == 0)
    def _():
        for g in (0, 1):
            pair_one_even[g].start()

    project(((0, 256), (256, 128)))
    keep_raw = local(12, raw.at[:, pl.ds(0, COLS_Q + 128)], raw_out)
    keep_raw.start()
    for g in (0, 1):
        kv_one[g].wait_recv()
        kv_two[g].start()

        @pl.when(side == 0)
        def _(g=g):
            pair_two_even[g].start()

        @pl.when(side == 1)
        def _(g=g):
            pair_one_odd[g].start()

    lax.fori_loop(0, 4 * rows // 64, prepare_queries, 0)
    keep = [
        local(13, kv_own, kv_out.at[4]),
        local(14, wide, wide_out),
        local(15, query, query_out),
    ]
    for copy in keep:
        copy.start()
    for g in (0, 1):
        kv_two[g].wait_recv()

        @pl.when(side == 1)
        def _(g=g):
            pair_two_odd[g].start()

    for g in (0, 1):
        pair_one_even[g].wait_recv()
        pair_two_even[g].wait_recv()
    down_on.wait_recv()
    slab_on.wait_recv()
    top_far.wait_recv()
    for copy in keep + keep_in + [keep_normed, keep_raw, keep_toks]:
        copy.wait()
    for copy in split + spread:
        copy.wait_send()
    for copy in (tok_near, tok_far, tok_on, top_far):
        copy.wait_send()
    for copy in [slab_on, down_on] + kv_one + kv_two + pair_one_even + pair_two_even:
        copy.wait_send()

    for step in range(line):
        swap_copy(step).wait_send()
        out_swap(step).wait()
        if step:
            ring_copy(step).wait_send()
            out_ring(step).wait_send()


def first(
    tokens, w_query, rest, w_gate, w_up, w_down, w_out, cotangent, cosine, sine, query_gain, key_gain
):
    rows, width = tokens.shape
    count = lax.axis_size("blk")
    w_rows, ff = w_gate.shape
    units = ff // 8
    block = 4 * rows
    anywhere = pl.BlockSpec(memory_space=pl.ANY)
    vmem = pl.BlockSpec(memory_space=pltpu.VMEM)
    shape = jax.ShapeDtypeStruct
    heads = QHEADS // 4
    slab = shape((4, 2 * w_rows, 2 * units), BF)
    dma = pltpu.SemaphoreType.DMA
    return pl.pallas_call(
        functools.partial(first_kernel, count // 2),
        out_shape=(
            shape((heads, block, 128), BF),
            shape((heads, block, 128), BF),
            shape((BACK + 1, 2, block, 128), BF),
            shape((block, COLS_Q + 128), F32),
            shape((block, width), BF),
            shape((4, count, w_rows, 2 * COLS_Q), BF),
            shape((rows, width), BF),
            shape((count,) + w_out.shape, BF),
            slab,
            slab,
            shape(w_down.shape, BF),
            shape((4, rows, width), BF),
            shape((8, width), F32),
        ),
        in_specs=[anywhere] * 8 + [vmem] * 4,
        out_specs=(anywhere,) * 12 + (vmem,),
        scratch_shapes=[
            pltpu.VMEM((4, rows, width), BF),
            pltpu.VMEM((block, width), BF),
            pltpu.VMEM((4, count, w_rows, 2 * COLS_Q), BF),
            pltpu.VMEM((block, COLS_IN), F32),
            pltpu.VMEM((heads, block, 128), BF),
            pltpu.VMEM((heads, block, 128), BF),
            pltpu.VMEM((2, block, 128), BF),
            pltpu.VMEM(w_gate.shape, BF),
            pltpu.VMEM(w_up.shape, BF),
            pltpu.VMEM((2, 4, w_rows, 2 * units), BF),
            dma((FIRST_TRANSFERS,)),
            dma((FIRST_TRANSFERS,)),
            dma((count // 2,)),
            dma((count // 2,)),
            dma((count // 2,)),
            dma((count // 2,)),
            dma((count // 2,)),
            dma((count // 2,)),
            dma((count // 2,)),
            dma((count // 2,)),
            dma((17,)),
        ],
        compiler_params=pltpu.CompilerParams(
            collective_id=2, has_side_effects=True, vmem_limit_bytes=48 << 20
        ),
        cost_estimate=pl.CostEstimate(
            flops=60_000_000_000, bytes_accessed=60_000_000, transcendentals=1_000_000
        ),
        name="first",
    )(
        tokens, w_query, rest, w_gate, w_up, w_down, w_out, cotangent, cosine, sine,
        query_gain, key_gain,
    )


THREE, ONE, FOUR_ON, TWO_ON = 0, 2, 4, 6
UNITS_HOME, DOWN_STEP = 8, 15
PART_MATE, PART_CORNER, PART_FAR, QUERY_HOME, REST_HOME = 17, 18, 19, 20, 23
LAST_TRANSFERS = 26


def head_means(block):
    low = lanes(block.shape) < HEAD
    first = jnp.sum(jnp.where(low, block, 0.0), axis=1, keepdims=True)
    second = jnp.sum(jnp.where(low, 0.0, block), axis=1, keepdims=True)
    return jnp.where(low, first, second) * (1.0 / HEAD)


class LineSum:
    def __init__(self, part, got, hold, arrive, sems, places, remote):
        self.part, self.got, self.hold, self.arrive = part, got, hold, arrive
        self.swap_sems, self.ring_sems = sems
        self.side, self.place, self.line, self.other, self.after = places
        self.remote = remote

    def target(self, step):
        return (self.place + self.line - step) % self.line

    def swap(self, step):
        to = self.target(step)
        return self.remote(
            step - 1,
            self.part(2 * to + 1 - self.side),
            self.got.at[to],
            self.other,
            *self.swap_sems,
        )

    def pass_on(self, step):
        return self.remote(
            step - 1, self.hold.at[step - 1], self.arrive.at[step - 1], self.after, *self.ring_sems
        )

    def start(self):
        for step in range(1, self.line + 1):
            self.swap(step).start()

    def step(self, step, out=None):
        to = self.target(step)
        self.swap(step).wait_recv()
        total = self.part(2 * to + self.side)[...].astype(F32) + self.got[to].astype(F32)
        if step > 1:
            self.pass_on(step - 1).wait_recv()
            total = total + self.arrive[step - 2].astype(F32)
        if step < self.line:
            self.hold[step - 1] = total.astype(BF)
            self.pass_on(step).start()
        else:
            out[...] = total.astype(out.dtype)

    def drain(self):
        for step in range(1, self.line + 1):
            self.swap(step).wait_send()
            if step < self.line:
                self.pass_on(step).wait_send()


def last_kernel(
    line,
    dq_four_ref,
    dq_two_ref,
    low_four_ref,
    low_two_ref,
    pair_two_ref,
    own_four_ref,
    own_two_ref,
    pair_four_ref,
    raw_ref,
    cos_ref,
    sin_ref,
    query_gain_ref,
    key_gain_ref,
    normed_ref,
    w_in_ref,
    toks_ref,
    gain_ref,
    gain_two_ref,
    units_ref,
    units_parts_ref,
    down_ref,
    down_parts_ref,
    slab_ref,
    grad_ref,
    dx_out,
    query_out,
    key_out,
    value_out,
    norm_out,
    gate_out,
    up_out,
    down_out,
    w_out_out,
    gains_out,
    low,
    three,
    one,
    four_in,
    two_in,
    raw,
    normed,
    turned,
    w_in,
    toks,
    scales,
    grads,
    query_part,
    rest_part,
    query_got,
    rest_got,
    query_hold,
    rest_hold,
    query_arrive,
    rest_arrive,
    query_sum,
    rest_sum,
    slab,
    slab_got,
    slab_hold,
    slab_arrive,
    units_sum,
    units_in,
    query_in,
    rest_in,
    down_own,
    down_in,
    parts,
    part_got,
    part_far,
    gain_rows,
    head_gains,
    gains_in,
    sends,
    recvs,
    line_sems,
    gain_sends,
    gain_recvs,
    locals_,
):
    me, at = lax.axis_index("head"), lax.axis_index("blk")
    count = lax.axis_size("blk")
    side, place = at % 2, at // 2
    odd = me % 2
    mate, beside, corner = me + 1 - 2 * odd, (me + 2) % 4, (me + 3 - 2 * odd) % 4
    other = at + 1 - 2 * side
    after, before = (at + 2) % count, (at + count - 2) % count
    rows, width = dx_out.shape
    block = 4 * rows
    w_rows = w_in_ref.shape[2]

    rounds = [(mate, at), (beside, at), (me, other)]
    bit = 1
    while bit < line:
        rounds.append((me, at + 2 * bit * (1 - 2 * ((place // bit) % 2))))
        bit *= 2
    barrier = pltpu.get_barrier_semaphore()
    peers = [(corner, at), (me, after), (me, before)]
    peers += [(head, other) for head in (mate, beside, corner)] + rounds
    for peer in peers:
        pl.semaphore_signal(barrier, inc=1, device_id=peer, device_id_type=MESH)

    pl.semaphore_wait(barrier, len(peers))

    def remote(index, source, target, device, send=sends, recv=recvs):
        return pltpu.make_async_remote_copy(
            src_ref=source,
            dst_ref=target,
            send_sem=send.at[index],
            recv_sem=recv.at[index],
            device_id=device,
            device_id_type=MESH,
        )

    def local(index, source, target):
        return pltpu.make_async_copy(source, target, locals_.at[index])

    units_own_part = parts.at[:, pl.ds(0, 2 * w_rows), pl.ds(0, units_ref.shape[2])]
    low_refs, own_refs = (low_four_ref, low_two_ref), (own_four_ref, own_two_ref)
    three_on = remote(THREE, pair_two_ref.at[0], three.at[1], (me, other))
    one_on = remote(ONE, pair_two_ref.at[1], one.at[1], (me, other))
    three_on.start()
    one_on.start()
    low_loads = [local(6 + g, low_refs[g], low.at[g]) for g in (0, 1)]
    pair_loads = [
        local(11, pair_four_ref.at[0], three.at[0]),
        local(12, pair_four_ref.at[1], one.at[0]),
    ]
    for copy in low_loads + pair_loads:
        copy.start()
    loads = [
        local(0, normed_ref, normed),
        local(1, raw_ref, raw),
        local(2, w_in_ref, w_in),
        local(3, toks_ref, toks),
        local(4, slab_ref, slab),
        local(5, down_parts_ref.at[(place + 1) % line], down_own.at[0]),
        local(15, down_parts_ref.at[place], down_own.at[1]),
        local(16, grad_ref, dx_out),
        local(8, units_ref, units_sum),
        local(9, units_parts_ref.at[:, place], units_own_part),
    ]
    for copy in loads:
        copy.start()
    down_on = remote(DOWN_STEP, down_ref, down_in.at[0], (me, after))
    down_on.start()
    down_last = remote(DOWN_STEP + 1, down_own.at[0], down_in.at[1], (me, after))
    targets = [(side, mate), (side, beside), (side, corner)]
    targets += [(1 - side, head) for head in (me, mate, beside, corner)]
    homes = []
    for i, (to_side, to_head) in enumerate(targets):
        device = (to_head, at if i < 3 else other)
        source = units_sum.at[
            to_head, pl.ds(pl.multiple_of(to_side * w_rows, 16), w_rows)
        ]
        homes.append(remote(UNITS_HOME + i, source, units_in.at[side * 4 + me], device))
    units_own = local(
        10,
        units_sum.at[me, pl.ds(pl.multiple_of(side * w_rows, 16), w_rows)],
        units_in.at[side * 4 + me],
    )

    places = (side, place, line, (me, other), (me, after))

    def line_sum(which, part, got, hold, arrive):
        sems = [(line_sems.at[which, i, 0], line_sems.at[which, i, 1]) for i in (0, 1)]
        return LineSum(part, got, hold, arrive, sems, places, remote)

    query_line = line_sum(
        0, lambda b: query_part.at[b], query_got, query_hold, query_arrive
    )
    rest_line = line_sum(1, lambda b: rest_part.at[b], rest_got, rest_hold, rest_arrive)
    slab_line = line_sum(2, lambda b: slab.at[b], slab_got, slab_hold, slab_arrive)

    four_on = [remote(FOUR_ON + g, low.at[g, 0], four_in.at[g], (me, before)) for g in (0, 1)]
    two_on = [remote(TWO_ON + g, low.at[g, 1], two_in.at[g], (me, before)) for g in (0, 1)]

    def add_pair(g):
        def tile_of(step, carry):
            tile = pl.ds(pl.multiple_of(step * 128, 128), 128)
            got_three, got_one = three[g, tile, :].astype(F32), one[g, tile, :].astype(F32)
            to_four = jnp.where(side == 0, 0.0, got_three)
            to_two = jnp.where(side == 0, got_three, got_one)
            low[g, 0, tile, :] = (low[g, 0, tile, :].astype(F32) + to_four).astype(BF)
            low[g, 1, tile, :] = (low[g, 1, tile, :].astype(F32) + to_two).astype(BF)
            return carry

        lax.fori_loop(0, block // 128, tile_of, 0)
        four_on[g].start()

    def add_four(g):
        def tile_of(step, carry):
            tile = pl.ds(pl.multiple_of(step * 128, 128), 128)
            low[g, 1, tile, :] = (
                low[g, 1, tile, :].astype(F32) + four_in[g, tile, :].astype(F32)
            ).astype(BF)
            return carry

        four_on[g].wait_recv()
        lax.fori_loop(0, block // 128, tile_of, 0)
        two_on[g].start()

    for copy in low_loads + pair_loads:
        copy.wait()
    add_pair(0)
    loads[8].wait()
    loads[9].wait()

    def add_units(step, carry):
        head, tile = step // (2 * w_rows // 16), step % (2 * w_rows // 16)
        tile = pl.ds(pl.multiple_of(tile * 16, 16), 16)
        total = units_sum[head, tile, :].astype(F32) + units_own_part[head, tile, :].astype(F32)
        units_sum[head, tile, :] = total.astype(BF)
        return carry

    lax.fori_loop(0, 8 * w_rows // 16, add_units, 0)
    for copy in homes:
        copy.start()
    units_own.start()
    loads[4].wait()
    slab_line.start()

    head_gains[...] = jnp.zeros_like(head_gains)
    gain_rows[...] = jnp.zeros_like(gain_rows)
    loads[0].wait()
    loads[1].wait()

    def head_back(out, cols, tile, gain_tile, gain_row):
        value = raw[tile, cols]
        scale = head_scale(value)
        grad = out * cos_ref[tile, :] + swap_halves(out * sin_ref[tile, :])
        head_gains[0, gain_row : gain_row + 1, :] += jnp.sum(
            grad * value * scale, axis=0, keepdims=True
        )
        inner = grad * gain_tile
        mean = head_means(inner * value)
        return (scale * inner - value * (scale * scale * scale * mean)).astype(BF)

    def query_rows(step, carry):
        tile = pl.ds(pl.multiple_of(step * 64, 64), 64)
        for i in range(3):
            t = odd + i if i < 2 else 2 * (1 - odd)
            cols = pl.ds(pl.multiple_of(t * 128, 128), 128)
            if i < 2:
                out = dq_four_ref[tile, i * 128 : (i + 1) * 128]
            else:
                out = dq_two_ref[tile, :]
            grads[tile, cols] = head_back(out, cols, tile, query_gain_ref[...], 0)
        return carry

    lax.fori_loop(0, block // 64, query_rows, 0)
    three_on.wait_recv()
    one_on.wait_recv()
    add_pair(1)
    add_four(0)
    per_tile = 256 // w_rows
    tiles_per_head = count // per_tile

    def query_weights(step, carry):
        span = pl.ds(pl.multiple_of(step * 256, 256), 256)
        turned[span, :] = transposed(normed[:, span])
        first = pl.ds(step % tiles_per_head * per_tile, per_tile)
        part = nn(turned[span, :], grads[:, 0:COLS_Q])
        query_part[first, step // tiles_per_head] = part.astype(BF).reshape(
            per_tile, w_rows, COLS_Q
        )
        return carry

    lax.fori_loop(0, width // 256, query_weights, 0)
    query_line.start()
    add_four(1)
    slab_line.step(1)

    loads[3].wait()

    def token_scales(step, carry):
        tile = pl.ds(pl.multiple_of(step % (rows // 32) * 32, 32), 32)
        value = toks[step // (rows // 32), tile, :].astype(F32)
        scales[pl.ds(pl.multiple_of(step * 32, 32), 32), :] = lax.rsqrt(
            jnp.mean(value * value, axis=1, keepdims=True) + EPS
        )
        return carry

    lax.fori_loop(0, block // 32, token_scales, 0)
    loads[5].wait()
    down_on.wait_recv()

    def add_down(step, carry):
        span = pl.ds(pl.multiple_of(step * 256, 256), 256)
        down_own[0, :, span] = (
            down_own[0, :, span].astype(F32) + down_in[0, :, span].astype(F32)
        ).astype(BF)
        return carry

    lax.fori_loop(0, width // 256, add_down, 0)
    down_last.start()
    query_line.step(1)
    for copy in two_on:
        copy.wait_recv()

    def key_rows(step, carry):
        tile = pl.ds(pl.multiple_of(step * 64, 64), 64)
        first_half = lanes((64, 128)) < HEAD
        both = []
        for g in (0, 1):
            from_pair = jnp.where(side == 0, one[g, tile, :].astype(F32), 0.0)
            both.append(own_refs[g][tile, :] + from_pair + two_in[g, tile, :].astype(F32))
        zero = jnp.where(odd == 0, both[0], both[1])
        unit = jnp.where(odd == 0, both[1], both[0])
        keys = jnp.where(first_half, zero, pltpu.roll(unit, HEAD, 1))
        values = jnp.where(first_half, pltpu.roll(zero, HEAD, 1), unit)
        cols = pl.ds(COLS_Q, 128)
        grads[tile, cols] = head_back(keys, cols, tile, key_gain_ref[...], 1)
        grads[tile, COLS_Q + 128 : COLS_Q + 256] = values.astype(BF)
        return carry

    lax.fori_loop(0, block // 64, key_rows, 0)

    def gain_round(i):
        return remote(i, head_gains.at[i], gains_in.at[i], rounds[i], gain_sends, gain_recvs)

    def gain_step(i):
        if 0 <= i < len(rounds):
            gain_round(i).wait_recv()
            head_gains[i + 1] = head_gains[i] + gains_in[i]
        if i + 1 < len(rounds):
            gain_round(i + 1).start()

    gain_step(-1)

    loads[2].wait()

    def token_cols(step, carry):
        span = pl.ds(pl.multiple_of(step * 256, 256), 256)
        first = pl.ds(step % tiles_per_head * per_tile, per_tile)
        weight = w_in[step // tiles_per_head, first, :, 0:COLS_IN].reshape(256, COLS_IN)
        part = nt(grads[...], weight)
        parts[:, :, span] = part.astype(BF).reshape(4, rows, 256)
        value = toks[:, :, span].reshape(block, 256).astype(F32)
        gain_rows[0:1, span] = jnp.sum(part * value * scales[...], axis=0, keepdims=True)
        return carry

    lax.fori_loop(0, width // 256, token_cols, 0)
    to_mate = [
        remote(PART_CORNER, parts.at[corner], part_got.at[1], (mate, at)),
        remote(PART_MATE, parts.at[mate], part_got.at[0], (mate, at)),
    ]
    for copy in to_mate:
        copy.start()
    gain_rows[1:2, :] = gain_two_ref[...]

    def rest_weights(step, carry):
        span = pl.ds(pl.multiple_of(step * 256, 256), 256)
        first = pl.ds(step % tiles_per_head * per_tile, per_tile)
        head = step // tiles_per_head
        part = nn(turned[span, :], grads[:, COLS_Q : COLS_Q + 256])
        rest_part[first, head, :, 0:256] = part.astype(BF).reshape(per_tile, w_rows, 256)
        gain_cols = transposed(gain_rows[:, span])
        rest_part[first, head, :, 256:384] = gain_cols.astype(BF).reshape(per_tile, w_rows, 128)
        return carry

    lax.fori_loop(0, width // 256, rest_weights, 0)
    rest_line.start()
    gain_step(0)
    to_mate[0].wait_recv()

    def add_part(step, carry):
        tile = pl.ds(pl.multiple_of(step * 32, 32), 32)
        parts[beside, tile, :] = (
            parts[beside, tile, :].astype(F32) + part_got[1, tile, :].astype(F32)
        ).astype(BF)
        return carry

    lax.fori_loop(0, rows // 32, add_part, 0)
    part_on = remote(PART_FAR, parts.at[beside], part_far, (beside, at))
    part_on.start()

    query_line.step(2, query_sum)
    slab_line.step(2, w_out_out)

    loads[6].wait()
    down_last.wait_recv()

    def down_rows(step, carry):
        span = pl.ds(pl.multiple_of(step * 256, 256), 256)
        down_out[:, span] = down_own[1, :, span].astype(F32) + down_in[1, :, span].astype(F32)
        return carry

    lax.fori_loop(0, width // 256, down_rows, 0)
    gain_step(1)
    for step in range(3, line + 1):
        query_line.step(step, query_sum)
    query_home = [
        remote(QUERY_HOME + i, query_sum.at[to], query_in.at[me], (to, at))
        for i, to in enumerate((mate, beside, corner))
    ]
    query_own = local(13, query_sum.at[me], query_in.at[me])
    for copy in query_home:
        copy.start()
    query_own.start()
    for copy in homes:
        copy.wait()
    units_own.wait()
    units = units_ref.shape[2] // 2
    ff_rows = units // line
    for j, out in enumerate((gate_out, up_out)):
        for head in range(4):
            sides = [
                units_in[4 * of_side + head, :, j * units : (j + 1) * units].astype(F32)
                for of_side in range(2)
            ]
            pieces = [
                sides[p % 2][:, p // 2 * ff_rows : (p // 2 + 1) * ff_rows]
                for p in range(2 * line)
            ]
            out[:, 2 * units * head : 2 * units * (head + 1)] = jnp.concatenate(pieces, axis=1)
    gain_step(2)
    rest_line.step(1)
    for step in range(2, line + 1):
        if step > 2:
            slab_line.step(step, w_out_out)
        rest_line.step(step, rest_sum)
        gain_step(step + 1)
    rest_home = [
        remote(REST_HOME + i, rest_sum.at[to], rest_in.at[me], (to, at))
        for i, to in enumerate((mate, beside, corner))
    ]
    rest_own = local(14, rest_sum.at[me], rest_in.at[me])
    for copy in rest_home:
        copy.start()
    rest_own.start()
    for i in range(line + 2, len(rounds)):
        gain_step(i)
    gains_out[...] = head_gains[len(rounds)]

    to_mate[1].wait_recv()
    part_on.wait_recv()
    loads[7].wait()

    def norm_back(step, carry):
        tile = pl.ds(pl.multiple_of(step * 32, 32), 32)
        grad = (
            parts[me, tile, :].astype(F32)
            + part_got[0, tile, :].astype(F32)
            + part_far[tile, :].astype(F32)
        )
        value = toks[me, tile, :].astype(F32)
        scale = lax.rsqrt(jnp.mean(value * value, axis=1, keepdims=True) + EPS)
        inner = grad * gain_ref[0:1, :]
        mean = jnp.mean(inner * value, axis=1, keepdims=True)
        dx_out[tile, :] += scale * inner - value * (scale * scale * scale * mean)
        return carry

    lax.fori_loop(0, rows // 32, norm_back, 0)

    for copy in query_home:
        copy.wait()
    query_own.wait()
    for g in range(4):
        query_out[:, g * COLS_Q : (g + 1) * COLS_Q] = query_in[g].astype(F32)
    for copy in rest_home:
        copy.wait()
    rest_own.wait()
    first_half = lanes((w_rows, 128)) < HEAD
    for j, out in enumerate((key_out, value_out)):
        tiles = [rest_in[g, :, j * 128 : (j + 1) * 128].astype(F32) for g in range(4)]
        moved = [pltpu.roll(tile, HEAD, 1) for tile in tiles]
        out[:, 0:128] = tiles[0] + jnp.where(first_half, 0.0, moved[1])
        out[:, 128:256] = jnp.where(first_half, moved[1], moved[2])
        out[:, 256:384] = tiles[3] + jnp.where(first_half, moved[2], 0.0)
    norm_out[...] = (
        rest_in[0, :, 256:384].astype(F32)
        + rest_in[1, :, 256:384].astype(F32)
        + rest_in[2, :, 256:384].astype(F32)
        + rest_in[3, :, 256:384].astype(F32)
    )
    for copy in four_on + two_on + to_mate:
        copy.wait_send()
    for copy in (three_on, one_on, down_on, down_last, part_on):
        copy.wait_send()
    for total in (query_line, rest_line, slab_line):
        total.drain()
    for i in range(len(rounds)):
        gain_round(i).wait_send()


def last(
    dq, dkv_low, pair_two, dkv_own, pair_four, raw, cosine, sine, query_gain, key_gain, normed, w_in, toks,
    gains, gain_two, units, units_parts, down, down_parts, slab, grad,
):
    _, rows, width = toks.shape
    _, count, w_rows, _ = w_in.shape
    line = count // 2
    block = 4 * rows
    anywhere = pl.BlockSpec(memory_space=pl.ANY)
    vmem = pl.BlockSpec(memory_space=pltpu.VMEM)
    shape = jax.ShapeDtypeStruct
    dma = pltpu.SemaphoreType.DMA
    rounds = 3 + int(math.log2(line))
    part = (4, w_rows, COLS_Q)
    out_rows = slab.shape[1]
    return pl.pallas_call(
        functools.partial(last_kernel, line),
        out_shape=(
            shape((rows, width), F32),
            shape((w_rows, 4 * COLS_Q), F32),
            shape((w_rows, KVHEADS * HEAD), F32),
            shape((w_rows, KVHEADS * HEAD), F32),
            shape((w_rows, 128), F32),
            shape((w_rows, 4 * units.shape[2]), F32),
            shape((w_rows, 4 * units.shape[2]), F32),
            shape(down.shape, F32),
            shape((out_rows, width), F32),
            shape((8, 128), F32),
        ),
        in_specs=[vmem] * 2 + [anywhere] * 3 + [vmem] * 2 + [anywhere] * 2 + [vmem] * 4
        + [anywhere] * 3 + [vmem] * 2 + [anywhere] * 6,
        out_specs=(vmem,) * 10,
        scratch_shapes=[
            pltpu.VMEM((2, 2, block, 128), BF),
            pltpu.VMEM((2, block, 128), BF),
            pltpu.VMEM((2, block, 128), BF),
            pltpu.VMEM((2, block, 128), BF),
            pltpu.VMEM((2, block, 128), BF),
            pltpu.VMEM((block, COLS_Q + 128), F32),
            pltpu.VMEM((block, width), BF),
            pltpu.VMEM((width, block), BF),
            pltpu.VMEM(w_in.shape, BF),
            pltpu.VMEM(toks.shape, BF),
            pltpu.VMEM((block, 1), F32),
            pltpu.VMEM((block, COLS_IN), BF),
            pltpu.VMEM((count, 4, w_rows, COLS_Q), BF),
            pltpu.VMEM((count, 4, w_rows, COLS_Q), BF),
            pltpu.VMEM((line,) + part, BF),
            pltpu.VMEM((line,) + part, BF),
            pltpu.VMEM((line - 1,) + part, BF),
            pltpu.VMEM((line - 1,) + part, BF),
            pltpu.VMEM((line - 1,) + part, BF),
            pltpu.VMEM((line - 1,) + part, BF),
            pltpu.VMEM(part, BF),
            pltpu.VMEM(part, BF),
            pltpu.VMEM(slab.shape, BF),
            pltpu.VMEM((line,) + slab.shape[1:], BF),
            pltpu.VMEM((line - 1,) + slab.shape[1:], BF),
            pltpu.VMEM((line - 1,) + slab.shape[1:], BF),
            pltpu.VMEM(units.shape, BF),
            pltpu.VMEM((8, w_rows, units.shape[2]), BF),
            pltpu.VMEM(part, BF),
            pltpu.VMEM(part, BF),
            pltpu.VMEM((2,) + down.shape, BF),
            pltpu.VMEM((2,) + down.shape, BF),
            pltpu.VMEM((4, rows, width), BF),
            pltpu.VMEM((2, rows, width), BF),
            pltpu.VMEM((rows, width), BF),
            pltpu.VMEM((128, width), F32),
            pltpu.VMEM((rounds + 1, 8, 128), F32),
            pltpu.VMEM((rounds, 8, 128), F32),
            dma((LAST_TRANSFERS,)),
            dma((LAST_TRANSFERS,)),
            dma((3, 2, 2, line)),
            dma((rounds,)),
            dma((rounds,)),
            dma((17,)),
        ],
        compiler_params=pltpu.CompilerParams(
            collective_id=3, has_side_effects=True, vmem_limit_bytes=58 << 20
        ),
        cost_estimate=pl.CostEstimate(
            flops=60_000_000_000, bytes_accessed=60_000_000, transcendentals=1_000_000
        ),
        name="last",
    )(
        *dq, *dkv_low, pair_two, *dkv_own, pair_four, raw, cosine, sine, query_gain, key_gain, normed, w_in,
        toks, gains, gain_two, units, units_parts, down, down_parts, slab, grad,
    )


def shards(
    tokens,
    doc_lengths,
    norm1_gain,
    w_query,
    w_key,
    w_value,
    query_gain,
    key_gain,
    w_out,
    norm2_gain,
    w_gate,
    w_up,
    w_down,
    cotangent,
):
    tok_rows, width = tokens.shape
    blocks = lax.axis_size("blk")
    groups = lax.axis_size("head")
    group_id = lax.axis_index("head")
    blk_place = lax.axis_index("blk")
    block_len = groups * tok_rows
    per_group = QHEADS // groups
    head_ratio = QHEADS // KVHEADS
    w_rows = w_query.shape[0]
    line = blocks // 2
    side = blk_place % 2
    ff_rows = w_down.shape[0]
    ff_cols = line * ff_rows
    q_cols = per_group * HEAD
    firsts = [g * per_group // head_ratio for g in range(groups)]
    odd = group_id % 2

    starts = jnp.cumsum(doc_lengths) - doc_lengths
    offsets = jnp.arange(block_len, dtype=jnp.int32)
    token_pos = blk_place * block_len + offsets
    inside = starts[None, :] <= token_pos[:, None]
    token_start = jnp.max(jnp.where(inside, starts[None, :], 0), axis=1)
    in_doc = token_pos - token_start
    rope_freq = jnp.exp(-math.log(10000.0) * jnp.arange(HEAD // 2, dtype=F32) / (HEAD // 2))
    rope_angle = in_doc.astype(F32)[:, None] * rope_freq[None, :]
    cosine, sine = jnp.cos(rope_angle), jnp.sin(rope_angle)
    cosine = jnp.concatenate([cosine] * 4, axis=1)
    sine = jnp.concatenate([-sine, sine] * 2, axis=1)
    window_start = token_start - (blk_place - BACK) * block_len
    tiles = block_len // TILE
    edges = jnp.stack(
        [window_start[::TILE], window_start[TILE - 1 :: TILE]], axis=1
    ).reshape(2 * tiles)
    meta = jnp.concatenate([odd[None].astype(jnp.int32), edges.astype(jnp.int32)])

    rest = []
    for g in range(groups):
        kv = slice(firsts[g] * HEAD, (firsts[g] + 2) * HEAD)
        rest += [
            w_key[:, kv],
            w_value[:, kv],
            norm1_gain[:, None],
            norm2_gain[:, None],
            jnp.zeros((w_rows, 126), BF),
        ]
    rest = jnp.concatenate(rest, axis=1).reshape(w_rows, groups, COLS_Q)
    rest = jnp.swapaxes(rest, 0, 1)
    query_row = jnp.concatenate([query_gain, query_gain]).astype(F32)[None, :]
    key_row = jnp.concatenate([key_gain, key_gain]).astype(F32)[None, :]
    (
        wide,
        queries,
        kv_window,
        raw,
        normed_one,
        w_in,
        top_far,
        w_blk,
        slab,
        slab_next,
        down_next,
        toks,
        gains,
    ) = first(
        tokens,
        w_query,
        rest,
        w_gate,
        w_up,
        w_down,
        w_out,
        cotangent,
        cosine,
        sine,
        query_row,
        key_row,
    )
    slabs, downs = [slab, slab_next], [w_down, down_next]
    for _ in range(line - 4):
        slabs.append(ring(slabs[-1], 2))
        downs.append(ring(downs[-1], 2))
    w_own = w_blk.reshape(q_cols, width)
    slabs, downs, w_own, top_far, top_own, queries = sync(
        slabs, downs, w_own, top_far, cotangent, queries
    )
    slabs.append(ring(slabs[-1], 2))
    downs.append(ring(downs[-1], 2))
    w_far = swap(w_own, "head", 2)
    top_across = swap(top_own, "blk", 1)
    top_corner = swap(top_far, "blk", 1)
    kept, attn_out = attend(meta, wide, kv_window, window_start[:, None])
    kept, attn_out, slabs, downs, w_far, top_across, top_corner = sync(
        kept, attn_out, slabs, downs, w_far, top_across, top_corner
    )
    if ff_rows % 16:
        downs.append(ring(downs[-1], 2))
        w_d = jnp.zeros((line, ff_rows, width), BF)
        for step, part in enumerate(downs):
            w_d = put(w_d, part, (blk_place // 2 - step) % line)
        downs = [w_d.reshape(ff_cols, width)]
    attn_out = attn_out.reshape(groups, tok_rows, q_cols)

    (
        resid,
        grad_resid,
        grad_attn,
        mixed,
        grad_mix,
        _,
        _,
        _,
        gu_parts,
        gu_moved,
        down_parts,
        weight_own,
        weight_in,
        out_own,
        out_far,
        out_across,
        out_corner,
        grad_gain_two,
    ) = middle(
        attn_out,
        tokens,
        w_own,
        w_far,
        gains[1:2],
        (cotangent, top_far, top_across, top_corner),
        slabs,
        downs,
    )
    down_parts = down_parts.reshape(line, ff_rows, width)
    gu_parts = gu_parts.reshape(groups, line, 2 * w_rows, 2 * ff_cols)
    down_sum = LineScatter(lambda p: take(down_parts, p))
    gu_sum = LineScatter(lambda p: take(gu_parts, p, 1))
    gu_sum.total = gu_moved
    gu_sum.add()
    down_sum.ahead(line - 4)
    gu_sum.ahead(line - 4)
    down_moved, gu_moved = down_sum.send(), gu_sum.send()

    out_far = swap(out_far, "head", 2)
    out_across = swap(out_across, "blk", 1)
    out_corner = lax.ppermute(
        out_corner,
        ("head", "blk"),
        [(i, (i // blocks ^ 2) * blocks + (i % blocks ^ 1)) for i in range(groups * blocks)],
    )
    back = functools.partial(
        attend_back,
        meta=meta,
        wide=wide,
        queries=queries,
        kv=kv_window,
        kept=kept,
        grads=grad_mix.reshape(block_len, q_cols),
        starts=window_start[None, :],
    )
    four = back(0)
    four, down_moved, gu_moved, out_far, out_across, out_corner, kv_window = sync(
        four, down_moved, gu_moved, out_far, out_across, out_corner, kv_window
    )
    down_sum.total, gu_sum.total = down_moved, gu_moved
    down_sum.add()
    gu_sum.add()
    gu_moved = gu_sum.send()
    pair_four = swap(four[2], "blk", 1)
    slab_far = swap((weight_own[1].astype(F32) + weight_in[1].astype(F32)).astype(BF), "head", 2)
    two = back(1, kv=kv_window)
    four, two, gu_moved, pair_four, slab_far = sync(four, two, gu_moved, pair_four, slab_far)
    out_act = (
        resid
        + out_own.astype(F32)
        + out_far.astype(F32)
        + out_across.astype(F32)
        + out_corner.astype(F32)
    ).astype(BF)
    out_slab = weight_own[0].astype(F32) + weight_in[0].astype(F32) + slab_far.astype(F32)
    out_slab = out_slab.astype(BF).reshape(blocks, w_out.shape[0], width)
    (
        d_tokens,
        d_w_query,
        d_w_key,
        d_w_value,
        norm_gains,
        d_w_gate,
        d_w_up,
        d_w_down,
        d_w_out,
        head_gains,
    ) = last(
        (four[0], two[0]),
        (four[1], two[1]),
        two[2],
        (four[3], two[3]),
        pair_four,
        raw,
        cosine,
        sine,
        query_row,
        key_row,
        normed_one,
        w_in,
        toks,
        gains,
        grad_gain_two,
        gu_moved,
        gu_parts,
        down_sum.total.astype(BF),
        down_parts,
        out_slab,
        grad_resid,
    )
    gain_sums = head_gains[:2, :HEAD] + head_gains[:2, HEAD:]
    d_norm1_gain, d_norm2_gain = norm_gains[:, 0], norm_gains[:, 1]
    return (
        out_act,
        d_tokens,
        d_norm1_gain,
        d_w_query,
        d_w_key,
        d_w_value,
        gain_sums[0],
        gain_sums[1],
        d_w_out,
        d_norm2_gain,
        d_w_gate,
        d_w_up,
        d_w_down,
    )


def solution(mesh):
    by_token = P(("blk", "head"), None)
    by_row = P(("head", "blk"), None)
    by_entry = P(("head", "blk"))
    in_specs = (
        by_token,
        P(),
        by_entry,
        by_row,
        by_row,
        by_row,
        P(),
        P(),
        by_row,
        by_entry,
        by_row,
        by_row,
        by_row,
        by_token,
    )
    out_specs = (
        by_token,
        by_token,
        by_entry,
        by_row,
        by_row,
        by_row,
        P(),
        P(),
        by_row,
        by_entry,
        by_row,
        by_row,
        by_row,
    )
    return jax.shard_map(shards, mesh=mesh, in_specs=in_specs, out_specs=out_specs, check_vma=False)
```
